32 devices in a mesh: comp: 2 (over x), sect: 4 (over y, core), slab: 4 (over z).
Axes of the slice: x: 2, y: 2, z: 4, core: 2. Of those that a mesh axis runs over, the one named last changes fastest.
Arguments:
- spectrum: float32 [1296, 256, 512], P('comp', 'slab', 'sect'), may hold values from 0 to 1
- land_mask: int32 [256, 512], P('slab', 'sect'), may hold values 0 or 1
- ice_mask: int32 [256, 512], P('slab', 'sect'), may hold values 0 or 1
- wind_u: float32 [256, 512], P('slab', 'sect'), may hold values from -6 to 6
- wind_v: float32 [256, 512], P('slab', 'sect'), may hold values from -6 to 6
- depth: float32 [256, 512], P('slab', 'sect'), may hold values from 2 to 20
Outputs:
- damped: float32 [1296, 256, 512], P('comp', 'slab', 'sect')
- level: float32 [256, 512], P('slab', 'sect')
The draws below stay inside these ranges and needn't reach their ends.
All inputs are finite; a program needn't handle non-finite values. No bound on the sum of `land_mask` or of `ice_mask` on one device may be relied on, other than what follows from the above.
Results may differ from the reference program's by a relative error of at most 0.00011.
Values sent between devices are 32-bit elements; how exact they have to be, the bound alone decides.
No kernel may reach another device: no remote copies, remote signals or barrier semaphores. Data moves between devices by JAX's collectives and lax.ppermute only.
A program may use at most 192 MiB of HBM per device.

```python
import math
import jax
import jax.numpy as jnp
from jax import lax

ND = 36
NF = 36
STEPS = 2
JAC = 4
K = 1296
NX = 256
NY = 512


def place_ends(entries, own_key, smallest, largest):
    longest = entries.shape.index(max(entries.shape))
    spots = []
    for shift in (0, 1):
        where = [jax.random.randint(jax.random.fold_in(own_key, axis), (), 0, length) for axis, length in enumerate(entries.shape)]
        where[longest] = (where[longest] + shift) % entries.shape[longest]
        spots.append(tuple(where))
    return entries.at[spots[0]].set(smallest).at[spots[1]].set(largest)


def block_levels(own_key, shape, pieces, smallest, high):
    level = 1.0
    for axis_at, parts in pieces:
        draws = jax.random.uniform(jax.random.fold_in(jax.random.fold_in(own_key, 6), axis_at), (parts,), jnp.float32, smallest / len(pieces), high / len(pieces))
        level = level * jnp.repeat(jnp.exp(draws), shape[axis_at] // parts).reshape((-1,) + (1,) * (len(shape) - 1 - axis_at))
    return level


def noise(rng, shape, scale, bound, split=(), kind=jnp.bfloat16):
    gain = block_levels(rng, shape, split, -0.22, 0.18) if split else 1.0
    result = jax.random.normal(rng, shape, jnp.float32) * scale * gain
    return jnp.minimum(jnp.maximum(result, -bound), bound).astype(kind)


def setup_inputs(seed: int = 0) -> dict:
    keys = jax.random.split(jax.random.key(seed), 7)
    return {
        "spectrum": jnp.clip(1.0 * jax.random.uniform(keys[0], (K, NX, NY), jnp.float32) ** block_levels(keys[0], (K, NX, NY), ((0, 2), (1, 4), (2, 4)), -0.2, 0.2), 0.0, 1.0),
        "land_mask": place_ends((jax.random.randint(keys[1], (NX, NY), 0, 5) < 1).astype(jnp.int32), jax.random.fold_in(keys[1], 1), 0, 1),
        "ice_mask": place_ends((jax.random.randint(keys[2], (NX, NY), 0, 8) < 1).astype(jnp.int32), jax.random.fold_in(keys[2], 1), 0, 1),
        "wind_u": noise(keys[3], (NX, NY), 1.5, 6.0, ((0, 4), (1, 4)), jnp.float32),
        "wind_v": noise(keys[4], (NX, NY), 1.5, 6.0, ((0, 4), (1, 4)), jnp.float32),
        "depth": jnp.clip(jnp.exp(math.log(20.0) - 2.3025851 * jax.random.uniform(keys[5], (NX, NY), jnp.float32) ** block_levels(keys[5], (NX, NY), ((0, 4), (1, 4)), -0.2, 0.2)), 2.0, 20.0),
    }


def tables(index):
    freq_index = (index // ND).astype(jnp.float32)
    angle_index = (index % ND).astype(jnp.float32)
    heading = 2.0 * math.pi * angle_index / ND
    return (jnp.cos(heading), jnp.sin(heading), jnp.power(1.1, -freq_index),
            jnp.power(1.1, freq_index - (NF - 1)), 0.5 + 0.5 * freq_index / (NF - 1))


def upwind(spectra, padded, wet_cells, speed_x, speed_y):
    upper_rows = padded[:, :-2, 1:-1]
    lower_rows = padded[:, 2:, 1:-1]
    left_cells = padded[:, 1:-1, :-2]
    right_cells = padded[:, 1:-1, 2:]
    change = (jnp.maximum(speed_x, 0.0) * (spectra - upper_rows) + jnp.minimum(speed_x, 0.0) * (lower_rows - spectra)
              + jnp.maximum(speed_y, 0.0) * (spectra - left_cells) + jnp.minimum(speed_y, 0.0) * (right_cells - spectra))
    return (spectra - change) * wet_cells


def forcing(spectra, energy, wind_east, wind_north, ice_cover, cosine, sine, high_ratio):
    project = cosine * wind_east + sine * wind_north
    growth = 0.5 * high_ratio * jnp.square(jnp.maximum(project, 0.0)) * (1.0 - ice_cover)
    return spectra * (1.0 + growth) / (1.0 + 2.0 * high_ratio * jnp.square(energy))


def stress_weights(cosine, sine, shoaling):
    return jnp.stack([shoaling * (cosine * cosine + 1.0) - 0.5, shoaling * (sine * sine + 1.0) - 0.5])


def solve(stress):
    padded = jnp.pad(stress, ((0, 0), (1, 1), (1, 1)))
    source_term = -((padded[0, 2:, 1:-1] + padded[0, :-2, 1:-1] - 2.0 * stress[0])
                    + (padded[1, 1:-1, 2:] + padded[1, 1:-1, :-2] - 2.0 * stress[1]))
    surge_level = source_term / 4.5
    for _ in range(JAC):
        neighbours = jnp.pad(surge_level, 1)
        surge_level = (source_term + neighbours[2:, 1:-1] + neighbours[:-2, 1:-1]
                       + neighbours[1:-1, 2:] + neighbours[1:-1, :-2]) / 4.5
    return surge_level


def reference(spectrum, land_mask, ice_mask, wind_u, wind_v, depth):
    total_comp = ND * NF
    wet_cells = (1 - land_mask).astype(jnp.float32)
    ice_cover = ice_mask.astype(jnp.float32)
    cosine, sine, low_ratio, high_ratio, shoaling = tables(jnp.arange(total_comp, dtype=jnp.int32))
    speed_x = (0.7 * low_ratio * cosine).reshape(NF, ND)
    speed_y = (0.7 * low_ratio * sine).reshape(NF, ND)
    blocks = spectrum.reshape(NF, ND, NX, NY)

    def propagate(packed):
        spectra, along_x, along_y = packed
        spectra = spectra * wet_cells
        for _ in range(STEPS):
            padded = jnp.pad(spectra, ((0, 0), (1, 1), (1, 1)))
            spectra = upwind(spectra, padded, wet_cells, along_x[:, None, None], along_y[:, None, None])
        return spectra

    spectra = lax.map(propagate, (blocks, speed_x, speed_y)).reshape(total_comp, NX, NY)
    energy = jnp.sum(spectra, axis=0) / total_comp
    sourced = forcing(spectra, energy, wind_u, wind_v, ice_cover, cosine[:, None, None],
                      sine[:, None, None], high_ratio[:, None, None])
    stress = jnp.einsum("sk,krc->src", stress_weights(cosine, sine, shoaling), sourced,
                        precision=lax.Precision.HIGHEST) / total_comp
    surge_level = solve(stress)
    final_energy = jnp.sum(sourced, axis=0) / total_comp
    damped = sourced / (1.0 + 4.0 * final_energy / (jnp.square(depth + surge_level) + 1.0))
    return damped, surge_level
```

```python
import functools
import math

import jax
import jax.numpy as jnp
import numpy as np
from jax import lax
from jax.experimental import pallas as pl
from jax.experimental.pallas import tpu as pltpu
from jax.sharding import PartitionSpec as P

ND = 36
NF = 36
STEPS = 2
JAC = 4


def extended(cells, sides, width):
    for axis, dim in sides:
        count = lax.axis_size(axis)
        ends = count - 1
        head = lax.slice_in_dim(cells, 0, width, axis=dim)
        tail = lax.slice_in_dim(cells, cells.shape[dim] - width, cells.shape[dim], axis=dim)
        cells = jnp.concatenate(
            [
                lax.ppermute(tail, axis, [(i, (i + 1) % count) for i in range(ends)]),
                cells,
                lax.ppermute(head, axis, [((i + 1) % count, i) for i in range(ends)]),
            ],
            axis=dim,
        )
    return cells


def tables(index):
    freq_index = (index // ND).astype(jnp.float32)
    angle_index = (index % ND).astype(jnp.float32)
    heading = 2.0 * math.pi * angle_index / ND
    return (
        jnp.cos(heading),
        jnp.sin(heading),
        jnp.power(1.1, -freq_index),
        jnp.power(1.1, freq_index - (NF - 1)),
        0.5 + 0.5 * freq_index / (NF - 1),
    )


def column(values):
    return values[:, None, None]


def advect(spectra, wet_cells, speed_x, speed_y):
    padded = extended(spectra, (("slab", 1), ("sect", 2)), 1)
    upper_rows = padded[:, :-2, 1:-1]
    lower_rows = padded[:, 2:, 1:-1]
    left_cells = padded[:, 1:-1, :-2]
    right_cells = padded[:, 1:-1, 2:]
    change = (
        jnp.maximum(speed_x, 0.0) * (spectra - upper_rows)
        + jnp.minimum(speed_x, 0.0) * (lower_rows - spectra)
        + jnp.maximum(speed_y, 0.0) * (spectra - left_cells)
        + jnp.minimum(speed_y, 0.0) * (right_cells - spectra)
    )
    return (spectra - change) * wet_cells


def forcing(spectra, energy, wind_east, wind_north, ice_cover, cosine, sine, high_ratio):
    project = cosine * wind_east + sine * wind_north
    growth = 0.5 * high_ratio * jnp.square(jnp.maximum(project, 0.0)) * (1.0 - ice_cover)
    return spectra * (1.0 + growth) / (1.0 + 2.0 * high_ratio * jnp.square(energy))


def stress_weights(cosine, sine, shoaling):
    return jnp.stack(
        [shoaling * (cosine * cosine + 1.0) - 0.5, shoaling * (sine * sine + 1.0) - 0.5]
    )


def surge_solve(stress):
    padded = extended(stress, (("slab", 1), ("sect", 2)), 1)
    source_term = -(
        padded[0, 2:, 1:-1]
        + padded[0, :-2, 1:-1]
        - 2.0 * stress[0]
        + (padded[1, 1:-1, 2:] + padded[1, 1:-1, :-2] - 2.0 * stress[1])
    )
    surge_level = source_term / 4.5
    for _ in range(JAC):
        neighbours = extended(surge_level, (("slab", 0), ("sect", 1)), 1)
        surge_level = (
            source_term
            + neighbours[2:, 1:-1]
            + neighbours[:-2, 1:-1]
            + neighbours[1:-1, 2:]
            + neighbours[1:-1, :-2]
        ) / 4.5
    return surge_level


def general(spectrum, land_mask, ice_mask, wind_u, wind_v, depth):
    groups = lax.axis_size("comp")
    member = lax.axis_index("comp")
    local_comp, block_rows, block_cols = spectrum.shape
    point_rows = block_rows // groups
    total_comp = ND * NF
    wet_cells = (1 - land_mask).astype(jnp.float32)
    ice_cover = ice_mask.astype(jnp.float32)

    def own_rows(values):
        return lax.dynamic_slice_in_dim(values, member * point_rows, point_rows, values.ndim - 2)

    own_index = member * local_comp + jnp.arange(local_comp, dtype=jnp.int32)
    cosine, sine, low_ratio, high_ratio, shoaling = tables(own_index)
    spectra = spectrum * wet_cells
    for _ in range(STEPS):
        spectra = advect(
            spectra, wet_cells, column(0.7 * low_ratio * cosine), column(0.7 * low_ratio * sine)
        )
    points = lax.all_to_all(spectra, "comp", split_axis=1, concat_axis=0, tiled=True)
    cosine_full, sine_full, _, high_full, shoal_full = tables(
        jnp.arange(total_comp, dtype=jnp.int32)
    )
    energy = jnp.sum(points, axis=0) / total_comp
    sourced = forcing(
        points,
        energy,
        own_rows(wind_u),
        own_rows(wind_v),
        own_rows(ice_cover),
        column(cosine_full),
        column(sine_full),
        column(high_full),
    )
    stress = (
        jnp.einsum(
            "sk,krc->src",
            stress_weights(cosine_full, sine_full, shoal_full),
            sourced,
            precision=lax.Precision.HIGHEST,
        )
        / total_comp
    )
    stress_block = lax.all_gather(stress, "comp", axis=1, tiled=True)
    level_block = surge_solve(stress_block)
    final_energy = jnp.sum(sourced, axis=0) / total_comp
    damped = sourced / (
        1.0 + 4.0 * final_energy / (jnp.square(own_rows(depth) + own_rows(level_block)) + 1.0)
    )
    result = lax.all_to_all(damped, "comp", split_axis=0, concat_axis=1, tiled=True)
    return (result, level_block)


LANES = 128
SUB = 8
CLASSES = 10
KINDS = 5
GROUP = 3
GROUPS = ND // GROUP
CORNERS = 8


def class_of(direction):
    folded = direction % 18
    return folded if folded <= 9 else 18 - folded


def heads_down(direction):
    return direction < 9 or direction >= 27


def heads_right(direction):
    return direction < 18


def row_slot(direction):
    if direction < 9:
        return direction
    return direction - 18 if direction >= 27 else direction - 9


def numpy_tables(members, freqs):
    j = np.arange(members * freqs, dtype=np.float64)
    heading = 2.0 * np.pi * np.arange(ND) / ND
    cosine, sine = np.cos(heading), np.sin(heading)
    low = 1.1 ** (-j)
    high = 1.1 ** (j - (NF - 1))
    shoal = 0.5 + 0.5 * j / (NF - 1)
    step_x = 0.7 * low[:, None] * np.abs(cosine)
    step_y = 0.7 * low[:, None] * np.abs(sine)
    keep = 1.0 - step_x - step_y
    alpha, beta, scale = step_x / keep, step_y / keep, keep * keep
    classes = np.arange(CLASSES)
    square = np.broadcast_to(cosine * cosine, alpha.shape)
    scalars = np.stack(
        [
            alpha[:, classes],
            beta[:, classes],
            scale[:, classes],
            np.broadcast_to(high[:, None], (j.size, CLASSES)),
            np.broadcast_to(shoal[:, None], (j.size, CLASSES)),
        ],
        axis=-1,
    ).astype(np.float32)

    kinds = np.stack(
        [
            2.0 * beta,
            beta * beta,
            alpha * beta,
            scale,
            scale * square,
            np.broadcast_to(high[:, None], alpha.shape),
            np.broadcast_to(cosine, alpha.shape),
            np.broadcast_to(sine, alpha.shape),
        ]
    )
    lanes = np.zeros((members, GROUPS, 8, LANES), np.float32)
    packed = kinds.reshape(8, members, freqs, GROUPS, GROUP)
    packed = np.repeat(packed.transpose(1, 3, 0, 4, 2), 2, axis=-1)
    lanes[..., : GROUP * 2 * freqs] = packed.reshape(members, GROUPS, 8, -1)

    rows = np.stack(
        [2.0 * alpha, alpha * alpha, alpha * beta, scale, np.broadcast_to(high[:, None], alpha.shape)]
    )[:, :, classes]
    rows = rows.reshape(5, members, freqs, CLASSES).transpose(1, 3, 0, 2)
    rows = np.broadcast_to(rows[..., None], rows.shape + (LANES,)).astype(np.float32)
    squares = (cosine * cosine)[classes].astype(np.float32)
    return np.concatenate([scalars.reshape(-1), squares]), lanes, rows


def iota(shape, axis):
    return lax.broadcasted_iota(jnp.int32, shape, axis)


def spread(values, column):
    return jnp.broadcast_to(values[:, column : column + 1], values.shape)


def shift_rows(values, step):
    rows = values.shape[0]
    edge = 0 if step > 0 else rows - 1
    moved = pltpu.roll(values, step % rows, 0)
    return jnp.where(iota(values.shape, 0) == edge, 0.0, moved)


def shift_lanes(values, step):
    lanes = values.shape[1]
    edge = 0 if step > 0 else lanes - 1
    moved = pltpu.roll(values, step % lanes, 1)
    return jnp.where(iota(values.shape, 1) == edge, 0.0, moved)


def slot_base(quadrant):
    return (0, 9, 9, 18)[quadrant]


def class_index(direction):
    folded = lax.rem(direction, 18)
    return jnp.where(folded <= 9, folded, 18 - folded)


def pack_kernel(
    freqs, member_ref, scalar_ref, lanes_ref, land_ref, ice_ref, east_ref, north_ref, spectrum_ref,
    kept_ref, growth_ref, wet_ref, right_ref, left_ref, down_ref, up_ref, packed_ref, sems,
):
    member = member_ref[0]

    def fetch(group):
        part = (slice(None), pl.ds(group * GROUP, GROUP))
        return pltpu.make_async_copy(spectrum_ref.at[part], kept_ref.at[part], sems.at[group])

    for group in range(GROUPS):
        fetch(group).start()

    wet_cells = (1 - land_ref[...]).astype(jnp.float32)
    wet_ref[...] = wet_cells
    open_water = 0.5 * (1.0 - ice_ref[...].astype(jnp.float32))
    shape = wet_cells.shape
    rows = shape[0]
    tiles = rows // SUB
    for direction in range(ND):
        angle = 2.0 * math.pi * direction / ND
        project = math.cos(angle) * east_ref[...] + math.sin(angle) * north_ref[...]
        growth_ref[direction] = open_water * jnp.square(jnp.maximum(project, 0.0))

    lane = iota(shape, 1)
    even = lane % 2 == 0
    tile_lane = iota((SUB, LANES), 1)
    down_ref[pl.ds(2 * 18 * freqs, CORNERS), :] = jnp.zeros((CORNERS, LANES), jnp.float32)
    up_ref[pl.ds(2 * 18 * freqs, CORNERS), :] = jnp.zeros((CORNERS, LANES), jnp.float32)

    for quadrant in range(4):
        to_right, to_down = quadrant in (0, 1), quadrant in (0, 3)
        side = 1 if to_right else -1
        fore = 1 if to_down else -1
        row_start = rows - SUB if to_down else 0
        row_near = SUB - 1 if to_down else 0
        wet_rows = wet_cells[row_start : row_start + SUB, :]
        row_out = down_ref if to_down else up_ref
        ahead, behind = (LANES - 1, LANES - 2) if to_right else (0, 1)
        wet_near, wet_far = spread(wet_cells, ahead), spread(wet_cells, behind)
        near_even = not to_right
        wet_packed = jnp.where(even == near_even, wet_near, wet_far)

        def one_group(index, carry):
            group = quadrant * GROUP + index
            fetch(group).wait()
            packed = [jnp.zeros((SUB, LANES), jnp.float32) for _ in range(tiles)]
            for i in range(GROUP):
                direction = group * GROUP + i
                kind = class_index(direction)
                row_values = []
                for j in range(freqs):
                    base = ((member * freqs + j) * CLASSES + kind) * KINDS
                    alpha, beta = scalar_ref[base], scalar_ref[base + 1]
                    place = i * 2 * freqs + 2 * j
                    here = (tile_lane >= place) & (tile_lane < place + 2)
                    turn = (place + 2 if to_right else place) % LANES
                    for tile in range(tiles):
                        cells = kept_ref[j, direction, tile * SUB : (tile + 1) * SUB, :]
                        packed[tile] = jnp.where(here, pltpu.roll(cells, turn, 1), packed[tile])
                        if tile * SUB == row_start:
                            near = cells * wet_rows
                            far = pltpu.roll(near, fore % SUB, 0)
                            beside = shift_lanes(near, side)
                            follow = wet_rows * (alpha * alpha * far + alpha * beta * beside)
                            row_values.append((near, follow))
                slot = (direction - slot_base(quadrant)) * freqs
                for j, (near, follow) in enumerate(row_values):
                    row_out[pl.ds(slot + j, 1), :] = near[row_near : row_near + 1, :]
                    row_out[pl.ds(18 * freqs + slot + j, 1), :] = follow[row_near : row_near + 1, :]
            for tile in range(tiles):
                packed_ref[tile * SUB : (tile + 1) * SUB, :] = packed[tile]
            values = packed_ref[...] * wet_packed
            near = pltpu.roll(values, 1 if near_even else LANES - 1, 1)
            table = lanes_ref[member, group]
            follow = wet_near * (table[1:2] * values + table[2:3] * shift_rows(near, fore))
            message = jnp.where(even == near_even, values, follow)
            message = jnp.where(lane == LANES - 1, wet_near, message)
            if to_right:
                right_ref[group] = message
            else:
                left_ref[group - GROUPS // 2] = message
            return carry

        lax.fori_loop(0, GROUP, one_group, 0)


def corner_kernel(
    freqs, wet_ref, right_ref, left_ref, down_in, up_in, down_ref, up_ref, rows_ref, sems
):
    rows = wet_ref.shape[0]
    last = iota((1, LANES), 1) == LANES - 1
    rows_ref[...] = jnp.zeros_like(rows_ref)
    for which, row in ((0, rows - 1), (1, 0)):
        for i in range(6):
            source = right_ref if i < 3 else left_ref
            if which == 0:
                index = i if i < 3 else i
            else:
                index = i + 3 if i < 3 else i - 3
            column = 0 if i < 3 else LANES - 1
            own = jnp.broadcast_to(wet_ref[row : row + 1, column : column + 1], (1, LANES))
            rows_ref[which, i : i + 1, :] = jnp.where(last, own, source[index, row : row + 1, :])
    start = 2 * 18 * freqs
    copies = [
        pltpu.make_async_copy(
            rows_ref.at[which], ref.at[pl.ds(start, CORNERS), :], sems.at[which]
        )
        for which, ref in ((0, down_ref), (1, up_ref))
    ]
    for copy in copies:
        copy.start()
    for copy in copies:
        copy.wait()


def main_kernel(
    freqs, squares, member_ref, scalar_ref, wet_ref, growth_ref, kept_in, kept_ref, a_ref, b_ref,
    energy_ref, first_ref,
):
    member = member_ref[0]
    rows = wet_ref.shape[0]
    tiles = rows // SUB
    per_freq = CLASSES - 1
    last = freqs * per_freq - 1
    lane = iota((SUB, LANES), 1)
    sub = iota((SUB, LANES), 0)
    not_first = jnp.where(lane == 0, 0.0, 1.0)
    not_last = jnp.where(lane == LANES - 1, 0.0, 1.0)
    top, bottom = sub == 0, sub == SUB - 1
    zero = jnp.zeros((SUB, LANES), jnp.float32)
    energy_ref[...] = jnp.zeros_like(energy_ref)
    a_ref[...] = jnp.zeros_like(a_ref)
    b_ref[...] = jnp.zeros_like(b_ref)

    def tile_at(tile):
        return pl.ds(tile * SUB, SUB)

    def unfold(item):
        j = lax.div(item, per_freq)
        index = lax.rem(item, per_freq)
        flat = index == 0
        directions = (
            index,
            jnp.where(flat, 9, 18 - index),
            18 + index,
            jnp.where(flat, 27, 36 - index),
        )
        kinds = (index, jnp.where(flat, 9, index))
        bases = [((member * freqs + j) * CLASSES + kind) * KINDS for kind in kinds]
        return j, directions, kinds, bases

    def step(cells, quadrant, bases):
        base = bases[quadrant % 2]
        alpha, beta = scalar_ref[base], scalar_ref[base + 1]
        to_down, to_right = quadrant in (0, 3), quadrant in (0, 1)
        turn, edge = (1, top) if to_down else (SUB - 1, bottom)
        side = 1 if to_right else LANES - 1
        across = beta * (not_first if to_right else not_last)
        turned = [pltpu.roll(values, turn, 0) for values in cells]
        result = []
        for tile in range(tiles):
            source = tile - 1 if to_down else tile + 1
            before = turned[source] if 0 <= source < tiles else zero
            ahead = jnp.where(edge, before, turned[tile])
            result.append(
                cells[tile] + alpha * ahead + across * pltpu.roll(cells[tile], side, 1)
            )
        return result

    def load_cells(j, directions):
        return [[kept_in[j, d, tile_at(t), :] for t in range(tiles)] for d in directions]

    def first_step(loaded, bases):
        stepped = []
        for quadrant in range(4):
            cells = [loaded[quadrant][t] * wet_ref[tile_at(t), :] for t in range(tiles)]
            stepped.append(
                [wet_ref[tile_at(t), :] * v for t, v in enumerate(step(cells, quadrant, bases))]
            )
        return stepped

    def store_first(slot, stepped):
        for quadrant in range(4):
            for tile in range(tiles):
                first_ref[slot, quadrant, tile_at(tile), :] = stepped[quadrant][tile]

    j, directions, kinds, bases = unfold(jnp.int32(0))
    store_first(0, first_step(load_cells(j, directions), bases))

    def body(item, carry):
        slot = lax.rem(item, 2)
        j, directions, kinds, bases = unfold(item)
        ahead_j, ahead_directions, _, ahead_bases = unfold(jnp.minimum(item + 1, last))
        first = [
            [first_ref[slot, quadrant, tile_at(t), :] for t in range(tiles)]
            for quadrant in range(4)
        ]
        loaded = load_cells(ahead_j, ahead_directions)
        at = [pl.ds(pl.multiple_of(j * rows, SUB) + t * SUB, SUB) for t in range(tiles)]
        growth = [[growth_ref[d, tile_at(t), :] for t in range(tiles)] for d in directions]
        totals = [(energy_ref[tile_at(t), :], a_ref[at[t], :], b_ref[at[t], :]) for t in range(tiles)]

        second = [step(first[quadrant], quadrant, bases) for quadrant in range(4)]
        scale, high = scalar_ref[bases[0] + 2], scalar_ref[bases[0] + 3]
        square_x, square_y = scalar_ref[squares + kinds[0]], scalar_ref[squares + kinds[1]]
        scaled_high = scale * high
        results = []
        for t in range(tiles):
            energy, whole, along = totals[t]
            plain_x = scale * (second[0][t] + second[2][t])
            plain_y = scale * (second[1][t] + second[3][t])
            grown_x = plain_x + scaled_high * (
                growth[0][t] * second[0][t] + growth[2][t] * second[2][t]
            )
            grown_y = plain_y + scaled_high * (
                growth[1][t] * second[1][t] + growth[3][t] * second[3][t]
            )
            results.append(
                (
                    energy + (plain_x + plain_y),
                    whole + (grown_x + grown_y),
                    along + (square_x * grown_x + square_y * grown_y),
                )
            )
        stepped = first_step(loaded, ahead_bases)

        for t in range(tiles):
            energy_ref[tile_at(t), :], a_ref[at[t], :], b_ref[at[t], :] = results[t]
        for quadrant, direction in enumerate(directions):
            for t in range(tiles):
                kept_ref[j, direction, tile_at(t), :] = second[quadrant][t]
        store_first(1 - slot, stepped)
        return carry

    lax.fori_loop(0, last + 1, body, 0)


def border_kernel(
    freqs, member_ref, lanes_ref, table_ref, wet_ref, ice_ref, east_ref, north_ref, growth_ref,
    right_ref, left_ref, down_ref, up_ref, a_in, b_in, energy_in,
    a_ref, b_ref, energy_ref, columns_ref, edges_ref,
):
    member = member_ref[0]
    wet_cells = wet_ref[...]
    shape = wet_cells.shape
    rows = shape[0]
    lane = iota(shape, 1)
    row = iota(shape, 0)
    even = lane % 2 == 0
    used = lane < GROUP * 2 * freqs
    a_ref[...] = a_in[...]
    b_ref[...] = b_in[...]
    energy_ref[...] = energy_in[...]
    start = 2 * 18 * freqs

    for to_right in (True, False):
        near_column, far_column = (0, 1) if to_right else (LANES - 1, LANES - 2)
        near_even = to_right
        wet_near, wet_far = spread(wet_cells, near_column), spread(wet_cells, far_column)

        def packed_field(values):
            return jnp.where(
                even == near_even, spread(values, near_column), spread(values, far_column)
            )

        east, north = packed_field(east_ref[...]), packed_field(north_ref[...])
        open_water = 0.5 * (1.0 - packed_field(ice_ref[...].astype(jnp.float32)))
        sums = [jnp.zeros(shape, jnp.float32) for _ in range(3)]
        for index in range(GROUPS // 2):
            group = index if to_right else index + GROUPS // 2
            to_down = heads_down(group * GROUP)
            fore = 1 if to_down else -1
            message = (right_ref if to_right else left_ref)[index]
            table = lanes_ref[member, group]
            entered = pltpu.roll(message, LANES - 1 if near_even else 1, 1)
            corner_index = index if to_down else (
                index - 3 if to_right else index + 3
            )
            corner = (down_ref if to_down else up_ref)[pl.ds(start + corner_index, 1), :]
            edge = 0 if to_down else rows - 1
            paths = corner[:, LANES - 1 :] + message[edge : edge + 1, LANES - 1 :]
            corner = pltpu.roll(
                jnp.broadcast_to(corner, (SUB, LANES)), LANES - 1 if near_even else 1, 1
            )[0:1]
            corner = jnp.broadcast_to(paths, (1, LANES)) * corner
            diagonal = shift_rows(wet_near * entered, fore)
            diagonal = jnp.where(row == edge, jnp.broadcast_to(corner, shape), diagonal)
            near = wet_near * (table[0:1] * entered + message + table[2:3] * diagonal)
            far = wet_near * wet_far * (table[1:2] * message)
            change = jnp.where(used, jnp.where(even == near_even, near, far), 0.0)
            columns_ref[group] = change
            project = table[6:7] * east + table[7:8] * north
            grown = change * (1.0 + table[5:6] * (open_water * jnp.square(jnp.maximum(project, 0.0))))
            sums[0] += table[3:4] * change
            sums[1] += table[3:4] * grown
            sums[2] += table[4:5] * grown
        width = 2 * freqs
        sums = [
            part + pltpu.roll(part, LANES - width, 1) + pltpu.roll(part, LANES - 2 * width, 1)
            for part in sums
        ]
        target = 0 if to_right else LANES - 2
        inside = (lane >= target) & (lane < target + 2)

        energy = jnp.zeros(shape, jnp.float32)
        for j in range(freqs):
            turn = (target - 2 * j) % LANES
            block = slice(j * rows, (j + 1) * rows)
            place = [jnp.where(inside, pltpu.roll(part, turn, 1), 0.0) for part in sums]
            a_ref[block, :] += place[1]
            b_ref[block, :] += place[2]
            energy = energy + place[0]
        energy_ref[...] += energy

    for to_down in (True, False):
        near_row, far_row = (0, 1) if to_down else (rows - 1, rows - 2)
        message_ref = down_ref if to_down else up_ref
        wet_near = wet_cells[near_row : near_row + 1, :]
        wet_both = wet_near * wet_cells[far_row : far_row + 1, :]
        directions = [d for d in range(ND) if heads_down(d) == to_down]
        totals = [jnp.zeros((freqs, LANES), jnp.float32) for _ in range(6)]
        for direction in directions:
            slot = row_slot(direction) * freqs
            entered = message_ref[slot : slot + freqs, :]
            follow = message_ref[18 * freqs + slot : 18 * freqs + slot + freqs, :]
            table = table_ref.at[member, class_of(direction)]
            side = 1 if heads_right(direction) else -1
            diagonal = shift_lanes(wet_near * entered, side)
            near = wet_near * (table[0] * entered + follow + table[2] * diagonal)
            far = wet_both * (table[1] * entered)
            square = math.cos(2.0 * math.pi * direction / ND) ** 2
            for place, (change, at) in enumerate(((near, near_row), (far, far_row))):
                edges_ref[(0 if to_down else 2) + place, slot : slot + freqs, :] = change
                growth = growth_ref[direction, at : at + 1, :]
                plain = table[3] * change
                grown = plain * (1.0 + table[4] * growth)
                totals[3 * place] += plain
                totals[3 * place + 1] += grown
                totals[3 * place + 2] += square * grown
        for place, at in enumerate((near_row, far_row)):
            energy_ref[at : at + 1, :] += jnp.sum(totals[3 * place], axis=0, keepdims=True)
            picked = pl.ds(at, freqs, stride=rows)
            a_ref[picked, :] += totals[3 * place + 1]
            b_ref[picked, :] += totals[3 * place + 2]


def stress_kernel(
    freqs, member_ref, scalar_ref, wet_ref, a_ref, b_ref, own_ref, other_ref, sums_ref, square_ref
):
    member = member_ref[0]
    wet_cells = wet_ref[...]
    rows = wet_cells.shape[0]
    energy = wet_cells * (own_ref[...] + other_ref[...]) / (ND * NF)
    square = jnp.square(energy)
    square_ref[...] = square

    def add(j, sums):
        base = (member * freqs + j) * CLASSES * KINDS
        high, shoal = scalar_ref[base + 3], scalar_ref[base + 4]
        block = pl.ds(pl.multiple_of(j * rows, SUB), rows)
        ratio = wet_cells / (1.0 + (2.0 * high) * square)
        whole = ratio * a_ref[block, :]
        along = ratio * b_ref[block, :]
        return (
            sums[0] + (shoal * along + (shoal - 0.5) * whole),
            sums[1] + ((2.0 * shoal - 0.5) * whole - shoal * along),
            sums[2] + whole,
        )

    zero = jnp.zeros(wet_cells.shape, jnp.float32)
    sums = lax.fori_loop(0, freqs, add, (zero, zero, zero))
    for index in range(3):
        sums_ref[index] = sums[index] / (ND * NF)


SLOTS = 3


def final_kernel(
    freqs, member_ref, scalar_ref, inside_ref, wet_ref, depth_ref, square_ref, sums_ref, left_ref,
    right_ref, above_ref, below_ref, growth_ref, kept_ref, columns_ref, edges_ref,
    result_ref, level_ref, ratio_ref, ring_ref, sems,
):
    member = member_ref[0]
    wet_cells = wet_ref[...]
    rows = wet_cells.shape[0]
    low_half = iota((rows, LANES), 1) < LANES // 2

    def framed(index):
        block = sums_ref[index]
        beside = jnp.where(low_half, right_ref[index], left_ref[index])
        middle = jnp.concatenate([block, beside], axis=1)
        return jnp.concatenate([middle, below_ref[index], above_ref[index]], axis=0)

    def around(values, axis):
        size = values.shape[axis]
        return pltpu.roll(values, 1, axis) + pltpu.roll(values, size - 1, axis)

    stress_x, stress_y = framed(0), framed(1)
    frame = stress_x.shape
    frame_row, frame_lane = iota(frame, 0), iota(frame, 1)
    flag = lambda index: inside_ref[index]
    row_ok = jnp.where(
        frame_row < rows, 1.0, jnp.where(frame_row < rows + SUB, flag(1), flag(0))
    )
    lane_ok = jnp.where(
        frame_lane < LANES, 1.0, jnp.where(frame_lane < LANES + LANES // 2, flag(3), flag(2))
    )
    inside = row_ok * lane_ok / 4.5
    source = -((around(stress_x, 0) - 2.0 * stress_x) + (around(stress_y, 1) - 2.0 * stress_y))
    level = inside * source
    for _ in range(JAC):
        level = inside * (source + around(level, 0) + around(level, 1))
    level = level[:rows, :LANES]
    level_ref[...] = level
    damping = 1.0 + 4.0 * sums_ref[2] / (jnp.square(depth_ref[...] + level) + 1.0)
    square = square_ref[...]
    tiles = rows // SUB
    for j in range(freqs):
        high = scalar_ref[(member * freqs + j) * CLASSES * KINDS + 3]
        ratio = wet_cells / ((1.0 + (2.0 * high) * square) * damping)
        ratio_ref[0, j] = ratio
        ratio_ref[1, j] = high * ratio

    tile_row, tile_lane = iota((SUB, LANES), 0), iota((SUB, LANES), 1)
    quarter = ND // 4

    def send(direction, slot):
        return pltpu.make_async_copy(
            ring_ref.at[slot], result_ref.at[:, pl.ds(direction, 1)], sems.at[slot]
        )

    for quadrant in range(4):
        to_right, to_down = quadrant in (0, 1), quadrant in (0, 3)
        target = 0 if to_right else LANES - 2
        at_side = (tile_lane >= target) & (tile_lane < target + 2)
        bank, edge_tile = (0, 0) if to_down else (2, tiles - 1)
        near_row = tile_row == (0 if to_down else SUB - 1)
        far_row = tile_row == (1 if to_down else SUB - 2)

        def one(index, carry):
            direction = quadrant * quarter + index
            slot = lax.rem(direction, SLOTS)

            @pl.when(direction >= SLOTS)
            def _():
                send(direction - SLOTS, slot).wait()

            kind = class_index(direction)
            group = lax.div(direction, GROUP)
            offset = 2 * freqs * lax.rem(direction, GROUP)
            row_at = (direction - slot_base(quadrant)) * freqs
            aligned = [
                pltpu.roll(
                    columns_ref[group, t * SUB : (t + 1) * SUB, :],
                    lax.rem(target - offset + LANES, LANES),
                    1,
                )
                for t in range(tiles)
            ]
            growth = [growth_ref[direction, t * SUB : (t + 1) * SUB, :] for t in range(tiles)]
            for j in range(freqs):
                scale = scalar_ref[((member * freqs + j) * CLASSES + kind) * KINDS + 2]
                near = jnp.broadcast_to(edges_ref[bank, pl.ds(row_at + j, 1), :], (SUB, LANES))
                far = jnp.broadcast_to(edges_ref[bank + 1, pl.ds(row_at + j, 1), :], (SUB, LANES))
                for t in range(tiles):
                    part = slice(t * SUB, (t + 1) * SUB)
                    entered = pltpu.roll(aligned[t], (LANES - 2 * j) % LANES, 1)
                    value = kept_ref[j, direction, part, :] + jnp.where(at_side, entered, 0.0)
                    if t == edge_tile:
                        value += jnp.where(near_row, near, jnp.where(far_row, far, 0.0))
                    factor = ratio_ref[0, j, part, :] + ratio_ref[1, j, part, :] * growth[t]
                    ring_ref[slot, j, 0, part, :] = value * (scale * factor)
            send(direction, slot).start()
            return carry

        lax.fori_loop(0, quarter, one, 0)
    for direction in range(ND - SLOTS, ND):
        send(direction, direction % SLOTS).wait()


def step_pairs(axis, step):
    count = lax.axis_size(axis)
    return [(i, i + step) for i in range(count) if 0 <= i + step < count]


def neighbour(values, axis, step):
    return lax.ppermute(values, axis, step_pairs(axis, step))


def others_sum(values, axis):
    count = lax.axis_size(axis)
    total = None
    for step in range(1, count):
        part = lax.ppermute(values, axis, [(i, (i + step) % count) for i in range(count)])
        total = part if total is None else total + part
    return jnp.zeros_like(values) if total is None else total


VMEM = pl.BlockSpec(memory_space=pltpu.VMEM)
SMEM = pl.BlockSpec(memory_space=pltpu.SMEM)
HBM = pl.BlockSpec(memory_space=pltpu.HBM)
ANY = pl.BlockSpec(memory_space=pl.ANY)


def in_vmem(*shape):
    return pltpu.VMEM(shape, jnp.float32)


def in_any(*shape):
    return jax.ShapeDtypeStruct(shape, jnp.float32)


def call(kernel, in_specs, out_shape, out_specs, flops, moved, scratch=(), aliases=None, limit=6):
    return pl.pallas_call(
        kernel,
        in_specs=in_specs,
        out_shape=out_shape,
        out_specs=out_specs,
        scratch_shapes=list(scratch),
        input_output_aliases=aliases or {},
        cost_estimate=pl.CostEstimate(flops=flops, bytes_accessed=moved, transcendentals=0),
        compiler_params=pltpu.CompilerParams(vmem_limit_bytes=limit << 20),
    )


def resident(spectrum, land_mask, ice_mask, wind_u, wind_v, depth):
    local_comp, rows, lanes = spectrum.shape
    freqs = local_comp // ND
    members = lax.axis_size("comp")
    member = lax.axis_index("comp").astype(jnp.int32).reshape(1)
    scalars, lane_table, row_table = numpy_tables(members, freqs)
    scalars, lane_table, row_table = map(jnp.asarray, (scalars, lane_table, row_table))
    cells = rows * lanes
    row_message = 2 * 18 * freqs + CORNERS
    block = (freqs, ND, rows, lanes)

    kept, growth, wet, to_right, to_left, to_down, to_up = call(
        functools.partial(pack_kernel, freqs),
        [SMEM, SMEM, VMEM, VMEM, VMEM, VMEM, VMEM, HBM],
        (
            in_vmem(*block),
            in_any(ND, rows, lanes),
            in_any(rows, lanes),
            in_any(GROUPS // 2, rows, lanes),
            in_any(GROUPS // 2, rows, lanes),
            in_any(row_message, lanes),
            in_any(row_message, lanes),
        ),
        (VMEM,) * 7,
        flops=local_comp * cells * 4,
        moved=local_comp * cells * 4,
        scratch=[pltpu.VMEM((rows, lanes), jnp.float32), pltpu.SemaphoreType.DMA((GROUPS,))],
    )(member, scalars, lane_table, land_mask, ice_mask, wind_u, wind_v, pltpu.with_memory_space_constraint(spectrum.reshape(block), pltpu.HBM))

    from_left = neighbour(to_right, "sect", 1)
    from_right = neighbour(to_left, "sect", -1)
    to_down, to_up = call(
        functools.partial(corner_kernel, freqs),
        [VMEM, VMEM, VMEM, ANY, ANY],
        (in_any(row_message, lanes), in_any(row_message, lanes)),
        (ANY, ANY),
        flops=100,
        moved=1 << 15,
        scratch=[pltpu.VMEM((2, CORNERS, lanes), jnp.float32), pltpu.SemaphoreType.DMA((2,))],
        aliases={3: 0, 4: 1},
    )(wet, from_left, from_right, to_down, to_up)
    from_above = neighbour(to_down, "slab", 1)
    from_below = neighbour(to_up, "slab", -1)

    kept, a_sums, b_sums, energy = call(
        functools.partial(main_kernel, freqs, scalars.size - CLASSES),
        [SMEM, SMEM, VMEM, VMEM, VMEM],
        (
            in_vmem(*block),
            in_any(freqs * rows, lanes),
            in_any(freqs * rows, lanes),
            in_any(rows, lanes),
        ),
        (VMEM,) * 4,
        flops=local_comp * cells * 16,
        moved=local_comp * cells * 8,
        scratch=[pltpu.VMEM((2, 4, rows, lanes), jnp.float32)],
        aliases={4: 0},
    )(member, scalars, wet, growth, kept)

    a_sums, b_sums, energy, columns, edges = call(
        functools.partial(border_kernel, freqs),
        [SMEM] + [VMEM] * 14,
        (
            in_any(freqs * rows, lanes),
            in_any(freqs * rows, lanes),
            in_any(rows, lanes),
            in_any(GROUPS, rows, lanes),
            in_any(4, 18 * freqs, lanes),
        ),
        (VMEM,) * 5,
        flops=cells * 1000,
        moved=cells * 400,
        aliases={12: 0, 13: 1, 14: 2},
    )(
        member, lane_table, row_table, wet, ice_mask, wind_u, wind_v, growth,
        from_left, from_right, from_above, from_below, a_sums, b_sums, energy,
    )

    sums, square = call(
        functools.partial(stress_kernel, freqs),
        [SMEM, SMEM] + [VMEM] * 5,
        (in_any(3, rows, lanes), in_any(rows, lanes)),
        (VMEM, VMEM),
        flops=cells * freqs * 12,
        moved=cells * freqs * 8,
    )(member, scalars, wet, a_sums, b_sums, energy, others_sum(energy, "comp"))
    sums = sums + others_sum(sums, "comp")

    stresses = sums[:2]
    left = neighbour(stresses, "sect", 1)
    right = neighbour(stresses, "sect", -1)
    beside = jnp.where(jnp.arange(lanes) < lanes // 2, right, left)
    strip = jnp.concatenate([stresses, beside], axis=2)
    above = neighbour(strip[:, rows - SUB :], "slab", 1)
    below = neighbour(strip[:, :SUB], "slab", -1)
    slab, sect = lax.axis_index("slab"), lax.axis_index("sect")
    inside = jnp.stack(
        [
            slab > 0,
            slab < lax.axis_size("slab") - 1,
            sect > 0,
            sect < lax.axis_size("sect") - 1,
        ]
    ).astype(jnp.float32)

    result, level = call(
        functools.partial(final_kernel, freqs),
        [SMEM, SMEM, SMEM] + [VMEM] * 12,
        (in_any(*block), in_any(rows, lanes)),
        (HBM, VMEM),
        flops=local_comp * cells * 6,
        moved=local_comp * cells * 8,
        scratch=[
            pltpu.VMEM((2, freqs, rows, lanes), jnp.float32),
            pltpu.VMEM((SLOTS, freqs, 1, rows, lanes), jnp.float32),
            pltpu.SemaphoreType.DMA((SLOTS,)),
        ],
    )(
        member, scalars, inside, wet, depth, square, sums, left, right, above, below, growth, kept,
        columns, edges,
    )
    return result.reshape(spectrum.shape), level


def local(spectrum, *fields):
    local_comp, rows, lanes = spectrum.shape
    whole_rings = local_comp % ND == 0 and GROUP * 2 * (local_comp // ND) < LANES - 1
    if whole_rings and lanes == LANES and rows % SUB == 0:
        return resident(spectrum, *fields)
    return general(spectrum, *fields)


def solution(mesh):
    in_specs = (
        P("comp", "slab", "sect"),
        P("slab", "sect"),
        P("slab", "sect"),
        P("slab", "sect"),
        P("slab", "sect"),
        P("slab", "sect"),
    )
    out_specs = (P("comp", "slab", "sect"), P("slab", "sect"))
    return jax.shard_map(local, mesh=mesh, in_specs=in_specs, out_specs=out_specs, check_vma=False)
```

```python
import functools
import math

import jax
import jax.numpy as jnp
import numpy as np
from jax import lax
from jax.experimental import pallas as pl
from jax.experimental.pallas import tpu as pltpu
from jax.sharding import PartitionSpec as P

ND = 36
NF = 36
STEPS = 2
JAC = 4


def extended(cells, sides, width):
    for axis, dim in sides:
        count = lax.axis_size(axis)
        ends = count - 1
        head = lax.slice_in_dim(cells, 0, width, axis=dim)
        tail = lax.slice_in_dim(cells, cells.shape[dim] - width, cells.shape[dim], axis=dim)
        cells = jnp.concatenate(
            [
                lax.ppermute(tail, axis, [(i, (i + 1) % count) for i in range(ends)]),
                cells,
                lax.ppermute(head, axis, [((i + 1) % count, i) for i in range(ends)]),
            ],
            axis=dim,
        )
    return cells


def tables(index):
    freq_index = (index // ND).astype(jnp.float32)
    angle_index = (index % ND).astype(jnp.float32)
    heading = 2.0 * math.pi * angle_index / ND
    return (
        jnp.cos(heading),
        jnp.sin(heading),
        jnp.power(1.1, -freq_index),
        jnp.power(1.1, freq_index - (NF - 1)),
        0.5 + 0.5 * freq_index / (NF - 1),
    )


def column(values):
    return values[:, None, None]


def advect(spectra, wet_cells, speed_x, speed_y):
    padded = extended(spectra, (("slab", 1), ("sect", 2)), 1)
    upper_rows = padded[:, :-2, 1:-1]
    lower_rows = padded[:, 2:, 1:-1]
    left_cells = padded[:, 1:-1, :-2]
    right_cells = padded[:, 1:-1, 2:]
    change = (
        jnp.maximum(speed_x, 0.0) * (spectra - upper_rows)
        + jnp.minimum(speed_x, 0.0) * (lower_rows - spectra)
        + jnp.maximum(speed_y, 0.0) * (spectra - left_cells)
        + jnp.minimum(speed_y, 0.0) * (right_cells - spectra)
    )
    return (spectra - change) * wet_cells


def forcing(spectra, energy, wind_east, wind_north, ice_cover, cosine, sine, high_ratio):
    project = cosine * wind_east + sine * wind_north
    growth = 0.5 * high_ratio * jnp.square(jnp.maximum(project, 0.0)) * (1.0 - ice_cover)
    return spectra * (1.0 + growth) / (1.0 + 2.0 * high_ratio * jnp.square(energy))


def stress_weights(cosine, sine, shoaling):
    return jnp.stack(
        [shoaling * (cosine * cosine + 1.0) - 0.5, shoaling * (sine * sine + 1.0) - 0.5]
    )


def surge_solve(stress):
    padded = extended(stress, (("slab", 1), ("sect", 2)), 1)
    source_term = -(
        padded[0, 2:, 1:-1]
        + padded[0, :-2, 1:-1]
        - 2.0 * stress[0]
        + (padded[1, 1:-1, 2:] + padded[1, 1:-1, :-2] - 2.0 * stress[1])
    )
    surge_level = source_term / 4.5
    for _ in range(JAC):
        neighbours = extended(surge_level, (("slab", 0), ("sect", 1)), 1)
        surge_level = (
            source_term
            + neighbours[2:, 1:-1]
            + neighbours[:-2, 1:-1]
            + neighbours[1:-1, 2:]
            + neighbours[1:-1, :-2]
        ) / 4.5
    return surge_level


def general(spectrum, land_mask, ice_mask, wind_u, wind_v, depth):
    groups = lax.axis_size("comp")
    member = lax.axis_index("comp")
    local_comp, block_rows, block_cols = spectrum.shape
    point_rows = block_rows // groups
    total_comp = ND * NF
    wet_cells = (1 - land_mask).astype(jnp.float32)
    ice_cover = ice_mask.astype(jnp.float32)

    def own_rows(values):
        return lax.dynamic_slice_in_dim(values, member * point_rows, point_rows, values.ndim - 2)

    own_index = member * local_comp + jnp.arange(local_comp, dtype=jnp.int32)
    cosine, sine, low_ratio, high_ratio, shoaling = tables(own_index)
    spectra = spectrum * wet_cells
    for _ in range(STEPS):
        spectra = advect(
            spectra, wet_cells, column(0.7 * low_ratio * cosine), column(0.7 * low_ratio * sine)
        )
    points = lax.all_to_all(spectra, "comp", split_axis=1, concat_axis=0, tiled=True)
    cosine_full, sine_full, _, high_full, shoal_full = tables(
        jnp.arange(total_comp, dtype=jnp.int32)
    )
    energy = jnp.sum(points, axis=0) / total_comp
    sourced = forcing(
        points,
        energy,
        own_rows(wind_u),
        own_rows(wind_v),
        own_rows(ice_cover),
        column(cosine_full),
        column(sine_full),
        column(high_full),
    )
    stress = (
        jnp.einsum(
            "sk,krc->src",
            stress_weights(cosine_full, sine_full, shoal_full),
            sourced,
            precision=lax.Precision.HIGHEST,
        )
        / total_comp
    )
    stress_block = lax.all_gather(stress, "comp", axis=1, tiled=True)
    level_block = surge_solve(stress_block)
    final_energy = jnp.sum(sourced, axis=0) / total_comp
    damped = sourced / (
        1.0 + 4.0 * final_energy / (jnp.square(own_rows(depth) + own_rows(level_block)) + 1.0)
    )
    result = lax.all_to_all(damped, "comp", split_axis=0, concat_axis=1, tiled=True)
    return (result, level_block)


LANES = 128
SUB = 8
CLASSES = 10
KINDS = 5
GROUP = 3
GROUPS = ND // GROUP
CORNERS = 8


def class_of(direction):
    folded = direction % 18
    return folded if folded <= 9 else 18 - folded


def heads_down(direction):
    return direction < 9 or direction >= 27


def heads_right(direction):
    return direction < 18


def row_slot(direction):
    if direction < 9:
        return direction
    return direction - 18 if direction >= 27 else direction - 9


def numpy_tables(members, freqs):
    j = np.arange(members * freqs, dtype=np.float64)
    heading = 2.0 * np.pi * np.arange(ND) / ND
    cosine, sine = np.cos(heading), np.sin(heading)
    low = 1.1 ** (-j)
    high = 1.1 ** (j - (NF - 1))
    shoal = 0.5 + 0.5 * j / (NF - 1)
    step_x = 0.7 * low[:, None] * np.abs(cosine)
    step_y = 0.7 * low[:, None] * np.abs(sine)
    keep = 1.0 - step_x - step_y
    alpha, beta, scale = step_x / keep, step_y / keep, keep * keep
    classes = np.arange(CLASSES)
    square = np.broadcast_to(cosine * cosine, alpha.shape)
    scalars = np.stack(
        [
            alpha[:, classes],
            beta[:, classes],
            scale[:, classes],
            np.broadcast_to(high[:, None], (j.size, CLASSES)),
            np.broadcast_to(shoal[:, None], (j.size, CLASSES)),
        ],
        axis=-1,
    ).astype(np.float32)

    kinds = np.stack(
        [
            2.0 * beta,
            beta * beta,
            alpha * beta,
            scale,
            scale * square,
            np.broadcast_to(high[:, None], alpha.shape),
            np.broadcast_to(cosine, alpha.shape),
            np.broadcast_to(sine, alpha.shape),
        ]
    )
    lanes = np.zeros((members, GROUPS, 8, LANES), np.float32)
    packed = kinds.reshape(8, members, freqs, GROUPS, GROUP)
    packed = np.repeat(packed.transpose(1, 3, 0, 4, 2), 2, axis=-1)
    lanes[..., : GROUP * 2 * freqs] = packed.reshape(members, GROUPS, 8, -1)

    rows = np.stack(
        [2.0 * alpha, alpha * alpha, alpha * beta, scale, np.broadcast_to(high[:, None], alpha.shape)]
    )[:, :, classes]
    rows = rows.reshape(5, members, freqs, CLASSES).transpose(1, 3, 0, 2)
    rows = np.broadcast_to(rows[..., None], rows.shape + (LANES,)).astype(np.float32)
    return scalars.reshape(-1), lanes, rows


def iota(shape, axis):
    return lax.broadcasted_iota(jnp.int32, shape, axis)


def spread(values, column):
    return jnp.broadcast_to(values[:, column : column + 1], values.shape)


def shift_rows(values, step):
    rows = values.shape[0]
    edge = 0 if step > 0 else rows - 1
    moved = pltpu.roll(values, step % rows, 0)
    return jnp.where(iota(values.shape, 0) == edge, 0.0, moved)


def shift_lanes(values, step):
    lanes = values.shape[1]
    edge = 0 if step > 0 else lanes - 1
    moved = pltpu.roll(values, step % lanes, 1)
    return jnp.where(iota(values.shape, 1) == edge, 0.0, moved)


DEPTH = 3


def slot_base(quadrant):
    return (0, 9, 9, 18)[quadrant]


def class_index(direction):
    folded = lax.rem(direction, 18)
    return jnp.where(folded <= 9, folded, 18 - folded)


def pack_kernel(
    freqs, member_ref, lanes_hbm, table_hbm, land_hbm, ice_hbm, east_hbm, north_hbm, spectrum_ref,
    growth_ref, wet_ref, right_ref, left_ref, down_ref, up_ref, edges_ref,
    kept_ref, lanes_ref, table_ref, land_ref, ice_ref, east_ref, north_ref, small_sems, sems,
):
    member = member_ref[0]
    small = [
        pltpu.make_async_copy(source, target, small_sems.at[index])
        for index, (source, target) in enumerate(
            (
                (land_hbm, land_ref),
                (ice_hbm, ice_ref),
                (east_hbm, east_ref),
                (north_hbm, north_ref),
                (lanes_hbm.at[member], lanes_ref),
                (table_hbm.at[member], table_ref),
            )
        )
    ]
    for copy in small:
        copy.start()

    rows = land_ref.shape[0]
    blocks_ref = kept_ref.reshape(freqs, ND, rows, LANES)

    def fetch(group):
        part = (slice(None), pl.ds(group * GROUP, GROUP))
        return pltpu.make_async_copy(spectrum_ref.at[part], blocks_ref.at[part], sems.at[group])

    for group in range(DEPTH):
        fetch(group).start()
    edges_ref[...] = jnp.zeros_like(edges_ref)
    for copy in small:
        copy.wait()

    wet_cells = (1 - land_ref[...]).astype(jnp.float32)
    wet_ref[...] = wet_cells
    open_water = 0.5 * (1.0 - ice_ref[...].astype(jnp.float32))
    shape = wet_cells.shape
    tiles = rows // SUB
    for direction in range(ND):
        angle = 2.0 * math.pi * direction / ND
        project = math.cos(angle) * east_ref[...] + math.sin(angle) * north_ref[...]
        growth_ref[direction] = open_water * jnp.square(jnp.maximum(project, 0.0))

    lane = iota(shape, 1)
    even = lane % 2 == 0
    tile_lane = iota((SUB, LANES), 1)
    down_ref[pl.ds(2 * 18 * freqs, CORNERS), :] = jnp.zeros((CORNERS, LANES), jnp.float32)
    up_ref[pl.ds(2 * 18 * freqs, CORNERS), :] = jnp.zeros((CORNERS, LANES), jnp.float32)

    half = GROUPS // 2
    for to_right in (True, False):
        target_ref = right_ref if to_right else left_ref

        def gather(index, carry):
            group = index + (0 if to_right else half)
            fetch(group).wait()

            @pl.when(group + DEPTH < GROUPS)
            def _():
                fetch(group + DEPTH).start()

            packed = [jnp.zeros((SUB, LANES), jnp.float32) for _ in range(tiles)]
            for i in range(GROUP):
                for j in range(freqs):
                    place = i * 2 * freqs + 2 * j
                    here = (tile_lane >= place) & (tile_lane < place + 2)
                    turn = (place + 2 if to_right else place) % LANES
                    first = pl.multiple_of((j * ND + group * GROUP + i) * rows, SUB)
                    for tile in range(tiles):
                        cells = kept_ref[pl.ds(first + tile * SUB, SUB), :]
                        packed[tile] = jnp.where(here, pltpu.roll(cells, turn, 1), packed[tile])
            for tile in range(tiles):
                target_ref[index, tile * SUB : (tile + 1) * SUB, :] = packed[tile]
            return carry

        lax.fori_loop(0, half, gather, 0)

    pending = []
    for group in range(GROUPS):
        to_right, fore = group < half, 1 if heads_down(group * GROUP) else -1
        ahead, behind = (LANES - 1, LANES - 2) if to_right else (0, 1)
        wet_near, wet_far = spread(wet_cells, ahead), spread(wet_cells, behind)
        near_even = not to_right
        target_ref, index = (right_ref, group) if to_right else (left_ref, group - half)
        values = target_ref[index] * jnp.where(even == near_even, wet_near, wet_far)
        near = pltpu.roll(values, 1 if near_even else LANES - 1, 1)
        table = lanes_ref[group]
        follow = wet_near * (table[1:2] * values + table[2:3] * shift_rows(near, fore))
        message = jnp.where(even == near_even, values, follow)
        pending.append((target_ref, index, jnp.where(lane == LANES - 1, wet_near, message)))
        if group:
            place_ref, index, message = pending.pop(0)
            place_ref[index] = message
    place_ref, index, message = pending.pop()
    place_ref[index] = message

    pending = []
    for direction in range(ND):
        to_down = heads_down(direction)
        near_row, far_row = (rows - 1, rows - 2) if to_down else (0, 1)
        wet_near = wet_cells[near_row : near_row + 1, :]
        wet_far = wet_cells[far_row : far_row + 1, :]
        table = table_ref.at[class_of(direction)]
        near = kept_ref[pl.ds(direction * rows + near_row, freqs, stride=ND * rows), :] * wet_near
        far = kept_ref[pl.ds(direction * rows + far_row, freqs, stride=ND * rows), :] * wet_far
        beside = shift_lanes(near, 1 if heads_right(direction) else -1)
        follow = wet_near * (table[1] * far + table[2] * beside)
        slot = row_slot(direction) * freqs
        pending.append((down_ref if to_down else up_ref, slot, near, follow))
        if len(pending) > 2 or direction == ND - 1:
            for place_ref, slot, near, follow in pending:
                place_ref[slot : slot + freqs, :] = near
                place_ref[18 * freqs + slot : 18 * freqs + slot + freqs, :] = follow
            pending = []


def corner_kernel(
    freqs, wet_ref, right_ref, left_ref, down_in, up_in, _after, down_ref, up_ref, rows_ref, sems
):
    rows = wet_ref.shape[0]
    last = iota((1, LANES), 1) == LANES - 1
    rows_ref[...] = jnp.zeros_like(rows_ref)
    for which, row in ((0, rows - 1), (1, 0)):
        for i in range(6):
            source = right_ref if i < 3 else left_ref
            if which == 0:
                index = i if i < 3 else i
            else:
                index = i + 3 if i < 3 else i - 3
            column = 0 if i < 3 else LANES - 1
            own = jnp.broadcast_to(wet_ref[row : row + 1, column : column + 1], (1, LANES))
            rows_ref[which, i : i + 1, :] = jnp.where(last, own, source[index, row : row + 1, :])
    start = 2 * 18 * freqs
    copies = [
        pltpu.make_async_copy(
            rows_ref.at[which], ref.at[pl.ds(start, CORNERS), :], sems.at[which]
        )
        for which, ref in ((0, down_ref), (1, up_ref))
    ]
    for copy in copies:
        copy.start()
    for copy in copies:
        copy.wait()


AHEAD = 3


def main_kernel(
    freqs, start, stop, member_ref, scalar_ref, wet_ref, growth_ref, spectrum_ref, *refs
):
    if start:
        _after, _kept_in, a_in, b_in, energy_in, *refs = refs
    kept_ref, a_ref, b_ref, energy_ref, ring_ref, sems, *first_refs = refs
    member = member_ref[0]
    nought = jnp.minimum(member, 0)
    rows = wet_ref.shape[0]
    tiles = rows // SUB

    def fetch(j):
        slot = lax.rem(j, AHEAD)
        return pltpu.make_async_copy(spectrum_ref.at[j], ring_ref.at[slot], sems.at[slot])

    for j in range(start, min(start + AHEAD, stop)):
        fetch(jnp.int32(j)).start()

    lane = iota((SUB, LANES), 1)
    sub = iota((SUB, LANES), 0)
    not_first = jnp.where(lane == 0, 0.0, 1.0)
    not_last = jnp.where(lane == LANES - 1, 0.0, 1.0)
    top, bottom = sub == 0, sub == SUB - 1
    energy_ref[...] = energy_in[...] if start else jnp.zeros_like(energy_ref)
    for first_ref in first_refs:
        first_ref[...] = jnp.zeros_like(first_ref)

    def tile_at(tile):
        return pl.ds(tile * SUB, SUB)

    def row_shift(quadrant):
        return -1 if quadrant in (0, 3) else 1

    def parts_of(kind):
        if kind == 0:
            return ((0, 0, 0), (9, 1, 9), (18, 2, 0), (27, 3, 9))
        return ((kind, 0, kind), (18 - kind, 1, kind), (18 + kind, 2, kind), (36 - kind, 3, kind))

    def frequency(j, carry):
        fetch(j).wait()
        slot = lax.rem(j, AHEAD)
        base = (member * freqs + j) * CLASSES * KINDS
        at = [pl.ds(pl.multiple_of(j * rows, SUB) + t * SUB, SUB) for t in range(tiles)]

        def speeds(part):
            at_class = base + part[2] * KINDS
            beta = scalar_ref[at_class + 1]
            return scalar_ref[at_class], beta * (not_first if part[1] in (0, 1) else not_last)

        def beside(cells, quadrant):
            return pltpu.roll(cells, 1 if quadrant in (0, 1) else LANES - 1, 1)

        def first_step(kind):
            parts = parts_of(kind)
            speed = [speeds(part) for part in parts]
            wet = [wet_ref[tile_at(t), :] for t in range(tiles)]
            for (direction, quadrant, _), (alpha, across) in zip(parts, speed):
                shift = row_shift(quadrant)
                edge = top if shift < 0 else bottom
                target = first_refs[kind % 2 * 4 + quadrant]
                cells = [ring_ref[slot, direction, tile_at(t), :] * wet[t] for t in range(tiles)]
                turned = [pltpu.roll(cells[t], -shift % SUB, 0) for t in range(tiles)]
                for t in range(tiles):
                    before = turned[t + shift] if 0 <= t + shift < tiles else 0.0
                    ahead = jnp.where(edge, before, turned[t])
                    after = cells[t] + alpha * ahead + across * beside(cells[t], quadrant)
                    target[tile_at(t + 1), :] = wet[t] * after

        def second_step(kind):
            parts = parts_of(kind)
            scale, high = scalar_ref[base + kind * KINDS + 2], scalar_ref[base + 3]
            scaled_high = scale * high
            speed = [speeds(part) for part in parts]
            for t in range(tiles):
                moved, grown = [], []
                for (direction, quadrant, _), (alpha, across) in zip(parts, speed):
                    source = first_refs[kind % 2 * 4 + quadrant]
                    cells = source[tile_at(t + 1), :]
                    ahead = source[pl.ds((t + 1) * SUB + row_shift(quadrant) + nought, SUB), :]
                    after = cells + alpha * ahead + across * beside(cells, quadrant)
                    kept_ref[j, direction, tile_at(t), :] = after
                    moved.append(after)
                    grown.append(growth_ref[direction, tile_at(t), :] * after)
                if kind == 0:
                    plain_x, plain_y = scale * (moved[0] + moved[2]), scale * (moved[1] + moved[3])
                    grown_x = plain_x + scaled_high * (grown[0] + grown[2])
                    grown_y = plain_y + scaled_high * (grown[1] + grown[3])
                    square = math.cos(0.5 * math.pi) ** 2
                    energy_ref[tile_at(t), :] += plain_x + plain_y
                    a_ref[at[t], :] = grown_x + grown_y
                    b_ref[at[t], :] = grown_x + square * grown_y
                else:
                    plain = scale * ((moved[0] + moved[1]) + (moved[2] + moved[3]))
                    whole = plain + scaled_high * ((grown[0] + grown[1]) + (grown[2] + grown[3]))
                    square = math.cos(2.0 * math.pi * kind / ND) ** 2
                    energy_ref[tile_at(t), :] += plain
                    a_ref[at[t], :] += whole
                    b_ref[at[t], :] += square * whole

        first_step(0)
        for kind in range(CLASSES - 1):
            if kind + 1 < CLASSES - 1:
                first_step(kind + 1)
            second_step(kind)

        @pl.when(j + AHEAD < stop)
        def _():
            fetch(j + AHEAD).start()

        return carry

    lax.fori_loop(start, stop, frequency, 0)


def edge_rows(freqs, to_down, direction, at):
    first = ((0 if to_down else 18) + row_slot(direction)) * freqs * SUB
    return pl.ds(first + at, freqs, stride=SUB)


def enter_kernel(
    freqs, member_ref, lanes_ref, table_ref, wet_ref, right_ref, left_ref, down_ref, up_ref,
    _edges_in, energy_in, columns_ref, edges_ref, energy_ref,
):
    member = member_ref[0]
    wet_cells = wet_ref[...]
    shape = wet_cells.shape
    rows = shape[0]
    lane = iota(shape, 1)
    row = iota(shape, 0)
    even = lane % 2 == 0
    width = 2 * freqs
    used = lane < GROUP * width
    energy = energy_in[...]
    start = 2 * 18 * freqs

    for to_right in (True, False):
        near_column, far_column = (0, 1) if to_right else (LANES - 1, LANES - 2)
        near_even = to_right
        wet_near, wet_far = spread(wet_cells, near_column), spread(wet_cells, far_column)
        total = jnp.zeros(shape, jnp.float32)
        for index in range(GROUPS // 2):
            group = index if to_right else index + GROUPS // 2
            to_down = heads_down(group * GROUP)
            fore = 1 if to_down else -1
            message = (right_ref if to_right else left_ref)[index]
            table = lanes_ref[member, group]
            turn = LANES - 1 if near_even else 1
            entered = pltpu.roll(message, turn, 1)
            corner_index = index if to_down else (index - 3 if to_right else index + 3)
            corner = (down_ref if to_down else up_ref)[pl.ds(start + corner_index, 1), :]
            edge = 0 if to_down else rows - 1
            paths = corner[:, LANES - 1 :] + message[edge : edge + 1, LANES - 1 :]
            corner = pltpu.roll(jnp.broadcast_to(corner, (SUB, LANES)), turn, 1)[0:1]
            corner = jnp.broadcast_to(paths, (1, LANES)) * corner
            diagonal = shift_rows(wet_near * entered, fore)
            diagonal = jnp.where(row == edge, jnp.broadcast_to(corner, shape), diagonal)
            near = wet_near * (table[0:1] * entered + message + table[2:3] * diagonal)
            far = wet_near * wet_far * (table[1:2] * message)
            change = jnp.where(used, jnp.where(even == near_even, near, far), 0.0)
            columns_ref[group] = change
            total += table[3:4] * change
        total += pltpu.roll(total, LANES - width, 1) + pltpu.roll(total, LANES - 2 * width, 1)
        target = 0 if to_right else LANES - 2
        inside = (lane >= target) & (lane < target + 2)
        for j in range(freqs):
            turned = pltpu.roll(total, (target - 2 * j) % LANES, 1)
            energy += jnp.where(inside, turned, 0.0)
    energy_ref[...] = energy

    for to_down in (True, False):
        near_row, far_row = (0, 1) if to_down else (rows - 1, rows - 2)
        message_ref = down_ref if to_down else up_ref
        wet_near = wet_cells[near_row : near_row + 1, :]
        wet_both = wet_near * wet_cells[far_row : far_row + 1, :]
        totals = [jnp.zeros((freqs, LANES), jnp.float32) for _ in range(2)]
        for direction in range(ND):
            if heads_down(direction) != to_down:
                continue
            slot = row_slot(direction) * freqs
            entered = message_ref[slot : slot + freqs, :]
            follow = message_ref[18 * freqs + slot : 18 * freqs + slot + freqs, :]
            table = table_ref.at[member, class_of(direction)]
            side = 1 if heads_right(direction) else -1
            diagonal = shift_lanes(wet_near * entered, side)
            near = wet_near * (table[0] * entered + follow + table[2] * diagonal)
            far = wet_both * (table[1] * entered)
            for place, (change, at) in enumerate(((near, near_row), (far, far_row))):
                edges_ref[edge_rows(freqs, to_down, direction, at % SUB), :] = change
                totals[place] += table[3] * change
        for total, at in zip(totals, (near_row, far_row)):
            energy_ref[at : at + 1, :] += jnp.sum(total, axis=0, keepdims=True)


def entered_kernel(
    freqs, member_ref, lanes_ref, table_ref, ice_ref, east_ref, north_ref, growth_ref, columns_ref,
    edges_ref, a_in, b_in, a_ref, b_ref,
):
    member = member_ref[0]
    shape = ice_ref.shape
    rows = shape[0]
    lane = iota(shape, 1)
    even = lane % 2 == 0
    width = 2 * freqs
    a_ref[...] = a_in[...]
    b_ref[...] = b_in[...]

    for to_right in (True, False):
        near_column, far_column = (0, 1) if to_right else (LANES - 1, LANES - 2)

        def packed_field(values):
            return jnp.where(
                even == to_right, spread(values, near_column), spread(values, far_column)
            )

        east, north = packed_field(east_ref[...]), packed_field(north_ref[...])
        open_water = 0.5 * (1.0 - packed_field(ice_ref[...].astype(jnp.float32)))
        sums = [jnp.zeros(shape, jnp.float32) for _ in range(2)]
        for index in range(GROUPS // 2):
            group = index if to_right else index + GROUPS // 2
            table = lanes_ref[member, group]
            project = table[6:7] * east + table[7:8] * north
            growth = open_water * jnp.square(jnp.maximum(project, 0.0))
            grown = columns_ref[group] * (1.0 + table[5:6] * growth)
            sums[0] += table[3:4] * grown
            sums[1] += table[4:5] * grown
        sums = [
            part + pltpu.roll(part, LANES - width, 1) + pltpu.roll(part, LANES - 2 * width, 1)
            for part in sums
        ]
        target = 0 if to_right else LANES - 2
        inside = (lane >= target) & (lane < target + 2)
        for j in range(freqs):
            turn = (target - 2 * j) % LANES
            block = slice(j * rows, (j + 1) * rows)
            place = [jnp.where(inside, pltpu.roll(part, turn, 1), 0.0) for part in sums]
            a_ref[block, :] += place[0]
            b_ref[block, :] += place[1]

    for to_down in (True, False):
        near_row, far_row = (0, 1) if to_down else (rows - 1, rows - 2)
        totals = [jnp.zeros((freqs, LANES), jnp.float32) for _ in range(4)]
        for direction in range(ND):
            if heads_down(direction) != to_down:
                continue
            table = table_ref.at[member, class_of(direction)]
            square = math.cos(2.0 * math.pi * direction / ND) ** 2
            for place, at in enumerate((near_row, far_row)):
                change = edges_ref[edge_rows(freqs, to_down, direction, at % SUB), :]
                growth = growth_ref[direction, at : at + 1, :]
                grown = (table[3] * change) * (1.0 + table[4] * growth)
                totals[2 * place] += grown
                totals[2 * place + 1] += square * grown
        for place, at in enumerate((near_row, far_row)):
            picked = pl.ds(at, freqs, stride=rows)
            a_ref[picked, :] += totals[2 * place]
            b_ref[picked, :] += totals[2 * place + 1]


def stress_kernel(
    freqs, member_ref, scalar_ref, wet_ref, a_ref, b_ref, own_ref, other_ref, sums_ref, square_ref
):
    member = member_ref[0]
    wet_cells = wet_ref[...]
    rows = wet_cells.shape[0]
    energy = wet_cells * (own_ref[...] + other_ref[...]) / (ND * NF)
    square = jnp.square(energy)
    square_ref[...] = square

    sums = [jnp.zeros(wet_cells.shape, jnp.float32) for _ in range(3)]
    for j in range(freqs):
        base = (member * freqs + j) * CLASSES * KINDS
        high, shoal = scalar_ref[base + 3], scalar_ref[base + 4]
        block = slice(j * rows, (j + 1) * rows)
        ratio = wet_cells / (1.0 + (2.0 * high) * square)
        whole = ratio * a_ref[block, :]
        along = ratio * b_ref[block, :]
        sums[0] += shoal * along + (shoal - 0.5) * whole
        sums[1] += (2.0 * shoal - 0.5) * whole - shoal * along
        sums[2] += whole
    for index in range(3):
        sums_ref[index] = sums[index] / (ND * NF)


def total_kernel(own_ref, other_ref, sums_ref, stress_ref):
    sums_ref[...] = own_ref[...] + other_ref[...]
    stress_ref[...] = sums_ref[0:2]


def strip_kernel(stress_ref, left_ref, right_ref, beside_ref, top_ref, bottom_ref):
    rows = stress_ref.shape[1]
    low_half = iota((rows, LANES), 1) < LANES // 2
    for index in range(2):
        beside = jnp.where(low_half, right_ref[index], left_ref[index])
        beside_ref[index] = beside
        for target, first in ((top_ref, 0), (bottom_ref, rows - SUB)):
            target[index, :, 0:LANES] = stress_ref[index, first : first + SUB, :]
            target[index, :, LANES:] = beside[first : first + SUB, :]


SLOTS = 3


def final_kernel(
    freqs, member_ref, scalar_ref, wet_ref, depth_ref, square_ref, sums_ref, beside_ref, above_ref, below_ref,
    growth_ref, kept_ref, columns_ref, edges_ref,
    result_ref, level_ref, ratio_ref, ring_ref, sems,
):
    member = member_ref[0]
    wet_cells = wet_ref[...]
    rows = wet_cells.shape[0]
    slab, slabs = lax.axis_index("slab"), lax.axis_size("slab")
    sect, sects = lax.axis_index("sect"), lax.axis_size("sect")
    above_ok = jnp.where(slab > 0, 1.0, 0.0)
    below_ok = jnp.where(slab < slabs - 1, 1.0, 0.0)
    left_ok = jnp.where(sect > 0, 1.0, 0.0)
    right_ok = jnp.where(sect < sects - 1, 1.0, 0.0)

    def framed(index):
        middle = jnp.concatenate([sums_ref[index], beside_ref[index]], axis=1)
        return jnp.concatenate([middle, below_ref[index], above_ref[index]], axis=0)

    def around(values, axis):
        size = values.shape[axis]
        return pltpu.roll(values, 1, axis) + pltpu.roll(values, size - 1, axis)

    stress_x, stress_y = framed(0), framed(1)
    frame = stress_x.shape
    frame_row, frame_lane = iota(frame, 0), iota(frame, 1)
    row_ok = jnp.where(frame_row < rows, 1.0, jnp.where(frame_row < rows + SUB, below_ok, above_ok))
    lane_ok = jnp.where(
        frame_lane < LANES, 1.0, jnp.where(frame_lane < LANES + LANES // 2, right_ok, left_ok)
    )
    inside = row_ok * lane_ok / 4.5
    source = -((around(stress_x, 0) - 2.0 * stress_x) + (around(stress_y, 1) - 2.0 * stress_y))
    level = inside * source
    for _ in range(JAC):
        level = inside * (source + around(level, 0) + around(level, 1))
    level = level[:rows, :LANES]
    level_ref[...] = level
    damping = 1.0 + 4.0 * sums_ref[2] / (jnp.square(depth_ref[...] + level) + 1.0)
    square = square_ref[...]
    tiles = rows // SUB
    for j in range(freqs):
        high = scalar_ref[(member * freqs + j) * CLASSES * KINDS + 3]
        ratio = wet_cells / ((1.0 + (2.0 * high) * square) * damping)
        ratio_ref[0, j] = ratio
        ratio_ref[1, j] = high * ratio

    tile_lane = iota((SUB, LANES), 1)
    quarter = ND // 4

    def send(direction, slot):
        return pltpu.make_async_copy(
            ring_ref.at[slot], result_ref.at[:, pl.ds(direction, 1)], sems.at[slot]
        )

    for quadrant in range(4):
        to_right, to_down = quadrant in (0, 1), quadrant in (0, 3)
        target = 0 if to_right else LANES - 2
        at_side = (tile_lane >= target) & (tile_lane < target + 2)
        bank, edge_tile = (0, 0) if to_down else (1, tiles - 1)

        def one(index, carry):
            direction = quadrant * quarter + index
            slot = lax.rem(direction, SLOTS)

            @pl.when(direction >= SLOTS)
            def _():
                send(direction - SLOTS, slot).wait()

            kind = class_index(direction)
            group = lax.div(direction, GROUP)
            offset = 2 * freqs * lax.rem(direction, GROUP)
            row_at = (bank * 18 + direction - slot_base(quadrant)) * freqs
            aligned = [
                pltpu.roll(
                    columns_ref[group, t * SUB : (t + 1) * SUB, :],
                    lax.rem(target - offset + LANES, LANES),
                    1,
                )
                for t in range(tiles)
            ]
            growth = [growth_ref[direction, t * SUB : (t + 1) * SUB, :] for t in range(tiles)]
            def damped(j):
                scale = scalar_ref[((member * freqs + j) * CLASSES + kind) * KINDS + 2]
                result = []
                for t in range(tiles):
                    part = slice(t * SUB, (t + 1) * SUB)
                    entered = pltpu.roll(aligned[t], (LANES - 2 * j) % LANES, 1)
                    value = kept_ref[j, direction, part, :] + jnp.where(at_side, entered, 0.0)
                    if t == edge_tile:
                        edge_at = pl.ds(pl.multiple_of((row_at + j) * SUB, SUB), SUB)
                        value += edges_ref[edge_at, :]
                    factor = ratio_ref[0, j, part, :] + ratio_ref[1, j, part, :] * growth[t]
                    result.append(value * (scale * factor))
                return result

            pending = [damped(j) for j in range(min(2, freqs))]
            for j in range(freqs):
                if j + 2 < freqs:
                    pending.append(damped(j + 2))
                for t, value in enumerate(pending.pop(0)):
                    ring_ref[slot, j, 0, t * SUB : (t + 1) * SUB, :] = value
            send(direction, slot).start()
            return carry

        lax.fori_loop(0, quarter, one, 0)
    for direction in range(ND - SLOTS, ND):
        send(direction, direction % SLOTS).wait()


def step_pairs(axis, step):
    count = lax.axis_size(axis)
    return [(i, i + step) for i in range(count) if 0 <= i + step < count]


def neighbour(values, axis, step):
    return lax.ppermute(values, axis, step_pairs(axis, step))


def others_sum(values, axis):
    count = lax.axis_size(axis)
    total = None
    for step in range(1, count):
        part = lax.ppermute(values, axis, [(i, (i + step) % count) for i in range(count)])
        total = part if total is None else total + part
    return jnp.zeros_like(values) if total is None else total


VMEM = pl.BlockSpec(memory_space=pltpu.VMEM)
SMEM = pl.BlockSpec(memory_space=pltpu.SMEM)
HBM = pl.BlockSpec(memory_space=pltpu.HBM)
ANY = pl.BlockSpec(memory_space=pl.ANY)


def in_vmem(*shape):
    return pltpu.VMEM(shape, jnp.float32)


def in_any(*shape):
    return jax.ShapeDtypeStruct(shape, jnp.float32)


def in_hbm(values):
    return pltpu.with_memory_space_constraint(values, pltpu.HBM)


def call(kernel, in_specs, out_shape, out_specs, flops, moved, scratch=(), aliases=None, limit=6):
    return pl.pallas_call(
        kernel,
        in_specs=in_specs,
        out_shape=out_shape,
        out_specs=out_specs,
        scratch_shapes=list(scratch),
        input_output_aliases=aliases or {},
        cost_estimate=pl.CostEstimate(flops=flops, bytes_accessed=moved, transcendentals=0),
        compiler_params=pltpu.CompilerParams(vmem_limit_bytes=limit << 20),
    )


def resident(spectrum, land_mask, ice_mask, wind_u, wind_v, depth):
    local_comp, rows, lanes = spectrum.shape
    freqs = local_comp // ND
    members = lax.axis_size("comp")
    member = lax.axis_index("comp").astype(jnp.int32).reshape(1)
    scalars, lane_table, row_table = numpy_tables(members, freqs)
    scalars, lane_table, row_table = map(jnp.asarray, (scalars, lane_table, row_table))
    cells = rows * lanes
    row_message = 2 * 18 * freqs + CORNERS
    block = (freqs, ND, rows, lanes)
    spectrum = spectrum.reshape(block)

    growth, wet, to_right, to_left, to_down, to_up, edges = call(
        functools.partial(pack_kernel, freqs),
        [SMEM] + [HBM] * 7,
        (
            in_any(ND, rows, lanes),
            in_any(rows, lanes),
            in_any(GROUPS // 2, rows, lanes),
            in_any(GROUPS // 2, rows, lanes),
            in_any(row_message, lanes),
            in_any(row_message, lanes),
            in_any(2 * 18 * freqs * SUB, lanes),
        ),
        (VMEM,) * 7,
        flops=local_comp * cells * 4,
        moved=local_comp * cells * 4,
        scratch=[
            pltpu.VMEM((local_comp * rows, lanes), jnp.float32),
            pltpu.VMEM(lane_table.shape[1:], jnp.float32),
            pltpu.VMEM(row_table.shape[1:], jnp.float32),
            pltpu.VMEM((rows, lanes), jnp.int32),
            pltpu.VMEM((rows, lanes), jnp.int32),
            pltpu.VMEM((rows, lanes), jnp.float32),
            pltpu.VMEM((rows, lanes), jnp.float32),
            pltpu.SemaphoreType.DMA((6,)),
            pltpu.SemaphoreType.DMA((GROUPS,)),
        ],
        limit=30,
    )(
        member,
        *map(in_hbm, (lane_table, row_table, land_mask, ice_mask, wind_u, wind_v, spectrum)),
    )

    def main_part(start, stop, *before):
        return call(
            functools.partial(main_kernel, freqs, start, stop),
            [SMEM, SMEM, VMEM, VMEM, HBM] + ([ANY, VMEM, VMEM, VMEM, VMEM] if before else []),
            (
                in_vmem(*block),
                in_any(freqs * rows, lanes),
                in_any(freqs * rows, lanes),
                in_any(rows, lanes),
            ),
            (VMEM,) * 4,
            flops=local_comp * cells * 16 * (stop - start) // freqs,
            moved=local_comp * cells * 8 * (stop - start) // freqs,
            scratch=[
                pltpu.VMEM((AHEAD, ND, rows, lanes), jnp.float32),
                pltpu.SemaphoreType.DMA((AHEAD,)),
            ]
            + [pltpu.VMEM((rows + 2 * SUB, lanes), jnp.float32)] * 8,
            aliases={6 + index: index for index in range(4)} if before else {},
            limit=8,
        )(member, scalars, wet, growth, in_hbm(spectrum), *before)

    early = max(1, freqs // 3)
    from_left = neighbour(to_right, "sect", 1)
    from_right = neighbour(to_left, "sect", -1)
    kept, *partial = main_part(0, early)
    to_down, to_up = call(
        functools.partial(corner_kernel, freqs),
        [VMEM, VMEM, VMEM, ANY, ANY, ANY],
        (in_any(row_message, lanes), in_any(row_message, lanes)),
        (ANY, ANY),
        flops=100,
        moved=1 << 15,
        scratch=[pltpu.VMEM((2, CORNERS, lanes), jnp.float32), pltpu.SemaphoreType.DMA((2,))],
        aliases={3: 0, 4: 1},
    )(wet, from_left, from_right, to_down, to_up, partial[-1])
    from_above = neighbour(to_down, "slab", 1)
    from_below = neighbour(to_up, "slab", -1)
    kept, a_sums, b_sums, energy = main_part(early, freqs, to_down, kept, *partial)

    columns, edges, energy = call(
        functools.partial(enter_kernel, freqs),
        [SMEM] + [VMEM] * 9,
        (
            in_any(GROUPS, rows, lanes),
            in_any(2 * 18 * freqs * SUB, lanes),
            in_any(rows, lanes),
        ),
        (VMEM,) * 3,
        flops=cells * 600,
        moved=cells * 200,
        aliases={8: 1, 9: 2},
    )(
        member, lane_table, row_table, wet, from_left, from_right, from_above, from_below, edges,
        energy,
    )
    energy_there = others_sum(energy, "comp")
    a_sums, b_sums = call(
        functools.partial(entered_kernel, freqs),
        [SMEM] + [VMEM] * 10,
        (in_any(freqs * rows, lanes), in_any(freqs * rows, lanes)),
        (VMEM,) * 2,
        flops=cells * 600,
        moved=cells * 200,
        aliases={9: 0, 10: 1},
    )(
        member, lane_table, row_table, ice_mask, wind_u, wind_v, growth, columns, edges,
        a_sums, b_sums,
    )

    sums, square = call(
        functools.partial(stress_kernel, freqs),
        [SMEM, SMEM] + [VMEM] * 5,
        (in_any(3, rows, lanes), in_any(rows, lanes)),
        (VMEM, VMEM),
        flops=cells * freqs * 12,
        moved=cells * freqs * 8,
    )(member, scalars, wet, a_sums, b_sums, energy, energy_there)
    sums, stress = call(
        total_kernel,
        [VMEM, VMEM],
        (in_any(3, rows, lanes), in_any(2, rows, lanes)),
        (VMEM, VMEM),
        flops=cells * 3,
        moved=cells * 44,
    )(sums, others_sum(sums, "comp"))
    left = neighbour(stress, "sect", 1)
    right = neighbour(stress, "sect", -1)
    beside, top, bottom = call(
        strip_kernel,
        [VMEM, VMEM, VMEM],
        (in_any(2, rows, lanes), in_any(2, SUB, 2 * lanes), in_any(2, SUB, 2 * lanes)),
        (VMEM, VMEM, VMEM),
        flops=cells * 4,
        moved=cells * 36,
    )(stress, left, right)
    above = neighbour(bottom, "slab", 1)
    below = neighbour(top, "slab", -1)

    result, level = call(
        functools.partial(final_kernel, freqs),
        [SMEM, SMEM] + [VMEM] * 11,
        (in_any(*block), in_any(rows, lanes)),
        (HBM, VMEM),
        flops=local_comp * cells * 6,
        moved=local_comp * cells * 8,
        scratch=[
            pltpu.VMEM((2, freqs, rows, lanes), jnp.float32),
            pltpu.VMEM((SLOTS, freqs, 1, rows, lanes), jnp.float32),
            pltpu.SemaphoreType.DMA((SLOTS,)),
        ],
    )(
        member, scalars, wet, depth, square, sums, beside, above, below, growth, kept,
        columns, edges,
    )
    return result.reshape(local_comp, rows, lanes), level


def local(spectrum, *fields):
    local_comp, rows, lanes = spectrum.shape
    whole_rings = local_comp % ND == 0 and GROUP * 2 * (local_comp // ND) < LANES - 1
    if whole_rings and lanes == LANES and rows % SUB == 0:
        return resident(spectrum, *fields)
    return general(spectrum, *fields)


def solution(mesh):
    in_specs = (
        P("comp", "slab", "sect"),
        P("slab", "sect"),
        P("slab", "sect"),
        P("slab", "sect"),
        P("slab", "sect"),
        P("slab", "sect"),
    )
    out_specs = (P("comp", "slab", "sect"), P("slab", "sect"))
    return jax.shard_map(local, mesh=mesh, in_specs=in_specs, out_specs=out_specs, check_vma=False)
```

```python
import functools
import math

import jax
import jax.numpy as jnp
import numpy as np
from jax import lax
from jax.experimental import pallas as pl
from jax.experimental.pallas import tpu as pltpu
from jax.sharding import PartitionSpec as P

ND = 36
NF = 36
STEPS = 2
JAC = 4


def extended(cells, sides, width):
    for axis, dim in sides:
        count = lax.axis_size(axis)
        ends = count - 1
        head = lax.slice_in_dim(cells, 0, width, axis=dim)
        tail = lax.slice_in_dim(cells, cells.shape[dim] - width, cells.shape[dim], axis=dim)
        cells = jnp.concatenate(
            [
                lax.ppermute(tail, axis, [(i, (i + 1) % count) for i in range(ends)]),
                cells,
                lax.ppermute(head, axis, [((i + 1) % count, i) for i in range(ends)]),
            ],
            axis=dim,
        )
    return cells


def tables(index):
    freq_index = (index // ND).astype(jnp.float32)
    angle_index = (index % ND).astype(jnp.float32)
    heading = 2.0 * math.pi * angle_index / ND
    return (
        jnp.cos(heading),
        jnp.sin(heading),
        jnp.power(1.1, -freq_index),
        jnp.power(1.1, freq_index - (NF - 1)),
        0.5 + 0.5 * freq_index / (NF - 1),
    )


def column(values):
    return values[:, None, None]


def advect(spectra, wet_cells, speed_x, speed_y):
    padded = extended(spectra, (("slab", 1), ("sect", 2)), 1)
    upper_rows = padded[:, :-2, 1:-1]
    lower_rows = padded[:, 2:, 1:-1]
    left_cells = padded[:, 1:-1, :-2]
    right_cells = padded[:, 1:-1, 2:]
    change = (
        jnp.maximum(speed_x, 0.0) * (spectra - upper_rows)
        + jnp.minimum(speed_x, 0.0) * (lower_rows - spectra)
        + jnp.maximum(speed_y, 0.0) * (spectra - left_cells)
        + jnp.minimum(speed_y, 0.0) * (right_cells - spectra)
    )
    return (spectra - change) * wet_cells


def forcing(spectra, energy, wind_east, wind_north, ice_cover, cosine, sine, high_ratio):
    project = cosine * wind_east + sine * wind_north
    growth = 0.5 * high_ratio * jnp.square(jnp.maximum(project, 0.0)) * (1.0 - ice_cover)
    return spectra * (1.0 + growth) / (1.0 + 2.0 * high_ratio * jnp.square(energy))


def stress_weights(cosine, sine, shoaling):
    return jnp.stack(
        [shoaling * (cosine * cosine + 1.0) - 0.5, shoaling * (sine * sine + 1.0) - 0.5]
    )


def surge_solve(stress):
    padded = extended(stress, (("slab", 1), ("sect", 2)), 1)
    source_term = -(
        padded[0, 2:, 1:-1]
        + padded[0, :-2, 1:-1]
        - 2.0 * stress[0]
        + (padded[1, 1:-1, 2:] + padded[1, 1:-1, :-2] - 2.0 * stress[1])
    )
    surge_level = source_term / 4.5
    for _ in range(JAC):
        neighbours = extended(surge_level, (("slab", 0), ("sect", 1)), 1)
        surge_level = (
            source_term
            + neighbours[2:, 1:-1]
            + neighbours[:-2, 1:-1]
            + neighbours[1:-1, 2:]
            + neighbours[1:-1, :-2]
        ) / 4.5
    return surge_level


def general(spectrum, land_mask, ice_mask, wind_u, wind_v, depth):
    groups = lax.axis_size("comp")
    member = lax.axis_index("comp")
    local_comp, block_rows, block_cols = spectrum.shape
    point_rows = block_rows // groups
    total_comp = ND * NF
    wet_cells = (1 - land_mask).astype(jnp.float32)
    ice_cover = ice_mask.astype(jnp.float32)

    def own_rows(values):
        return lax.dynamic_slice_in_dim(values, member * point_rows, point_rows, values.ndim - 2)

    own_index = member * local_comp + jnp.arange(local_comp, dtype=jnp.int32)
    cosine, sine, low_ratio, high_ratio, shoaling = tables(own_index)
    spectra = spectrum * wet_cells
    for _ in range(STEPS):
        spectra = advect(
            spectra, wet_cells, column(0.7 * low_ratio * cosine), column(0.7 * low_ratio * sine)
        )
    points = lax.all_to_all(spectra, "comp", split_axis=1, concat_axis=0, tiled=True)
    cosine_full, sine_full, _, high_full, shoal_full = tables(
        jnp.arange(total_comp, dtype=jnp.int32)
    )
    energy = jnp.sum(points, axis=0) / total_comp
    sourced = forcing(
        points,
        energy,
        own_rows(wind_u),
        own_rows(wind_v),
        own_rows(ice_cover),
        column(cosine_full),
        column(sine_full),
        column(high_full),
    )
    stress = (
        jnp.einsum(
            "sk,krc->src",
            stress_weights(cosine_full, sine_full, shoal_full),
            sourced,
            precision=lax.Precision.HIGHEST,
        )
        / total_comp
    )
    stress_block = lax.all_gather(stress, "comp", axis=1, tiled=True)
    level_block = surge_solve(stress_block)
    final_energy = jnp.sum(sourced, axis=0) / total_comp
    damped = sourced / (
        1.0 + 4.0 * final_energy / (jnp.square(own_rows(depth) + own_rows(level_block)) + 1.0)
    )
    result = lax.all_to_all(damped, "comp", split_axis=0, concat_axis=1, tiled=True)
    return (result, level_block)


LANES = 128
SUB = 8
CLASSES = 10
KINDS = 5
GROUP = 3
GROUPS = ND // GROUP
CORNERS = 8


def class_of(direction):
    folded = direction % 18
    return folded if folded <= 9 else 18 - folded


def heads_down(direction):
    return direction < 9 or direction >= 27


def heads_right(direction):
    return direction < 18


def row_slot(direction):
    if direction < 9:
        return direction
    return direction - 18 if direction >= 27 else direction - 9


def numpy_tables(members, freqs):
    j = np.arange(members * freqs, dtype=np.float64)
    heading = 2.0 * np.pi * np.arange(ND) / ND
    cosine, sine = np.cos(heading), np.sin(heading)
    low = 1.1 ** (-j)
    high = 1.1 ** (j - (NF - 1))
    shoal = 0.5 + 0.5 * j / (NF - 1)
    step_x = 0.7 * low[:, None] * np.abs(cosine)
    step_y = 0.7 * low[:, None] * np.abs(sine)
    keep = 1.0 - step_x - step_y
    alpha, beta, scale = step_x / keep, step_y / keep, keep * keep
    classes = np.arange(CLASSES)
    square = np.broadcast_to(cosine * cosine, alpha.shape)
    scalars = np.stack(
        [
            alpha[:, classes],
            beta[:, classes],
            scale[:, classes],
            np.broadcast_to(high[:, None], (j.size, CLASSES)),
            np.broadcast_to(shoal[:, None], (j.size, CLASSES)),
        ],
        axis=-1,
    ).astype(np.float32)

    kinds = np.stack(
        [
            2.0 * beta,
            beta * beta,
            alpha * beta,
            scale,
            scale * square,
            np.broadcast_to(high[:, None], alpha.shape),
            np.broadcast_to(cosine, alpha.shape),
            np.broadcast_to(sine, alpha.shape),
        ]
    )
    lanes = np.zeros((members, GROUPS, 8, LANES), np.float32)
    packed = kinds.reshape(8, members, freqs, GROUPS, GROUP)
    packed = np.repeat(packed.transpose(1, 3, 0, 4, 2), 2, axis=-1)
    lanes[..., : GROUP * 2 * freqs] = packed.reshape(members, GROUPS, 8, -1)

    rows = np.stack(
        [2.0 * alpha, alpha * alpha, alpha * beta, scale, np.broadcast_to(high[:, None], alpha.shape)]
    )[:, :, classes]
    rows = rows.reshape(5, members, freqs, CLASSES).transpose(1, 3, 0, 2)
    rows = np.broadcast_to(rows[..., None], rows.shape + (LANES,)).astype(np.float32)
    return scalars.reshape(-1), lanes, rows


def iota(shape, axis):
    return lax.broadcasted_iota(jnp.int32, shape, axis)


def spread(values, column):
    return jnp.broadcast_to(values[:, column : column + 1], values.shape)


def shift_rows(values, step):
    rows = values.shape[0]
    edge = 0 if step > 0 else rows - 1
    moved = pltpu.roll(values, step % rows, 0)
    return jnp.where(iota(values.shape, 0) == edge, 0.0, moved)


def shift_lanes(values, step):
    lanes = values.shape[1]
    edge = 0 if step > 0 else lanes - 1
    moved = pltpu.roll(values, step % lanes, 1)
    return jnp.where(iota(values.shape, 1) == edge, 0.0, moved)


SLOTS = 4


def sides(quadrant):
    return 1 if quadrant in (0, 3) else -1, 1 if quadrant in (0, 1) else -1


def pack_kernel(
    freqs, member_ref, scalar_ref, lanes_hbm, table_hbm, land_hbm, ice_hbm, east_hbm, north_hbm,
    spectrum_ref, kept_ref, growth_ref, wet_ref, right_ref, left_ref, down_ref, up_ref, edges_ref,
    ring_ref, near_ref, far_ref, lanes_ref, table_ref, land_ref, ice_ref, east_ref, north_ref,
    small_sems, sems, *masked_refs,
):
    member = member_ref[0]
    nought = jnp.minimum(member, 0)
    small = [
        pltpu.make_async_copy(source, target, small_sems.at[index])
        for index, (source, target) in enumerate(
            (
                (land_hbm, land_ref),
                (ice_hbm, ice_ref),
                (east_hbm, east_ref),
                (north_hbm, north_ref),
                (lanes_hbm.at[member], lanes_ref),
                (table_hbm.at[member], table_ref),
            )
        )
    ]
    for copy in small:
        copy.start()
    rows = land_ref.shape[0]

    def fetch(j):
        slot = lax.rem(j, SLOTS)
        return pltpu.make_async_copy(spectrum_ref.at[j], ring_ref.at[slot], sems.at[slot])

    for j in range(min(SLOTS, freqs)):
        fetch(jnp.int32(j)).start()
    edges_ref[...] = jnp.zeros_like(edges_ref)
    for masked_ref in masked_refs:
        masked_ref[...] = jnp.zeros_like(masked_ref)
    down_ref[pl.ds(2 * 18 * freqs, CORNERS), :] = jnp.zeros((CORNERS, LANES), jnp.float32)
    up_ref[pl.ds(2 * 18 * freqs, CORNERS), :] = jnp.zeros((CORNERS, LANES), jnp.float32)
    right_ref[...] = jnp.zeros_like(right_ref)
    left_ref[...] = jnp.zeros_like(left_ref)
    for copy in small:
        copy.wait()

    wet_cells = (1 - land_ref[...]).astype(jnp.float32)
    wet_ref[...] = wet_cells
    open_water = 0.5 * (1.0 - ice_ref[...].astype(jnp.float32))
    shape = wet_cells.shape
    tiles = rows // SUB
    for direction in range(ND):
        angle = 2.0 * math.pi * direction / ND
        project = math.cos(angle) * east_ref[...] + math.sin(angle) * north_ref[...]
        growth_ref[direction] = open_water * jnp.square(jnp.maximum(project, 0.0))

    lane = iota(shape, 1)
    even = lane % 2 == 0
    tile_lane = iota((SUB, LANES), 1)
    not_first = jnp.where(tile_lane == 0, 0.0, 1.0)
    not_last = jnp.where(tile_lane == LANES - 1, 0.0, 1.0)
    quarter = ND // 4
    half = GROUPS // 2

    def tile_at(tile):
        return slice(tile * SUB, (tile + 1) * SUB)

    def mask_and_pack(j, quadrant):
        slot = lax.rem(j, SLOTS)
        to_down, to_right = sides(quadrant)
        wet = [wet_ref[tile_at(t), :] for t in range(tiles)]
        for i in range(quarter):
            direction = quadrant * quarter + i
            place = direction % GROUP * 2 * freqs + 2 * j
            here = (tile_lane >= place) & (tile_lane < place + 2)
            turn = lax.rem(place + 2, LANES) if to_right > 0 else place
            side_ref = right_ref if to_right > 0 else left_ref
            group = direction // GROUP % half
            target = masked_refs[quadrant % 2 * quarter + i]
            for t in range(tiles):
                cells = ring_ref[slot, direction, tile_at(t), :] * wet[t]
                target[tile_at(t + 1), :] = cells
                pltpu.store(
                    side_ref.at[group, tile_at(t), :], pltpu.roll(cells, turn, 1), mask=here
                )

    def first_step(j, quadrant):
        to_down, to_right = sides(quadrant)
        wet = [wet_ref[tile_at(t), :] for t in range(tiles)]
        near_row, far_row = (rows - 1, rows - 2) if to_down > 0 else (0, 1)
        for i in range(quarter):
            direction = quadrant * quarter + i
            base = ((member * freqs + j) * CLASSES + class_of(direction)) * KINDS
            alpha = scalar_ref[base]
            across = scalar_ref[base + 1] * (not_first if to_right > 0 else not_last)
            source = masked_refs[quadrant % 2 * quarter + i]
            near_ref[pl.ds(direction * freqs + j, 1), :] = source[
                SUB + near_row : SUB + near_row + 1, :
            ]
            far_ref[pl.ds(direction * freqs + j, 1), :] = source[
                SUB + far_row : SUB + far_row + 1, :
            ]
            for t in range(tiles):
                cells = source[tile_at(t + 1), :]
                ahead = source[pl.ds((t + 1) * SUB - to_down + nought, SUB), :]
                beside = pltpu.roll(cells, to_right % LANES, 1)
                kept_ref[j, direction, tile_at(t), :] = wet[t] * (
                    cells + alpha * ahead + across * beside
                )

    fetch(jnp.int32(0)).wait()
    mask_and_pack(jnp.int32(0), 0)

    def frequency(j, carry):
        fetch(j + 1).wait()
        for quadrant in range(4):
            mask_and_pack(j + quadrant // 3, (quadrant + 1) % 4)
            first_step(j, quadrant)

        @pl.when(j + SLOTS < freqs)
        def _():
            fetch(j + SLOTS).start()

        return carry

    lax.fori_loop(0, freqs - 1, frequency, 0)
    last = jnp.int32(freqs - 1)
    for quadrant in range(4):
        if quadrant < 3:
            mask_and_pack(last, quadrant + 1)
        first_step(last, quadrant)

    pending = []
    for group in range(GROUPS):
        to_right, fore = group < half, 1 if heads_down(group * GROUP) else -1
        ahead, behind = (LANES - 1, LANES - 2) if to_right else (0, 1)
        wet_near = spread(wet_cells, ahead)
        near_even = not to_right
        target_ref, index = (right_ref, group) if to_right else (left_ref, group - half)
        values = target_ref[index]
        near = pltpu.roll(values, 1 if near_even else LANES - 1, 1)
        table = lanes_ref[group]
        follow = wet_near * (table[1:2] * values + table[2:3] * shift_rows(near, fore))
        message = jnp.where(even == near_even, values, follow)
        pending.append((target_ref, index, jnp.where(lane == LANES - 1, wet_near, message)))
        if group:
            place_ref, index, message = pending.pop(0)
            place_ref[index] = message
    place_ref, index, message = pending.pop()
    place_ref[index] = message

    pending = []
    for direction in range(ND):
        to_down = heads_down(direction)
        near_row = rows - 1 if to_down else 0
        wet_near = wet_cells[near_row : near_row + 1, :]
        table = table_ref.at[class_of(direction)]
        near = near_ref[direction * freqs : (direction + 1) * freqs, :]
        far = far_ref[direction * freqs : (direction + 1) * freqs, :]
        beside = shift_lanes(near, 1 if heads_right(direction) else -1)
        follow = wet_near * (table[1] * far + table[2] * beside)
        slot = row_slot(direction) * freqs
        pending.append((down_ref if to_down else up_ref, slot, near, follow))
        if len(pending) > 2 or direction == ND - 1:
            for place_ref, slot, near, follow in pending:
                place_ref[slot : slot + freqs, :] = near
                place_ref[18 * freqs + slot : 18 * freqs + slot + freqs, :] = follow
            pending = []


def corner_kernel(
    freqs, wet_ref, right_ref, left_ref, down_in, up_in, _after, down_ref, up_ref, rows_ref, sems
):
    rows = wet_ref.shape[0]
    last = iota((1, LANES), 1) == LANES - 1
    rows_ref[...] = jnp.zeros_like(rows_ref)
    for which, row in ((0, rows - 1), (1, 0)):
        for i in range(6):
            source = right_ref if i < 3 else left_ref
            if which == 0:
                index = i if i < 3 else i
            else:
                index = i + 3 if i < 3 else i - 3
            column = 0 if i < 3 else LANES - 1
            own = jnp.broadcast_to(wet_ref[row : row + 1, column : column + 1], (1, LANES))
            rows_ref[which, i : i + 1, :] = jnp.where(last, own, source[index, row : row + 1, :])
    start = 2 * 18 * freqs
    copies = [
        pltpu.make_async_copy(
            rows_ref.at[which], ref.at[pl.ds(start, CORNERS), :], sems.at[which]
        )
        for which, ref in ((0, down_ref), (1, up_ref))
    ]
    for copy in copies:
        copy.start()
    for copy in copies:
        copy.wait()


def main_kernel(freqs, start, stop, member_ref, scalar_ref, wet_ref, growth_ref, *refs):
    if start:
        _after, kept_in, a_in, b_in, energy_in, kept_ref, a_ref, b_ref, energy_ref = refs
    else:
        kept_in, kept_ref, a_ref, b_ref, energy_ref = refs
    member = member_ref[0]
    nought = jnp.minimum(member, 0)
    rows = wet_ref.shape[0]
    tiles = rows // SUB
    lane = iota((SUB, LANES), 1)
    sub = iota((SUB, LANES), 0)
    not_first = jnp.where(lane == 0, 0.0, 1.0)
    not_last = jnp.where(lane == LANES - 1, 0.0, 1.0)
    top, bottom = sub == 0, sub == SUB - 1
    energy_ref[...] = energy_in[...] if start else jnp.zeros_like(energy_ref)

    def tile_at(tile):
        return pl.ds(tile * SUB, SUB)

    def parts_of(kind):
        if kind == 0:
            return ((0, 0, 0), (18, 2, 0), (9, 1, 9), (27, 3, 9))
        return ((kind, 0, kind), (18 + kind, 2, kind), (18 - kind, 1, kind), (36 - kind, 3, kind))

    def frequency(j, carry):
        base = (member * freqs + j) * CLASSES * KINDS
        at = [pl.ds(pl.multiple_of(j * rows, SUB) + t * SUB, SUB) for t in range(tiles)]

        def second_step(part):
            direction, quadrant, kind = part
            to_down, to_right = sides(quadrant)
            alpha = scalar_ref[base + kind * KINDS]
            across = scalar_ref[base + kind * KINDS + 1] * (not_first if to_right > 0 else not_last)
            result = []
            for t in range(tiles):
                cells = kept_in[j, direction, tile_at(t), :]
                if 0 <= t * SUB - to_down <= rows - SUB:
                    ahead = kept_in[j, direction, pl.ds(t * SUB - to_down + nought, SUB), :]
                else:
                    ahead = pltpu.roll(cells, to_down % SUB, 0)
                    ahead = jnp.where(top if to_down > 0 else bottom, 0.0, ahead)
                beside = pltpu.roll(cells, to_right % LANES, 1)
                result.append(cells + alpha * ahead + across * beside)
            return result

        def put(parts, results):
            for (direction, _, _), result in zip(parts, results):
                for t in range(tiles):
                    kept_ref[j, direction, tile_at(t), :] = result[t]

        pending = None
        for kind in range(CLASSES - 1):
            parts = parts_of(kind)
            scale, high = scalar_ref[base + kind * KINDS + 2], scalar_ref[base + 3]
            scaled_high = scale * high
            pairs = []
            for pair in (parts[:2], parts[2:]):
                results = [second_step(part) for part in pair]
                plain = [x + y for x, y in zip(*results)]
                grown = [
                    growth_ref[pair[0][0], tile_at(t), :] * results[0][t]
                    + growth_ref[pair[1][0], tile_at(t), :] * results[1][t]
                    for t in range(tiles)
                ]
                pairs.append((plain, grown))
                if pending is not None:
                    put(*pending)
                pending = pair, results
            (plain_x, grown_x), (plain_y, grown_y) = pairs
            for t in range(tiles):
                if kind == 0:
                    plain = scale * plain_x[t], scale * plain_y[t]
                    whole = [
                        p + scaled_high * g for p, g in zip(plain, (grown_x[t], grown_y[t]))
                    ]
                    square = math.cos(0.5 * math.pi) ** 2
                    energy_ref[tile_at(t), :] += plain[0] + plain[1]
                    a_ref[at[t], :] = whole[0] + whole[1]
                    b_ref[at[t], :] = whole[0] + square * whole[1]
                else:
                    plain = scale * (plain_x[t] + plain_y[t])
                    whole = plain + scaled_high * (grown_x[t] + grown_y[t])
                    square = math.cos(2.0 * math.pi * kind / ND) ** 2
                    energy_ref[tile_at(t), :] += plain
                    a_ref[at[t], :] += whole
                    b_ref[at[t], :] += square * whole
        put(*pending)
        return carry

    lax.fori_loop(start, stop, frequency, 0)


def edge_rows(freqs, to_down, direction, at):
    first = ((0 if to_down else 18) + row_slot(direction)) * freqs * SUB
    return pl.ds(first + at, freqs, stride=SUB)


def enter_kernel(
    freqs, member_ref, lanes_ref, table_ref, wet_ref, right_ref, left_ref, down_ref, up_ref,
    _edges_in, energy_in, columns_ref, edges_ref, energy_ref,
):
    member = member_ref[0]
    wet_cells = wet_ref[...]
    shape = wet_cells.shape
    rows = shape[0]
    lane = iota(shape, 1)
    row = iota(shape, 0)
    even = lane % 2 == 0
    width = 2 * freqs
    used = lane < GROUP * width
    energy = energy_in[...]
    start = 2 * 18 * freqs

    for to_right in (True, False):
        near_column, far_column = (0, 1) if to_right else (LANES - 1, LANES - 2)
        near_even = to_right
        wet_near, wet_far = spread(wet_cells, near_column), spread(wet_cells, far_column)
        total = jnp.zeros(shape, jnp.float32)
        for index in range(GROUPS // 2):
            group = index if to_right else index + GROUPS // 2
            to_down = heads_down(group * GROUP)
            fore = 1 if to_down else -1
            message = (right_ref if to_right else left_ref)[index]
            table = lanes_ref[member, group]
            turn = LANES - 1 if near_even else 1
            entered = pltpu.roll(message, turn, 1)
            corner_index = index if to_down else (index - 3 if to_right else index + 3)
            corner = (down_ref if to_down else up_ref)[pl.ds(start + corner_index, 1), :]
            edge = 0 if to_down else rows - 1
            paths = corner[:, LANES - 1 :] + message[edge : edge + 1, LANES - 1 :]
            corner = pltpu.roll(jnp.broadcast_to(corner, (SUB, LANES)), turn, 1)[0:1]
            corner = jnp.broadcast_to(paths, (1, LANES)) * corner
            diagonal = shift_rows(wet_near * entered, fore)
            diagonal = jnp.where(row == edge, jnp.broadcast_to(corner, shape), diagonal)
            near = wet_near * (table[0:1] * entered + message + table[2:3] * diagonal)
            far = wet_near * wet_far * (table[1:2] * message)
            change = jnp.where(used, jnp.where(even == near_even, near, far), 0.0)
            columns_ref[group] = change
            total += table[3:4] * change
        total += pltpu.roll(total, LANES - width, 1) + pltpu.roll(total, LANES - 2 * width, 1)
        target = 0 if to_right else LANES - 2
        inside = (lane >= target) & (lane < target + 2)
        for j in range(freqs):
            turned = pltpu.roll(total, (target - 2 * j) % LANES, 1)
            energy += jnp.where(inside, turned, 0.0)
    energy_ref[...] = energy

    for to_down in (True, False):
        near_row, far_row = (0, 1) if to_down else (rows - 1, rows - 2)
        message_ref = down_ref if to_down else up_ref
        wet_near = wet_cells[near_row : near_row + 1, :]
        wet_both = wet_near * wet_cells[far_row : far_row + 1, :]
        totals = [jnp.zeros((freqs, LANES), jnp.float32) for _ in range(2)]
        for direction in range(ND):
            if heads_down(direction) != to_down:
                continue
            slot = row_slot(direction) * freqs
            entered = message_ref[slot : slot + freqs, :]
            follow = message_ref[18 * freqs + slot : 18 * freqs + slot + freqs, :]
            table = table_ref.at[member, class_of(direction)]
            side = 1 if heads_right(direction) else -1
            diagonal = shift_lanes(wet_near * entered, side)
            near = wet_near * (table[0] * entered + follow + table[2] * diagonal)
            far = wet_both * (table[1] * entered)
            for place, (change, at) in enumerate(((near, near_row), (far, far_row))):
                edges_ref[edge_rows(freqs, to_down, direction, at % SUB), :] = change
                totals[place] += table[3] * change
        for total, at in zip(totals, (near_row, far_row)):
            energy_ref[at : at + 1, :] += jnp.sum(total, axis=0, keepdims=True)


def entered_kernel(
    freqs, member_ref, lanes_ref, table_ref, ice_ref, east_ref, north_ref, growth_ref, columns_ref,
    edges_ref, a_in, b_in, a_ref, b_ref,
):
    member = member_ref[0]
    shape = ice_ref.shape
    rows = shape[0]
    lane = iota(shape, 1)
    even = lane % 2 == 0
    width = 2 * freqs
    a_ref[...] = a_in[...]
    b_ref[...] = b_in[...]

    for to_right in (True, False):
        near_column, far_column = (0, 1) if to_right else (LANES - 1, LANES - 2)

        def packed_field(values):
            return jnp.where(
                even == to_right, spread(values, near_column), spread(values, far_column)
            )

        east, north = packed_field(east_ref[...]), packed_field(north_ref[...])
        open_water = 0.5 * (1.0 - packed_field(ice_ref[...].astype(jnp.float32)))
        sums = [jnp.zeros(shape, jnp.float32) for _ in range(2)]
        for index in range(GROUPS // 2):
            group = index if to_right else index + GROUPS // 2
            table = lanes_ref[member, group]
            project = table[6:7] * east + table[7:8] * north
            growth = open_water * jnp.square(jnp.maximum(project, 0.0))
            grown = columns_ref[group] * (1.0 + table[5:6] * growth)
            sums[0] += table[3:4] * grown
            sums[1] += table[4:5] * grown
        sums = [
            part + pltpu.roll(part, LANES - width, 1) + pltpu.roll(part, LANES - 2 * width, 1)
            for part in sums
        ]
        target = 0 if to_right else LANES - 2
        inside = (lane >= target) & (lane < target + 2)
        for j in range(freqs):
            turn = (target - 2 * j) % LANES
            block = slice(j * rows, (j + 1) * rows)
            place = [jnp.where(inside, pltpu.roll(part, turn, 1), 0.0) for part in sums]
            a_ref[block, :] += place[0]
            b_ref[block, :] += place[1]

    for to_down in (True, False):
        near_row, far_row = (0, 1) if to_down else (rows - 1, rows - 2)
        totals = [jnp.zeros((freqs, LANES), jnp.float32) for _ in range(4)]
        for direction in range(ND):
            if heads_down(direction) != to_down:
                continue
            table = table_ref.at[member, class_of(direction)]
            square = math.cos(2.0 * math.pi * direction / ND) ** 2
            for place, at in enumerate((near_row, far_row)):
                change = edges_ref[edge_rows(freqs, to_down, direction, at % SUB), :]
                growth = growth_ref[direction, at : at + 1, :]
                grown = (table[3] * change) * (1.0 + table[4] * growth)
                totals[2 * place] += grown
                totals[2 * place + 1] += square * grown
        for place, at in enumerate((near_row, far_row)):
            picked = pl.ds(at, freqs, stride=rows)
            a_ref[picked, :] += totals[2 * place]
            b_ref[picked, :] += totals[2 * place + 1]


def stress_kernel(
    freqs, member_ref, scalar_ref, wet_ref, a_ref, b_ref, own_ref, other_ref, sums_ref, square_ref
):
    member = member_ref[0]
    wet_cells = wet_ref[...]
    rows = wet_cells.shape[0]
    energy = wet_cells * (own_ref[...] + other_ref[...]) / (ND * NF)
    square = jnp.square(energy)
    square_ref[...] = square

    sums = [jnp.zeros(wet_cells.shape, jnp.float32) for _ in range(3)]
    for j in range(freqs):
        base = (member * freqs + j) * CLASSES * KINDS
        high, shoal = scalar_ref[base + 3], scalar_ref[base + 4]
        block = slice(j * rows, (j + 1) * rows)
        ratio = wet_cells / (1.0 + (2.0 * high) * square)
        whole = ratio * a_ref[block, :]
        along = ratio * b_ref[block, :]
        sums[0] += shoal * along + (shoal - 0.5) * whole
        sums[1] += (2.0 * shoal - 0.5) * whole - shoal * along
        sums[2] += whole
    for index in range(3):
        sums_ref[index] = sums[index] / (ND * NF)


def total_kernel(own_ref, other_ref, sums_ref, stress_ref):
    sums_ref[...] = own_ref[...] + other_ref[...]
    stress_ref[...] = sums_ref[0:2]


def strip_kernel(stress_ref, left_ref, right_ref, beside_ref, top_ref, bottom_ref):
    rows = stress_ref.shape[1]
    low_half = iota((rows, LANES), 1) < LANES // 2
    for index in range(2):
        beside = jnp.where(low_half, right_ref[index], left_ref[index])
        beside_ref[index] = beside
        for target, first in ((top_ref, 0), (bottom_ref, rows - SUB)):
            target[index, :, 0:LANES] = stress_ref[index, first : first + SUB, :]
            target[index, :, LANES:] = beside[first : first + SUB, :]


def final_kernel(
    freqs, member_ref, scalar_ref, wet_ref, depth_ref, square_ref, sums_ref, beside_ref, above_ref, below_ref,
    growth_ref, kept_ref, columns_ref, edges_ref,
    result_ref, level_ref, ratio_ref, ring_ref, sems,
):
    member = member_ref[0]
    wet_cells = wet_ref[...]
    rows = wet_cells.shape[0]
    slab, slabs = lax.axis_index("slab"), lax.axis_size("slab")
    sect, sects = lax.axis_index("sect"), lax.axis_size("sect")
    above_ok = jnp.where(slab > 0, 1.0, 0.0)
    below_ok = jnp.where(slab < slabs - 1, 1.0, 0.0)
    left_ok = jnp.where(sect > 0, 1.0, 0.0)
    right_ok = jnp.where(sect < sects - 1, 1.0, 0.0)

    def framed(index):
        middle = jnp.concatenate([sums_ref[index], beside_ref[index]], axis=1)
        return jnp.concatenate([middle, below_ref[index], above_ref[index]], axis=0)

    def around(values, axis):
        size = values.shape[axis]
        return pltpu.roll(values, 1, axis) + pltpu.roll(values, size - 1, axis)

    stress_x, stress_y = framed(0), framed(1)
    frame = stress_x.shape
    frame_row, frame_lane = iota(frame, 0), iota(frame, 1)
    row_ok = jnp.where(frame_row < rows, 1.0, jnp.where(frame_row < rows + SUB, below_ok, above_ok))
    lane_ok = jnp.where(
        frame_lane < LANES, 1.0, jnp.where(frame_lane < LANES + LANES // 2, right_ok, left_ok)
    )
    inside = row_ok * lane_ok / 4.5
    source = -((around(stress_x, 0) - 2.0 * stress_x) + (around(stress_y, 1) - 2.0 * stress_y))
    level = inside * source
    for _ in range(JAC):
        level = inside * (source + around(level, 0) + around(level, 1))
    level = level[:rows, :LANES]
    level_ref[...] = level
    damping = 1.0 + 4.0 * sums_ref[2] / (jnp.square(depth_ref[...] + level) + 1.0)
    square = square_ref[...]
    tiles = rows // SUB
    for j in range(freqs):
        high = scalar_ref[(member * freqs + j) * CLASSES * KINDS + 3]
        ratio = wet_cells / ((1.0 + (2.0 * high) * square) * damping)
        ratio_ref[0, j] = ratio
        ratio_ref[1, j] = high * ratio

    tile_lane = iota((SUB, LANES), 1)
    quarter = ND // 4

    def send(j, quadrant):
        slot = lax.rem(j, 2)
        return pltpu.make_async_copy(
            ring_ref.at[slot, quadrant],
            result_ref.at[j, pl.ds(quadrant * quarter, quarter)],
            sems.at[slot, quadrant],
        )

    def frequency(j, carry):
        slot = lax.rem(j, 2)

        @pl.when(j >= 2)
        def _():
            for quadrant in range(4):
                send(j - 2, quadrant).wait()

        def damped(quadrant, i):
            direction = quadrant * quarter + i
            to_down, to_right = sides(quadrant)
            base = ((member * freqs + j) * CLASSES + class_of(direction)) * KINDS
            scale = scalar_ref[base + 2]
            target = 0 if to_right > 0 else LANES - 2
            at_side = (tile_lane >= target) & (tile_lane < target + 2)
            turn = target - direction % GROUP * 2 * freqs + LANES - 2 * j
            turn = lax.rem(turn + LANES, LANES)
            edge_tile = 0 if to_down > 0 else tiles - 1
            edge = ((0 if to_down > 0 else 18) + row_slot(direction)) * freqs + j
            result = []
            for t in range(tiles):
                part = slice(t * SUB, (t + 1) * SUB)
                entered = pltpu.roll(columns_ref[direction // GROUP, part, :], turn, 1)
                value = kept_ref[j, direction, part, :] + jnp.where(at_side, entered, 0.0)
                if t == edge_tile:
                    value += edges_ref[pl.ds(pl.multiple_of(edge * SUB, SUB), SUB), :]
                growth = growth_ref[direction, part, :]
                factor = ratio_ref[0, j, part, :] + ratio_ref[1, j, part, :] * growth
                result.append(value * (scale * factor))
            return result

        pending = []
        for direction in range(ND + 2):
            if direction < ND:
                pending.append(damped(*divmod(direction, quarter)))
            if direction >= 2:
                quadrant, i = divmod(direction - 2, quarter)
                for t, value in enumerate(pending.pop(0)):
                    ring_ref[slot, quadrant, i, t * SUB : (t + 1) * SUB, :] = value
                if i == quarter - 1:
                    send(j, quadrant).start()
        return carry

    lax.fori_loop(0, freqs, frequency, 0)
    for j in range(max(0, freqs - 2), freqs):
        for quadrant in range(4):
            send(jnp.int32(j), quadrant).wait()


def step_pairs(axis, step):
    count = lax.axis_size(axis)
    return [(i, i + step) for i in range(count) if 0 <= i + step < count]


def neighbour(values, axis, step):
    return lax.ppermute(values, axis, step_pairs(axis, step))


def others_sum(values, axis):
    count = lax.axis_size(axis)
    total = None
    for step in range(1, count):
        part = lax.ppermute(values, axis, [(i, (i + step) % count) for i in range(count)])
        total = part if total is None else total + part
    return jnp.zeros_like(values) if total is None else total


VMEM = pl.BlockSpec(memory_space=pltpu.VMEM)
SMEM = pl.BlockSpec(memory_space=pltpu.SMEM)
HBM = pl.BlockSpec(memory_space=pltpu.HBM)
ANY = pl.BlockSpec(memory_space=pl.ANY)


def in_vmem(*shape):
    return pltpu.VMEM(shape, jnp.float32)


def in_any(*shape):
    return jax.ShapeDtypeStruct(shape, jnp.float32)


def in_hbm(values):
    return pltpu.with_memory_space_constraint(values, pltpu.HBM)


def call(kernel, in_specs, out_shape, out_specs, flops, moved, scratch=(), aliases=None, limit=6):
    return pl.pallas_call(
        kernel,
        in_specs=in_specs,
        out_shape=out_shape,
        out_specs=out_specs,
        scratch_shapes=list(scratch),
        input_output_aliases=aliases or {},
        cost_estimate=pl.CostEstimate(flops=flops, bytes_accessed=moved, transcendentals=0),
        compiler_params=pltpu.CompilerParams(vmem_limit_bytes=limit << 20),
    )


def resident(spectrum, land_mask, ice_mask, wind_u, wind_v, depth):
    local_comp, rows, lanes = spectrum.shape
    freqs = local_comp // ND
    members = lax.axis_size("comp")
    member = lax.axis_index("comp").astype(jnp.int32).reshape(1)
    scalars, lane_table, row_table = numpy_tables(members, freqs)
    scalars, lane_table, row_table = map(jnp.asarray, (scalars, lane_table, row_table))
    cells = rows * lanes
    row_message = 2 * 18 * freqs + CORNERS
    block = (freqs, ND, rows, lanes)
    spectrum = spectrum.reshape(block)

    kept, growth, wet, to_right, to_left, to_down, to_up, edges = call(
        functools.partial(pack_kernel, freqs),
        [SMEM, SMEM] + [HBM] * 7,
        (
            in_vmem(*block),
            in_any(ND, rows, lanes),
            in_any(rows, lanes),
            in_any(GROUPS // 2, rows, lanes),
            in_any(GROUPS // 2, rows, lanes),
            in_any(row_message, lanes),
            in_any(row_message, lanes),
            in_any(2 * 18 * freqs * SUB, lanes),
        ),
        (VMEM,) * 8,
        flops=local_comp * cells * 8,
        moved=local_comp * cells * 8,
        scratch=[
            pltpu.VMEM((SLOTS, ND, rows, lanes), jnp.float32),
            pltpu.VMEM((ND * freqs, lanes), jnp.float32),
            pltpu.VMEM((ND * freqs, lanes), jnp.float32),
            pltpu.VMEM(lane_table.shape[1:], jnp.float32),
            pltpu.VMEM(row_table.shape[1:], jnp.float32),
            pltpu.VMEM((rows, lanes), jnp.int32),
            pltpu.VMEM((rows, lanes), jnp.int32),
            pltpu.VMEM((rows, lanes), jnp.float32),
            pltpu.VMEM((rows, lanes), jnp.float32),
            pltpu.SemaphoreType.DMA((6,)),
            pltpu.SemaphoreType.DMA((SLOTS,)),
        ]
        + [pltpu.VMEM((rows + 2 * SUB, lanes), jnp.float32)] * (ND // 2),
        limit=12,
    )(
        member,
        scalars,
        *map(in_hbm, (lane_table, row_table, land_mask, ice_mask, wind_u, wind_v, spectrum)),
    )

    def main_part(start, stop, *before):
        return call(
            functools.partial(main_kernel, freqs, start, stop),
            [SMEM, SMEM, VMEM, VMEM] + ([ANY] + [VMEM] * 4 if start else [VMEM]),
            (
                in_vmem(*block),
                in_any(freqs * rows, lanes),
                in_any(freqs * rows, lanes),
                in_any(rows, lanes),
            ),
            (VMEM,) * 4,
            flops=local_comp * cells * 9 * (stop - start) // freqs,
            moved=local_comp * cells * 8 * (stop - start) // freqs,
            aliases={5 + index: index for index in range(4)} if start else {4: 0},
        )(member, scalars, wet, growth, *before)

    early = max(1, freqs // 3)
    from_left = neighbour(to_right, "sect", 1)
    from_right = neighbour(to_left, "sect", -1)
    kept, *partial = main_part(0, early, kept)
    to_down, to_up = call(
        functools.partial(corner_kernel, freqs),
        [VMEM, VMEM, VMEM, ANY, ANY, ANY],
        (in_any(row_message, lanes), in_any(row_message, lanes)),
        (ANY, ANY),
        flops=100,
        moved=1 << 15,
        scratch=[pltpu.VMEM((2, CORNERS, lanes), jnp.float32), pltpu.SemaphoreType.DMA((2,))],
        aliases={3: 0, 4: 1},
    )(wet, from_left, from_right, to_down, to_up, partial[-1])
    from_above = neighbour(to_down, "slab", 1)
    from_below = neighbour(to_up, "slab", -1)
    kept, a_sums, b_sums, energy = main_part(early, freqs, to_down, kept, *partial)

    columns, edges, energy = call(
        functools.partial(enter_kernel, freqs),
        [SMEM] + [VMEM] * 9,
        (
            in_any(GROUPS, rows, lanes),
            in_any(2 * 18 * freqs * SUB, lanes),
            in_any(rows, lanes),
        ),
        (VMEM,) * 3,
        flops=cells * 600,
        moved=cells * 200,
        aliases={8: 1, 9: 2},
    )(
        member, lane_table, row_table, wet, from_left, from_right, from_above, from_below, edges,
        energy,
    )
    energy_there = others_sum(energy, "comp")
    a_sums, b_sums = call(
        functools.partial(entered_kernel, freqs),
        [SMEM] + [VMEM] * 10,
        (in_any(freqs * rows, lanes), in_any(freqs * rows, lanes)),
        (VMEM,) * 2,
        flops=cells * 600,
        moved=cells * 200,
        aliases={9: 0, 10: 1},
    )(
        member, lane_table, row_table, ice_mask, wind_u, wind_v, growth, columns, edges,
        a_sums, b_sums,
    )

    sums, square = call(
        functools.partial(stress_kernel, freqs),
        [SMEM, SMEM] + [VMEM] * 5,
        (in_any(3, rows, lanes), in_any(rows, lanes)),
        (VMEM, VMEM),
        flops=cells * freqs * 12,
        moved=cells * freqs * 8,
    )(member, scalars, wet, a_sums, b_sums, energy, energy_there)
    sums, stress = call(
        total_kernel,
        [VMEM, VMEM],
        (in_any(3, rows, lanes), in_any(2, rows, lanes)),
        (VMEM, VMEM),
        flops=cells * 3,
        moved=cells * 44,
    )(sums, others_sum(sums, "comp"))
    left = neighbour(stress, "sect", 1)
    right = neighbour(stress, "sect", -1)
    beside, top, bottom = call(
        strip_kernel,
        [VMEM, VMEM, VMEM],
        (in_any(2, rows, lanes), in_any(2, SUB, 2 * lanes), in_any(2, SUB, 2 * lanes)),
        (VMEM, VMEM, VMEM),
        flops=cells * 4,
        moved=cells * 36,
    )(stress, left, right)
    above = neighbour(bottom, "slab", 1)
    below = neighbour(top, "slab", -1)

    result, level = call(
        functools.partial(final_kernel, freqs),
        [SMEM, SMEM] + [VMEM] * 11,
        (in_any(*block), in_any(rows, lanes)),
        (HBM, VMEM),
        flops=local_comp * cells * 6,
        moved=local_comp * cells * 8,
        scratch=[
            pltpu.VMEM((2, freqs, rows, lanes), jnp.float32),
            pltpu.VMEM((2, 4, ND // 4, rows, lanes), jnp.float32),
            pltpu.SemaphoreType.DMA((2, 4)),
        ],
    )(
        member, scalars, wet, depth, square, sums, beside, above, below, growth, kept,
        columns, edges,
    )
    return result.reshape(local_comp, rows, lanes), level


def local(spectrum, *fields):
    local_comp, rows, lanes = spectrum.shape
    whole_rings = local_comp % ND == 0 and GROUP * 2 * (local_comp // ND) < LANES - 1
    if whole_rings and lanes == LANES and rows % SUB == 0:
        return resident(spectrum, *fields)
    return general(spectrum, *fields)


def solution(mesh):
    in_specs = (
        P("comp", "slab", "sect"),
        P("slab", "sect"),
        P("slab", "sect"),
        P("slab", "sect"),
        P("slab", "sect"),
        P("slab", "sect"),
    )
    out_specs = (P("comp", "slab", "sect"), P("slab", "sect"))
    return jax.shard_map(local, mesh=mesh, in_specs=in_specs, out_specs=out_specs, check_vma=False)
```

```python
import functools
import math

import jax
import jax.numpy as jnp
import numpy as np
from jax import lax
from jax.experimental import pallas as pl
from jax.experimental.pallas import tpu as pltpu
from jax.sharding import PartitionSpec as P

ND = 36
NF = 36
STEPS = 2
JAC = 4


def extended(cells, sides, width):
    for axis, dim in sides:
        count = lax.axis_size(axis)
        ends = count - 1
        head = lax.slice_in_dim(cells, 0, width, axis=dim)
        tail = lax.slice_in_dim(cells, cells.shape[dim] - width, cells.shape[dim], axis=dim)
        cells = jnp.concatenate(
            [
                lax.ppermute(tail, axis, [(i, (i + 1) % count) for i in range(ends)]),
                cells,
                lax.ppermute(head, axis, [((i + 1) % count, i) for i in range(ends)]),
            ],
            axis=dim,
        )
    return cells


def tables(index):
    freq_index = (index // ND).astype(jnp.float32)
    angle_index = (index % ND).astype(jnp.float32)
    heading = 2.0 * math.pi * angle_index / ND
    return (
        jnp.cos(heading),
        jnp.sin(heading),
        jnp.power(1.1, -freq_index),
        jnp.power(1.1, freq_index - (NF - 1)),
        0.5 + 0.5 * freq_index / (NF - 1),
    )


def column(values):
    return values[:, None, None]


def advect(spectra, wet_cells, speed_x, speed_y):
    padded = extended(spectra, (("slab", 1), ("sect", 2)), 1)
    upper_rows = padded[:, :-2, 1:-1]
    lower_rows = padded[:, 2:, 1:-1]
    left_cells = padded[:, 1:-1, :-2]
    right_cells = padded[:, 1:-1, 2:]
    change = (
        jnp.maximum(speed_x, 0.0) * (spectra - upper_rows)
        + jnp.minimum(speed_x, 0.0) * (lower_rows - spectra)
        + jnp.maximum(speed_y, 0.0) * (spectra - left_cells)
        + jnp.minimum(speed_y, 0.0) * (right_cells - spectra)
    )
    return (spectra - change) * wet_cells


def forcing(spectra, energy, wind_east, wind_north, ice_cover, cosine, sine, high_ratio):
    project = cosine * wind_east + sine * wind_north
    growth = 0.5 * high_ratio * jnp.square(jnp.maximum(project, 0.0)) * (1.0 - ice_cover)
    return spectra * (1.0 + growth) / (1.0 + 2.0 * high_ratio * jnp.square(energy))


def stress_weights(cosine, sine, shoaling):
    return jnp.stack(
        [shoaling * (cosine * cosine + 1.0) - 0.5, shoaling * (sine * sine + 1.0) - 0.5]
    )


def surge_solve(stress):
    padded = extended(stress, (("slab", 1), ("sect", 2)), 1)
    source_term = -(
        padded[0, 2:, 1:-1]
        + padded[0, :-2, 1:-1]
        - 2.0 * stress[0]
        + (padded[1, 1:-1, 2:] + padded[1, 1:-1, :-2] - 2.0 * stress[1])
    )
    surge_level = source_term / 4.5
    for _ in range(JAC):
        neighbours = extended(surge_level, (("slab", 0), ("sect", 1)), 1)
        surge_level = (
            source_term
            + neighbours[2:, 1:-1]
            + neighbours[:-2, 1:-1]
            + neighbours[1:-1, 2:]
            + neighbours[1:-1, :-2]
        ) / 4.5
    return surge_level


def general(spectrum, land_mask, ice_mask, wind_u, wind_v, depth):
    groups = lax.axis_size("comp")
    member = lax.axis_index("comp")
    local_comp, block_rows, block_cols = spectrum.shape
    point_rows = block_rows // groups
    total_comp = ND * NF
    wet_cells = (1 - land_mask).astype(jnp.float32)
    ice_cover = ice_mask.astype(jnp.float32)

    def own_rows(values):
        return lax.dynamic_slice_in_dim(values, member * point_rows, point_rows, values.ndim - 2)

    own_index = member * local_comp + jnp.arange(local_comp, dtype=jnp.int32)
    cosine, sine, low_ratio, high_ratio, shoaling = tables(own_index)
    spectra = spectrum * wet_cells
    for _ in range(STEPS):
        spectra = advect(
            spectra, wet_cells, column(0.7 * low_ratio * cosine), column(0.7 * low_ratio * sine)
        )
    points = lax.all_to_all(spectra, "comp", split_axis=1, concat_axis=0, tiled=True)
    cosine_full, sine_full, _, high_full, shoal_full = tables(
        jnp.arange(total_comp, dtype=jnp.int32)
    )
    energy = jnp.sum(points, axis=0) / total_comp
    sourced = forcing(
        points,
        energy,
        own_rows(wind_u),
        own_rows(wind_v),
        own_rows(ice_cover),
        column(cosine_full),
        column(sine_full),
        column(high_full),
    )
    stress = (
        jnp.einsum(
            "sk,krc->src",
            stress_weights(cosine_full, sine_full, shoal_full),
            sourced,
            precision=lax.Precision.HIGHEST,
        )
        / total_comp
    )
    stress_block = lax.all_gather(stress, "comp", axis=1, tiled=True)
    level_block = surge_solve(stress_block)
    final_energy = jnp.sum(sourced, axis=0) / total_comp
    damped = sourced / (
        1.0 + 4.0 * final_energy / (jnp.square(own_rows(depth) + own_rows(level_block)) + 1.0)
    )
    result = lax.all_to_all(damped, "comp", split_axis=0, concat_axis=1, tiled=True)
    return (result, level_block)


LANES = 128
SUB = 8
CLASSES = 10
KINDS = 5
GROUP = 3
GROUPS = ND // GROUP
CORNERS = 8


def class_of(direction):
    folded = direction % 18
    return folded if folded <= 9 else 18 - folded


def heads_down(direction):
    return direction < 9 or direction >= 27


def heads_right(direction):
    return direction < 18


def row_slot(direction):
    if direction < 9:
        return direction
    return direction - 18 if direction >= 27 else direction - 9


def numpy_tables(members, freqs):
    j = np.arange(members * freqs, dtype=np.float64)
    heading = 2.0 * np.pi * np.arange(ND) / ND
    cosine, sine = np.cos(heading), np.sin(heading)
    low = 1.1 ** (-j)
    high = 1.1 ** (j - (NF - 1))
    shoal = 0.5 + 0.5 * j / (NF - 1)
    step_x = 0.7 * low[:, None] * np.abs(cosine)
    step_y = 0.7 * low[:, None] * np.abs(sine)
    keep = 1.0 - step_x - step_y
    alpha, beta, scale = step_x / keep, step_y / keep, keep * keep
    classes = np.arange(CLASSES)
    square = np.broadcast_to(cosine * cosine, alpha.shape)
    scalars = np.stack(
        [
            alpha[:, classes],
            beta[:, classes],
            scale[:, classes],
            np.broadcast_to(high[:, None], (j.size, CLASSES)),
            np.broadcast_to(shoal[:, None], (j.size, CLASSES)),
        ],
        axis=-1,
    ).astype(np.float32)

    kinds = np.stack(
        [
            2.0 * beta,
            beta * beta,
            alpha * beta,
            scale,
            scale * square,
            np.broadcast_to(high[:, None], alpha.shape),
            np.broadcast_to(cosine, alpha.shape),
            np.broadcast_to(sine, alpha.shape),
        ]
    )
    lanes = np.zeros((members, GROUPS, 8, LANES), np.float32)
    packed = kinds.reshape(8, members, freqs, GROUPS, GROUP)
    packed = np.repeat(packed.transpose(1, 3, 0, 4, 2), 2, axis=-1)
    lanes[..., : GROUP * 2 * freqs] = packed.reshape(members, GROUPS, 8, -1)

    rows = np.stack(
        [2.0 * alpha, alpha * alpha, alpha * beta, scale, np.broadcast_to(high[:, None], alpha.shape)]
    )[:, :, classes]
    rows = rows.reshape(5, members, freqs, CLASSES).transpose(1, 3, 0, 2)
    rows = np.broadcast_to(rows[..., None], rows.shape + (LANES,)).astype(np.float32)
    return scalars.reshape(-1), lanes, rows


def odd_position(axis):
    return lax.rem(lax.axis_index(axis), 2) == 1


def iota(shape, axis):
    return lax.broadcasted_iota(jnp.int32, shape, axis)


def spread(values, column):
    return jnp.broadcast_to(values[:, column : column + 1], values.shape)


def shift_rows(values, step):
    rows = values.shape[0]
    edge = 0 if step > 0 else rows - 1
    moved = pltpu.roll(values, step % rows, 0)
    return jnp.where(iota(values.shape, 0) == edge, 0.0, moved)


def shift_lanes(values, step):
    lanes = values.shape[1]
    edge = 0 if step > 0 else lanes - 1
    moved = pltpu.roll(values, step % lanes, 1)
    return jnp.where(iota(values.shape, 1) == edge, 0.0, moved)


DEPTH = 3


def sides(quadrant):
    return 1 if quadrant in (0, 3) else -1, 1 if quadrant in (0, 1) else -1


def pack_kernel(
    freqs, member_ref, lanes_hbm, table_hbm, land_hbm, ice_hbm, east_hbm, north_hbm, spectrum_ref,
    growth_ref, wet_ref, swap_side_ref, other_side_ref, swap_row_ref, other_row_ref, edges_ref,
    kept_ref, right_ref, left_ref, lanes_ref, table_ref, land_ref, ice_ref, east_ref, north_ref, small_sems, sems,
):
    member = member_ref[0]
    small = [
        pltpu.make_async_copy(source, target, small_sems.at[index])
        for index, (source, target) in enumerate(
            (
                (land_hbm, land_ref),
                (ice_hbm, ice_ref),
                (east_hbm, east_ref),
                (north_hbm, north_ref),
                (lanes_hbm.at[member], lanes_ref),
                (table_hbm.at[member], table_ref),
            )
        )
    ]
    for copy in small:
        copy.start()

    rows = land_ref.shape[0]
    blocks_ref = kept_ref.reshape(freqs, ND, rows, LANES)

    def fetch(group):
        part = (slice(None), pl.ds(group * GROUP, GROUP))
        return pltpu.make_async_copy(spectrum_ref.at[part], blocks_ref.at[part], sems.at[group])

    for group in range(DEPTH):
        fetch(group).start()
    edges_ref[...] = jnp.zeros_like(edges_ref)
    for copy in small:
        copy.wait()

    wet_cells = (1 - land_ref[...]).astype(jnp.float32)
    wet_ref[...] = wet_cells
    open_water = 0.5 * (1.0 - ice_ref[...].astype(jnp.float32))
    shape = wet_cells.shape
    tiles = rows // SUB
    for direction in range(ND):
        angle = 2.0 * math.pi * direction / ND
        project = math.cos(angle) * east_ref[...] + math.sin(angle) * north_ref[...]
        growth_ref[direction] = open_water * jnp.square(jnp.maximum(project, 0.0))

    lane = iota(shape, 1)
    even = lane % 2 == 0
    tile_lane = iota((SUB, LANES), 1)
    for row_ref in (swap_row_ref, other_row_ref):
        row_ref[pl.ds(2 * 18 * freqs, CORNERS), :] = jnp.zeros((CORNERS, LANES), jnp.float32)
    odd_sect, odd_slab = odd_position("sect"), odd_position("slab")

    half = GROUPS // 2
    for to_right in (True, False):
        target_ref = right_ref if to_right else left_ref

        def gather(index, carry):
            group = index + (0 if to_right else half)
            fetch(group).wait()

            @pl.when(group + DEPTH < GROUPS)
            def _():
                fetch(group + DEPTH).start()

            packed = [jnp.zeros((SUB, LANES), jnp.float32) for _ in range(tiles)]
            for i in range(GROUP):
                for j in range(freqs):
                    place = i * 2 * freqs + 2 * j
                    here = (tile_lane >= place) & (tile_lane < place + 2)
                    turn = (place + 2 if to_right else place) % LANES
                    first = pl.multiple_of((j * ND + group * GROUP + i) * rows, SUB)
                    for tile in range(tiles):
                        cells = kept_ref[pl.ds(first + tile * SUB, SUB), :]
                        packed[tile] = jnp.where(here, pltpu.roll(cells, turn, 1), packed[tile])
            for tile in range(tiles):
                target_ref[index, tile * SUB : (tile + 1) * SUB, :] = packed[tile]
            return carry

        lax.fori_loop(0, half, gather, 0)

    def side_message(group):
        to_right, fore = group < half, 1 if heads_down(group * GROUP) else -1
        ahead, behind = (LANES - 1, LANES - 2) if to_right else (0, 1)
        wet_near, wet_far = spread(wet_cells, ahead), spread(wet_cells, behind)
        near_even = not to_right
        packed = right_ref[group] if to_right else left_ref[group - half]
        values = packed * jnp.where(even == near_even, wet_near, wet_far)
        near = pltpu.roll(values, 1 if near_even else LANES - 1, 1)
        table = lanes_ref[group]
        follow = wet_near * (table[1:2] * values + table[2:3] * shift_rows(near, fore))
        message = jnp.where(even == near_even, values, follow)
        return jnp.where(lane == LANES - 1, wet_near, message)

    def row_message(direction):
        to_down = heads_down(direction)
        near_row, far_row = (rows - 1, rows - 2) if to_down else (0, 1)
        wet_near = wet_cells[near_row : near_row + 1, :]
        wet_far = wet_cells[far_row : far_row + 1, :]
        table = table_ref.at[class_of(direction)]
        near = kept_ref[pl.ds(direction * rows + near_row, freqs, stride=ND * rows), :] * wet_near
        far = kept_ref[pl.ds(direction * rows + far_row, freqs, stride=ND * rows), :] * wet_far
        beside = shift_lanes(near, 1 if heads_right(direction) else -1)
        return near, wet_near * (table[1] * far + table[2] * beside)

    for index in range(half):
        right, left = side_message(index), side_message(index + half)
        swap_side_ref[index] = jnp.where(odd_sect, left, right)
        other_side_ref[index] = jnp.where(odd_sect, right, left)
    by_slot = {(heads_down(d), row_slot(d)): d for d in range(ND)}
    for slot in range(18):
        pairs = zip(row_message(by_slot[True, slot]), row_message(by_slot[False, slot]))
        for which, (down, up) in enumerate(pairs):
            first = (which * 18 + slot) * freqs
            swap_row_ref[first : first + freqs, :] = jnp.where(odd_slab, up, down)
            other_row_ref[first : first + freqs, :] = jnp.where(odd_slab, down, up)


def corner_kernel(
    freqs, wet_ref, swapped_ref, other_ref, swap_in, other_in, _after, swap_row_ref, other_row_ref,
    rows_ref, sems,
):
    rows = wet_ref.shape[0]
    odd_sect, odd_slab = odd_position("sect"), odd_position("slab")
    last = iota((1, LANES), 1) == LANES - 1
    rows_ref[...] = jnp.zeros_like(rows_ref)
    for i in range(6):
        from_left = i < 3
        column = 0 if from_left else LANES - 1
        ends = []
        for row, index in ((rows - 1, i), (0, i + 3 if from_left else i - 3)):
            swapped = swapped_ref[index, row : row + 1, :]
            other = other_ref[index, row : row + 1, :]
            came = jnp.where(odd_sect == from_left, swapped, other)
            own = jnp.broadcast_to(wet_ref[row : row + 1, column : column + 1], (1, LANES))
            ends.append(jnp.where(last, own, came))
        rows_ref[0, i : i + 1, :] = jnp.where(odd_slab, *ends[::-1])
        rows_ref[1, i : i + 1, :] = jnp.where(odd_slab, *ends)
    start = 2 * 18 * freqs
    copies = [
        pltpu.make_async_copy(
            rows_ref.at[which], ref.at[pl.ds(start, CORNERS), :], sems.at[which]
        )
        for which, ref in ((0, swap_row_ref), (1, other_row_ref))
    ]
    for copy in copies:
        copy.start()
    for copy in copies:
        copy.wait()


def main_kernel(
    freqs, start, stop, member_ref, scalar_ref, wet_ref, growth_ref, spectrum_ref, *refs
):
    if start:
        _after, _kept_in, a_in, b_in, energy_in, *refs = refs
    kept_ref, a_ref, b_ref, energy_ref, ring0, ring1, sums_ref, sems, *first_refs = refs
    rings = (ring0, ring1)
    member = member_ref[0]
    nought = jnp.minimum(member, 0)
    rows = wet_ref.shape[0]
    tiles = rows // SUB

    def fetch(j, which):
        return pltpu.make_async_copy(spectrum_ref.at[j], rings[which], sems.at[which])

    for which in range(min(2, stop - start)):
        fetch(start + which, which).start()

    lane = iota((SUB, LANES), 1)
    sub = iota((SUB, LANES), 0)
    not_first = jnp.where(lane == 0, 0.0, 1.0)
    not_last = jnp.where(lane == LANES - 1, 0.0, 1.0)
    top, bottom = sub == 0, sub == SUB - 1
    energy_ref[...] = energy_in[...] if start else jnp.zeros_like(energy_ref)
    for first_ref in first_refs:
        first_ref[...] = jnp.zeros_like(first_ref)

    def tile_at(tile):
        return slice(tile * SUB, (tile + 1) * SUB)

    def parts_of(kind):
        if kind == 0:
            return ((0, 0, 0), (9, 1, 9), (18, 2, 0), (27, 3, 9))
        return ((kind, 0, kind), (18 - kind, 1, kind), (18 + kind, 2, kind), (36 - kind, 3, kind))

    def frequency(j, which):
        fetch(j, which).wait()
        ring_ref = rings[which]
        base = (member * freqs + j) * CLASSES * KINDS

        def speeds(part):
            _, quadrant, kind = part
            across = scalar_ref[base + kind * KINDS + 1]
            across = across * (not_first if quadrant in (0, 1) else not_last)
            return scalar_ref[base + kind * KINDS], across

        walks = [(kind, part) for kind in range(CLASSES - 1) for part in parts_of(kind)]
        wet = [wet_ref[tile_at(t), :] for t in range(tiles)]
        held = {}

        def mask(walk):
            direction = walks[walk][1][0]
            target = first_refs[walk % 4]
            cells = [ring_ref[direction, tile_at(t), :] * wet[t] for t in range(tiles)]
            for t in range(tiles):
                target[tile_at(t + 1), :] = cells[t]
            held[walk] = cells

        def step(walk, source, cells):
            _, quadrant, _ = walks[walk][1]
            alpha, across = speeds(walks[walk][1])
            to_down, to_right = sides(quadrant)
            ahead = [source[pl.ds((t + 1) * SUB - to_down + nought, SUB), :] for t in range(tiles)]
            return [
                cells[t] + alpha * ahead[t] + across * pltpu.roll(cells[t], to_right % LANES, 1)
                for t in range(tiles)
            ]

        def first_step(walk):
            after = step(walk, first_refs[walk % 4], held[walk])
            cells = [wet[t] * after[t] for t in range(tiles)]
            target = first_refs[4 + walk % 4]
            for t in range(tiles):
                target[tile_at(t + 1), :] = cells[t]
            held[walk] = cells

        def second_step(walk):
            direction = walks[walk][1][0]
            after = step(walk, first_refs[4 + walk % 4], held.pop(walk))
            for t in range(tiles):
                kept_ref[j, direction, tile_at(t), :] = after[t]
            return after, [growth_ref[direction, tile_at(t), :] * after[t] for t in range(tiles)]

        def plus(one, other):
            return [x + y for x, y in zip(one, other)]

        def add_up(kind, moved, grown):
            scale, high = scalar_ref[base + kind * KINDS + 2], scalar_ref[base + 3]
            scaled_high = scale * high
            if kind == 0:
                plain_x, plain_y = plus(moved[0], moved[2]), plus(moved[1], moved[3])
                grown_x, grown_y = plus(grown[0], grown[2]), plus(grown[1], grown[3])
                square = math.cos(0.5 * math.pi) ** 2
                for t in range(tiles):
                    plain = scale * plain_x[t], scale * plain_y[t]
                    whole_x = plain[0] + scaled_high * grown_x[t]
                    whole_y = plain[1] + scaled_high * grown_y[t]
                    energy_ref[tile_at(t), :] += plain[0] + plain[1]
                    sums_ref[0, tile_at(t), :] = whole_x + whole_y
                    sums_ref[1, tile_at(t), :] = whole_x + square * whole_y
            else:
                square = math.cos(2.0 * math.pi * kind / ND) ** 2
                for t in range(tiles):
                    plain = scale * moved[t]
                    whole = plain + scaled_high * grown[t]
                    energy_ref[tile_at(t), :] += plain
                    sums_ref[0, tile_at(t), :] += whole
                    sums_ref[1, tile_at(t), :] += square * whole

        moved, grown = [], []
        for walk in range(len(walks) + 2):
            if walk < len(walks):
                mask(walk)
            if 1 <= walk <= len(walks):
                first_step(walk - 1)
            if walk >= 2:
                kind = walks[walk - 2][0]
                after, with_growth = second_step(walk - 2)
                if kind and moved:
                    moved, grown = plus(moved, after), plus(grown, with_growth)
                elif kind:
                    moved, grown = after, with_growth
                else:
                    moved.append(after)
                    grown.append(with_growth)
                if walk % 4 == 1:
                    add_up(kind, moved, grown)
                    moved, grown = [], []
        at = pl.ds(pl.multiple_of(j * rows, SUB), rows)
        a_ref[at, :] = sums_ref[0]
        b_ref[at, :] = sums_ref[1]

    def pair(index, carry):
        for which in range(2):
            j = start + 2 * index + which
            frequency(j, which)

            @pl.when(j + 2 < stop)
            def _():
                fetch(j + 2, which).start()

        return carry

    lax.fori_loop(0, (stop - start) // 2, pair, 0)
    if (stop - start) % 2:
        frequency(jnp.int32(stop - 1), 0)


def edge_rows(freqs, to_down, direction, at):
    first = ((0 if to_down else 18) + row_slot(direction)) * freqs * SUB
    return pl.ds(first + at, freqs, stride=SUB)


def enter_kernel(
    freqs, member_ref, lanes_ref, table_ref, wet_ref, swap_side_ref, other_side_ref, swap_row_ref,
    other_row_ref, _edges_in, energy_in, columns_ref, edges_ref, energy_ref,
):
    member = member_ref[0]
    wet_cells = wet_ref[...]
    shape = wet_cells.shape
    rows = shape[0]
    lane = iota(shape, 1)
    row = iota(shape, 0)
    even = lane % 2 == 0
    width = 2 * freqs
    used = lane < GROUP * width
    energy = energy_in[...]
    start = 2 * 18 * freqs
    odd_sect, odd_slab = odd_position("sect"), odd_position("slab")

    def from_rows(to_down, part):
        return jnp.where(odd_slab == to_down, swap_row_ref[part, :], other_row_ref[part, :])

    for to_right in (True, False):
        near_column, far_column = (0, 1) if to_right else (LANES - 1, LANES - 2)
        near_even = to_right
        wet_near, wet_far = spread(wet_cells, near_column), spread(wet_cells, far_column)
        total = jnp.zeros(shape, jnp.float32)
        for index in range(GROUPS // 2):
            group = index if to_right else index + GROUPS // 2
            to_down = heads_down(group * GROUP)
            fore = 1 if to_down else -1
            message = jnp.where(odd_sect == to_right, swap_side_ref[index], other_side_ref[index])
            table = lanes_ref[member, group]
            turn = LANES - 1 if near_even else 1
            entered = pltpu.roll(message, turn, 1)
            corner_index = index if to_down else (index - 3 if to_right else index + 3)
            corner = from_rows(to_down, slice(start + corner_index, start + corner_index + 1))
            edge = 0 if to_down else rows - 1
            paths = corner[:, LANES - 1 :] + message[edge : edge + 1, LANES - 1 :]
            corner = pltpu.roll(jnp.broadcast_to(corner, (SUB, LANES)), turn, 1)[0:1]
            corner = jnp.broadcast_to(paths, (1, LANES)) * corner
            diagonal = shift_rows(wet_near * entered, fore)
            diagonal = jnp.where(row == edge, jnp.broadcast_to(corner, shape), diagonal)
            near = wet_near * (table[0:1] * entered + message + table[2:3] * diagonal)
            far = wet_near * wet_far * (table[1:2] * message)
            change = jnp.where(used, jnp.where(even == near_even, near, far), 0.0)
            columns_ref[group] = change
            total += table[3:4] * change
        total += pltpu.roll(total, LANES - width, 1) + pltpu.roll(total, LANES - 2 * width, 1)
        target = 0 if to_right else LANES - 2
        inside = (lane >= target) & (lane < target + 2)
        for j in range(freqs):
            turned = pltpu.roll(total, (target - 2 * j) % LANES, 1)
            energy += jnp.where(inside, turned, 0.0)
    energy_ref[...] = energy

    for to_down in (True, False):
        near_row, far_row = (0, 1) if to_down else (rows - 1, rows - 2)
        wet_near = wet_cells[near_row : near_row + 1, :]
        wet_both = wet_near * wet_cells[far_row : far_row + 1, :]
        totals = [jnp.zeros((freqs, LANES), jnp.float32) for _ in range(2)]
        for direction in range(ND):
            if heads_down(direction) != to_down:
                continue
            slot = row_slot(direction) * freqs
            entered = from_rows(to_down, slice(slot, slot + freqs))
            follow = from_rows(to_down, slice(18 * freqs + slot, 18 * freqs + slot + freqs))
            table = table_ref.at[member, class_of(direction)]
            side = 1 if heads_right(direction) else -1
            diagonal = shift_lanes(wet_near * entered, side)
            near = wet_near * (table[0] * entered + follow + table[2] * diagonal)
            far = wet_both * (table[1] * entered)
            for place, (change, at) in enumerate(((near, near_row), (far, far_row))):
                edges_ref[edge_rows(freqs, to_down, direction, at % SUB), :] = change
                totals[place] += table[3] * change
        for total, at in zip(totals, (near_row, far_row)):
            energy_ref[at : at + 1, :] += jnp.sum(total, axis=0, keepdims=True)


def entered_kernel(
    freqs, member_ref, lanes_ref, table_ref, ice_ref, east_ref, north_ref, growth_ref, columns_ref,
    edges_ref, a_in, b_in, a_ref, b_ref,
):
    member = member_ref[0]
    shape = ice_ref.shape
    rows = shape[0]
    lane = iota(shape, 1)
    even = lane % 2 == 0
    width = 2 * freqs
    a_ref[...] = a_in[...]
    b_ref[...] = b_in[...]

    for to_right in (True, False):
        near_column, far_column = (0, 1) if to_right else (LANES - 1, LANES - 2)

        def packed_field(values):
            return jnp.where(
                even == to_right, spread(values, near_column), spread(values, far_column)
            )

        east, north = packed_field(east_ref[...]), packed_field(north_ref[...])
        open_water = 0.5 * (1.0 - packed_field(ice_ref[...].astype(jnp.float32)))
        sums = [jnp.zeros(shape, jnp.float32) for _ in range(2)]
        for index in range(GROUPS // 2):
            group = index if to_right else index + GROUPS // 2
            table = lanes_ref[member, group]
            project = table[6:7] * east + table[7:8] * north
            growth = open_water * jnp.square(jnp.maximum(project, 0.0))
            grown = columns_ref[group] * (1.0 + table[5:6] * growth)
            sums[0] += table[3:4] * grown
            sums[1] += table[4:5] * grown
        sums = [
            part + pltpu.roll(part, LANES - width, 1) + pltpu.roll(part, LANES - 2 * width, 1)
            for part in sums
        ]
        target = 0 if to_right else LANES - 2
        inside = (lane >= target) & (lane < target + 2)
        for j in range(freqs):
            turn = (target - 2 * j) % LANES
            block = slice(j * rows, (j + 1) * rows)
            place = [jnp.where(inside, pltpu.roll(part, turn, 1), 0.0) for part in sums]
            a_ref[block, :] += place[0]
            b_ref[block, :] += place[1]

    for to_down in (True, False):
        near_row, far_row = (0, 1) if to_down else (rows - 1, rows - 2)
        totals = [jnp.zeros((freqs, LANES), jnp.float32) for _ in range(4)]
        for direction in range(ND):
            if heads_down(direction) != to_down:
                continue
            table = table_ref.at[member, class_of(direction)]
            square = math.cos(2.0 * math.pi * direction / ND) ** 2
            for place, at in enumerate((near_row, far_row)):
                change = edges_ref[edge_rows(freqs, to_down, direction, at % SUB), :]
                growth = growth_ref[direction, at : at + 1, :]
                grown = (table[3] * change) * (1.0 + table[4] * growth)
                totals[2 * place] += grown
                totals[2 * place + 1] += square * grown
        for place, at in enumerate((near_row, far_row)):
            picked = pl.ds(at, freqs, stride=rows)
            a_ref[picked, :] += totals[2 * place]
            b_ref[picked, :] += totals[2 * place + 1]


def stress_kernel(
    freqs, member_ref, scalar_ref, wet_ref, a_ref, b_ref, own_ref, other_ref, sums_ref, ratio_ref
):
    member = member_ref[0]
    wet_cells = wet_ref[...]
    rows = wet_cells.shape[0]
    energy = wet_cells * (own_ref[...] + other_ref[...]) / (ND * NF)
    square = jnp.square(energy)

    sums = [jnp.zeros(wet_cells.shape, jnp.float32) for _ in range(3)]
    for j in range(freqs):
        base = (member * freqs + j) * CLASSES * KINDS
        high, shoal = scalar_ref[base + 3], scalar_ref[base + 4]
        block = slice(j * rows, (j + 1) * rows)
        ratio = wet_cells / (1.0 + (2.0 * high) * square)
        ratio_ref[j] = ratio
        whole = ratio * a_ref[block, :]
        along = ratio * b_ref[block, :]
        sums[0] += shoal * along + (shoal - 0.5) * whole
        sums[1] += (2.0 * shoal - 0.5) * whole - shoal * along
        sums[2] += whole
    for index in range(3):
        sums_ref[index] = sums[index] / (ND * NF)


def total_kernel(own_ref, other_ref, sums_ref, stress_ref):
    sums_ref[...] = own_ref[...] + other_ref[...]
    stress_ref[...] = sums_ref[0:2]


def strip_kernel(stress_ref, swapped_ref, other_ref, beside_ref, first_ref, second_ref):
    rows = stress_ref.shape[1]
    low_half = iota((rows, LANES), 1) < LANES // 2
    odd_sect = lax.rem(lax.axis_index("sect"), 2) == 1
    odd_slab = lax.rem(lax.axis_index("slab"), 2) == 1
    for index in range(2):
        swapped, other = swapped_ref[index], other_ref[index]
        beside = jnp.where(low_half != odd_sect, swapped, other)
        beside_ref[index] = beside
        ends = [
            jnp.concatenate([values[first : first + SUB] for values in (stress_ref[index], beside)], 1)
            for first in (0, rows - SUB)
        ]
        first_ref[index] = jnp.where(odd_slab, *ends)
        second_ref[index] = jnp.where(odd_slab, *ends[::-1])


BEHIND = 8


def final_kernel(
    freqs, member_ref, scalar_ref, depth_ref, ratios_ref, sums_ref, beside_ref, swapped_ref,
    other_ref, growth_ref, kept_ref, columns_ref, edges_ref,
    result_ref, level_ref, damping_ref, ring0, ring1, sems,
):
    member = member_ref[0]
    rings = (ring0, ring1)
    rows = depth_ref.shape[0]
    slab, slabs = lax.axis_index("slab"), lax.axis_size("slab")
    sect, sects = lax.axis_index("sect"), lax.axis_size("sect")
    above_ok = jnp.where(slab > 0, 1.0, 0.0)
    below_ok = jnp.where(slab < slabs - 1, 1.0, 0.0)
    left_ok = jnp.where(sect > 0, 1.0, 0.0)
    right_ok = jnp.where(sect < sects - 1, 1.0, 0.0)

    odd = lax.rem(slab, 2) == 1

    def framed(index):
        middle = jnp.concatenate([sums_ref[index], beside_ref[index]], axis=1)
        swapped, other = swapped_ref[index], other_ref[index]
        below = jnp.where(odd, other, swapped)
        above = jnp.where(odd, swapped, other)
        return jnp.concatenate([middle, below, above], axis=0)

    def around(values, axis):
        size = values.shape[axis]
        return pltpu.roll(values, 1, axis) + pltpu.roll(values, size - 1, axis)

    stress_x, stress_y = framed(0), framed(1)
    frame = stress_x.shape
    frame_row, frame_lane = iota(frame, 0), iota(frame, 1)
    row_ok = jnp.where(frame_row < rows, 1.0, jnp.where(frame_row < rows + SUB, below_ok, above_ok))
    lane_ok = jnp.where(
        frame_lane < LANES, 1.0, jnp.where(frame_lane < LANES + LANES // 2, right_ok, left_ok)
    )
    inside = row_ok * lane_ok / 4.5
    source = -((around(stress_x, 0) - 2.0 * stress_x) + (around(stress_y, 1) - 2.0 * stress_y))
    level = inside * source
    for _ in range(JAC):
        level = inside * (source + around(level, 0) + around(level, 1))
    level = level[:rows, :LANES]
    level_ref[...] = level
    damping = 1.0 / (1.0 + 4.0 * sums_ref[2] / (jnp.square(depth_ref[...] + level) + 1.0))
    tiles = rows // SUB
    damping_ref[...] = damping
    tile_lane = iota((SUB, LANES), 1)

    def send(j, which):
        return pltpu.make_async_copy(rings[which], result_ref.at[j], sems.at[which])

    def frequency(j, which):
        @pl.when(j >= 2)
        def _():
            send(j - 2, which).wait()

        base = (member * freqs + j) * CLASSES * KINDS
        high = scalar_ref[base + 3]
        scales = [scalar_ref[base + kind * KINDS + 2] for kind in range(CLASSES)]

        def damped(direction, t, ratio, high_ratio):
            to_down, to_right = sides(direction // (ND // 4))
            part = slice(t * SUB, (t + 1) * SUB)
            target = 0 if to_right > 0 else LANES - 2
            at_side = (tile_lane >= target) & (tile_lane < target + 2)
            turn = target - direction % GROUP * 2 * freqs + 2 * LANES - 2 * j
            entered = pltpu.roll(columns_ref[direction // GROUP, part, :], lax.rem(turn, LANES), 1)
            value = kept_ref[j, direction, part, :] + jnp.where(at_side, entered, 0.0)
            if t == (0 if to_down > 0 else tiles - 1):
                edge = ((0 if to_down > 0 else 18) + row_slot(direction)) * freqs + j
                value += edges_ref[pl.ds(pl.multiple_of(edge * SUB, SUB), SUB), :]
            factor = ratio + high_ratio * growth_ref[direction, part, :]
            return value * (scales[class_of(direction)] * factor)

        pending = []
        for t in range(tiles):
            part = slice(t * SUB, (t + 1) * SUB)
            ratio = ratios_ref[j, part, :] * damping_ref[part, :]
            high_ratio = high * ratio
            for direction in range(ND):
                pending.append((direction, part, damped(direction, t, ratio, high_ratio)))
                if len(pending) > BEHIND:
                    target, place, value = pending.pop(0)
                    rings[which][target, place, :] = value
        for target, place, value in pending:
            rings[which][target, place, :] = value
        send(j, which).start()

    def pair(index, carry):
        for which in range(2):
            frequency(2 * index + which, which)
        return carry

    lax.fori_loop(0, freqs // 2, pair, 0)
    if freqs % 2:
        frequency(jnp.int32(freqs - 1), 0)
    for j in range(max(0, freqs - 2), freqs):
        send(j, j % 2).wait()


def swap(values, axis, first):
    count = lax.axis_size(axis)
    pairs = [(i, i + 1) for i in range(first, count - 1, 2)]
    return lax.ppermute(values, axis, pairs + [(b, a) for a, b in pairs])


def others_sum(values, axis):
    count = lax.axis_size(axis)
    total = None
    for step in range(1, count):
        part = lax.ppermute(values, axis, [(i, (i + step) % count) for i in range(count)])
        total = part if total is None else total + part
    return jnp.zeros_like(values) if total is None else total


VMEM = pl.BlockSpec(memory_space=pltpu.VMEM)
SMEM = pl.BlockSpec(memory_space=pltpu.SMEM)
HBM = pl.BlockSpec(memory_space=pltpu.HBM)
ANY = pl.BlockSpec(memory_space=pl.ANY)


def in_vmem(*shape):
    return pltpu.VMEM(shape, jnp.float32)


def in_any(*shape):
    return jax.ShapeDtypeStruct(shape, jnp.float32)


def in_hbm(values):
    return pltpu.with_memory_space_constraint(values, pltpu.HBM)


def call(kernel, in_specs, out_shape, out_specs, flops, moved, scratch=(), aliases=None, limit=6):
    return pl.pallas_call(
        kernel,
        in_specs=in_specs,
        out_shape=out_shape,
        out_specs=out_specs,
        scratch_shapes=list(scratch),
        input_output_aliases=aliases or {},
        cost_estimate=pl.CostEstimate(flops=flops, bytes_accessed=moved, transcendentals=0),
        compiler_params=pltpu.CompilerParams(vmem_limit_bytes=limit << 20),
    )


def resident(spectrum, land_mask, ice_mask, wind_u, wind_v, depth):
    local_comp, rows, lanes = spectrum.shape
    freqs = local_comp // ND
    members = lax.axis_size("comp")
    member = lax.axis_index("comp").astype(jnp.int32).reshape(1)
    scalars, lane_table, row_table = numpy_tables(members, freqs)
    scalars, lane_table, row_table = map(jnp.asarray, (scalars, lane_table, row_table))
    cells = rows * lanes
    row_message = 2 * 18 * freqs + CORNERS
    block = (freqs, ND, rows, lanes)
    spectrum = spectrum.reshape(block)

    growth, wet, swap_side, other_side, swap_row, other_row, edges = call(
        functools.partial(pack_kernel, freqs),
        [SMEM] + [HBM] * 7,
        (
            in_any(ND, rows, lanes),
            in_any(rows, lanes),
            in_any(GROUPS // 2, rows, lanes),
            in_any(GROUPS // 2, rows, lanes),
            in_any(row_message, lanes),
            in_any(row_message, lanes),
            in_any(2 * 18 * freqs * SUB, lanes),
        ),
        (VMEM,) * 7,
        flops=local_comp * cells * 4,
        moved=local_comp * cells * 4,
        scratch=[
            pltpu.VMEM((local_comp * rows, lanes), jnp.float32),
            pltpu.VMEM((GROUPS // 2, rows, lanes), jnp.float32),
            pltpu.VMEM((GROUPS // 2, rows, lanes), jnp.float32),
            pltpu.VMEM(lane_table.shape[1:], jnp.float32),
            pltpu.VMEM(row_table.shape[1:], jnp.float32),
            pltpu.VMEM((rows, lanes), jnp.int32),
            pltpu.VMEM((rows, lanes), jnp.int32),
            pltpu.VMEM((rows, lanes), jnp.float32),
            pltpu.VMEM((rows, lanes), jnp.float32),
            pltpu.SemaphoreType.DMA((6,)),
            pltpu.SemaphoreType.DMA((GROUPS,)),
        ],
        limit=30,
    )(
        member,
        *map(in_hbm, (lane_table, row_table, land_mask, ice_mask, wind_u, wind_v, spectrum)),
    )

    def main_part(start, stop, *before):
        return call(
            functools.partial(main_kernel, freqs, start, stop),
            [SMEM, SMEM, VMEM, VMEM, HBM] + ([ANY, VMEM, VMEM, VMEM, VMEM] if before else []),
            (
                in_vmem(*block),
                in_any(freqs * rows, lanes),
                in_any(freqs * rows, lanes),
                in_any(rows, lanes),
            ),
            (VMEM,) * 4,
            flops=local_comp * cells * 16 * (stop - start) // freqs,
            moved=local_comp * cells * 8 * (stop - start) // freqs,
            scratch=[
                pltpu.VMEM((ND, rows, lanes), jnp.float32),
                pltpu.VMEM((ND, rows, lanes), jnp.float32),
                pltpu.VMEM((2, rows, lanes), jnp.float32),
                pltpu.SemaphoreType.DMA((2,)),
            ]
            + [pltpu.VMEM((rows + 2 * SUB, lanes), jnp.float32)] * 8,
            aliases={6 + index: index for index in range(4)} if before else {},
        )(member, scalars, wet, growth, in_hbm(spectrum), *before)

    early = max(1, freqs // 3)
    swap_side, other_side = swap(swap_side, "sect", 0), swap(other_side, "sect", 1)
    kept, *partial = main_part(0, early)
    swap_row, other_row = call(
        functools.partial(corner_kernel, freqs),
        [VMEM, VMEM, VMEM, ANY, ANY, ANY],
        (in_any(row_message, lanes), in_any(row_message, lanes)),
        (ANY, ANY),
        flops=100,
        moved=1 << 15,
        scratch=[pltpu.VMEM((2, CORNERS, lanes), jnp.float32), pltpu.SemaphoreType.DMA((2,))],
        aliases={3: 0, 4: 1},
    )(wet, swap_side, other_side, swap_row, other_row, partial[-1])
    swapped_row = swap(swap_row, "slab", 0)
    other_row = swap(other_row, "slab", 1)
    kept, a_sums, b_sums, energy = main_part(early, freqs, swap_row, kept, *partial)

    columns, edges, energy = call(
        functools.partial(enter_kernel, freqs),
        [SMEM] + [VMEM] * 9,
        (
            in_any(GROUPS, rows, lanes),
            in_any(2 * 18 * freqs * SUB, lanes),
            in_any(rows, lanes),
        ),
        (VMEM,) * 3,
        flops=cells * 600,
        moved=cells * 200,
        aliases={8: 1, 9: 2},
    )(
        member, lane_table, row_table, wet, swap_side, other_side, swapped_row, other_row, edges,
        energy,
    )
    energy_there = others_sum(energy, "comp")
    a_sums, b_sums = call(
        functools.partial(entered_kernel, freqs),
        [SMEM] + [VMEM] * 10,
        (in_any(freqs * rows, lanes), in_any(freqs * rows, lanes)),
        (VMEM,) * 2,
        flops=cells * 600,
        moved=cells * 200,
        aliases={9: 0, 10: 1},
    )(
        member, lane_table, row_table, ice_mask, wind_u, wind_v, growth, columns, edges,
        a_sums, b_sums,
    )

    sums, ratios = call(
        functools.partial(stress_kernel, freqs),
        [SMEM, SMEM] + [VMEM] * 5,
        (in_any(3, rows, lanes), in_any(freqs, rows, lanes)),
        (VMEM, VMEM),
        flops=cells * freqs * 12,
        moved=cells * freqs * 8,
    )(member, scalars, wet, a_sums, b_sums, energy, energy_there)
    sums, stress = call(
        total_kernel,
        [VMEM, VMEM],
        (in_any(3, rows, lanes), in_any(2, rows, lanes)),
        (VMEM, VMEM),
        flops=cells * 3,
        moved=cells * 44,
    )(sums, others_sum(sums, "comp"))
    beside, first, second = call(
        strip_kernel,
        [VMEM, VMEM, VMEM],
        (in_any(2, rows, lanes), in_any(2, SUB, 2 * lanes), in_any(2, SUB, 2 * lanes)),
        (VMEM, VMEM, VMEM),
        flops=cells * 4,
        moved=cells * 36,
    )(stress, swap(stress, "sect", 0), swap(stress, "sect", 1))
    aside, beyond = swap(first, "slab", 0), swap(second, "slab", 1)

    result, level = call(
        functools.partial(final_kernel, freqs),
        [SMEM, SMEM] + [VMEM] * 10,
        (in_any(*block), in_any(rows, lanes)),
        (HBM, VMEM),
        flops=local_comp * cells * 6,
        moved=local_comp * cells * 8,
        scratch=[
            pltpu.VMEM((rows, lanes), jnp.float32),
            pltpu.VMEM((ND, rows, lanes), jnp.float32),
            pltpu.VMEM((ND, rows, lanes), jnp.float32),
            pltpu.SemaphoreType.DMA((2,)),
        ],
    )(
        member, scalars, depth, ratios, sums, beside, aside, beyond, growth, kept,
        columns, edges,
    )
    return result.reshape(local_comp, rows, lanes), level


def local(spectrum, *fields):
    local_comp, rows, lanes = spectrum.shape
    whole_rings = local_comp % ND == 0 and GROUP * 2 * (local_comp // ND) < LANES - 1
    if whole_rings and lanes == LANES and rows % SUB == 0:
        return resident(spectrum, *fields)
    return general(spectrum, *fields)


def solution(mesh):
    in_specs = (
        P("comp", "slab", "sect"),
        P("slab", "sect"),
        P("slab", "sect"),
        P("slab", "sect"),
        P("slab", "sect"),
        P("slab", "sect"),
    )
    out_specs = (P("comp", "slab", "sect"), P("slab", "sect"))
    return jax.shard_map(local, mesh=mesh, in_specs=in_specs, out_specs=out_specs, check_vma=False)
```

```python
import functools
import math

import jax
import jax.numpy as jnp
import numpy as np
from jax import lax
from jax.experimental import pallas as pl
from jax.experimental.pallas import tpu as pltpu
from jax.sharding import PartitionSpec as P

ND = 36
NF = 36
STEPS = 2
JAC = 4


def extended(cells, sides, width):
    for axis, dim in sides:
        count = lax.axis_size(axis)
        ends = count - 1
        head = lax.slice_in_dim(cells, 0, width, axis=dim)
        tail = lax.slice_in_dim(cells, cells.shape[dim] - width, cells.shape[dim], axis=dim)
        cells = jnp.concatenate(
            [
                lax.ppermute(tail, axis, [(i, (i + 1) % count) for i in range(ends)]),
                cells,
                lax.ppermute(head, axis, [((i + 1) % count, i) for i in range(ends)]),
            ],
            axis=dim,
        )
    return cells


def tables(index):
    freq_index = (index // ND).astype(jnp.float32)
    angle_index = (index % ND).astype(jnp.float32)
    heading = 2.0 * math.pi * angle_index / ND
    return (
        jnp.cos(heading),
        jnp.sin(heading),
        jnp.power(1.1, -freq_index),
        jnp.power(1.1, freq_index - (NF - 1)),
        0.5 + 0.5 * freq_index / (NF - 1),
    )


def column(values):
    return values[:, None, None]


def advect(spectra, wet_cells, speed_x, speed_y):
    padded = extended(spectra, (("slab", 1), ("sect", 2)), 1)
    upper_rows = padded[:, :-2, 1:-1]
    lower_rows = padded[:, 2:, 1:-1]
    left_cells = padded[:, 1:-1, :-2]
    right_cells = padded[:, 1:-1, 2:]
    change = (
        jnp.maximum(speed_x, 0.0) * (spectra - upper_rows)
        + jnp.minimum(speed_x, 0.0) * (lower_rows - spectra)
        + jnp.maximum(speed_y, 0.0) * (spectra - left_cells)
        + jnp.minimum(speed_y, 0.0) * (right_cells - spectra)
    )
    return (spectra - change) * wet_cells


def forcing(spectra, energy, wind_east, wind_north, ice_cover, cosine, sine, high_ratio):
    project = cosine * wind_east + sine * wind_north
    growth = 0.5 * high_ratio * jnp.square(jnp.maximum(project, 0.0)) * (1.0 - ice_cover)
    return spectra * (1.0 + growth) / (1.0 + 2.0 * high_ratio * jnp.square(energy))


def stress_weights(cosine, sine, shoaling):
    return jnp.stack(
        [shoaling * (cosine * cosine + 1.0) - 0.5, shoaling * (sine * sine + 1.0) - 0.5]
    )


def surge_solve(stress):
    padded = extended(stress, (("slab", 1), ("sect", 2)), 1)
    source_term = -(
        padded[0, 2:, 1:-1]
        + padded[0, :-2, 1:-1]
        - 2.0 * stress[0]
        + (padded[1, 1:-1, 2:] + padded[1, 1:-1, :-2] - 2.0 * stress[1])
    )
    surge_level = source_term / 4.5
    for _ in range(JAC):
        neighbours = extended(surge_level, (("slab", 0), ("sect", 1)), 1)
        surge_level = (
            source_term
            + neighbours[2:, 1:-1]
            + neighbours[:-2, 1:-1]
            + neighbours[1:-1, 2:]
            + neighbours[1:-1, :-2]
        ) / 4.5
    return surge_level


def general(spectrum, land_mask, ice_mask, wind_u, wind_v, depth):
    groups = lax.axis_size("comp")
    member = lax.axis_index("comp")
    local_comp, block_rows, block_cols = spectrum.shape
    point_rows = block_rows // groups
    total_comp = ND * NF
    wet_cells = (1 - land_mask).astype(jnp.float32)
    ice_cover = ice_mask.astype(jnp.float32)

    def own_rows(values):
        return lax.dynamic_slice_in_dim(values, member * point_rows, point_rows, values.ndim - 2)

    own_index = member * local_comp + jnp.arange(local_comp, dtype=jnp.int32)
    cosine, sine, low_ratio, high_ratio, shoaling = tables(own_index)
    spectra = spectrum * wet_cells
    for _ in range(STEPS):
        spectra = advect(
            spectra, wet_cells, column(0.7 * low_ratio * cosine), column(0.7 * low_ratio * sine)
        )
    points = lax.all_to_all(spectra, "comp", split_axis=1, concat_axis=0, tiled=True)
    cosine_full, sine_full, _, high_full, shoal_full = tables(
        jnp.arange(total_comp, dtype=jnp.int32)
    )
    energy = jnp.sum(points, axis=0) / total_comp
    sourced = forcing(
        points,
        energy,
        own_rows(wind_u),
        own_rows(wind_v),
        own_rows(ice_cover),
        column(cosine_full),
        column(sine_full),
        column(high_full),
    )
    stress = (
        jnp.einsum(
            "sk,krc->src",
            stress_weights(cosine_full, sine_full, shoal_full),
            sourced,
            precision=lax.Precision.HIGHEST,
        )
        / total_comp
    )
    stress_block = lax.all_gather(stress, "comp", axis=1, tiled=True)
    level_block = surge_solve(stress_block)
    final_energy = jnp.sum(sourced, axis=0) / total_comp
    damped = sourced / (
        1.0 + 4.0 * final_energy / (jnp.square(own_rows(depth) + own_rows(level_block)) + 1.0)
    )
    result = lax.all_to_all(damped, "comp", split_axis=0, concat_axis=1, tiled=True)
    return (result, level_block)


LANES = 128
SUB = 8
CLASSES = 10
KINDS = 5
GROUP = 3
GROUPS = ND // GROUP
CORNERS = 8


def class_of(direction):
    folded = direction % 18
    return folded if folded <= 9 else 18 - folded


def heads_down(direction):
    return direction < 9 or direction >= 27


def heads_right(direction):
    return direction < 18


def row_slot(direction):
    if direction < 9:
        return direction
    return direction - 18 if direction >= 27 else direction - 9


def numpy_tables(members, freqs):
    j = np.arange(members * freqs, dtype=np.float64)
    heading = 2.0 * np.pi * np.arange(ND) / ND
    cosine, sine = np.cos(heading), np.sin(heading)
    low = 1.1 ** (-j)
    high = 1.1 ** (j - (NF - 1))
    shoal = 0.5 + 0.5 * j / (NF - 1)
    step_x = 0.7 * low[:, None] * np.abs(cosine)
    step_y = 0.7 * low[:, None] * np.abs(sine)
    keep = 1.0 - step_x - step_y
    alpha, beta, scale = step_x / keep, step_y / keep, keep * keep
    classes = np.arange(CLASSES)
    square = np.broadcast_to(cosine * cosine, alpha.shape)
    scalars = np.stack(
        [
            alpha[:, classes],
            beta[:, classes],
            scale[:, classes],
            np.broadcast_to(high[:, None], (j.size, CLASSES)),
            np.broadcast_to(shoal[:, None], (j.size, CLASSES)),
        ],
        axis=-1,
    ).astype(np.float32)

    kinds = np.stack(
        [
            2.0 * beta,
            beta * beta,
            alpha * beta,
            scale,
            scale * square,
            np.broadcast_to(high[:, None], alpha.shape),
            np.broadcast_to(cosine, alpha.shape),
            np.broadcast_to(sine, alpha.shape),
        ]
    )
    lanes = np.zeros((members, GROUPS, 8, LANES), np.float32)
    packed = kinds.reshape(8, members, freqs, GROUPS, GROUP)
    packed = np.repeat(packed.transpose(1, 3, 0, 4, 2), 2, axis=-1)
    lanes[..., : GROUP * 2 * freqs] = packed.reshape(members, GROUPS, 8, -1)

    rows = np.stack(
        [2.0 * alpha, alpha * alpha, alpha * beta, scale, np.broadcast_to(high[:, None], alpha.shape)]
    )[:, :, classes]
    rows = rows.reshape(5, members, freqs, CLASSES).transpose(1, 3, 0, 2)
    rows = np.broadcast_to(rows[..., None], rows.shape + (LANES,)).astype(np.float32)
    return scalars.reshape(-1), lanes, rows


def odd_position(axis):
    return lax.rem(lax.axis_index(axis), 2) == 1


def iota(shape, axis):
    return lax.broadcasted_iota(jnp.int32, shape, axis)


def spread(values, column):
    return jnp.broadcast_to(values[:, column : column + 1], values.shape)


def shift_rows(values, step):
    rows = values.shape[0]
    edge = 0 if step > 0 else rows - 1
    moved = pltpu.roll(values, step % rows, 0)
    return jnp.where(iota(values.shape, 0) == edge, 0.0, moved)


def shift_lanes(values, step):
    lanes = values.shape[1]
    edge = 0 if step > 0 else lanes - 1
    moved = pltpu.roll(values, step % lanes, 1)
    return jnp.where(iota(values.shape, 1) == edge, 0.0, moved)


DEPTH = 3


def sides(quadrant):
    return 1 if quadrant in (0, 3) else -1, 1 if quadrant in (0, 1) else -1


def pack_kernel(
    freqs, member_ref, lanes_hbm, table_hbm, land_hbm, ice_hbm, east_hbm, north_hbm, spectrum_ref,
    growth_ref, wet_ref, swap_side_ref, other_side_ref, swap_row_ref, other_row_ref, edges_ref,
    kept_ref, right_ref, left_ref, lanes_ref, table_ref, land_ref, ice_ref, east_ref, north_ref, small_sems, sems,
):
    member = member_ref[0]
    small = [
        pltpu.make_async_copy(source, target, small_sems.at[index])
        for index, (source, target) in enumerate(
            (
                (land_hbm, land_ref),
                (ice_hbm, ice_ref),
                (east_hbm, east_ref),
                (north_hbm, north_ref),
                (lanes_hbm.at[member], lanes_ref),
                (table_hbm.at[member], table_ref),
            )
        )
    ]
    for copy in small:
        copy.start()

    rows = land_ref.shape[0]
    blocks_ref = kept_ref.reshape(freqs, ND, rows, LANES)

    def fetch(group):
        part = (slice(None), pl.ds(group * GROUP, GROUP))
        return pltpu.make_async_copy(spectrum_ref.at[part], blocks_ref.at[part], sems.at[group])

    for group in range(DEPTH):
        fetch(group).start()
    edges_ref[...] = jnp.zeros_like(edges_ref)
    for copy in small:
        copy.wait()

    wet_cells = (1 - land_ref[...]).astype(jnp.float32)
    wet_ref[...] = wet_cells
    open_water = 0.5 * (1.0 - ice_ref[...].astype(jnp.float32))
    shape = wet_cells.shape
    tiles = rows // SUB
    for direction in range(ND):
        angle = 2.0 * math.pi * direction / ND
        project = math.cos(angle) * east_ref[...] + math.sin(angle) * north_ref[...]
        growth_ref[direction] = open_water * jnp.square(jnp.maximum(project, 0.0))

    lane = iota(shape, 1)
    even = lane % 2 == 0
    tile_lane = iota((SUB, LANES), 1)
    for row_ref in (swap_row_ref, other_row_ref):
        row_ref[pl.ds(2 * 18 * freqs, CORNERS), :] = jnp.zeros((CORNERS, LANES), jnp.float32)
    odd_sect, odd_slab = odd_position("sect"), odd_position("slab")

    half = GROUPS // 2
    for to_right in (True, False):
        target_ref = right_ref if to_right else left_ref

        def gather(index, carry):
            group = index + (0 if to_right else half)
            fetch(group).wait()

            @pl.when(group + DEPTH < GROUPS)
            def _():
                fetch(group + DEPTH).start()

            packed = [jnp.zeros((SUB, LANES), jnp.float32) for _ in range(tiles)]
            for i in range(GROUP):
                for j in range(freqs):
                    place = i * 2 * freqs + 2 * j
                    here = (tile_lane >= place) & (tile_lane < place + 2)
                    turn = (place + 2 if to_right else place) % LANES
                    first = pl.multiple_of((j * ND + group * GROUP + i) * rows, SUB)
                    for tile in range(tiles):
                        cells = kept_ref[pl.ds(first + tile * SUB, SUB), :]
                        packed[tile] = jnp.where(here, pltpu.roll(cells, turn, 1), packed[tile])
            for tile in range(tiles):
                target_ref[index, tile * SUB : (tile + 1) * SUB, :] = packed[tile]
            return carry

        lax.fori_loop(0, half, gather, 0)

    def side_message(group):
        to_right, fore = group < half, 1 if heads_down(group * GROUP) else -1
        ahead, behind = (LANES - 1, LANES - 2) if to_right else (0, 1)
        wet_near, wet_far = spread(wet_cells, ahead), spread(wet_cells, behind)
        near_even = not to_right
        packed = right_ref[group] if to_right else left_ref[group - half]
        values = packed * jnp.where(even == near_even, wet_near, wet_far)
        near = pltpu.roll(values, 1 if near_even else LANES - 1, 1)
        table = lanes_ref[group]
        follow = wet_near * (table[1:2] * values + table[2:3] * shift_rows(near, fore))
        message = jnp.where(even == near_even, values, follow)
        return jnp.where(lane == LANES - 1, wet_near, message)

    def row_message(direction):
        to_down = heads_down(direction)
        near_row, far_row = (rows - 1, rows - 2) if to_down else (0, 1)
        wet_near = wet_cells[near_row : near_row + 1, :]
        wet_far = wet_cells[far_row : far_row + 1, :]
        table = table_ref.at[class_of(direction)]
        near = kept_ref[pl.ds(direction * rows + near_row, freqs, stride=ND * rows), :] * wet_near
        far = kept_ref[pl.ds(direction * rows + far_row, freqs, stride=ND * rows), :] * wet_far
        beside = shift_lanes(near, 1 if heads_right(direction) else -1)
        return near, wet_near * (table[1] * far + table[2] * beside)

    for index in range(half):
        right, left = side_message(index), side_message(index + half)
        swap_side_ref[index] = jnp.where(odd_sect, left, right)
        other_side_ref[index] = jnp.where(odd_sect, right, left)
    by_slot = {(heads_down(d), row_slot(d)): d for d in range(ND)}
    for slot in range(18):
        pairs = zip(row_message(by_slot[True, slot]), row_message(by_slot[False, slot]))
        for which, (down, up) in enumerate(pairs):
            first = (which * 18 + slot) * freqs
            swap_row_ref[first : first + freqs, :] = jnp.where(odd_slab, up, down)
            other_row_ref[first : first + freqs, :] = jnp.where(odd_slab, down, up)


def corner_kernel(
    freqs, wet_ref, swapped_ref, other_ref, swap_in, other_in, _after, swap_row_ref, other_row_ref,
    rows_ref, sems,
):
    rows = wet_ref.shape[0]
    odd_sect, odd_slab = odd_position("sect"), odd_position("slab")
    last = iota((1, LANES), 1) == LANES - 1
    rows_ref[...] = jnp.zeros_like(rows_ref)
    for i in range(6):
        from_left = i < 3
        column = 0 if from_left else LANES - 1
        ends = []
        for row, index in ((rows - 1, i), (0, i + 3 if from_left else i - 3)):
            swapped = swapped_ref[index, row : row + 1, :]
            other = other_ref[index, row : row + 1, :]
            came = jnp.where(odd_sect == from_left, swapped, other)
            own = jnp.broadcast_to(wet_ref[row : row + 1, column : column + 1], (1, LANES))
            ends.append(jnp.where(last, own, came))
        rows_ref[0, i : i + 1, :] = jnp.where(odd_slab, *ends[::-1])
        rows_ref[1, i : i + 1, :] = jnp.where(odd_slab, *ends)
    start = 2 * 18 * freqs
    copies = [
        pltpu.make_async_copy(
            rows_ref.at[which], ref.at[pl.ds(start, CORNERS), :], sems.at[which]
        )
        for which, ref in ((0, swap_row_ref), (1, other_row_ref))
    ]
    for copy in copies:
        copy.start()
    for copy in copies:
        copy.wait()


def main_kernel(
    freqs, start, stop, member_ref, scalar_ref, wet_ref, growth_ref, spectrum_ref, *refs
):
    if start:
        _after, _kept_in, a_in, b_in, energy_in, *refs = refs
    kept_ref, a_ref, b_ref, energy_ref, ring0, ring1, sums_ref, sems, *first_refs = refs
    rings = (ring0, ring1)
    member = member_ref[0]
    rows = wet_ref.shape[0]
    tiles = rows // SUB

    def fetch(j, which):
        return pltpu.make_async_copy(spectrum_ref.at[j], rings[which], sems.at[which])

    for which in range(min(2, stop - start)):
        fetch(start + which, which).start()

    lane = iota((SUB, LANES), 1)
    sub = iota((SUB, LANES), 0)
    not_first = jnp.where(lane == 0, 0.0, 1.0)
    not_last = jnp.where(lane == LANES - 1, 0.0, 1.0)
    top, bottom = sub == 0, sub == SUB - 1
    energy_ref[...] = energy_in[...] if start else jnp.zeros_like(energy_ref)

    def tile_at(tile):
        return slice(tile * SUB, (tile + 1) * SUB)

    def parts_of(kind):
        if kind == 0:
            return ((0, 0, 0), (9, 1, 9), (18, 2, 0), (27, 3, 9))
        return ((kind, 0, kind), (18 - kind, 1, kind), (18 + kind, 2, kind), (36 - kind, 3, kind))

    def frequency(j, which):
        fetch(j, which).wait()
        ring_ref = rings[which]
        base = (member * freqs + j) * CLASSES * KINDS

        def speeds(part):
            _, quadrant, kind = part
            across = scalar_ref[base + kind * KINDS + 1]
            across = across * (not_first if quadrant in (0, 1) else not_last)
            return scalar_ref[base + kind * KINDS], across

        def step(load, part, speed):
            _, quadrant, _ = part
            alpha, across = speed
            to_down, to_right = sides(quadrant)
            edge = top if to_down > 0 else bottom
            cells, turned = {}, {}

            def get(t):
                if t not in cells:
                    cells[t] = load(t)
                    turned[t] = pltpu.roll(cells[t], to_down % SUB, 0)
                return turned[t]

            def at(t):
                ahead = jnp.where(
                    edge, get(t - to_down) if 0 <= t - to_down < tiles else 0.0, get(t)
                )
                beside = pltpu.roll(cells[t], to_right % LANES, 1)
                return cells[t] + alpha * ahead + across * beside

            return at

        def first_step(kind):
            for part in parts_of(kind):
                direction, quadrant, _ = part
                target = first_refs[kind % 2 * 4 + quadrant]
                after = step(
                    lambda t: ring_ref[direction, tile_at(t), :] * wet_ref[tile_at(t), :],
                    part,
                    speeds(part),
                )
                for t in range(tiles):
                    target[tile_at(t), :] = wet_ref[tile_at(t), :] * after(t)

        def second_step(kind):
            parts = parts_of(kind)
            scale, high = scalar_ref[base + kind * KINDS + 2], scalar_ref[base + 3]
            scaled_high = scale * high
            sources = [first_refs[kind % 2 * 4 + quadrant] for _, quadrant, _ in parts]
            steps = [
                step(lambda t, source=source: source[tile_at(t), :], part, speeds(part))
                for part, source in zip(parts, sources)
            ]
            for t in range(tiles):
                moved, grown = [], []
                for (direction, _, _), after_at in zip(parts, steps):
                    after = after_at(t)
                    kept_ref[j, direction, tile_at(t), :] = after
                    moved.append(after)
                    grown.append(growth_ref[direction, tile_at(t), :] * after)
                if kind == 0:
                    plain_x, plain_y = scale * (moved[0] + moved[2]), scale * (moved[1] + moved[3])
                    grown_x = plain_x + scaled_high * (grown[0] + grown[2])
                    grown_y = plain_y + scaled_high * (grown[1] + grown[3])
                    square = math.cos(0.5 * math.pi) ** 2
                    energy_ref[tile_at(t), :] += plain_x + plain_y
                    sums_ref[0, tile_at(t), :] = grown_x + grown_y
                    sums_ref[1, tile_at(t), :] = grown_x + square * grown_y
                else:
                    plain = scale * ((moved[0] + moved[1]) + (moved[2] + moved[3]))
                    whole = plain + scaled_high * ((grown[0] + grown[1]) + (grown[2] + grown[3]))
                    square = math.cos(2.0 * math.pi * kind / ND) ** 2
                    energy_ref[tile_at(t), :] += plain
                    sums_ref[0, tile_at(t), :] += whole
                    sums_ref[1, tile_at(t), :] += square * whole

        first_step(0)
        for kind in range(CLASSES - 1):
            if kind + 1 < CLASSES - 1:
                first_step(kind + 1)
            second_step(kind)
        at = pl.ds(pl.multiple_of(j * rows, SUB), rows)
        a_ref[at, :] = sums_ref[0]
        b_ref[at, :] = sums_ref[1]

    def pair(index, carry):
        for which in range(2):
            j = start + 2 * index + which
            frequency(j, which)

            @pl.when(j + 2 < stop)
            def _():
                fetch(j + 2, which).start()

        return carry

    lax.fori_loop(0, (stop - start) // 2, pair, 0)
    if (stop - start) % 2:
        frequency(jnp.int32(stop - 1), 0)


def edge_rows(freqs, to_down, direction, at):
    first = ((0 if to_down else 18) + row_slot(direction)) * freqs * SUB
    return pl.ds(first + at, freqs, stride=SUB)


def enter_kernel(
    freqs, member_ref, lanes_ref, table_ref, wet_ref, swap_side_ref, other_side_ref, swap_row_ref,
    other_row_ref, _edges_in, energy_in, columns_ref, edges_ref, energy_ref,
):
    member = member_ref[0]
    wet_cells = wet_ref[...]
    shape = wet_cells.shape
    rows = shape[0]
    lane = iota(shape, 1)
    row = iota(shape, 0)
    even = lane % 2 == 0
    width = 2 * freqs
    used = lane < GROUP * width
    energy = energy_in[...]
    start = 2 * 18 * freqs
    odd_sect, odd_slab = odd_position("sect"), odd_position("slab")

    def from_rows(to_down, part):
        return jnp.where(odd_slab == to_down, swap_row_ref[part, :], other_row_ref[part, :])

    for to_right in (True, False):
        near_column, far_column = (0, 1) if to_right else (LANES - 1, LANES - 2)
        near_even = to_right
        wet_near, wet_far = spread(wet_cells, near_column), spread(wet_cells, far_column)
        total = jnp.zeros(shape, jnp.float32)
        for index in range(GROUPS // 2):
            group = index if to_right else index + GROUPS // 2
            to_down = heads_down(group * GROUP)
            fore = 1 if to_down else -1
            message = jnp.where(odd_sect == to_right, swap_side_ref[index], other_side_ref[index])
            table = lanes_ref[member, group]
            turn = LANES - 1 if near_even else 1
            entered = pltpu.roll(message, turn, 1)
            corner_index = index if to_down else (index - 3 if to_right else index + 3)
            corner = from_rows(to_down, slice(start + corner_index, start + corner_index + 1))
            edge = 0 if to_down else rows - 1
            paths = corner[:, LANES - 1 :] + message[edge : edge + 1, LANES - 1 :]
            corner = pltpu.roll(jnp.broadcast_to(corner, (SUB, LANES)), turn, 1)[0:1]
            corner = jnp.broadcast_to(paths, (1, LANES)) * corner
            diagonal = shift_rows(wet_near * entered, fore)
            diagonal = jnp.where(row == edge, jnp.broadcast_to(corner, shape), diagonal)
            near = wet_near * (table[0:1] * entered + message + table[2:3] * diagonal)
            far = wet_near * wet_far * (table[1:2] * message)
            change = jnp.where(used, jnp.where(even == near_even, near, far), 0.0)
            columns_ref[group] = change
            total += table[3:4] * change
        total += pltpu.roll(total, LANES - width, 1) + pltpu.roll(total, LANES - 2 * width, 1)
        target = 0 if to_right else LANES - 2
        inside = (lane >= target) & (lane < target + 2)
        for j in range(freqs):
            turned = pltpu.roll(total, (target - 2 * j) % LANES, 1)
            energy += jnp.where(inside, turned, 0.0)
    energy_ref[...] = energy

    for to_down in (True, False):
        near_row, far_row = (0, 1) if to_down else (rows - 1, rows - 2)
        wet_near = wet_cells[near_row : near_row + 1, :]
        wet_both = wet_near * wet_cells[far_row : far_row + 1, :]
        totals = [jnp.zeros((freqs, LANES), jnp.float32) for _ in range(2)]
        for direction in range(ND):
            if heads_down(direction) != to_down:
                continue
            slot = row_slot(direction) * freqs
            entered = from_rows(to_down, slice(slot, slot + freqs))
            follow = from_rows(to_down, slice(18 * freqs + slot, 18 * freqs + slot + freqs))
            table = table_ref.at[member, class_of(direction)]
            side = 1 if heads_right(direction) else -1
            diagonal = shift_lanes(wet_near * entered, side)
            near = wet_near * (table[0] * entered + follow + table[2] * diagonal)
            far = wet_both * (table[1] * entered)
            for place, (change, at) in enumerate(((near, near_row), (far, far_row))):
                edges_ref[edge_rows(freqs, to_down, direction, at % SUB), :] = change
                totals[place] += table[3] * change
        for total, at in zip(totals, (near_row, far_row)):
            energy_ref[at : at + 1, :] += jnp.sum(total, axis=0, keepdims=True)


def entered_kernel(
    freqs, member_ref, lanes_ref, table_ref, ice_ref, east_ref, north_ref, growth_ref, columns_ref,
    edges_ref, a_in, b_in, a_ref, b_ref,
):
    member = member_ref[0]
    shape = ice_ref.shape
    rows = shape[0]
    lane = iota(shape, 1)
    even = lane % 2 == 0
    width = 2 * freqs
    a_ref[...] = a_in[...]
    b_ref[...] = b_in[...]

    for to_right in (True, False):
        near_column, far_column = (0, 1) if to_right else (LANES - 1, LANES - 2)

        def packed_field(values):
            return jnp.where(
                even == to_right, spread(values, near_column), spread(values, far_column)
            )

        east, north = packed_field(east_ref[...]), packed_field(north_ref[...])
        open_water = 0.5 * (1.0 - packed_field(ice_ref[...].astype(jnp.float32)))
        sums = [jnp.zeros(shape, jnp.float32) for _ in range(2)]
        for index in range(GROUPS // 2):
            group = index if to_right else index + GROUPS // 2
            table = lanes_ref[member, group]
            project = table[6:7] * east + table[7:8] * north
            growth = open_water * jnp.square(jnp.maximum(project, 0.0))
            grown = columns_ref[group] * (1.0 + table[5:6] * growth)
            sums[0] += table[3:4] * grown
            sums[1] += table[4:5] * grown
        sums = [
            part + pltpu.roll(part, LANES - width, 1) + pltpu.roll(part, LANES - 2 * width, 1)
            for part in sums
        ]
        target = 0 if to_right else LANES - 2
        inside = (lane >= target) & (lane < target + 2)
        for j in range(freqs):
            turn = (target - 2 * j) % LANES
            block = slice(j * rows, (j + 1) * rows)
            place = [jnp.where(inside, pltpu.roll(part, turn, 1), 0.0) for part in sums]
            a_ref[block, :] += place[0]
            b_ref[block, :] += place[1]

    for to_down in (True, False):
        near_row, far_row = (0, 1) if to_down else (rows - 1, rows - 2)
        totals = [jnp.zeros((freqs, LANES), jnp.float32) for _ in range(4)]
        for direction in range(ND):
            if heads_down(direction) != to_down:
                continue
            table = table_ref.at[member, class_of(direction)]
            square = math.cos(2.0 * math.pi * direction / ND) ** 2
            for place, at in enumerate((near_row, far_row)):
                change = edges_ref[edge_rows(freqs, to_down, direction, at % SUB), :]
                growth = growth_ref[direction, at : at + 1, :]
                grown = (table[3] * change) * (1.0 + table[4] * growth)
                totals[2 * place] += grown
                totals[2 * place + 1] += square * grown
        for place, at in enumerate((near_row, far_row)):
            picked = pl.ds(at, freqs, stride=rows)
            a_ref[picked, :] += totals[2 * place]
            b_ref[picked, :] += totals[2 * place + 1]


def stress_kernel(
    freqs, member_ref, scalar_ref, wet_ref, a_ref, b_ref, own_ref, other_ref, sums_ref, ratio_ref
):
    member = member_ref[0]
    wet_cells = wet_ref[...]
    rows = wet_cells.shape[0]
    energy = wet_cells * (own_ref[...] + other_ref[...]) / (ND * NF)
    square = jnp.square(energy)

    sums = [jnp.zeros(wet_cells.shape, jnp.float32) for _ in range(3)]
    for j in range(freqs):
        base = (member * freqs + j) * CLASSES * KINDS
        high, shoal = scalar_ref[base + 3], scalar_ref[base + 4]
        block = slice(j * rows, (j + 1) * rows)
        ratio = wet_cells / (1.0 + (2.0 * high) * square)
        ratio_ref[j] = ratio
        whole = ratio * a_ref[block, :]
        along = ratio * b_ref[block, :]
        sums[0] += shoal * along + (shoal - 0.5) * whole
        sums[1] += (2.0 * shoal - 0.5) * whole - shoal * along
        sums[2] += whole
    for index in range(3):
        sums_ref[index] = sums[index] / (ND * NF)


def total_kernel(own_ref, other_ref, sums_ref, stress_ref):
    sums_ref[...] = own_ref[...] + other_ref[...]
    stress_ref[...] = sums_ref[0:2]


def strip_kernel(stress_ref, swapped_ref, other_ref, beside_ref, first_ref, second_ref):
    rows = stress_ref.shape[1]
    low_half = iota((rows, LANES), 1) < LANES // 2
    odd_sect = lax.rem(lax.axis_index("sect"), 2) == 1
    odd_slab = lax.rem(lax.axis_index("slab"), 2) == 1
    for index in range(2):
        swapped, other = swapped_ref[index], other_ref[index]
        beside = jnp.where(low_half != odd_sect, swapped, other)
        beside_ref[index] = beside
        ends = [
            jnp.concatenate([values[first : first + SUB] for values in (stress_ref[index], beside)], 1)
            for first in (0, rows - SUB)
        ]
        first_ref[index] = jnp.where(odd_slab, *ends)
        second_ref[index] = jnp.where(odd_slab, *ends[::-1])


BEHIND = 16


def final_kernel(
    freqs, member_ref, scalar_ref, depth_ref, ratios_ref, sums_ref, beside_ref, swapped_ref,
    other_ref, growth_ref, kept_ref, columns_ref, edges_ref,
    result_ref, level_ref, damping_ref, turning_ref, ring0, ring1, sems,
):
    member = member_ref[0]
    rings = (ring0, ring1)
    rows = depth_ref.shape[0]
    slab, slabs = lax.axis_index("slab"), lax.axis_size("slab")
    sect, sects = lax.axis_index("sect"), lax.axis_size("sect")
    above_ok = jnp.where(slab > 0, 1.0, 0.0)
    below_ok = jnp.where(slab < slabs - 1, 1.0, 0.0)
    left_ok = jnp.where(sect > 0, 1.0, 0.0)
    right_ok = jnp.where(sect < sects - 1, 1.0, 0.0)

    odd = lax.rem(slab, 2) == 1

    def framed(index):
        middle = jnp.concatenate([sums_ref[index], beside_ref[index]], axis=1)
        swapped, other = swapped_ref[index], other_ref[index]
        below = jnp.where(odd, other, swapped)
        above = jnp.where(odd, swapped, other)
        return jnp.concatenate([middle, below, above], axis=0)

    def around(values, axis):
        size = values.shape[axis]
        return pltpu.roll(values, 1, axis) + pltpu.roll(values, size - 1, axis)

    stress_x, stress_y = framed(0), framed(1)
    frame = stress_x.shape
    frame_row, frame_lane = iota(frame, 0), iota(frame, 1)
    row_ok = jnp.where(frame_row < rows, 1.0, jnp.where(frame_row < rows + SUB, below_ok, above_ok))
    lane_ok = jnp.where(
        frame_lane < LANES, 1.0, jnp.where(frame_lane < LANES + LANES // 2, right_ok, left_ok)
    )
    inside = row_ok * lane_ok / 4.5
    source = -((around(stress_x, 0) - 2.0 * stress_x) + (around(stress_y, 1) - 2.0 * stress_y))
    level = inside * source
    for _ in range(JAC):
        level = inside * (source + around(level, 0) + around(level, 1))
    level = level[:rows, :LANES]
    level_ref[...] = level
    damping = 1.0 / (1.0 + 4.0 * sums_ref[2] / (jnp.square(depth_ref[...] + level) + 1.0))
    tiles = rows // SUB
    damping_ref[...] = damping
    turning_ref[...] = columns_ref[...]
    tile_lane = iota((SUB, LANES), 1)

    def send(j, which):
        return pltpu.make_async_copy(rings[which], result_ref.at[j], sems.at[which])

    def frequency(j, which):
        @pl.when(j >= 2)
        def _():
            send(j - 2, which).wait()

        base = (member * freqs + j) * CLASSES * KINDS
        high = scalar_ref[base + 3]
        scales = [scalar_ref[base + kind * KINDS + 2] for kind in range(CLASSES)]

        def damped(direction, t, ratio, high_ratio):
            to_down, to_right = sides(direction // (ND // 4))
            part = slice(t * SUB, (t + 1) * SUB)
            target = 0 if to_right > 0 else LANES - 2
            at_side = (tile_lane >= target) & (tile_lane < target + 2)
            turn = (target - direction % GROUP * 2 * freqs) % LANES
            entered = turning_ref[direction // GROUP, part, :]
            if turn:
                entered = pltpu.roll(entered, turn, 1)
            value = kept_ref[j, direction, part, :] + jnp.where(at_side, entered, 0.0)
            if t == (0 if to_down > 0 else tiles - 1):
                edge = ((0 if to_down > 0 else 18) + row_slot(direction)) * freqs + j
                value += edges_ref[pl.ds(pl.multiple_of(edge * SUB, SUB), SUB), :]
            factor = ratio + high_ratio * growth_ref[direction, part, :]
            return value * (scales[class_of(direction)] * factor)

        pending = []
        for t in range(tiles):
            part = slice(t * SUB, (t + 1) * SUB)
            ratio = ratios_ref[j, part, :] * damping_ref[part, :]
            high_ratio = high * ratio
            for direction in range(ND):
                pending.append((direction, part, damped(direction, t, ratio, high_ratio)))
                if len(pending) > BEHIND:
                    target, place, value = pending.pop(0)
                    rings[which][target, place, :] = value
        for target, place, value in pending:
            rings[which][target, place, :] = value
        send(j, which).start()
        turned = [pltpu.roll(turning_ref[group], LANES - 2, 1) for group in range(GROUPS)]
        for group in range(GROUPS):
            turning_ref[group] = turned[group]

    def pair(index, carry):
        for which in range(2):
            frequency(2 * index + which, which)
        return carry

    lax.fori_loop(0, freqs // 2, pair, 0)
    if freqs % 2:
        frequency(jnp.int32(freqs - 1), 0)
    for j in range(max(0, freqs - 2), freqs):
        send(j, j % 2).wait()


def swap(values, axis, first):
    count = lax.axis_size(axis)
    pairs = [(i, i + 1) for i in range(first, count - 1, 2)]
    return lax.ppermute(values, axis, pairs + [(b, a) for a, b in pairs])


def others_sum(values, axis):
    count = lax.axis_size(axis)
    total = None
    for step in range(1, count):
        part = lax.ppermute(values, axis, [(i, (i + step) % count) for i in range(count)])
        total = part if total is None else total + part
    return jnp.zeros_like(values) if total is None else total


VMEM = pl.BlockSpec(memory_space=pltpu.VMEM)
SMEM = pl.BlockSpec(memory_space=pltpu.SMEM)
HBM = pl.BlockSpec(memory_space=pltpu.HBM)
ANY = pl.BlockSpec(memory_space=pl.ANY)


def in_vmem(*shape):
    return pltpu.VMEM(shape, jnp.float32)


def in_any(*shape):
    return jax.ShapeDtypeStruct(shape, jnp.float32)


def in_hbm(values):
    return pltpu.with_memory_space_constraint(values, pltpu.HBM)


def call(kernel, in_specs, out_shape, out_specs, flops, moved, scratch=(), aliases=None, limit=6):
    return pl.pallas_call(
        kernel,
        in_specs=in_specs,
        out_shape=out_shape,
        out_specs=out_specs,
        scratch_shapes=list(scratch),
        input_output_aliases=aliases or {},
        cost_estimate=pl.CostEstimate(flops=flops, bytes_accessed=moved, transcendentals=0),
        compiler_params=pltpu.CompilerParams(vmem_limit_bytes=limit << 20),
    )


def resident(spectrum, land_mask, ice_mask, wind_u, wind_v, depth):
    local_comp, rows, lanes = spectrum.shape
    freqs = local_comp // ND
    members = lax.axis_size("comp")
    member = lax.axis_index("comp").astype(jnp.int32).reshape(1)
    scalars, lane_table, row_table = numpy_tables(members, freqs)
    scalars, lane_table, row_table = map(jnp.asarray, (scalars, lane_table, row_table))
    cells = rows * lanes
    row_message = 2 * 18 * freqs + CORNERS
    block = (freqs, ND, rows, lanes)
    spectrum = spectrum.reshape(block)

    growth, wet, swap_side, other_side, swap_row, other_row, edges = call(
        functools.partial(pack_kernel, freqs),
        [SMEM] + [HBM] * 7,
        (
            in_any(ND, rows, lanes),
            in_any(rows, lanes),
            in_any(GROUPS // 2, rows, lanes),
            in_any(GROUPS // 2, rows, lanes),
            in_any(row_message, lanes),
            in_any(row_message, lanes),
            in_any(2 * 18 * freqs * SUB, lanes),
        ),
        (VMEM,) * 7,
        flops=local_comp * cells * 4,
        moved=local_comp * cells * 4,
        scratch=[
            pltpu.VMEM((local_comp * rows, lanes), jnp.float32),
            pltpu.VMEM((GROUPS // 2, rows, lanes), jnp.float32),
            pltpu.VMEM((GROUPS // 2, rows, lanes), jnp.float32),
            pltpu.VMEM(lane_table.shape[1:], jnp.float32),
            pltpu.VMEM(row_table.shape[1:], jnp.float32),
            pltpu.VMEM((rows, lanes), jnp.int32),
            pltpu.VMEM((rows, lanes), jnp.int32),
            pltpu.VMEM((rows, lanes), jnp.float32),
            pltpu.VMEM((rows, lanes), jnp.float32),
            pltpu.SemaphoreType.DMA((6,)),
            pltpu.SemaphoreType.DMA((GROUPS,)),
        ],
        limit=30,
    )(
        member,
        *map(in_hbm, (lane_table, row_table, land_mask, ice_mask, wind_u, wind_v, spectrum)),
    )

    def main_part(start, stop, *before):
        return call(
            functools.partial(main_kernel, freqs, start, stop),
            [SMEM, SMEM, VMEM, VMEM, HBM] + ([ANY, VMEM, VMEM, VMEM, VMEM] if before else []),
            (
                in_vmem(*block),
                in_any(freqs * rows, lanes),
                in_any(freqs * rows, lanes),
                in_any(rows, lanes),
            ),
            (VMEM,) * 4,
            flops=local_comp * cells * 16 * (stop - start) // freqs,
            moved=local_comp * cells * 8 * (stop - start) // freqs,
            scratch=[
                pltpu.VMEM((ND, rows, lanes), jnp.float32),
                pltpu.VMEM((ND, rows, lanes), jnp.float32),
                pltpu.VMEM((2, rows, lanes), jnp.float32),
                pltpu.SemaphoreType.DMA((2,)),
            ]
            + [pltpu.VMEM((rows, lanes), jnp.float32)] * 8,
            aliases={6 + index: index for index in range(4)} if before else {},
        )(member, scalars, wet, growth, in_hbm(spectrum), *before)

    early = max(1, freqs // 3)
    swap_side, other_side = swap(swap_side, "sect", 0), swap(other_side, "sect", 1)
    kept, *partial = main_part(0, early)
    swap_row, other_row = call(
        functools.partial(corner_kernel, freqs),
        [VMEM, VMEM, VMEM, ANY, ANY, ANY],
        (in_any(row_message, lanes), in_any(row_message, lanes)),
        (ANY, ANY),
        flops=100,
        moved=1 << 15,
        scratch=[pltpu.VMEM((2, CORNERS, lanes), jnp.float32), pltpu.SemaphoreType.DMA((2,))],
        aliases={3: 0, 4: 1},
    )(wet, swap_side, other_side, swap_row, other_row, partial[-1])
    swapped_row = swap(swap_row, "slab", 0)
    other_row = swap(other_row, "slab", 1)
    kept, a_sums, b_sums, energy = main_part(early, freqs, swap_row, kept, *partial)

    columns, edges, energy = call(
        functools.partial(enter_kernel, freqs),
        [SMEM] + [VMEM] * 9,
        (
            in_any(GROUPS, rows, lanes),
            in_any(2 * 18 * freqs * SUB, lanes),
            in_any(rows, lanes),
        ),
        (VMEM,) * 3,
        flops=cells * 600,
        moved=cells * 200,
        aliases={8: 1, 9: 2},
    )(
        member, lane_table, row_table, wet, swap_side, other_side, swapped_row, other_row, edges,
        energy,
    )
    energy_there = others_sum(energy, "comp")
    a_sums, b_sums = call(
        functools.partial(entered_kernel, freqs),
        [SMEM] + [VMEM] * 10,
        (in_any(freqs * rows, lanes), in_any(freqs * rows, lanes)),
        (VMEM,) * 2,
        flops=cells * 600,
        moved=cells * 200,
        aliases={9: 0, 10: 1},
    )(
        member, lane_table, row_table, ice_mask, wind_u, wind_v, growth, columns, edges,
        a_sums, b_sums,
    )

    sums, ratios = call(
        functools.partial(stress_kernel, freqs),
        [SMEM, SMEM] + [VMEM] * 5,
        (in_any(3, rows, lanes), in_any(freqs, rows, lanes)),
        (VMEM, VMEM),
        flops=cells * freqs * 12,
        moved=cells * freqs * 8,
    )(member, scalars, wet, a_sums, b_sums, energy, energy_there)
    sums, stress = call(
        total_kernel,
        [VMEM, VMEM],
        (in_any(3, rows, lanes), in_any(2, rows, lanes)),
        (VMEM, VMEM),
        flops=cells * 3,
        moved=cells * 44,
    )(sums, others_sum(sums, "comp"))
    beside, first, second = call(
        strip_kernel,
        [VMEM, VMEM, VMEM],
        (in_any(2, rows, lanes), in_any(2, SUB, 2 * lanes), in_any(2, SUB, 2 * lanes)),
        (VMEM, VMEM, VMEM),
        flops=cells * 4,
        moved=cells * 36,
    )(stress, swap(stress, "sect", 0), swap(stress, "sect", 1))
    aside, beyond = swap(first, "slab", 0), swap(second, "slab", 1)

    result, level = call(
        functools.partial(final_kernel, freqs),
        [SMEM, SMEM] + [VMEM] * 10,
        (in_any(*block), in_any(rows, lanes)),
        (HBM, VMEM),
        flops=local_comp * cells * 6,
        moved=local_comp * cells * 8,
        scratch=[
            pltpu.VMEM((rows, lanes), jnp.float32),
            pltpu.VMEM((GROUPS, rows, lanes), jnp.float32),
            pltpu.VMEM((ND, rows, lanes), jnp.float32),
            pltpu.VMEM((ND, rows, lanes), jnp.float32),
            pltpu.SemaphoreType.DMA((2,)),
        ],
    )(
        member, scalars, depth, ratios, sums, beside, aside, beyond, growth, kept,
        columns, edges,
    )
    return result.reshape(local_comp, rows, lanes), level


def local(spectrum, *fields):
    local_comp, rows, lanes = spectrum.shape
    whole_rings = local_comp % ND == 0 and GROUP * 2 * (local_comp // ND) < LANES - 1
    if whole_rings and lanes == LANES and rows % SUB == 0:
        return resident(spectrum, *fields)
    return general(spectrum, *fields)


def solution(mesh):
    in_specs = (
        P("comp", "slab", "sect"),
        P("slab", "sect"),
        P("slab", "sect"),
        P("slab", "sect"),
        P("slab", "sect"),
        P("slab", "sect"),
    )
    out_specs = (P("comp", "slab", "sect"), P("slab", "sect"))
    return jax.shard_map(local, mesh=mesh, in_specs=in_specs, out_specs=out_specs, check_vma=False)
```

```python
import functools
import math

import jax
import jax.numpy as jnp
import numpy as np
from jax import lax
from jax.experimental import pallas as pl
from jax.experimental.pallas import tpu as pltpu
from jax.sharding import PartitionSpec as P

ND = 36
NF = 36
STEPS = 2
JAC = 4


def extended(cells, sides, width):
    for axis, dim in sides:
        count = lax.axis_size(axis)
        ends = count - 1
        head = lax.slice_in_dim(cells, 0, width, axis=dim)
        tail = lax.slice_in_dim(cells, cells.shape[dim] - width, cells.shape[dim], axis=dim)
        cells = jnp.concatenate(
            [
                lax.ppermute(tail, axis, [(i, (i + 1) % count) for i in range(ends)]),
                cells,
                lax.ppermute(head, axis, [((i + 1) % count, i) for i in range(ends)]),
            ],
            axis=dim,
        )
    return cells


def tables(index):
    freq_index = (index // ND).astype(jnp.float32)
    angle_index = (index % ND).astype(jnp.float32)
    heading = 2.0 * math.pi * angle_index / ND
    return (
        jnp.cos(heading),
        jnp.sin(heading),
        jnp.power(1.1, -freq_index),
        jnp.power(1.1, freq_index - (NF - 1)),
        0.5 + 0.5 * freq_index / (NF - 1),
    )


def column(values):
    return values[:, None, None]


def advect(spectra, wet_cells, speed_x, speed_y):
    padded = extended(spectra, (("slab", 1), ("sect", 2)), 1)
    upper_rows = padded[:, :-2, 1:-1]
    lower_rows = padded[:, 2:, 1:-1]
    left_cells = padded[:, 1:-1, :-2]
    right_cells = padded[:, 1:-1, 2:]
    change = (
        jnp.maximum(speed_x, 0.0) * (spectra - upper_rows)
        + jnp.minimum(speed_x, 0.0) * (lower_rows - spectra)
        + jnp.maximum(speed_y, 0.0) * (spectra - left_cells)
        + jnp.minimum(speed_y, 0.0) * (right_cells - spectra)
    )
    return (spectra - change) * wet_cells


def forcing(spectra, energy, wind_east, wind_north, ice_cover, cosine, sine, high_ratio):
    project = cosine * wind_east + sine * wind_north
    growth = 0.5 * high_ratio * jnp.square(jnp.maximum(project, 0.0)) * (1.0 - ice_cover)
    return spectra * (1.0 + growth) / (1.0 + 2.0 * high_ratio * jnp.square(energy))


def stress_weights(cosine, sine, shoaling):
    return jnp.stack(
        [shoaling * (cosine * cosine + 1.0) - 0.5, shoaling * (sine * sine + 1.0) - 0.5]
    )


def surge_solve(stress):
    padded = extended(stress, (("slab", 1), ("sect", 2)), 1)
    source_term = -(
        padded[0, 2:, 1:-1]
        + padded[0, :-2, 1:-1]
        - 2.0 * stress[0]
        + (padded[1, 1:-1, 2:] + padded[1, 1:-1, :-2] - 2.0 * stress[1])
    )
    surge_level = source_term / 4.5
    for _ in range(JAC):
        neighbours = extended(surge_level, (("slab", 0), ("sect", 1)), 1)
        surge_level = (
            source_term
            + neighbours[2:, 1:-1]
            + neighbours[:-2, 1:-1]
            + neighbours[1:-1, 2:]
            + neighbours[1:-1, :-2]
        ) / 4.5
    return surge_level


def general(spectrum, land_mask, ice_mask, wind_u, wind_v, depth):
    groups = lax.axis_size("comp")
    member = lax.axis_index("comp")
    local_comp, block_rows, block_cols = spectrum.shape
    point_rows = block_rows // groups
    total_comp = ND * NF
    wet_cells = (1 - land_mask).astype(jnp.float32)
    ice_cover = ice_mask.astype(jnp.float32)

    def own_rows(values):
        return lax.dynamic_slice_in_dim(values, member * point_rows, point_rows, values.ndim - 2)

    own_index = member * local_comp + jnp.arange(local_comp, dtype=jnp.int32)
    cosine, sine, low_ratio, high_ratio, shoaling = tables(own_index)
    spectra = spectrum * wet_cells
    for _ in range(STEPS):
        spectra = advect(
            spectra, wet_cells, column(0.7 * low_ratio * cosine), column(0.7 * low_ratio * sine)
        )
    points = lax.all_to_all(spectra, "comp", split_axis=1, concat_axis=0, tiled=True)
    cosine_full, sine_full, _, high_full, shoal_full = tables(
        jnp.arange(total_comp, dtype=jnp.int32)
    )
    energy = jnp.sum(points, axis=0) / total_comp
    sourced = forcing(
        points,
        energy,
        own_rows(wind_u),
        own_rows(wind_v),
        own_rows(ice_cover),
        column(cosine_full),
        column(sine_full),
        column(high_full),
    )
    stress = (
        jnp.einsum(
            "sk,krc->src",
            stress_weights(cosine_full, sine_full, shoal_full),
            sourced,
            precision=lax.Precision.HIGHEST,
        )
        / total_comp
    )
    stress_block = lax.all_gather(stress, "comp", axis=1, tiled=True)
    level_block = surge_solve(stress_block)
    final_energy = jnp.sum(sourced, axis=0) / total_comp
    damped = sourced / (
        1.0 + 4.0 * final_energy / (jnp.square(own_rows(depth) + own_rows(level_block)) + 1.0)
    )
    result = lax.all_to_all(damped, "comp", split_axis=0, concat_axis=1, tiled=True)
    return (result, level_block)


LANES = 128
SUB = 8
CLASSES = 10
KINDS = 5
GROUP = 3
GROUPS = ND // GROUP
CORNERS = 8


def class_of(direction):
    folded = direction % 18
    return folded if folded <= 9 else 18 - folded


def heads_down(direction):
    return direction < 9 or direction >= 27


def heads_right(direction):
    return direction < 18


def row_slot(direction):
    if direction < 9:
        return direction
    return direction - 18 if direction >= 27 else direction - 9


def numpy_tables(members, freqs):
    j = np.arange(members * freqs, dtype=np.float64)
    heading = 2.0 * np.pi * np.arange(ND) / ND
    cosine, sine = np.cos(heading), np.sin(heading)
    low = 1.1 ** (-j)
    high = 1.1 ** (j - (NF - 1))
    shoal = 0.5 + 0.5 * j / (NF - 1)
    step_x = 0.7 * low[:, None] * np.abs(cosine)
    step_y = 0.7 * low[:, None] * np.abs(sine)
    keep = 1.0 - step_x - step_y
    alpha, beta, scale = step_x / keep, step_y / keep, keep * keep
    classes = np.arange(CLASSES)
    square = np.broadcast_to(cosine * cosine, alpha.shape)
    scalars = np.stack(
        [
            alpha[:, classes],
            beta[:, classes],
            scale[:, classes],
            np.broadcast_to(high[:, None], (j.size, CLASSES)),
            np.broadcast_to(shoal[:, None], (j.size, CLASSES)),
        ],
        axis=-1,
    ).astype(np.float32)

    kinds = np.stack(
        [
            2.0 * beta,
            beta * beta,
            alpha * beta,
            scale,
            scale * square,
            np.broadcast_to(high[:, None], alpha.shape),
            np.broadcast_to(cosine, alpha.shape),
            np.broadcast_to(sine, alpha.shape),
        ]
    )
    lanes = np.zeros((members, GROUPS, 8, LANES), np.float32)
    packed = kinds.reshape(8, members, freqs, GROUPS, GROUP)
    packed = np.repeat(packed.transpose(1, 3, 0, 4, 2), 2, axis=-1)
    lanes[..., : GROUP * 2 * freqs] = packed.reshape(members, GROUPS, 8, -1)

    rows = np.stack(
        [2.0 * alpha, alpha * alpha, alpha * beta, scale, np.broadcast_to(high[:, None], alpha.shape)]
    )[:, :, classes]
    rows = rows.reshape(5, members, freqs, CLASSES).transpose(1, 3, 0, 2)
    rows = np.broadcast_to(rows[..., None], rows.shape + (LANES,)).astype(np.float32)
    return scalars.reshape(-1), lanes, rows


def odd_position(axis):
    return lax.rem(lax.axis_index(axis), 2) == 1


def iota(shape, axis):
    return lax.broadcasted_iota(jnp.int32, shape, axis)


def spread(values, column):
    return jnp.broadcast_to(values[:, column : column + 1], values.shape)


def shift_rows(values, step):
    rows = values.shape[0]
    edge = 0 if step > 0 else rows - 1
    moved = pltpu.roll(values, step % rows, 0)
    return jnp.where(iota(values.shape, 0) == edge, 0.0, moved)


def shift_lanes(values, step):
    lanes = values.shape[1]
    edge = 0 if step > 0 else lanes - 1
    moved = pltpu.roll(values, step % lanes, 1)
    return jnp.where(iota(values.shape, 1) == edge, 0.0, moved)


DEPTH = 3


def sides(quadrant):
    return 1 if quadrant in (0, 3) else -1, 1 if quadrant in (0, 1) else -1


def pack_kernel(
    freqs, member_ref, lanes_hbm, table_hbm, land_hbm, ice_hbm, east_hbm, north_hbm, spectrum_ref,
    growth_ref, wet_ref, swap_side_ref, other_side_ref, swap_row_ref, other_row_ref, edges_ref,
    kept_ref, right_ref, left_ref, lanes_ref, table_ref, land_ref, ice_ref, east_ref, north_ref, small_sems, sems,
):
    member = member_ref[0]
    small = [
        pltpu.make_async_copy(source, target, small_sems.at[index])
        for index, (source, target) in enumerate(
            (
                (land_hbm, land_ref),
                (ice_hbm, ice_ref),
                (east_hbm, east_ref),
                (north_hbm, north_ref),
                (lanes_hbm.at[member], lanes_ref),
                (table_hbm.at[member], table_ref),
            )
        )
    ]
    for copy in small:
        copy.start()

    rows = land_ref.shape[0]
    blocks_ref = kept_ref.reshape(freqs, ND, rows, LANES)

    def fetch(group):
        part = (slice(None), pl.ds(group * GROUP, GROUP))
        return pltpu.make_async_copy(spectrum_ref.at[part], blocks_ref.at[part], sems.at[group])

    for group in range(DEPTH):
        fetch(group).start()
    edges_ref[...] = jnp.zeros_like(edges_ref)
    for copy in small:
        copy.wait()

    wet_cells = (1 - land_ref[...]).astype(jnp.float32)
    wet_ref[...] = wet_cells
    open_water = 0.5 * (1.0 - ice_ref[...].astype(jnp.float32))
    shape = wet_cells.shape
    tiles = rows // SUB
    for direction in range(ND):
        angle = 2.0 * math.pi * direction / ND
        project = math.cos(angle) * east_ref[...] + math.sin(angle) * north_ref[...]
        growth_ref[direction] = open_water * jnp.square(jnp.maximum(project, 0.0))

    lane = iota(shape, 1)
    even = lane % 2 == 0
    tile_lane = iota((SUB, LANES), 1)
    for row_ref in (swap_row_ref, other_row_ref):
        row_ref[pl.ds(2 * 18 * freqs, CORNERS), :] = jnp.zeros((CORNERS, LANES), jnp.float32)
    odd_sect, odd_slab = odd_position("sect"), odd_position("slab")

    half = GROUPS // 2

    def gather_all(to_right):
        target_ref = right_ref if to_right else left_ref

        def gather(index, carry):
            group = index + (0 if to_right else half)
            fetch(group).wait()

            @pl.when(group + DEPTH < GROUPS)
            def _():
                fetch(group + DEPTH).start()

            packed = [jnp.zeros((SUB, LANES), jnp.float32) for _ in range(tiles)]
            for i in range(GROUP):
                for j in range(freqs):
                    place = i * 2 * freqs + 2 * j
                    here = (tile_lane >= place) & (tile_lane < place + 2)
                    turn = (place + 2 if to_right else place) % LANES
                    first = pl.multiple_of((j * ND + group * GROUP + i) * rows, SUB)
                    for tile in range(tiles):
                        cells = kept_ref[pl.ds(first + tile * SUB, SUB), :]
                        packed[tile] = jnp.where(here, pltpu.roll(cells, turn, 1), packed[tile])
            for tile in range(tiles):
                target_ref[index, tile * SUB : (tile + 1) * SUB, :] = packed[tile]
            return carry

        lax.fori_loop(0, half, gather, 0)

    def side_message(group):
        to_right, fore = group < half, 1 if heads_down(group * GROUP) else -1
        ahead, behind = (LANES - 1, LANES - 2) if to_right else (0, 1)
        wet_near, wet_far = spread(wet_cells, ahead), spread(wet_cells, behind)
        near_even = not to_right
        packed = right_ref[group] if to_right else left_ref[group - half]
        values = packed * jnp.where(even == near_even, wet_near, wet_far)
        near = pltpu.roll(values, 1 if near_even else LANES - 1, 1)
        table = lanes_ref[group]
        follow = wet_near * (table[1:2] * values + table[2:3] * shift_rows(near, fore))
        message = jnp.where(even == near_even, values, follow)
        return jnp.where(lane == LANES - 1, wet_near, message)

    def row_message(direction):
        to_down = heads_down(direction)
        near_row, far_row = (rows - 1, rows - 2) if to_down else (0, 1)
        wet_near = wet_cells[near_row : near_row + 1, :]
        wet_far = wet_cells[far_row : far_row + 1, :]
        table = table_ref.at[class_of(direction)]
        near = kept_ref[pl.ds(direction * rows + near_row, freqs, stride=ND * rows), :] * wet_near
        far = kept_ref[pl.ds(direction * rows + far_row, freqs, stride=ND * rows), :] * wet_far
        beside = shift_lanes(near, 1 if heads_right(direction) else -1)
        return near, wet_near * (table[1] * far + table[2] * beside)

    def row_messages(slots):
        for slot in slots:
            pairs = zip(row_message(by_slot[True, slot]), row_message(by_slot[False, slot]))
            for which, (down, up) in enumerate(pairs):
                first = (which * 18 + slot) * freqs
                swap_row_ref[first : first + freqs, :] = jnp.where(odd_slab, up, down)
                other_row_ref[first : first + freqs, :] = jnp.where(odd_slab, down, up)

    by_slot = {(heads_down(d), row_slot(d)): d for d in range(ND)}
    gather_all(True)
    rights = [side_message(index) for index in range(half)]
    for index in range(half):
        right_ref[index] = rights[index]
    row_messages(range(9))
    gather_all(False)
    for index in range(half):
        right, left = right_ref[index], side_message(index + half)
        swap_side_ref[index] = jnp.where(odd_sect, left, right)
        other_side_ref[index] = jnp.where(odd_sect, right, left)
    row_messages(range(9, 18))


def corner_kernel(
    freqs, wet_ref, swapped_ref, other_ref, swap_in, other_in, _after, swap_row_ref, other_row_ref,
    rows_ref, sems,
):
    rows = wet_ref.shape[0]
    odd_sect, odd_slab = odd_position("sect"), odd_position("slab")
    last = iota((1, LANES), 1) == LANES - 1
    rows_ref[...] = jnp.zeros_like(rows_ref)
    for i in range(6):
        from_left = i < 3
        column = 0 if from_left else LANES - 1
        ends = []
        for row, index in ((rows - 1, i), (0, i + 3 if from_left else i - 3)):
            swapped = swapped_ref[index, row : row + 1, :]
            other = other_ref[index, row : row + 1, :]
            came = jnp.where(odd_sect == from_left, swapped, other)
            own = jnp.broadcast_to(wet_ref[row : row + 1, column : column + 1], (1, LANES))
            ends.append(jnp.where(last, own, came))
        rows_ref[0, i : i + 1, :] = jnp.where(odd_slab, *ends[::-1])
        rows_ref[1, i : i + 1, :] = jnp.where(odd_slab, *ends)
    start = 2 * 18 * freqs
    copies = [
        pltpu.make_async_copy(
            rows_ref.at[which], ref.at[pl.ds(start, CORNERS), :], sems.at[which]
        )
        for which, ref in ((0, swap_row_ref), (1, other_row_ref))
    ]
    for copy in copies:
        copy.start()
    for copy in copies:
        copy.wait()


AHEAD = 3


def main_kernel(
    freqs, start, stop, member_ref, scalar_ref, wet_ref, growth_ref, spectrum_ref, *refs
):
    if start:
        _after, _kept_in, a_in, b_in, energy_in, *refs = refs
    kept_ref, a_ref, b_ref, energy_ref, ring_ref, sems, *first_refs = refs
    member = member_ref[0]
    nought = jnp.minimum(member, 0)
    rows = wet_ref.shape[0]
    tiles = rows // SUB

    def fetch(j):
        slot = lax.rem(j, AHEAD)
        return pltpu.make_async_copy(spectrum_ref.at[j], ring_ref.at[slot], sems.at[slot])

    for j in range(start, min(start + AHEAD, stop)):
        fetch(jnp.int32(j)).start()

    lane = iota((SUB, LANES), 1)
    sub = iota((SUB, LANES), 0)
    not_first = jnp.where(lane == 0, 0.0, 1.0)
    not_last = jnp.where(lane == LANES - 1, 0.0, 1.0)
    top, bottom = sub == 0, sub == SUB - 1
    energy_ref[...] = energy_in[...] if start else jnp.zeros_like(energy_ref)
    for first_ref in first_refs:
        first_ref[...] = jnp.zeros_like(first_ref)

    def tile_at(tile):
        return pl.ds(tile * SUB, SUB)

    def row_shift(quadrant):
        return -1 if quadrant in (0, 3) else 1

    def parts_of(kind):
        if kind == 0:
            return ((0, 0, 0), (9, 1, 9), (18, 2, 0), (27, 3, 9))
        return ((kind, 0, kind), (18 - kind, 1, kind), (18 + kind, 2, kind), (36 - kind, 3, kind))

    def frequency(j, carry):
        fetch(j).wait()
        slot = lax.rem(j, AHEAD)
        base = (member * freqs + j) * CLASSES * KINDS
        at = [pl.ds(pl.multiple_of(j * rows, SUB) + t * SUB, SUB) for t in range(tiles)]

        def speeds(part):
            at_class = base + part[2] * KINDS
            beta = scalar_ref[at_class + 1]
            return scalar_ref[at_class], beta * (not_first if part[1] in (0, 1) else not_last)

        def beside(cells, quadrant):
            return pltpu.roll(cells, 1 if quadrant in (0, 1) else LANES - 1, 1)

        def first_step(kind):
            parts = parts_of(kind)
            speed = [speeds(part) for part in parts]
            wet = [wet_ref[tile_at(t), :] for t in range(tiles)]
            for (direction, quadrant, _), (alpha, across) in zip(parts, speed):
                shift = row_shift(quadrant)
                edge = top if shift < 0 else bottom
                target = first_refs[kind % 2 * 4 + quadrant]
                cells = [ring_ref[slot, direction, tile_at(t), :] * wet[t] for t in range(tiles)]
                turned = [pltpu.roll(cells[t], -shift % SUB, 0) for t in range(tiles)]
                for t in range(tiles):
                    before = turned[t + shift] if 0 <= t + shift < tiles else 0.0
                    ahead = jnp.where(edge, before, turned[t])
                    after = cells[t] + alpha * ahead + across * beside(cells[t], quadrant)
                    target[tile_at(t + 1), :] = wet[t] * after

        def second_step(kind):
            parts = parts_of(kind)
            scale, high = scalar_ref[base + kind * KINDS + 2], scalar_ref[base + 3]
            scaled_high = scale * high
            speed = [speeds(part) for part in parts]
            for t in range(tiles):
                moved, grown = [], []
                for (direction, quadrant, _), (alpha, across) in zip(parts, speed):
                    source = first_refs[kind % 2 * 4 + quadrant]
                    cells = source[tile_at(t + 1), :]
                    ahead = source[pl.ds((t + 1) * SUB + row_shift(quadrant) + nought, SUB), :]
                    after = cells + alpha * ahead + across * beside(cells, quadrant)
                    kept_ref[j, direction, tile_at(t), :] = after
                    moved.append(after)
                    grown.append(growth_ref[direction, tile_at(t), :] * after)
                if kind == 0:
                    plain_x, plain_y = scale * (moved[0] + moved[2]), scale * (moved[1] + moved[3])
                    grown_x = plain_x + scaled_high * (grown[0] + grown[2])
                    grown_y = plain_y + scaled_high * (grown[1] + grown[3])
                    square = math.cos(0.5 * math.pi) ** 2
                    energy_ref[tile_at(t), :] += plain_x + plain_y
                    a_ref[at[t], :] = grown_x + grown_y
                    b_ref[at[t], :] = grown_x + square * grown_y
                else:
                    plain = scale * ((moved[0] + moved[1]) + (moved[2] + moved[3]))
                    whole = plain + scaled_high * ((grown[0] + grown[1]) + (grown[2] + grown[3]))
                    square = math.cos(2.0 * math.pi * kind / ND) ** 2
                    energy_ref[tile_at(t), :] += plain
                    a_ref[at[t], :] += whole
                    b_ref[at[t], :] += square * whole

        first_step(0)
        for kind in range(CLASSES - 1):
            if kind + 1 < CLASSES - 1:
                first_step(kind + 1)
            second_step(kind)

        @pl.when(j + AHEAD < stop)
        def _():
            fetch(j + AHEAD).start()

        return carry

    lax.fori_loop(start, stop, frequency, 0)


def edge_rows(freqs, to_down, direction, at):
    first = ((0 if to_down else 18) + row_slot(direction)) * freqs * SUB
    return pl.ds(first + at, freqs, stride=SUB)


def enter_kernel(
    freqs, member_ref, lanes_ref, table_ref, wet_ref, swap_side_ref, other_side_ref, swap_row_ref,
    other_row_ref, _edges_in, energy_in, columns_ref, edges_ref, energy_ref,
):
    member = member_ref[0]
    wet_cells = wet_ref[...]
    shape = wet_cells.shape
    rows = shape[0]
    lane = iota(shape, 1)
    row = iota(shape, 0)
    even = lane % 2 == 0
    width = 2 * freqs
    used = lane < GROUP * width
    energy = energy_in[...]
    start = 2 * 18 * freqs
    odd_sect, odd_slab = odd_position("sect"), odd_position("slab")

    def from_rows(to_down, part):
        return jnp.where(odd_slab == to_down, swap_row_ref[part, :], other_row_ref[part, :])

    for to_right in (True, False):
        near_column, far_column = (0, 1) if to_right else (LANES - 1, LANES - 2)
        near_even = to_right
        wet_near, wet_far = spread(wet_cells, near_column), spread(wet_cells, far_column)
        total = jnp.zeros(shape, jnp.float32)
        for index in range(GROUPS // 2):
            group = index if to_right else index + GROUPS // 2
            to_down = heads_down(group * GROUP)
            fore = 1 if to_down else -1
            message = jnp.where(odd_sect == to_right, swap_side_ref[index], other_side_ref[index])
            table = lanes_ref[member, group]
            turn = LANES - 1 if near_even else 1
            entered = pltpu.roll(message, turn, 1)
            corner_index = index if to_down else (index - 3 if to_right else index + 3)
            corner = from_rows(to_down, slice(start + corner_index, start + corner_index + 1))
            edge = 0 if to_down else rows - 1
            paths = corner[:, LANES - 1 :] + message[edge : edge + 1, LANES - 1 :]
            corner = pltpu.roll(jnp.broadcast_to(corner, (SUB, LANES)), turn, 1)[0:1]
            corner = jnp.broadcast_to(paths, (1, LANES)) * corner
            diagonal = shift_rows(wet_near * entered, fore)
            diagonal = jnp.where(row == edge, jnp.broadcast_to(corner, shape), diagonal)
            near = wet_near * (table[0:1] * entered + message + table[2:3] * diagonal)
            far = wet_near * wet_far * (table[1:2] * message)
            change = jnp.where(used, jnp.where(even == near_even, near, far), 0.0)
            columns_ref[group] = change
            total += table[3:4] * change
        total += pltpu.roll(total, LANES - width, 1) + pltpu.roll(total, LANES - 2 * width, 1)
        target = 0 if to_right else LANES - 2
        inside = (lane >= target) & (lane < target + 2)
        for j in range(freqs):
            turned = pltpu.roll(total, (target - 2 * j) % LANES, 1)
            energy += jnp.where(inside, turned, 0.0)
    energy_ref[...] = energy

    for to_down in (True, False):
        near_row, far_row = (0, 1) if to_down else (rows - 1, rows - 2)
        wet_near = wet_cells[near_row : near_row + 1, :]
        wet_both = wet_near * wet_cells[far_row : far_row + 1, :]
        totals = [jnp.zeros((freqs, LANES), jnp.float32) for _ in range(2)]
        for direction in range(ND):
            if heads_down(direction) != to_down:
                continue
            slot = row_slot(direction) * freqs
            entered = from_rows(to_down, slice(slot, slot + freqs))
            follow = from_rows(to_down, slice(18 * freqs + slot, 18 * freqs + slot + freqs))
            table = table_ref.at[member, class_of(direction)]
            side = 1 if heads_right(direction) else -1
            diagonal = shift_lanes(wet_near * entered, side)
            near = wet_near * (table[0] * entered + follow + table[2] * diagonal)
            far = wet_both * (table[1] * entered)
            for place, (change, at) in enumerate(((near, near_row), (far, far_row))):
                edges_ref[edge_rows(freqs, to_down, direction, at % SUB), :] = change
                totals[place] += table[3] * change
        for total, at in zip(totals, (near_row, far_row)):
            energy_ref[at : at + 1, :] += jnp.sum(total, axis=0, keepdims=True)


def entered_kernel(
    freqs, member_ref, lanes_ref, table_ref, ice_ref, east_ref, north_ref, growth_ref, columns_ref,
    edges_ref, a_in, b_in, a_ref, b_ref,
):
    member = member_ref[0]
    shape = ice_ref.shape
    rows = shape[0]
    lane = iota(shape, 1)
    even = lane % 2 == 0
    width = 2 * freqs
    a_ref[...] = a_in[...]
    b_ref[...] = b_in[...]

    for to_right in (True, False):
        near_column, far_column = (0, 1) if to_right else (LANES - 1, LANES - 2)

        def packed_field(values):
            return jnp.where(
                even == to_right, spread(values, near_column), spread(values, far_column)
            )

        east, north = packed_field(east_ref[...]), packed_field(north_ref[...])
        open_water = 0.5 * (1.0 - packed_field(ice_ref[...].astype(jnp.float32)))
        sums = [jnp.zeros(shape, jnp.float32) for _ in range(2)]
        for index in range(GROUPS // 2):
            group = index if to_right else index + GROUPS // 2
            table = lanes_ref[member, group]
            project = table[6:7] * east + table[7:8] * north
            growth = open_water * jnp.square(jnp.maximum(project, 0.0))
            grown = columns_ref[group] * (1.0 + table[5:6] * growth)
            sums[0] += table[3:4] * grown
            sums[1] += table[4:5] * grown
        sums = [
            part + pltpu.roll(part, LANES - width, 1) + pltpu.roll(part, LANES - 2 * width, 1)
            for part in sums
        ]
        target = 0 if to_right else LANES - 2
        inside = (lane >= target) & (lane < target + 2)
        for j in range(freqs):
            turn = (target - 2 * j) % LANES
            block = slice(j * rows, (j + 1) * rows)
            place = [jnp.where(inside, pltpu.roll(part, turn, 1), 0.0) for part in sums]
            a_ref[block, :] += place[0]
            b_ref[block, :] += place[1]

    for to_down in (True, False):
        near_row, far_row = (0, 1) if to_down else (rows - 1, rows - 2)
        totals = [jnp.zeros((freqs, LANES), jnp.float32) for _ in range(4)]
        for direction in range(ND):
            if heads_down(direction) != to_down:
                continue
            table = table_ref.at[member, class_of(direction)]
            square = math.cos(2.0 * math.pi * direction / ND) ** 2
            for place, at in enumerate((near_row, far_row)):
                change = edges_ref[edge_rows(freqs, to_down, direction, at % SUB), :]
                growth = growth_ref[direction, at : at + 1, :]
                grown = (table[3] * change) * (1.0 + table[4] * growth)
                totals[2 * place] += grown
                totals[2 * place + 1] += square * grown
        for place, at in enumerate((near_row, far_row)):
            picked = pl.ds(at, freqs, stride=rows)
            a_ref[picked, :] += totals[2 * place]
            b_ref[picked, :] += totals[2 * place + 1]


def stress_kernel(
    freqs, member_ref, scalar_ref, wet_ref, a_ref, b_ref, own_ref, other_ref, sums_ref, ratio_ref
):
    member = member_ref[0]
    wet_cells = wet_ref[...]
    rows = wet_cells.shape[0]
    energy = wet_cells * (own_ref[...] + other_ref[...]) / (ND * NF)
    square = jnp.square(energy)

    sums = [jnp.zeros(wet_cells.shape, jnp.float32) for _ in range(3)]
    for j in range(freqs):
        base = (member * freqs + j) * CLASSES * KINDS
        high, shoal = scalar_ref[base + 3], scalar_ref[base + 4]
        block = slice(j * rows, (j + 1) * rows)
        ratio = wet_cells / (1.0 + (2.0 * high) * square)
        ratio_ref[j] = ratio
        whole = ratio * a_ref[block, :]
        along = ratio * b_ref[block, :]
        sums[0] += shoal * along + (shoal - 0.5) * whole
        sums[1] += (2.0 * shoal - 0.5) * whole - shoal * along
        sums[2] += whole
    for index in range(3):
        sums_ref[index] = sums[index] / (ND * NF)


def total_kernel(own_ref, other_ref, sums_ref, stress_ref):
    sums_ref[...] = own_ref[...] + other_ref[...]
    stress_ref[...] = sums_ref[0:2]


def strip_kernel(stress_ref, swapped_ref, other_ref, beside_ref, first_ref, second_ref):
    rows = stress_ref.shape[1]
    low_half = iota((rows, LANES), 1) < LANES // 2
    odd_sect = lax.rem(lax.axis_index("sect"), 2) == 1
    odd_slab = lax.rem(lax.axis_index("slab"), 2) == 1
    for index in range(2):
        swapped, other = swapped_ref[index], other_ref[index]
        beside = jnp.where(low_half != odd_sect, swapped, other)
        beside_ref[index] = beside
        ends = [
            jnp.concatenate([values[first : first + SUB] for values in (stress_ref[index], beside)], 1)
            for first in (0, rows - SUB)
        ]
        first_ref[index] = jnp.where(odd_slab, *ends)
        second_ref[index] = jnp.where(odd_slab, *ends[::-1])


BEHIND = 12


def final_kernel(
    freqs, member_ref, scalar_ref, depth_ref, ratios_ref, sums_ref, beside_ref, swapped_ref,
    other_ref, growth_ref, kept_ref, columns_ref, edges_ref,
    result_ref, level_ref, damping_ref, turning_ref, ring0, ring1, sems,
):
    member = member_ref[0]
    rings = (ring0, ring1)
    rows = depth_ref.shape[0]
    slab, slabs = lax.axis_index("slab"), lax.axis_size("slab")
    sect, sects = lax.axis_index("sect"), lax.axis_size("sect")
    above_ok = jnp.where(slab > 0, 1.0, 0.0)
    below_ok = jnp.where(slab < slabs - 1, 1.0, 0.0)
    left_ok = jnp.where(sect > 0, 1.0, 0.0)
    right_ok = jnp.where(sect < sects - 1, 1.0, 0.0)

    odd = lax.rem(slab, 2) == 1

    def framed(index):
        middle = jnp.concatenate([sums_ref[index], beside_ref[index]], axis=1)
        swapped, other = swapped_ref[index], other_ref[index]
        below = jnp.where(odd, other, swapped)
        above = jnp.where(odd, swapped, other)
        return jnp.concatenate([middle, below, above], axis=0)

    def around(values, axis):
        size = values.shape[axis]
        return pltpu.roll(values, 1, axis) + pltpu.roll(values, size - 1, axis)

    stress_x, stress_y = framed(0), framed(1)
    frame = stress_x.shape
    frame_row, frame_lane = iota(frame, 0), iota(frame, 1)
    row_ok = jnp.where(frame_row < rows, 1.0, jnp.where(frame_row < rows + SUB, below_ok, above_ok))
    lane_ok = jnp.where(
        frame_lane < LANES, 1.0, jnp.where(frame_lane < LANES + LANES // 2, right_ok, left_ok)
    )
    inside = row_ok * lane_ok / 4.5
    source = -((around(stress_x, 0) - 2.0 * stress_x) + (around(stress_y, 1) - 2.0 * stress_y))
    level = inside * source
    for _ in range(JAC):
        level = inside * (source + around(level, 0) + around(level, 1))
    level = level[:rows, :LANES]
    level_ref[...] = level
    damping = 1.0 / (1.0 + 4.0 * sums_ref[2] / (jnp.square(depth_ref[...] + level) + 1.0))
    tiles = rows // SUB
    damping_ref[...] = damping
    turning_ref[...] = columns_ref[...]
    tile_lane = iota((SUB, LANES), 1)

    def send(j, which, piece):
        part = pl.ds(piece * ND // 4, ND // 4)
        return pltpu.make_async_copy(
            rings[which].at[part], result_ref.at[j, part], sems.at[which, piece]
        )

    def frequency(j, which):
        @pl.when(j >= 2)
        def _():
            for piece in range(4):
                send(j - 2, which, piece).wait()

        base = (member * freqs + j) * CLASSES * KINDS
        high = scalar_ref[base + 3]

        def damped(direction, t, ratio, high_ratio):
            to_down, to_right = sides(direction // (ND // 4))
            part = slice(t * SUB, (t + 1) * SUB)
            target = 0 if to_right > 0 else LANES - 2
            at_side = (tile_lane >= target) & (tile_lane < target + 2)
            turn = (target - direction % GROUP * 2 * freqs) % LANES
            entered = turning_ref[direction // GROUP, part, :]
            if turn:
                entered = pltpu.roll(entered, turn, 1)
            value = kept_ref[j, direction, part, :] + jnp.where(at_side, entered, 0.0)
            if t == (0 if to_down > 0 else tiles - 1):
                edge = ((0 if to_down > 0 else 18) + row_slot(direction)) * freqs + j
                value += edges_ref[pl.ds(pl.multiple_of(edge * SUB, SUB), SUB), :]
            return value * (ratio + high_ratio * growth_ref[direction, part, :])

        pending = []
        for kind in range(CLASSES - 1):
            together = (0, 9, 18, 27) if kind == 0 else (kind, 18 - kind, 18 + kind, 36 - kind)
            scale = scalar_ref[base + kind * KINDS + 2]
            for t in range(tiles):
                part = slice(t * SUB, (t + 1) * SUB)
                ratio = scale * (ratios_ref[j, part, :] * damping_ref[part, :])
                high_ratio = high * ratio
                for direction in together:
                    pending.append((direction, part, damped(direction, t, ratio, high_ratio)))
                while len(pending) > BEHIND:
                    target, place, value = pending.pop(0)
                    rings[which][target, place, :] = value
        for target, place, value in pending:
            rings[which][target, place, :] = value
        for piece in range(4):
            send(j, which, piece).start()
        turned = [pltpu.roll(turning_ref[group], LANES - 2, 1) for group in range(GROUPS)]
        for group in range(GROUPS):
            turning_ref[group] = turned[group]

    def pair(index, carry):
        for which in range(2):
            frequency(2 * index + which, which)
        return carry

    lax.fori_loop(0, freqs // 2, pair, 0)
    if freqs % 2:
        frequency(jnp.int32(freqs - 1), 0)
    for j in range(max(0, freqs - 2), freqs):
        for piece in range(4):
            send(j, j % 2, piece).wait()


def swap(values, axis, first):
    count = lax.axis_size(axis)
    pairs = [(i, i + 1) for i in range(first, count - 1, 2)]
    return lax.ppermute(values, axis, pairs + [(b, a) for a, b in pairs])


def others_sum(values, axis):
    count = lax.axis_size(axis)
    total = None
    for step in range(1, count):
        part = lax.ppermute(values, axis, [(i, (i + step) % count) for i in range(count)])
        total = part if total is None else total + part
    return jnp.zeros_like(values) if total is None else total


VMEM = pl.BlockSpec(memory_space=pltpu.VMEM)
SMEM = pl.BlockSpec(memory_space=pltpu.SMEM)
HBM = pl.BlockSpec(memory_space=pltpu.HBM)
ANY = pl.BlockSpec(memory_space=pl.ANY)


def in_vmem(*shape):
    return pltpu.VMEM(shape, jnp.float32)


def in_any(*shape):
    return jax.ShapeDtypeStruct(shape, jnp.float32)


def in_hbm(values):
    return pltpu.with_memory_space_constraint(values, pltpu.HBM)


def call(kernel, in_specs, out_shape, out_specs, flops, moved, scratch=(), aliases=None, limit=6):
    return pl.pallas_call(
        kernel,
        in_specs=in_specs,
        out_shape=out_shape,
        out_specs=out_specs,
        scratch_shapes=list(scratch),
        input_output_aliases=aliases or {},
        cost_estimate=pl.CostEstimate(flops=flops, bytes_accessed=moved, transcendentals=0),
        compiler_params=pltpu.CompilerParams(vmem_limit_bytes=limit << 20),
    )


def resident(spectrum, land_mask, ice_mask, wind_u, wind_v, depth):
    local_comp, rows, lanes = spectrum.shape
    freqs = local_comp // ND
    members = lax.axis_size("comp")
    member = lax.axis_index("comp").astype(jnp.int32).reshape(1)
    scalars, lane_table, row_table = numpy_tables(members, freqs)
    scalars, lane_table, row_table = map(jnp.asarray, (scalars, lane_table, row_table))
    cells = rows * lanes
    row_message = 2 * 18 * freqs + CORNERS
    block = (freqs, ND, rows, lanes)
    spectrum = spectrum.reshape(block)

    growth, wet, swap_side, other_side, swap_row, other_row, edges = call(
        functools.partial(pack_kernel, freqs),
        [SMEM] + [HBM] * 7,
        (
            in_any(ND, rows, lanes),
            in_any(rows, lanes),
            in_any(GROUPS // 2, rows, lanes),
            in_any(GROUPS // 2, rows, lanes),
            in_any(row_message, lanes),
            in_any(row_message, lanes),
            in_any(2 * 18 * freqs * SUB, lanes),
        ),
        (VMEM,) * 7,
        flops=local_comp * cells * 4,
        moved=local_comp * cells * 4,
        scratch=[
            pltpu.VMEM((local_comp * rows, lanes), jnp.float32),
            pltpu.VMEM((GROUPS // 2, rows, lanes), jnp.float32),
            pltpu.VMEM((GROUPS // 2, rows, lanes), jnp.float32),
            pltpu.VMEM(lane_table.shape[1:], jnp.float32),
            pltpu.VMEM(row_table.shape[1:], jnp.float32),
            pltpu.VMEM((rows, lanes), jnp.int32),
            pltpu.VMEM((rows, lanes), jnp.int32),
            pltpu.VMEM((rows, lanes), jnp.float32),
            pltpu.VMEM((rows, lanes), jnp.float32),
            pltpu.SemaphoreType.DMA((6,)),
            pltpu.SemaphoreType.DMA((GROUPS,)),
        ],
        limit=30,
    )(
        member,
        *map(in_hbm, (lane_table, row_table, land_mask, ice_mask, wind_u, wind_v, spectrum)),
    )

    def main_part(start, stop, *before):
        return call(
            functools.partial(main_kernel, freqs, start, stop),
            [SMEM, SMEM, VMEM, VMEM, HBM] + ([ANY, VMEM, VMEM, VMEM, VMEM] if before else []),
            (
                in_vmem(*block),
                in_any(freqs * rows, lanes),
                in_any(freqs * rows, lanes),
                in_any(rows, lanes),
            ),
            (VMEM,) * 4,
            flops=local_comp * cells * 16 * (stop - start) // freqs,
            moved=local_comp * cells * 8 * (stop - start) // freqs,
            scratch=[
                pltpu.VMEM((AHEAD, ND, rows, lanes), jnp.float32),
                pltpu.SemaphoreType.DMA((AHEAD,)),
            ]
            + [pltpu.VMEM((rows + 2 * SUB, lanes), jnp.float32)] * 8,
            aliases={6 + index: index for index in range(4)} if before else {},
            limit=8,
        )(member, scalars, wet, growth, in_hbm(spectrum), *before)

    early = max(1, freqs // 3)
    swap_side, other_side = swap(swap_side, "sect", 0), swap(other_side, "sect", 1)
    kept, *partial = main_part(0, early)
    swap_row, other_row = call(
        functools.partial(corner_kernel, freqs),
        [VMEM, VMEM, VMEM, ANY, ANY, ANY],
        (in_any(row_message, lanes), in_any(row_message, lanes)),
        (ANY, ANY),
        flops=100,
        moved=1 << 15,
        scratch=[pltpu.VMEM((2, CORNERS, lanes), jnp.float32), pltpu.SemaphoreType.DMA((2,))],
        aliases={3: 0, 4: 1},
    )(wet, swap_side, other_side, swap_row, other_row, partial[-1])
    swapped_row = swap(swap_row, "slab", 0)
    other_row = swap(other_row, "slab", 1)
    kept, a_sums, b_sums, energy = main_part(early, freqs, swap_row, kept, *partial)

    columns, edges, energy = call(
        functools.partial(enter_kernel, freqs),
        [SMEM] + [VMEM] * 9,
        (
            in_any(GROUPS, rows, lanes),
            in_any(2 * 18 * freqs * SUB, lanes),
            in_any(rows, lanes),
        ),
        (VMEM,) * 3,
        flops=cells * 600,
        moved=cells * 200,
        aliases={8: 1, 9: 2},
    )(
        member, lane_table, row_table, wet, swap_side, other_side, swapped_row, other_row, edges,
        energy,
    )
    energy_there = others_sum(energy, "comp")
    a_sums, b_sums = call(
        functools.partial(entered_kernel, freqs),
        [SMEM] + [VMEM] * 10,
        (in_any(freqs * rows, lanes), in_any(freqs * rows, lanes)),
        (VMEM,) * 2,
        flops=cells * 600,
        moved=cells * 200,
        aliases={9: 0, 10: 1},
    )(
        member, lane_table, row_table, ice_mask, wind_u, wind_v, growth, columns, edges,
        a_sums, b_sums,
    )

    sums, ratios = call(
        functools.partial(stress_kernel, freqs),
        [SMEM, SMEM] + [VMEM] * 5,
        (in_any(3, rows, lanes), in_any(freqs, rows, lanes)),
        (VMEM, VMEM),
        flops=cells * freqs * 12,
        moved=cells * freqs * 8,
    )(member, scalars, wet, a_sums, b_sums, energy, energy_there)
    sums, stress = call(
        total_kernel,
        [VMEM, VMEM],
        (in_any(3, rows, lanes), in_any(2, rows, lanes)),
        (VMEM, VMEM),
        flops=cells * 3,
        moved=cells * 44,
    )(sums, others_sum(sums, "comp"))
    beside, first, second = call(
        strip_kernel,
        [VMEM, VMEM, VMEM],
        (in_any(2, rows, lanes), in_any(2, SUB, 2 * lanes), in_any(2, SUB, 2 * lanes)),
        (VMEM, VMEM, VMEM),
        flops=cells * 4,
        moved=cells * 36,
    )(stress, swap(stress, "sect", 0), swap(stress, "sect", 1))
    aside, beyond = swap(first, "slab", 0), swap(second, "slab", 1)

    result, level = call(
        functools.partial(final_kernel, freqs),
        [SMEM, SMEM] + [VMEM] * 10,
        (in_any(*block), in_any(rows, lanes)),
        (HBM, VMEM),
        flops=local_comp * cells * 6,
        moved=local_comp * cells * 8,
        scratch=[
            pltpu.VMEM((rows, lanes), jnp.float32),
            pltpu.VMEM((GROUPS, rows, lanes), jnp.float32),
            pltpu.VMEM((ND, rows, lanes), jnp.float32),
            pltpu.VMEM((ND, rows, lanes), jnp.float32),
            pltpu.SemaphoreType.DMA((2, 4)),
        ],
    )(
        member, scalars, depth, ratios, sums, beside, aside, beyond, growth, kept,
        columns, edges,
    )
    return result.reshape(local_comp, rows, lanes), level


def local(spectrum, *fields):
    local_comp, rows, lanes = spectrum.shape
    whole_rings = local_comp % ND == 0 and GROUP * 2 * (local_comp // ND) < LANES - 1
    if whole_rings and lanes == LANES and rows % SUB == 0:
        return resident(spectrum, *fields)
    return general(spectrum, *fields)


def solution(mesh):
    in_specs = (
        P("comp", "slab", "sect"),
        P("slab", "sect"),
        P("slab", "sect"),
        P("slab", "sect"),
        P("slab", "sect"),
        P("slab", "sect"),
    )
    out_specs = (P("comp", "slab", "sect"), P("slab", "sect"))
    return jax.shard_map(local, mesh=mesh, in_specs=in_specs, out_specs=out_specs, check_vma=False)
```

```python
import functools
import math

import jax
import jax.numpy as jnp
import numpy as np
from jax import lax
from jax.experimental import pallas as pl
from jax.experimental.pallas import tpu as pltpu
from jax.sharding import PartitionSpec as P

ND = 36
NF = 36
STEPS = 2
JAC = 4


def extended(cells, sides, width):
    for axis, dim in sides:
        count = lax.axis_size(axis)
        ends = count - 1
        head = lax.slice_in_dim(cells, 0, width, axis=dim)
        tail = lax.slice_in_dim(cells, cells.shape[dim] - width, cells.shape[dim], axis=dim)
        cells = jnp.concatenate(
            [
                lax.ppermute(tail, axis, [(i, (i + 1) % count) for i in range(ends)]),
                cells,
                lax.ppermute(head, axis, [((i + 1) % count, i) for i in range(ends)]),
            ],
            axis=dim,
        )
    return cells


def tables(index):
    freq_index = (index // ND).astype(jnp.float32)
    angle_index = (index % ND).astype(jnp.float32)
    heading = 2.0 * math.pi * angle_index / ND
    return (
        jnp.cos(heading),
        jnp.sin(heading),
        jnp.power(1.1, -freq_index),
        jnp.power(1.1, freq_index - (NF - 1)),
        0.5 + 0.5 * freq_index / (NF - 1),
    )


def column(values):
    return values[:, None, None]


def advect(spectra, wet_cells, speed_x, speed_y):
    padded = extended(spectra, (("slab", 1), ("sect", 2)), 1)
    upper_rows = padded[:, :-2, 1:-1]
    lower_rows = padded[:, 2:, 1:-1]
    left_cells = padded[:, 1:-1, :-2]
    right_cells = padded[:, 1:-1, 2:]
    change = (
        jnp.maximum(speed_x, 0.0) * (spectra - upper_rows)
        + jnp.minimum(speed_x, 0.0) * (lower_rows - spectra)
        + jnp.maximum(speed_y, 0.0) * (spectra - left_cells)
        + jnp.minimum(speed_y, 0.0) * (right_cells - spectra)
    )
    return (spectra - change) * wet_cells


def forcing(spectra, energy, wind_east, wind_north, ice_cover, cosine, sine, high_ratio):
    project = cosine * wind_east + sine * wind_north
    growth = 0.5 * high_ratio * jnp.square(jnp.maximum(project, 0.0)) * (1.0 - ice_cover)
    return spectra * (1.0 + growth) / (1.0 + 2.0 * high_ratio * jnp.square(energy))


def stress_weights(cosine, sine, shoaling):
    return jnp.stack(
        [shoaling * (cosine * cosine + 1.0) - 0.5, shoaling * (sine * sine + 1.0) - 0.5]
    )


def surge_solve(stress):
    padded = extended(stress, (("slab", 1), ("sect", 2)), 1)
    source_term = -(
        padded[0, 2:, 1:-1]
        + padded[0, :-2, 1:-1]
        - 2.0 * stress[0]
        + (padded[1, 1:-1, 2:] + padded[1, 1:-1, :-2] - 2.0 * stress[1])
    )
    surge_level = source_term / 4.5
    for _ in range(JAC):
        neighbours = extended(surge_level, (("slab", 0), ("sect", 1)), 1)
        surge_level = (
            source_term
            + neighbours[2:, 1:-1]
            + neighbours[:-2, 1:-1]
            + neighbours[1:-1, 2:]
            + neighbours[1:-1, :-2]
        ) / 4.5
    return surge_level


def general(spectrum, land_mask, ice_mask, wind_u, wind_v, depth):
    groups = lax.axis_size("comp")
    member = lax.axis_index("comp")
    local_comp, block_rows, block_cols = spectrum.shape
    point_rows = block_rows // groups
    total_comp = ND * NF
    wet_cells = (1 - land_mask).astype(jnp.float32)
    ice_cover = ice_mask.astype(jnp.float32)

    def own_rows(values):
        return lax.dynamic_slice_in_dim(values, member * point_rows, point_rows, values.ndim - 2)

    own_index = member * local_comp + jnp.arange(local_comp, dtype=jnp.int32)
    cosine, sine, low_ratio, high_ratio, shoaling = tables(own_index)
    spectra = spectrum * wet_cells
    for _ in range(STEPS):
        spectra = advect(
            spectra, wet_cells, column(0.7 * low_ratio * cosine), column(0.7 * low_ratio * sine)
        )
    points = lax.all_to_all(spectra, "comp", split_axis=1, concat_axis=0, tiled=True)
    cosine_full, sine_full, _, high_full, shoal_full = tables(
        jnp.arange(total_comp, dtype=jnp.int32)
    )
    energy = jnp.sum(points, axis=0) / total_comp
    sourced = forcing(
        points,
        energy,
        own_rows(wind_u),
        own_rows(wind_v),
        own_rows(ice_cover),
        column(cosine_full),
        column(sine_full),
        column(high_full),
    )
    stress = (
        jnp.einsum(
            "sk,krc->src",
            stress_weights(cosine_full, sine_full, shoal_full),
            sourced,
            precision=lax.Precision.HIGHEST,
        )
        / total_comp
    )
    stress_block = lax.all_gather(stress, "comp", axis=1, tiled=True)
    level_block = surge_solve(stress_block)
    final_energy = jnp.sum(sourced, axis=0) / total_comp
    damped = sourced / (
        1.0 + 4.0 * final_energy / (jnp.square(own_rows(depth) + own_rows(level_block)) + 1.0)
    )
    result = lax.all_to_all(damped, "comp", split_axis=0, concat_axis=1, tiled=True)
    return (result, level_block)


LANES = 128
SUB = 8
CLASSES = 10
KINDS = 5
GROUP = 3
GROUPS = ND // GROUP
CORNERS = 8


def class_of(direction):
    folded = direction % 18
    return folded if folded <= 9 else 18 - folded


def heads_down(direction):
    return direction < 9 or direction >= 27


def heads_right(direction):
    return direction < 18


def row_slot(direction):
    if direction < 9:
        return direction
    return direction - 18 if direction >= 27 else direction - 9


def numpy_tables(members, freqs):
    j = np.arange(members * freqs, dtype=np.float64)
    heading = 2.0 * np.pi * np.arange(ND) / ND
    cosine, sine = np.cos(heading), np.sin(heading)
    low = 1.1 ** (-j)
    high = 1.1 ** (j - (NF - 1))
    shoal = 0.5 + 0.5 * j / (NF - 1)
    step_x = 0.7 * low[:, None] * np.abs(cosine)
    step_y = 0.7 * low[:, None] * np.abs(sine)
    keep = 1.0 - step_x - step_y
    alpha, beta, scale = step_x / keep, step_y / keep, keep * keep
    classes = np.arange(CLASSES)
    square = np.broadcast_to(cosine * cosine, alpha.shape)
    scalars = np.stack(
        [
            alpha[:, classes],
            beta[:, classes],
            scale[:, classes],
            np.broadcast_to(high[:, None], (j.size, CLASSES)),
            np.broadcast_to(shoal[:, None], (j.size, CLASSES)),
        ],
        axis=-1,
    ).astype(np.float32)

    kinds = np.stack(
        [
            2.0 * beta,
            beta * beta,
            alpha * beta,
            scale,
            scale * square,
            np.broadcast_to(high[:, None], alpha.shape),
            np.broadcast_to(cosine, alpha.shape),
            np.broadcast_to(sine, alpha.shape),
        ]
    )
    lanes = np.zeros((members, GROUPS, 8, LANES), np.float32)
    packed = kinds.reshape(8, members, freqs, GROUPS, GROUP)
    packed = np.repeat(packed.transpose(1, 3, 0, 4, 2), 2, axis=-1)
    lanes[..., : GROUP * 2 * freqs] = packed.reshape(members, GROUPS, 8, -1)

    rows = np.stack(
        [2.0 * alpha, alpha * alpha, alpha * beta, scale, np.broadcast_to(high[:, None], alpha.shape)]
    )[:, :, classes]
    rows = rows.reshape(5, members, freqs, CLASSES).transpose(1, 3, 0, 2)
    rows = np.broadcast_to(rows[..., None], rows.shape + (LANES,)).astype(np.float32)
    return scalars.reshape(-1), lanes, rows


def odd_position(axis):
    return lax.rem(lax.axis_index(axis), 2) == 1


def iota(shape, axis):
    return lax.broadcasted_iota(jnp.int32, shape, axis)


def spread(values, column):
    return jnp.broadcast_to(values[:, column : column + 1], values.shape)


def shift_rows(values, step):
    rows = values.shape[0]
    edge = 0 if step > 0 else rows - 1
    moved = pltpu.roll(values, step % rows, 0)
    return jnp.where(iota(values.shape, 0) == edge, 0.0, moved)


def shift_lanes(values, step):
    lanes = values.shape[1]
    edge = 0 if step > 0 else lanes - 1
    moved = pltpu.roll(values, step % lanes, 1)
    return jnp.where(iota(values.shape, 1) == edge, 0.0, moved)


DEPTH = 5


def sides(quadrant):
    return 1 if quadrant in (0, 3) else -1, 1 if quadrant in (0, 1) else -1


def pack_kernel(
    freqs, member_ref, lanes_hbm, table_hbm, land_hbm, ice_hbm, east_hbm, north_hbm, spectrum_ref,
    growth_ref, wet_ref, swap_side_ref, other_side_ref, swap_row_ref, other_row_ref, edges_ref,
    kept_ref, right_ref, left_ref, lanes_ref, table_ref, land_ref, ice_ref, east_ref, north_ref, small_sems, sems,
):
    member = member_ref[0]
    small = [
        pltpu.make_async_copy(source, target, small_sems.at[index])
        for index, (source, target) in enumerate(
            (
                (land_hbm, land_ref),
                (ice_hbm, ice_ref),
                (east_hbm, east_ref),
                (north_hbm, north_ref),
                (lanes_hbm.at[member], lanes_ref),
                (table_hbm.at[member], table_ref),
            )
        )
    ]
    for copy in small:
        copy.start()

    rows = land_ref.shape[0]
    blocks_ref = kept_ref.reshape(freqs, ND, rows, LANES)

    def fetch(group):
        part = (slice(None), pl.ds(group * GROUP, GROUP))
        return pltpu.make_async_copy(spectrum_ref.at[part], blocks_ref.at[part], sems.at[group])

    for group in range(DEPTH):
        fetch(group).start()
    edges_ref[...] = jnp.zeros_like(edges_ref)
    for copy in small:
        copy.wait()

    wet_cells = (1 - land_ref[...]).astype(jnp.float32)
    wet_ref[...] = wet_cells
    open_water = 0.5 * (1.0 - ice_ref[...].astype(jnp.float32))
    shape = wet_cells.shape
    tiles = rows // SUB
    for direction in range(ND):
        angle = 2.0 * math.pi * direction / ND
        project = math.cos(angle) * east_ref[...] + math.sin(angle) * north_ref[...]
        growth_ref[direction] = open_water * jnp.square(jnp.maximum(project, 0.0))

    lane = iota(shape, 1)
    even = lane % 2 == 0
    tile_lane = iota((SUB, LANES), 1)
    for row_ref in (swap_row_ref, other_row_ref):
        row_ref[pl.ds(2 * 18 * freqs, CORNERS), :] = jnp.zeros((CORNERS, LANES), jnp.float32)
    odd_sect, odd_slab = odd_position("sect"), odd_position("slab")

    half = GROUPS // 2

    def gather_all(to_right):
        target_ref = right_ref if to_right else left_ref

        def gather(index, carry):
            group = index + (0 if to_right else half)
            fetch(group).wait()

            @pl.when(group + DEPTH < GROUPS)
            def _():
                fetch(group + DEPTH).start()

            packed = [jnp.zeros((SUB, LANES), jnp.float32) for _ in range(tiles)]
            for i in range(GROUP):
                for j in range(freqs):
                    place = i * 2 * freqs + 2 * j
                    here = (tile_lane >= place) & (tile_lane < place + 2)
                    turn = (place + 2 if to_right else place) % LANES
                    first = pl.multiple_of((j * ND + group * GROUP + i) * rows, SUB)
                    for tile in range(tiles):
                        cells = kept_ref[pl.ds(first + tile * SUB, SUB), :]
                        packed[tile] = jnp.where(here, pltpu.roll(cells, turn, 1), packed[tile])
            for tile in range(tiles):
                target_ref[index, tile * SUB : (tile + 1) * SUB, :] = packed[tile]
            return carry

        lax.fori_loop(0, half, gather, 0)

    def side_message(group):
        to_right, fore = group < half, 1 if heads_down(group * GROUP) else -1
        ahead, behind = (LANES - 1, LANES - 2) if to_right else (0, 1)
        wet_near, wet_far = spread(wet_cells, ahead), spread(wet_cells, behind)
        near_even = not to_right
        packed = right_ref[group] if to_right else left_ref[group - half]
        values = packed * jnp.where(even == near_even, wet_near, wet_far)
        near = pltpu.roll(values, 1 if near_even else LANES - 1, 1)
        table = lanes_ref[group]
        follow = wet_near * (table[1:2] * values + table[2:3] * shift_rows(near, fore))
        message = jnp.where(even == near_even, values, follow)
        return jnp.where(lane == LANES - 1, wet_near, message)

    def row_message(direction):
        to_down = heads_down(direction)
        near_row, far_row = (rows - 1, rows - 2) if to_down else (0, 1)
        wet_near = wet_cells[near_row : near_row + 1, :]
        wet_far = wet_cells[far_row : far_row + 1, :]
        table = table_ref.at[class_of(direction)]
        near = kept_ref[pl.ds(direction * rows + near_row, freqs, stride=ND * rows), :] * wet_near
        far = kept_ref[pl.ds(direction * rows + far_row, freqs, stride=ND * rows), :] * wet_far
        beside = shift_lanes(near, 1 if heads_right(direction) else -1)
        return near, wet_near * (table[1] * far + table[2] * beside)

    def row_messages(slots):
        for slot in slots:
            pairs = zip(row_message(by_slot[True, slot]), row_message(by_slot[False, slot]))
            for which, (down, up) in enumerate(pairs):
                first = (which * 18 + slot) * freqs
                swap_row_ref[first : first + freqs, :] = jnp.where(odd_slab, up, down)
                other_row_ref[first : first + freqs, :] = jnp.where(odd_slab, down, up)

    by_slot = {(heads_down(d), row_slot(d)): d for d in range(ND)}
    gather_all(True)
    rights = [side_message(index) for index in range(half)]
    for index in range(half):
        right_ref[index] = rights[index]
    row_messages(range(9))
    gather_all(False)
    for index in range(half):
        right, left = right_ref[index], side_message(index + half)
        swap_side_ref[index] = jnp.where(odd_sect, left, right)
        other_side_ref[index] = jnp.where(odd_sect, right, left)
    row_messages(range(9, 18))


def corner_kernel(
    freqs, wet_ref, swapped_ref, other_ref, swap_in, other_in, _after, swap_row_ref, other_row_ref,
    rows_ref, sems,
):
    rows = wet_ref.shape[0]
    odd_sect, odd_slab = odd_position("sect"), odd_position("slab")
    last = iota((1, LANES), 1) == LANES - 1
    rows_ref[...] = jnp.zeros_like(rows_ref)
    for i in range(6):
        from_left = i < 3
        column = 0 if from_left else LANES - 1
        ends = []
        for row, index in ((rows - 1, i), (0, i + 3 if from_left else i - 3)):
            swapped = swapped_ref[index, row : row + 1, :]
            other = other_ref[index, row : row + 1, :]
            came = jnp.where(odd_sect == from_left, swapped, other)
            own = jnp.broadcast_to(wet_ref[row : row + 1, column : column + 1], (1, LANES))
            ends.append(jnp.where(last, own, came))
        rows_ref[0, i : i + 1, :] = jnp.where(odd_slab, *ends[::-1])
        rows_ref[1, i : i + 1, :] = jnp.where(odd_slab, *ends)
    start = 2 * 18 * freqs
    copies = [
        pltpu.make_async_copy(
            rows_ref.at[which], ref.at[pl.ds(start, CORNERS), :], sems.at[which]
        )
        for which, ref in ((0, swap_row_ref), (1, other_row_ref))
    ]
    for copy in copies:
        copy.start()
    for copy in copies:
        copy.wait()


AHEAD = 3


def main_kernel(
    freqs, start, stop, member_ref, scalar_ref, wet_ref, growth_ref, spectrum_ref, *refs
):
    if start:
        _after, _kept_in, a_in, b_in, energy_in, *refs = refs
    kept_ref, a_ref, b_ref, energy_ref, ring_ref, sems, *first_refs = refs
    member = member_ref[0]
    nought = jnp.minimum(member, 0)
    rows = wet_ref.shape[0]
    tiles = rows // SUB

    def fetch(j):
        slot = lax.rem(j, AHEAD)
        return pltpu.make_async_copy(spectrum_ref.at[j], ring_ref.at[slot], sems.at[slot])

    for j in range(start, min(start + AHEAD, stop)):
        fetch(jnp.int32(j)).start()

    lane = iota((SUB, LANES), 1)
    sub = iota((SUB, LANES), 0)
    not_first = jnp.where(lane == 0, 0.0, 1.0)
    not_last = jnp.where(lane == LANES - 1, 0.0, 1.0)
    top, bottom = sub == 0, sub == SUB - 1
    energy_ref[...] = energy_in[...] if start else jnp.zeros_like(energy_ref)
    for first_ref in first_refs:
        first_ref[...] = jnp.zeros_like(first_ref)

    def tile_at(tile):
        return pl.ds(tile * SUB, SUB)

    def row_shift(quadrant):
        return -1 if quadrant in (0, 3) else 1

    def parts_of(kind):
        if kind == 0:
            return ((0, 0, 0), (9, 1, 9), (18, 2, 0), (27, 3, 9))
        return ((kind, 0, kind), (18 - kind, 1, kind), (18 + kind, 2, kind), (36 - kind, 3, kind))

    def frequency(j, carry):
        fetch(j).wait()
        slot = lax.rem(j, AHEAD)
        base = (member * freqs + j) * CLASSES * KINDS
        at = [pl.ds(pl.multiple_of(j * rows, SUB) + t * SUB, SUB) for t in range(tiles)]

        def speeds(part):
            at_class = base + part[2] * KINDS
            beta = scalar_ref[at_class + 1]
            return scalar_ref[at_class], beta * (not_first if part[1] in (0, 1) else not_last)

        def beside(cells, quadrant):
            return pltpu.roll(cells, 1 if quadrant in (0, 1) else LANES - 1, 1)

        def first_step(kind):
            parts = parts_of(kind)
            speed = [speeds(part) for part in parts]
            wet = [wet_ref[tile_at(t), :] for t in range(tiles)]
            for (direction, quadrant, _), (alpha, across) in zip(parts, speed):
                shift = row_shift(quadrant)
                edge = top if shift < 0 else bottom
                target = first_refs[kind % 2 * 4 + quadrant]
                cells = [ring_ref[slot, direction, tile_at(t), :] * wet[t] for t in range(tiles)]
                turned = [pltpu.roll(cells[t], -shift % SUB, 0) for t in range(tiles)]
                for t in range(tiles):
                    before = turned[t + shift] if 0 <= t + shift < tiles else 0.0
                    ahead = jnp.where(edge, before, turned[t])
                    after = cells[t] + alpha * ahead + across * beside(cells[t], quadrant)
                    target[tile_at(t + 1), :] = wet[t] * after

        def second_step(kind):
            parts = parts_of(kind)
            scale, high = scalar_ref[base + kind * KINDS + 2], scalar_ref[base + 3]
            scaled_high = scale * high
            speed = [speeds(part) for part in parts]
            for t in range(tiles):
                moved, grown = [], []
                for (direction, quadrant, _), (alpha, across) in zip(parts, speed):
                    source = first_refs[kind % 2 * 4 + quadrant]
                    cells = source[tile_at(t + 1), :]
                    ahead = source[pl.ds((t + 1) * SUB + row_shift(quadrant) + nought, SUB), :]
                    after = cells + alpha * ahead + across * beside(cells, quadrant)
                    kept_ref[j, direction, tile_at(t), :] = after
                    moved.append(after)
                    grown.append(growth_ref[direction, tile_at(t), :] * after)
                if kind == 0:
                    plain_x, plain_y = scale * (moved[0] + moved[2]), scale * (moved[1] + moved[3])
                    grown_x = plain_x + scaled_high * (grown[0] + grown[2])
                    grown_y = plain_y + scaled_high * (grown[1] + grown[3])
                    square = math.cos(0.5 * math.pi) ** 2
                    energy_ref[tile_at(t), :] += plain_x + plain_y
                    a_ref[at[t], :] = grown_x + grown_y
                    b_ref[at[t], :] = grown_x + square * grown_y
                else:
                    plain = scale * ((moved[0] + moved[1]) + (moved[2] + moved[3]))
                    whole = plain + scaled_high * ((grown[0] + grown[1]) + (grown[2] + grown[3]))
                    square = math.cos(2.0 * math.pi * kind / ND) ** 2
                    energy_ref[tile_at(t), :] += plain
                    a_ref[at[t], :] += whole
                    b_ref[at[t], :] += square * whole

        first_step(0)
        for kind in range(CLASSES - 1):
            if kind + 1 < CLASSES - 1:
                first_step(kind + 1)
            second_step(kind)

        @pl.when(j + AHEAD < stop)
        def _():
            fetch(j + AHEAD).start()

        return carry

    lax.fori_loop(start, stop, frequency, 0)


def edge_rows(freqs, to_down, direction, at):
    first = ((0 if to_down else 18) + row_slot(direction)) * freqs * SUB
    return pl.ds(first + at, freqs, stride=SUB)


def enter_kernel(
    freqs, member_ref, lanes_ref, table_ref, wet_ref, swap_side_ref, other_side_ref, swap_row_ref,
    other_row_ref, _edges_in, energy_in, columns_ref, edges_ref, energy_ref,
):
    member = member_ref[0]
    wet_cells = wet_ref[...]
    shape = wet_cells.shape
    rows = shape[0]
    lane = iota(shape, 1)
    row = iota(shape, 0)
    even = lane % 2 == 0
    width = 2 * freqs
    used = lane < GROUP * width
    energy = energy_in[...]
    start = 2 * 18 * freqs
    odd_sect, odd_slab = odd_position("sect"), odd_position("slab")

    def from_rows(to_down, part):
        return jnp.where(odd_slab == to_down, swap_row_ref[part, :], other_row_ref[part, :])

    for to_right in (True, False):
        near_column, far_column = (0, 1) if to_right else (LANES - 1, LANES - 2)
        near_even = to_right
        wet_near, wet_far = spread(wet_cells, near_column), spread(wet_cells, far_column)
        total = jnp.zeros(shape, jnp.float32)
        for index in range(GROUPS // 2):
            group = index if to_right else index + GROUPS // 2
            to_down = heads_down(group * GROUP)
            fore = 1 if to_down else -1
            message = jnp.where(odd_sect == to_right, swap_side_ref[index], other_side_ref[index])
            table = lanes_ref[member, group]
            turn = LANES - 1 if near_even else 1
            entered = pltpu.roll(message, turn, 1)
            corner_index = index if to_down else (index - 3 if to_right else index + 3)
            corner = from_rows(to_down, slice(start + corner_index, start + corner_index + 1))
            edge = 0 if to_down else rows - 1
            paths = corner[:, LANES - 1 :] + message[edge : edge + 1, LANES - 1 :]
            corner = pltpu.roll(jnp.broadcast_to(corner, (SUB, LANES)), turn, 1)[0:1]
            corner = jnp.broadcast_to(paths, (1, LANES)) * corner
            diagonal = shift_rows(wet_near * entered, fore)
            diagonal = jnp.where(row == edge, jnp.broadcast_to(corner, shape), diagonal)
            near = wet_near * (table[0:1] * entered + message + table[2:3] * diagonal)
            far = wet_near * wet_far * (table[1:2] * message)
            change = jnp.where(used, jnp.where(even == near_even, near, far), 0.0)
            columns_ref[group] = change
            total += table[3:4] * change
        total += pltpu.roll(total, LANES - width, 1) + pltpu.roll(total, LANES - 2 * width, 1)
        target = 0 if to_right else LANES - 2
        inside = (lane >= target) & (lane < target + 2)
        for j in range(freqs):
            turned = pltpu.roll(total, (target - 2 * j) % LANES, 1)
            energy += jnp.where(inside, turned, 0.0)
    energy_ref[...] = energy

    for to_down in (True, False):
        near_row, far_row = (0, 1) if to_down else (rows - 1, rows - 2)
        wet_near = wet_cells[near_row : near_row + 1, :]
        wet_both = wet_near * wet_cells[far_row : far_row + 1, :]
        totals = [jnp.zeros((freqs, LANES), jnp.float32) for _ in range(2)]
        for direction in range(ND):
            if heads_down(direction) != to_down:
                continue
            slot = row_slot(direction) * freqs
            entered = from_rows(to_down, slice(slot, slot + freqs))
            follow = from_rows(to_down, slice(18 * freqs + slot, 18 * freqs + slot + freqs))
            table = table_ref.at[member, class_of(direction)]
            side = 1 if heads_right(direction) else -1
            diagonal = shift_lanes(wet_near * entered, side)
            near = wet_near * (table[0] * entered + follow + table[2] * diagonal)
            far = wet_both * (table[1] * entered)
            for place, (change, at) in enumerate(((near, near_row), (far, far_row))):
                edges_ref[edge_rows(freqs, to_down, direction, at % SUB), :] = change
                totals[place] += table[3] * change
        for total, at in zip(totals, (near_row, far_row)):
            energy_ref[at : at + 1, :] += jnp.sum(total, axis=0, keepdims=True)


def entered_kernel(
    freqs, member_ref, lanes_ref, table_ref, ice_ref, east_ref, north_ref, growth_ref, columns_ref,
    edges_ref, a_in, b_in, a_ref, b_ref,
):
    member = member_ref[0]
    shape = ice_ref.shape
    rows = shape[0]
    lane = iota(shape, 1)
    even = lane % 2 == 0
    width = 2 * freqs
    a_ref[...] = a_in[...]
    b_ref[...] = b_in[...]

    for to_right in (True, False):
        near_column, far_column = (0, 1) if to_right else (LANES - 1, LANES - 2)

        def packed_field(values):
            return jnp.where(
                even == to_right, spread(values, near_column), spread(values, far_column)
            )

        east, north = packed_field(east_ref[...]), packed_field(north_ref[...])
        open_water = 0.5 * (1.0 - packed_field(ice_ref[...].astype(jnp.float32)))
        sums = [jnp.zeros(shape, jnp.float32) for _ in range(2)]
        for index in range(GROUPS // 2):
            group = index if to_right else index + GROUPS // 2
            table = lanes_ref[member, group]
            project = table[6:7] * east + table[7:8] * north
            growth = open_water * jnp.square(jnp.maximum(project, 0.0))
            grown = columns_ref[group] * (1.0 + table[5:6] * growth)
            sums[0] += table[3:4] * grown
            sums[1] += table[4:5] * grown
        sums = [
            part + pltpu.roll(part, LANES - width, 1) + pltpu.roll(part, LANES - 2 * width, 1)
            for part in sums
        ]
        target = 0 if to_right else LANES - 2
        inside = (lane >= target) & (lane < target + 2)
        for j in range(freqs):
            turn = (target - 2 * j) % LANES
            block = slice(j * rows, (j + 1) * rows)
            place = [jnp.where(inside, pltpu.roll(part, turn, 1), 0.0) for part in sums]
            a_ref[block, :] += place[0]
            b_ref[block, :] += place[1]

    for to_down in (True, False):
        near_row, far_row = (0, 1) if to_down else (rows - 1, rows - 2)
        totals = [jnp.zeros((freqs, LANES), jnp.float32) for _ in range(4)]
        for direction in range(ND):
            if heads_down(direction) != to_down:
                continue
            table = table_ref.at[member, class_of(direction)]
            square = math.cos(2.0 * math.pi * direction / ND) ** 2
            for place, at in enumerate((near_row, far_row)):
                change = edges_ref[edge_rows(freqs, to_down, direction, at % SUB), :]
                growth = growth_ref[direction, at : at + 1, :]
                grown = (table[3] * change) * (1.0 + table[4] * growth)
                totals[2 * place] += grown
                totals[2 * place + 1] += square * grown
        for place, at in enumerate((near_row, far_row)):
            picked = pl.ds(at, freqs, stride=rows)
            a_ref[picked, :] += totals[2 * place]
            b_ref[picked, :] += totals[2 * place + 1]


def stress_kernel(
    freqs, member_ref, scalar_ref, wet_ref, a_ref, b_ref, own_ref, other_ref, sums_ref, final_ref,
    ratio_ref,
):
    member = member_ref[0]
    wet_cells = wet_ref[...]
    rows = wet_cells.shape[0]
    energy = wet_cells * (own_ref[...] + other_ref[...]) / (ND * NF)
    square = jnp.square(energy)

    sums = [jnp.zeros(wet_cells.shape, jnp.float32) for _ in range(3)]
    for j in range(freqs):
        base = (member * freqs + j) * CLASSES * KINDS
        high, shoal = scalar_ref[base + 3], scalar_ref[base + 4]
        block = slice(j * rows, (j + 1) * rows)
        ratio = wet_cells / (1.0 + (2.0 * high) * square)
        ratio_ref[j] = ratio
        whole = ratio * a_ref[block, :]
        along = ratio * b_ref[block, :]
        sums[0] += shoal * along + (shoal - 0.5) * whole
        sums[1] += (2.0 * shoal - 0.5) * whole - shoal * along
        sums[2] += whole
    for index in range(2):
        sums_ref[index] = sums[index] / (ND * NF)
    final_ref[...] = sums[2] / (ND * NF)


def total_kernel(own_ref, other_ref, sum_ref):
    sum_ref[...] = own_ref[...] + other_ref[...]


def strip_kernel(stress_ref, swapped_ref, other_ref, beside_ref, first_ref, second_ref):
    rows = stress_ref.shape[1]
    low_half = iota((rows, LANES), 1) < LANES // 2
    odd_sect = lax.rem(lax.axis_index("sect"), 2) == 1
    odd_slab = lax.rem(lax.axis_index("slab"), 2) == 1
    for index in range(2):
        swapped, other = swapped_ref[index], other_ref[index]
        beside = jnp.where(low_half != odd_sect, swapped, other)
        beside_ref[index] = beside
        ends = [
            jnp.concatenate([values[first : first + SUB] for values in (stress_ref[index], beside)], 1)
            for first in (0, rows - SUB)
        ]
        first_ref[index] = jnp.where(odd_slab, *ends)
        second_ref[index] = jnp.where(odd_slab, *ends[::-1])


BEHIND = 12
RINGS = 6


def final_kernel(
    freqs, member_ref, scalar_ref, depth_ref, ratios_ref, sums_ref, own_ref, there_ref, beside_ref,
    swapped_ref, other_ref, growth_ref, kept_ref, columns_ref, edges_ref,
    result_ref, level_ref, damping_ref, turning_ref, sems, *rings,
):
    member = member_ref[0]
    rows = depth_ref.shape[0]
    slab, slabs = lax.axis_index("slab"), lax.axis_size("slab")
    sect, sects = lax.axis_index("sect"), lax.axis_size("sect")
    above_ok = jnp.where(slab > 0, 1.0, 0.0)
    below_ok = jnp.where(slab < slabs - 1, 1.0, 0.0)
    left_ok = jnp.where(sect > 0, 1.0, 0.0)
    right_ok = jnp.where(sect < sects - 1, 1.0, 0.0)

    odd = lax.rem(slab, 2) == 1

    def framed(index):
        middle = jnp.concatenate([sums_ref[index], beside_ref[index]], axis=1)
        swapped, other = swapped_ref[index], other_ref[index]
        below = jnp.where(odd, other, swapped)
        above = jnp.where(odd, swapped, other)
        return jnp.concatenate([middle, below, above], axis=0)

    def around(values, axis):
        size = values.shape[axis]
        return pltpu.roll(values, 1, axis) + pltpu.roll(values, size - 1, axis)

    stress_x, stress_y = framed(0), framed(1)
    frame = stress_x.shape
    frame_row, frame_lane = iota(frame, 0), iota(frame, 1)
    row_ok = jnp.where(frame_row < rows, 1.0, jnp.where(frame_row < rows + SUB, below_ok, above_ok))
    lane_ok = jnp.where(
        frame_lane < LANES, 1.0, jnp.where(frame_lane < LANES + LANES // 2, right_ok, left_ok)
    )
    inside = row_ok * lane_ok / 4.5
    source = -((around(stress_x, 0) - 2.0 * stress_x) + (around(stress_y, 1) - 2.0 * stress_y))
    level = inside * source
    for _ in range(JAC):
        level = inside * (source + around(level, 0) + around(level, 1))
    level = level[:rows, :LANES]
    level_ref[...] = level
    final = own_ref[...] + there_ref[...]
    damping = 1.0 / (1.0 + 4.0 * final / (jnp.square(depth_ref[...] + level) + 1.0))
    tiles = rows // SUB
    damping_ref[...] = damping
    turning_ref[...] = columns_ref[...]
    tile_lane = iota((SUB, LANES), 1)

    def send(j, which, piece):
        part = pl.ds(piece * ND // 4, ND // 4)
        return pltpu.make_async_copy(
            rings[which].at[part], result_ref.at[j, part], sems.at[which, piece]
        )

    def frequency(j, which):
        @pl.when(j >= RINGS)
        def _():
            for piece in range(4):
                send(j - RINGS, which, piece).wait()

        base = (member * freqs + j) * CLASSES * KINDS
        high = scalar_ref[base + 3]

        def damped(direction, t, ratio, high_ratio):
            to_down, to_right = sides(direction // (ND // 4))
            part = slice(t * SUB, (t + 1) * SUB)
            target = 0 if to_right > 0 else LANES - 2
            at_side = (tile_lane >= target) & (tile_lane < target + 2)
            turn = (target - direction % GROUP * 2 * freqs) % LANES
            entered = turning_ref[direction // GROUP, part, :]
            if turn:
                entered = pltpu.roll(entered, turn, 1)
            value = kept_ref[j, direction, part, :] + jnp.where(at_side, entered, 0.0)
            if t == (0 if to_down > 0 else tiles - 1):
                edge = ((0 if to_down > 0 else 18) + row_slot(direction)) * freqs + j
                value += edges_ref[pl.ds(pl.multiple_of(edge * SUB, SUB), SUB), :]
            return value * (ratio + high_ratio * growth_ref[direction, part, :])

        pending = []
        for kind in range(CLASSES - 1):
            together = (0, 9, 18, 27) if kind == 0 else (kind, 18 - kind, 18 + kind, 36 - kind)
            scale = scalar_ref[base + kind * KINDS + 2]
            for t in range(tiles):
                part = slice(t * SUB, (t + 1) * SUB)
                ratio = scale * (ratios_ref[j, part, :] * damping_ref[part, :])
                high_ratio = high * ratio
                for direction in together:
                    pending.append((direction, part, damped(direction, t, ratio, high_ratio)))
                while len(pending) > BEHIND:
                    target, place, value = pending.pop(0)
                    rings[which][target, place, :] = value
        for target, place, value in pending:
            rings[which][target, place, :] = value
        for piece in range(4):
            send(j, which, piece).start()
        turned = [pltpu.roll(turning_ref[group], LANES - 2, 1) for group in range(GROUPS)]
        for group in range(GROUPS):
            turning_ref[group] = turned[group]

    def turn(index, carry):
        for which in range(RINGS):
            frequency(RINGS * index + which, which)
        return carry

    whole_turns = freqs // RINGS
    lax.fori_loop(0, whole_turns, turn, 0)
    for j in range(whole_turns * RINGS, freqs):
        frequency(jnp.int32(j), j % RINGS)
    for j in range(max(0, freqs - RINGS), freqs):
        for piece in range(4):
            send(j, j % RINGS, piece).wait()


def swap(values, axis, first):
    count = lax.axis_size(axis)
    pairs = [(i, i + 1) for i in range(first, count - 1, 2)]
    return lax.ppermute(values, axis, pairs + [(b, a) for a, b in pairs])


def others_sum(values, axis):
    count = lax.axis_size(axis)
    total = None
    for step in range(1, count):
        part = lax.ppermute(values, axis, [(i, (i + step) % count) for i in range(count)])
        total = part if total is None else total + part
    return jnp.zeros_like(values) if total is None else total


VMEM = pl.BlockSpec(memory_space=pltpu.VMEM)
SMEM = pl.BlockSpec(memory_space=pltpu.SMEM)
HBM = pl.BlockSpec(memory_space=pltpu.HBM)
ANY = pl.BlockSpec(memory_space=pl.ANY)


def in_vmem(*shape):
    return pltpu.VMEM(shape, jnp.float32)


def in_any(*shape):
    return jax.ShapeDtypeStruct(shape, jnp.float32)


def in_hbm(values):
    return pltpu.with_memory_space_constraint(values, pltpu.HBM)


def call(kernel, in_specs, out_shape, out_specs, flops, moved, scratch=(), aliases=None, limit=6):
    return pl.pallas_call(
        kernel,
        in_specs=in_specs,
        out_shape=out_shape,
        out_specs=out_specs,
        scratch_shapes=list(scratch),
        input_output_aliases=aliases or {},
        cost_estimate=pl.CostEstimate(flops=flops, bytes_accessed=moved, transcendentals=0),
        compiler_params=pltpu.CompilerParams(vmem_limit_bytes=limit << 20),
    )


def resident(spectrum, land_mask, ice_mask, wind_u, wind_v, depth):
    local_comp, rows, lanes = spectrum.shape
    freqs = local_comp // ND
    members = lax.axis_size("comp")
    member = lax.axis_index("comp").astype(jnp.int32).reshape(1)
    scalars, lane_table, row_table = numpy_tables(members, freqs)
    scalars, lane_table, row_table = map(jnp.asarray, (scalars, lane_table, row_table))
    cells = rows * lanes
    row_message = 2 * 18 * freqs + CORNERS
    block = (freqs, ND, rows, lanes)
    spectrum = spectrum.reshape(block)

    growth, wet, swap_side, other_side, swap_row, other_row, edges = call(
        functools.partial(pack_kernel, freqs),
        [SMEM] + [HBM] * 7,
        (
            in_any(ND, rows, lanes),
            in_any(rows, lanes),
            in_any(GROUPS // 2, rows, lanes),
            in_any(GROUPS // 2, rows, lanes),
            in_any(row_message, lanes),
            in_any(row_message, lanes),
            in_any(2 * 18 * freqs * SUB, lanes),
        ),
        (VMEM,) * 7,
        flops=local_comp * cells * 4,
        moved=local_comp * cells * 4,
        scratch=[
            pltpu.VMEM((local_comp * rows, lanes), jnp.float32),
            pltpu.VMEM((GROUPS // 2, rows, lanes), jnp.float32),
            pltpu.VMEM((GROUPS // 2, rows, lanes), jnp.float32),
            pltpu.VMEM(lane_table.shape[1:], jnp.float32),
            pltpu.VMEM(row_table.shape[1:], jnp.float32),
            pltpu.VMEM((rows, lanes), jnp.int32),
            pltpu.VMEM((rows, lanes), jnp.int32),
            pltpu.VMEM((rows, lanes), jnp.float32),
            pltpu.VMEM((rows, lanes), jnp.float32),
            pltpu.SemaphoreType.DMA((6,)),
            pltpu.SemaphoreType.DMA((GROUPS,)),
        ],
        limit=30,
    )(
        member,
        *map(in_hbm, (lane_table, row_table, land_mask, ice_mask, wind_u, wind_v, spectrum)),
    )

    def main_part(start, stop, *before):
        return call(
            functools.partial(main_kernel, freqs, start, stop),
            [SMEM, SMEM, VMEM, VMEM, HBM] + ([ANY, VMEM, VMEM, VMEM, VMEM] if before else []),
            (
                in_vmem(*block),
                in_any(freqs * rows, lanes),
                in_any(freqs * rows, lanes),
                in_any(rows, lanes),
            ),
            (VMEM,) * 4,
            flops=local_comp * cells * 16 * (stop - start) // freqs,
            moved=local_comp * cells * 8 * (stop - start) // freqs,
            scratch=[
                pltpu.VMEM((AHEAD, ND, rows, lanes), jnp.float32),
                pltpu.SemaphoreType.DMA((AHEAD,)),
            ]
            + [pltpu.VMEM((rows + 2 * SUB, lanes), jnp.float32)] * 8,
            aliases={6 + index: index for index in range(4)} if before else {},
            limit=8,
        )(member, scalars, wet, growth, in_hbm(spectrum), *before)

    early = max(1, freqs // 3)
    swap_side, other_side = swap(swap_side, "sect", 0), swap(other_side, "sect", 1)
    kept, *partial = main_part(0, early)
    swap_row, other_row = call(
        functools.partial(corner_kernel, freqs),
        [VMEM, VMEM, VMEM, ANY, ANY, ANY],
        (in_any(row_message, lanes), in_any(row_message, lanes)),
        (ANY, ANY),
        flops=100,
        moved=1 << 15,
        scratch=[pltpu.VMEM((2, CORNERS, lanes), jnp.float32), pltpu.SemaphoreType.DMA((2,))],
        aliases={3: 0, 4: 1},
    )(wet, swap_side, other_side, swap_row, other_row, partial[-1])
    swapped_row = swap(swap_row, "slab", 0)
    other_row = swap(other_row, "slab", 1)
    kept, a_sums, b_sums, energy = main_part(early, freqs, swap_row, kept, *partial)

    columns, edges, energy = call(
        functools.partial(enter_kernel, freqs),
        [SMEM] + [VMEM] * 9,
        (
            in_any(GROUPS, rows, lanes),
            in_any(2 * 18 * freqs * SUB, lanes),
            in_any(rows, lanes),
        ),
        (VMEM,) * 3,
        flops=cells * 600,
        moved=cells * 200,
        aliases={8: 1, 9: 2},
    )(
        member, lane_table, row_table, wet, swap_side, other_side, swapped_row, other_row, edges,
        energy,
    )
    energy_there = others_sum(energy, "comp")
    a_sums, b_sums = call(
        functools.partial(entered_kernel, freqs),
        [SMEM] + [VMEM] * 10,
        (in_any(freqs * rows, lanes), in_any(freqs * rows, lanes)),
        (VMEM,) * 2,
        flops=cells * 600,
        moved=cells * 200,
        aliases={9: 0, 10: 1},
    )(
        member, lane_table, row_table, ice_mask, wind_u, wind_v, growth, columns, edges,
        a_sums, b_sums,
    )

    stress, final, ratios = call(
        functools.partial(stress_kernel, freqs),
        [SMEM, SMEM] + [VMEM] * 5,
        (in_any(2, rows, lanes), in_any(rows, lanes), in_any(freqs, rows, lanes)),
        (VMEM, VMEM, VMEM),
        flops=cells * freqs * 12,
        moved=cells * freqs * 8,
    )(member, scalars, wet, a_sums, b_sums, energy, energy_there)
    stress = call(
        total_kernel,
        [VMEM, VMEM],
        in_any(2, rows, lanes),
        VMEM,
        flops=cells * 2,
        moved=cells * 24,
    )(stress, others_sum(stress, "comp"))
    final_there = others_sum(final, "comp")
    beside, first, second = call(
        strip_kernel,
        [VMEM, VMEM, VMEM],
        (in_any(2, rows, lanes), in_any(2, SUB, 2 * lanes), in_any(2, SUB, 2 * lanes)),
        (VMEM, VMEM, VMEM),
        flops=cells * 4,
        moved=cells * 36,
    )(stress, swap(stress, "sect", 0), swap(stress, "sect", 1))
    aside, beyond = swap(first, "slab", 0), swap(second, "slab", 1)

    result, level = call(
        functools.partial(final_kernel, freqs),
        [SMEM, SMEM] + [VMEM] * 12,
        (in_any(*block), in_any(rows, lanes)),
        (HBM, VMEM),
        flops=local_comp * cells * 6,
        moved=local_comp * cells * 8,
        scratch=[
            pltpu.VMEM((rows, lanes), jnp.float32),
            pltpu.VMEM((GROUPS, rows, lanes), jnp.float32),
            pltpu.SemaphoreType.DMA((RINGS, 4)),
        ]
        + [pltpu.VMEM((ND, rows, lanes), jnp.float32)] * RINGS,
        limit=12,
    )(
        member, scalars, depth, ratios, stress, final, final_there, beside, aside, beyond, growth, kept,
        columns, edges,
    )
    return result.reshape(local_comp, rows, lanes), level


def local(spectrum, *fields):
    local_comp, rows, lanes = spectrum.shape
    whole_rings = local_comp % ND == 0 and GROUP * 2 * (local_comp // ND) < LANES - 1
    if whole_rings and lanes == LANES and rows % SUB == 0:
        return resident(spectrum, *fields)
    return general(spectrum, *fields)


def solution(mesh):
    in_specs = (
        P("comp", "slab", "sect"),
        P("slab", "sect"),
        P("slab", "sect"),
        P("slab", "sect"),
        P("slab", "sect"),
        P("slab", "sect"),
    )
    out_specs = (P("comp", "slab", "sect"), P("slab", "sect"))
    return jax.shard_map(local, mesh=mesh, in_specs=in_specs, out_specs=out_specs, check_vma=False)
```

```python
import functools
import math

import jax
import jax.numpy as jnp
import numpy as np
from jax import lax
from jax.experimental import pallas as pl
from jax.experimental.pallas import tpu as pltpu
from jax.sharding import PartitionSpec as P

ND = 36
NF = 36
STEPS = 2
JAC = 4


def extended(cells, sides, width):
    for axis, dim in sides:
        count = lax.axis_size(axis)
        ends = count - 1
        head = lax.slice_in_dim(cells, 0, width, axis=dim)
        tail = lax.slice_in_dim(cells, cells.shape[dim] - width, cells.shape[dim], axis=dim)
        cells = jnp.concatenate(
            [
                lax.ppermute(tail, axis, [(i, (i + 1) % count) for i in range(ends)]),
                cells,
                lax.ppermute(head, axis, [((i + 1) % count, i) for i in range(ends)]),
            ],
            axis=dim,
        )
    return cells


def tables(index):
    freq_index = (index // ND).astype(jnp.float32)
    angle_index = (index % ND).astype(jnp.float32)
    heading = 2.0 * math.pi * angle_index / ND
    return (
        jnp.cos(heading),
        jnp.sin(heading),
        jnp.power(1.1, -freq_index),
        jnp.power(1.1, freq_index - (NF - 1)),
        0.5 + 0.5 * freq_index / (NF - 1),
    )


def column(values):
    return values[:, None, None]


def advect(spectra, wet_cells, speed_x, speed_y):
    padded = extended(spectra, (("slab", 1), ("sect", 2)), 1)
    upper_rows = padded[:, :-2, 1:-1]
    lower_rows = padded[:, 2:, 1:-1]
    left_cells = padded[:, 1:-1, :-2]
    right_cells = padded[:, 1:-1, 2:]
    change = (
        jnp.maximum(speed_x, 0.0) * (spectra - upper_rows)
        + jnp.minimum(speed_x, 0.0) * (lower_rows - spectra)
        + jnp.maximum(speed_y, 0.0) * (spectra - left_cells)
        + jnp.minimum(speed_y, 0.0) * (right_cells - spectra)
    )
    return (spectra - change) * wet_cells


def forcing(spectra, energy, wind_east, wind_north, ice_cover, cosine, sine, high_ratio):
    project = cosine * wind_east + sine * wind_north
    growth = 0.5 * high_ratio * jnp.square(jnp.maximum(project, 0.0)) * (1.0 - ice_cover)
    return spectra * (1.0 + growth) / (1.0 + 2.0 * high_ratio * jnp.square(energy))


def stress_weights(cosine, sine, shoaling):
    return jnp.stack(
        [shoaling * (cosine * cosine + 1.0) - 0.5, shoaling * (sine * sine + 1.0) - 0.5]
    )


def surge_solve(stress):
    padded = extended(stress, (("slab", 1), ("sect", 2)), 1)
    source_term = -(
        padded[0, 2:, 1:-1]
        + padded[0, :-2, 1:-1]
        - 2.0 * stress[0]
        + (padded[1, 1:-1, 2:] + padded[1, 1:-1, :-2] - 2.0 * stress[1])
    )
    surge_level = source_term / 4.5
    for _ in range(JAC):
        neighbours = extended(surge_level, (("slab", 0), ("sect", 1)), 1)
        surge_level = (
            source_term
            + neighbours[2:, 1:-1]
            + neighbours[:-2, 1:-1]
            + neighbours[1:-1, 2:]
            + neighbours[1:-1, :-2]
        ) / 4.5
    return surge_level


def general(spectrum, land_mask, ice_mask, wind_u, wind_v, depth):
    groups = lax.axis_size("comp")
    member = lax.axis_index("comp")
    local_comp, block_rows, block_cols = spectrum.shape
    point_rows = block_rows // groups
    total_comp = ND * NF
    wet_cells = (1 - land_mask).astype(jnp.float32)
    ice_cover = ice_mask.astype(jnp.float32)

    def own_rows(values):
        return lax.dynamic_slice_in_dim(values, member * point_rows, point_rows, values.ndim - 2)

    own_index = member * local_comp + jnp.arange(local_comp, dtype=jnp.int32)
    cosine, sine, low_ratio, high_ratio, shoaling = tables(own_index)
    spectra = spectrum * wet_cells
    for _ in range(STEPS):
        spectra = advect(
            spectra, wet_cells, column(0.7 * low_ratio * cosine), column(0.7 * low_ratio * sine)
        )
    points = lax.all_to_all(spectra, "comp", split_axis=1, concat_axis=0, tiled=True)
    cosine_full, sine_full, _, high_full, shoal_full = tables(
        jnp.arange(total_comp, dtype=jnp.int32)
    )
    energy = jnp.sum(points, axis=0) / total_comp
    sourced = forcing(
        points,
        energy,
        own_rows(wind_u),
        own_rows(wind_v),
        own_rows(ice_cover),
        column(cosine_full),
        column(sine_full),
        column(high_full),
    )
    stress = (
        jnp.einsum(
            "sk,krc->src",
            stress_weights(cosine_full, sine_full, shoal_full),
            sourced,
            precision=lax.Precision.HIGHEST,
        )
        / total_comp
    )
    stress_block = lax.all_gather(stress, "comp", axis=1, tiled=True)
    level_block = surge_solve(stress_block)
    final_energy = jnp.sum(sourced, axis=0) / total_comp
    damped = sourced / (
        1.0 + 4.0 * final_energy / (jnp.square(own_rows(depth) + own_rows(level_block)) + 1.0)
    )
    result = lax.all_to_all(damped, "comp", split_axis=0, concat_axis=1, tiled=True)
    return (result, level_block)


LANES = 128
SUB = 8
CLASSES = 10
KINDS = 5
GROUP = 3
GROUPS = ND // GROUP
CORNERS = 8


def class_of(direction):
    folded = direction % 18
    return folded if folded <= 9 else 18 - folded


def heads_down(direction):
    return direction < 9 or direction >= 27


def heads_right(direction):
    return direction < 18


def row_slot(direction):
    if direction < 9:
        return direction
    return direction - 18 if direction >= 27 else direction - 9


def numpy_tables(members, freqs):
    j = np.arange(members * freqs, dtype=np.float64)
    heading = 2.0 * np.pi * np.arange(ND) / ND
    cosine, sine = np.cos(heading), np.sin(heading)
    low = 1.1 ** (-j)
    high = 1.1 ** (j - (NF - 1))
    shoal = 0.5 + 0.5 * j / (NF - 1)
    step_x = 0.7 * low[:, None] * np.abs(cosine)
    step_y = 0.7 * low[:, None] * np.abs(sine)
    keep = 1.0 - step_x - step_y
    alpha, beta, scale = step_x / keep, step_y / keep, keep * keep
    classes = np.arange(CLASSES)
    square = np.broadcast_to(cosine * cosine, alpha.shape)
    scalars = np.stack(
        [
            alpha[:, classes],
            beta[:, classes],
            scale[:, classes],
            np.broadcast_to(high[:, None], (j.size, CLASSES)),
            np.broadcast_to(shoal[:, None], (j.size, CLASSES)),
        ],
        axis=-1,
    ).astype(np.float32)

    kinds = np.stack(
        [
            2.0 * beta,
            beta * beta,
            alpha * beta,
            scale,
            scale * square,
            np.broadcast_to(high[:, None], alpha.shape),
            np.broadcast_to(cosine, alpha.shape),
            np.broadcast_to(sine, alpha.shape),
        ]
    )
    lanes = np.zeros((members, GROUPS, 8, LANES), np.float32)
    packed = kinds.reshape(8, members, freqs, GROUPS, GROUP)
    packed = np.repeat(packed.transpose(1, 3, 0, 4, 2), 2, axis=-1)
    lanes[..., : GROUP * 2 * freqs] = packed.reshape(members, GROUPS, 8, -1)

    rows = np.stack(
        [2.0 * alpha, alpha * alpha, alpha * beta, scale, np.broadcast_to(high[:, None], alpha.shape)]
    )[:, :, classes]
    rows = rows.reshape(5, members, freqs, CLASSES).transpose(1, 3, 0, 2)
    rows = np.broadcast_to(rows[..., None], rows.shape + (LANES,)).astype(np.float32)
    return scalars.reshape(-1), lanes, rows


def odd_position(axis):
    return lax.rem(lax.axis_index(axis), 2) == 1


def iota(shape, axis):
    return lax.broadcasted_iota(jnp.int32, shape, axis)


def spread(values, column):
    return jnp.broadcast_to(values[:, column : column + 1], values.shape)


def shift_rows(values, step):
    rows = values.shape[0]
    edge = 0 if step > 0 else rows - 1
    moved = pltpu.roll(values, step % rows, 0)
    return jnp.where(iota(values.shape, 0) == edge, 0.0, moved)


def shift_lanes(values, step):
    lanes = values.shape[1]
    edge = 0 if step > 0 else lanes - 1
    moved = pltpu.roll(values, step % lanes, 1)
    return jnp.where(iota(values.shape, 1) == edge, 0.0, moved)


DEPTH = 2


def sides(quadrant):
    return 1 if quadrant in (0, 3) else -1, 1 if quadrant in (0, 1) else -1


def pack_kernel(
    freqs, member_ref, lanes_hbm, table_hbm, land_hbm, ice_hbm, east_hbm, north_hbm, spectrum_ref,
    kept_ref, growth_ref, wet_ref, swap_side_ref, other_side_ref, swap_row_ref, other_row_ref,
    edges_ref, ring_ref, right_ref, left_ref, lanes_ref, table_ref, land_ref, ice_ref, east_ref, north_ref, small_sems, sems,
):
    member = member_ref[0]
    small = [
        pltpu.make_async_copy(source, target, small_sems.at[index])
        for index, (source, target) in enumerate(
            (
                (land_hbm, land_ref),
                (ice_hbm, ice_ref),
                (east_hbm, east_ref),
                (north_hbm, north_ref),
                (lanes_hbm.at[member], lanes_ref),
                (table_hbm.at[member], table_ref),
            )
        )
    ]
    for copy in small:
        copy.start()

    rows = land_ref.shape[0]
    flat_ref = kept_ref.reshape(freqs * ND * rows, LANES)

    def fetch(group):
        slot = lax.rem(group, DEPTH + 1)
        part = (slice(None), pl.ds(group * GROUP, GROUP))
        return pltpu.make_async_copy(spectrum_ref.at[part], ring_ref.at[slot], sems.at[slot])

    for group in range(DEPTH):
        fetch(jnp.int32(group)).start()
    edges_ref[...] = jnp.zeros_like(edges_ref)
    for copy in small:
        copy.wait()

    wet_cells = (1 - land_ref[...]).astype(jnp.float32)
    wet_ref[...] = wet_cells
    open_water = 0.5 * (1.0 - ice_ref[...].astype(jnp.float32))
    shape = wet_cells.shape
    tiles = rows // SUB
    for direction in range(ND):
        angle = 2.0 * math.pi * direction / ND
        project = math.cos(angle) * east_ref[...] + math.sin(angle) * north_ref[...]
        growth_ref[direction] = open_water * jnp.square(jnp.maximum(project, 0.0))

    lane = iota(shape, 1)
    even = lane % 2 == 0
    tile_lane = iota((SUB, LANES), 1)
    for row_ref in (swap_row_ref, other_row_ref):
        row_ref[pl.ds(2 * 18 * freqs, CORNERS), :] = jnp.zeros((CORNERS, LANES), jnp.float32)
    odd_sect, odd_slab = odd_position("sect"), odd_position("slab")

    half = GROUPS // 2

    def gather_all(to_right):
        target_ref = right_ref if to_right else left_ref

        def gather(index, carry):
            group = index + (0 if to_right else half)
            fetch(group).wait()

            @pl.when(group + DEPTH < GROUPS)
            def _():
                fetch(group + DEPTH).start()

            slot = lax.rem(group, DEPTH + 1)
            packed = [jnp.zeros((SUB, LANES), jnp.float32) for _ in range(tiles)]
            wet = [wet_ref[tile * SUB : (tile + 1) * SUB, :] for tile in range(tiles)]
            pending = []

            def put(count):
                while len(pending) > count:
                    at, cells = pending.pop(0)
                    flat_ref[pl.ds(at, SUB), :] = cells

            for i in range(GROUP):
                for j in range(freqs):
                    place = i * 2 * freqs + 2 * j
                    here = (tile_lane >= place) & (tile_lane < place + 2)
                    turn = (place + 2 if to_right else place) % LANES
                    first = pl.multiple_of((j * ND + group * GROUP + i) * rows, SUB)
                    for tile in range(tiles):
                        cells = ring_ref[slot, j, i, tile * SUB : (tile + 1) * SUB, :] * wet[tile]
                        packed[tile] = jnp.where(here, pltpu.roll(cells, turn, 1), packed[tile])
                        pending.append((first + tile * SUB, cells))
                    put(2 * tiles)
            put(0)
            for tile in range(tiles):
                target_ref[index, tile * SUB : (tile + 1) * SUB, :] = packed[tile]
            return carry

        lax.fori_loop(0, half, gather, 0)

    def side_message(group):
        to_right, fore = group < half, 1 if heads_down(group * GROUP) else -1
        wet_near = spread(wet_cells, LANES - 1 if to_right else 0)
        near_even = not to_right
        values = right_ref[group] if to_right else left_ref[group - half]
        near = pltpu.roll(values, 1 if near_even else LANES - 1, 1)
        table = lanes_ref[group]
        follow = wet_near * (table[1:2] * values + table[2:3] * shift_rows(near, fore))
        message = jnp.where(even == near_even, values, follow)
        return jnp.where(lane == LANES - 1, wet_near, message)

    def row_message(direction):
        to_down = heads_down(direction)
        near_row, far_row = (rows - 1, rows - 2) if to_down else (0, 1)
        wet_near = wet_cells[near_row : near_row + 1, :]
        table = table_ref.at[class_of(direction)]
        near = flat_ref[pl.ds(direction * rows + near_row, freqs, stride=ND * rows), :]
        far = flat_ref[pl.ds(direction * rows + far_row, freqs, stride=ND * rows), :]
        beside = shift_lanes(near, 1 if heads_right(direction) else -1)
        return near, wet_near * (table[1] * far + table[2] * beside)

    def row_messages(slots):
        for slot in slots:
            pairs = zip(row_message(by_slot[True, slot]), row_message(by_slot[False, slot]))
            for which, (down, up) in enumerate(pairs):
                first = (which * 18 + slot) * freqs
                swap_row_ref[first : first + freqs, :] = jnp.where(odd_slab, up, down)
                other_row_ref[first : first + freqs, :] = jnp.where(odd_slab, down, up)

    by_slot = {(heads_down(d), row_slot(d)): d for d in range(ND)}
    gather_all(True)
    rights = [side_message(index) for index in range(half)]
    for index in range(half):
        right_ref[index] = rights[index]
    row_messages(range(9))
    gather_all(False)
    for index in range(half):
        right, left = right_ref[index], side_message(index + half)
        swap_side_ref[index] = jnp.where(odd_sect, left, right)
        other_side_ref[index] = jnp.where(odd_sect, right, left)
    row_messages(range(9, 18))


def corner_kernel(
    freqs, wet_ref, swapped_ref, other_ref, swap_in, other_in, _after, swap_row_ref, other_row_ref,
    rows_ref, sems,
):
    rows = wet_ref.shape[0]
    odd_sect, odd_slab = odd_position("sect"), odd_position("slab")
    last = iota((1, LANES), 1) == LANES - 1
    rows_ref[...] = jnp.zeros_like(rows_ref)
    for i in range(6):
        from_left = i < 3
        column = 0 if from_left else LANES - 1
        ends = []
        for row, index in ((rows - 1, i), (0, i + 3 if from_left else i - 3)):
            swapped = swapped_ref[index, row : row + 1, :]
            other = other_ref[index, row : row + 1, :]
            came = jnp.where(odd_sect == from_left, swapped, other)
            own = jnp.broadcast_to(wet_ref[row : row + 1, column : column + 1], (1, LANES))
            ends.append(jnp.where(last, own, came))
        rows_ref[0, i : i + 1, :] = jnp.where(odd_slab, *ends[::-1])
        rows_ref[1, i : i + 1, :] = jnp.where(odd_slab, *ends)
    start = 2 * 18 * freqs
    copies = [
        pltpu.make_async_copy(
            rows_ref.at[which], ref.at[pl.ds(start, CORNERS), :], sems.at[which]
        )
        for which, ref in ((0, swap_row_ref), (1, other_row_ref))
    ]
    for copy in copies:
        copy.start()
    for copy in copies:
        copy.wait()


AHEAD = 3


def main_kernel(
    freqs, start, stop, member_ref, scalar_ref, wet_ref, growth_ref, masked_ref, *refs
):
    if start:
        _after, a_in, b_in, energy_in, *refs = refs
    kept_ref, a_ref, b_ref, energy_ref, ring_ref, sems, *first_refs = refs
    member = member_ref[0]
    nought = jnp.minimum(member, 0)
    rows = wet_ref.shape[0]
    tiles = rows // SUB

    def fetch(j):
        slot = lax.rem(j, AHEAD)
        return pltpu.make_async_copy(masked_ref.at[j], ring_ref.at[slot], sems.at[slot])

    for j in range(start, min(start + AHEAD, stop)):
        fetch(jnp.int32(j)).start()

    lane = iota((SUB, LANES), 1)
    sub = iota((SUB, LANES), 0)
    not_first = jnp.where(lane == 0, 0.0, 1.0)
    not_last = jnp.where(lane == LANES - 1, 0.0, 1.0)
    top, bottom = sub == 0, sub == SUB - 1
    energy_ref[...] = energy_in[...] if start else jnp.zeros_like(energy_ref)
    for first_ref in first_refs:
        first_ref[...] = jnp.zeros_like(first_ref)

    def tile_at(tile):
        return pl.ds(tile * SUB, SUB)

    def row_shift(quadrant):
        return -1 if quadrant in (0, 3) else 1

    def parts_of(kind):
        if kind == 0:
            return ((0, 0, 0), (9, 1, 9), (18, 2, 0), (27, 3, 9))
        return ((kind, 0, kind), (18 - kind, 1, kind), (18 + kind, 2, kind), (36 - kind, 3, kind))

    def frequency(j, carry):
        fetch(j).wait()
        slot = lax.rem(j, AHEAD)
        base = (member * freqs + j) * CLASSES * KINDS
        at = [pl.ds(pl.multiple_of(j * rows, SUB) + t * SUB, SUB) for t in range(tiles)]

        def speeds(part):
            at_class = base + part[2] * KINDS
            beta = scalar_ref[at_class + 1]
            return scalar_ref[at_class], beta * (not_first if part[1] in (0, 1) else not_last)

        def beside(cells, quadrant):
            return pltpu.roll(cells, 1 if quadrant in (0, 1) else LANES - 1, 1)

        def first_step(kind):
            parts = parts_of(kind)
            speed = [speeds(part) for part in parts]
            wet = [wet_ref[tile_at(t), :] for t in range(tiles)]
            for (direction, quadrant, _), (alpha, across) in zip(parts, speed):
                shift = row_shift(quadrant)
                edge = top if shift < 0 else bottom
                target = first_refs[kind % 2 * 4 + quadrant]
                for t in range(tiles):
                    cells = ring_ref[slot, direction, tile_at(t), :]
                    if 0 <= t * SUB + shift <= rows - SUB:
                        ahead = ring_ref[slot, direction, pl.ds(t * SUB + shift + nought, SUB), :]
                    else:
                        ahead = jnp.where(edge, 0.0, pltpu.roll(cells, -shift % SUB, 0))
                    after = cells + alpha * ahead + across * beside(cells, quadrant)
                    target[tile_at(t + 1), :] = wet[t] * after

        def second_step(kind):
            parts = parts_of(kind)
            scale, high = scalar_ref[base + kind * KINDS + 2], scalar_ref[base + 3]
            scaled_high = scale * high
            speed = [speeds(part) for part in parts]
            for t in range(tiles):
                moved, grown = [], []
                for (direction, quadrant, _), (alpha, across) in zip(parts, speed):
                    source = first_refs[kind % 2 * 4 + quadrant]
                    cells = source[tile_at(t + 1), :]
                    ahead = source[pl.ds((t + 1) * SUB + row_shift(quadrant) + nought, SUB), :]
                    after = cells + alpha * ahead + across * beside(cells, quadrant)
                    kept_ref[j, direction, tile_at(t), :] = after
                    moved.append(after)
                    grown.append(growth_ref[direction, tile_at(t), :] * after)
                if kind == 0:
                    plain_x, plain_y = scale * (moved[0] + moved[2]), scale * (moved[1] + moved[3])
                    grown_x = plain_x + scaled_high * (grown[0] + grown[2])
                    grown_y = plain_y + scaled_high * (grown[1] + grown[3])
                    square = math.cos(0.5 * math.pi) ** 2
                    energy_ref[tile_at(t), :] += plain_x + plain_y
                    a_ref[at[t], :] = grown_x + grown_y
                    b_ref[at[t], :] = grown_x + square * grown_y
                else:
                    plain = scale * ((moved[0] + moved[1]) + (moved[2] + moved[3]))
                    whole = plain + scaled_high * ((grown[0] + grown[1]) + (grown[2] + grown[3]))
                    square = math.cos(2.0 * math.pi * kind / ND) ** 2
                    energy_ref[tile_at(t), :] += plain
                    a_ref[at[t], :] += whole
                    b_ref[at[t], :] += square * whole

        first_step(0)
        for kind in range(CLASSES - 1):
            if kind + 1 < CLASSES - 1:
                first_step(kind + 1)
            second_step(kind)

        @pl.when(j + AHEAD < stop)
        def _():
            fetch(j + AHEAD).start()

        return carry

    lax.fori_loop(start, stop, frequency, 0)


def edge_rows(freqs, to_down, direction, at):
    first = ((0 if to_down else 18) + row_slot(direction)) * freqs * SUB
    return pl.ds(first + at, freqs, stride=SUB)


def enter_kernel(
    freqs, member_ref, lanes_ref, table_ref, wet_ref, swap_side_ref, other_side_ref, swap_row_ref,
    other_row_ref, _edges_in, energy_in, columns_ref, edges_ref, energy_ref,
):
    member = member_ref[0]
    wet_cells = wet_ref[...]
    shape = wet_cells.shape
    rows = shape[0]
    lane = iota(shape, 1)
    row = iota(shape, 0)
    even = lane % 2 == 0
    width = 2 * freqs
    used = lane < GROUP * width
    energy = energy_in[...]
    start = 2 * 18 * freqs
    odd_sect, odd_slab = odd_position("sect"), odd_position("slab")

    def from_rows(to_down, part):
        return jnp.where(odd_slab == to_down, swap_row_ref[part, :], other_row_ref[part, :])

    for to_right in (True, False):
        near_column, far_column = (0, 1) if to_right else (LANES - 1, LANES - 2)
        near_even = to_right
        wet_near, wet_far = spread(wet_cells, near_column), spread(wet_cells, far_column)
        total = jnp.zeros(shape, jnp.float32)
        for index in range(GROUPS // 2):
            group = index if to_right else index + GROUPS // 2
            to_down = heads_down(group * GROUP)
            fore = 1 if to_down else -1
            message = jnp.where(odd_sect == to_right, swap_side_ref[index], other_side_ref[index])
            table = lanes_ref[member, group]
            turn = LANES - 1 if near_even else 1
            entered = pltpu.roll(message, turn, 1)
            corner_index = index if to_down else (index - 3 if to_right else index + 3)
            corner = from_rows(to_down, slice(start + corner_index, start + corner_index + 1))
            edge = 0 if to_down else rows - 1
            paths = corner[:, LANES - 1 :] + message[edge : edge + 1, LANES - 1 :]
            corner = pltpu.roll(jnp.broadcast_to(corner, (SUB, LANES)), turn, 1)[0:1]
            corner = jnp.broadcast_to(paths, (1, LANES)) * corner
            diagonal = shift_rows(wet_near * entered, fore)
            diagonal = jnp.where(row == edge, jnp.broadcast_to(corner, shape), diagonal)
            near = wet_near * (table[0:1] * entered + message + table[2:3] * diagonal)
            far = wet_near * wet_far * (table[1:2] * message)
            change = jnp.where(used, jnp.where(even == near_even, near, far), 0.0)
            columns_ref[group] = change
            total += table[3:4] * change
        total += pltpu.roll(total, LANES - width, 1) + pltpu.roll(total, LANES - 2 * width, 1)
        target = 0 if to_right else LANES - 2
        inside = (lane >= target) & (lane < target + 2)
        for j in range(freqs):
            turned = pltpu.roll(total, (target - 2 * j) % LANES, 1)
            energy += jnp.where(inside, turned, 0.0)
    energy_ref[...] = energy

    for to_down in (True, False):
        near_row, far_row = (0, 1) if to_down else (rows - 1, rows - 2)
        wet_near = wet_cells[near_row : near_row + 1, :]
        wet_both = wet_near * wet_cells[far_row : far_row + 1, :]
        totals = [jnp.zeros((freqs, LANES), jnp.float32) for _ in range(2)]
        for direction in range(ND):
            if heads_down(direction) != to_down:
                continue
            slot = row_slot(direction) * freqs
            entered = from_rows(to_down, slice(slot, slot + freqs))
            follow = from_rows(to_down, slice(18 * freqs + slot, 18 * freqs + slot + freqs))
            table = table_ref.at[member, class_of(direction)]
            side = 1 if heads_right(direction) else -1
            diagonal = shift_lanes(wet_near * entered, side)
            near = wet_near * (table[0] * entered + follow + table[2] * diagonal)
            far = wet_both * (table[1] * entered)
            for place, (change, at) in enumerate(((near, near_row), (far, far_row))):
                edges_ref[edge_rows(freqs, to_down, direction, at % SUB), :] = change
                totals[place] += table[3] * change
        for total, at in zip(totals, (near_row, far_row)):
            energy_ref[at : at + 1, :] += jnp.sum(total, axis=0, keepdims=True)


def entered_kernel(
    freqs, member_ref, lanes_ref, table_ref, ice_ref, east_ref, north_ref, growth_ref, columns_ref,
    edges_ref, a_in, b_in, a_ref, b_ref,
):
    member = member_ref[0]
    shape = ice_ref.shape
    rows = shape[0]
    lane = iota(shape, 1)
    even = lane % 2 == 0
    width = 2 * freqs
    a_ref[...] = a_in[...]
    b_ref[...] = b_in[...]

    for to_right in (True, False):
        near_column, far_column = (0, 1) if to_right else (LANES - 1, LANES - 2)

        def packed_field(values):
            return jnp.where(
                even == to_right, spread(values, near_column), spread(values, far_column)
            )

        east, north = packed_field(east_ref[...]), packed_field(north_ref[...])
        open_water = 0.5 * (1.0 - packed_field(ice_ref[...].astype(jnp.float32)))
        sums = [jnp.zeros(shape, jnp.float32) for _ in range(2)]
        for index in range(GROUPS // 2):
            group = index if to_right else index + GROUPS // 2
            table = lanes_ref[member, group]
            project = table[6:7] * east + table[7:8] * north
            growth = open_water * jnp.square(jnp.maximum(project, 0.0))
            grown = columns_ref[group] * (1.0 + table[5:6] * growth)
            sums[0] += table[3:4] * grown
            sums[1] += table[4:5] * grown
        sums = [
            part + pltpu.roll(part, LANES - width, 1) + pltpu.roll(part, LANES - 2 * width, 1)
            for part in sums
        ]
        target = 0 if to_right else LANES - 2
        inside = (lane >= target) & (lane < target + 2)
        for j in range(freqs):
            turn = (target - 2 * j) % LANES
            block = slice(j * rows, (j + 1) * rows)
            place = [jnp.where(inside, pltpu.roll(part, turn, 1), 0.0) for part in sums]
            a_ref[block, :] += place[0]
            b_ref[block, :] += place[1]

    for to_down in (True, False):
        near_row, far_row = (0, 1) if to_down else (rows - 1, rows - 2)
        totals = [jnp.zeros((freqs, LANES), jnp.float32) for _ in range(4)]
        for direction in range(ND):
            if heads_down(direction) != to_down:
                continue
            table = table_ref.at[member, class_of(direction)]
            square = math.cos(2.0 * math.pi * direction / ND) ** 2
            for place, at in enumerate((near_row, far_row)):
                change = edges_ref[edge_rows(freqs, to_down, direction, at % SUB), :]
                growth = growth_ref[direction, at : at + 1, :]
                grown = (table[3] * change) * (1.0 + table[4] * growth)
                totals[2 * place] += grown
                totals[2 * place + 1] += square * grown
        for place, at in enumerate((near_row, far_row)):
            picked = pl.ds(at, freqs, stride=rows)
            a_ref[picked, :] += totals[2 * place]
            b_ref[picked, :] += totals[2 * place + 1]


def stress_kernel(
    freqs, member_ref, scalar_ref, wet_ref, a_ref, b_ref, own_ref, other_ref, sums_ref, ratio_ref
):
    member = member_ref[0]
    wet_cells = wet_ref[...]
    rows = wet_cells.shape[0]
    energy = wet_cells * (own_ref[...] + other_ref[...]) / (ND * NF)
    square = jnp.square(energy)

    sums = [jnp.zeros(wet_cells.shape, jnp.float32) for _ in range(3)]
    for j in range(freqs):
        base = (member * freqs + j) * CLASSES * KINDS
        high, shoal = scalar_ref[base + 3], scalar_ref[base + 4]
        block = slice(j * rows, (j + 1) * rows)
        ratio = wet_cells / (1.0 + (2.0 * high) * square)
        ratio_ref[j] = ratio
        whole = ratio * a_ref[block, :]
        along = ratio * b_ref[block, :]
        sums[0] += shoal * along + (shoal - 0.5) * whole
        sums[1] += (2.0 * shoal - 0.5) * whole - shoal * along
        sums[2] += whole
    for index in range(3):
        sums_ref[index] = sums[index] / (ND * NF)


def total_kernel(own_ref, other_ref, sums_ref, stress_ref):
    sums_ref[...] = own_ref[...] + other_ref[...]
    stress_ref[...] = sums_ref[0:2]


def strip_kernel(stress_ref, swapped_ref, other_ref, beside_ref, first_ref, second_ref):
    rows = stress_ref.shape[1]
    low_half = iota((rows, LANES), 1) < LANES // 2
    odd_sect = lax.rem(lax.axis_index("sect"), 2) == 1
    odd_slab = lax.rem(lax.axis_index("slab"), 2) == 1
    for index in range(2):
        swapped, other = swapped_ref[index], other_ref[index]
        beside = jnp.where(low_half != odd_sect, swapped, other)
        beside_ref[index] = beside
        ends = [
            jnp.concatenate([values[first : first + SUB] for values in (stress_ref[index], beside)], 1)
            for first in (0, rows - SUB)
        ]
        first_ref[index] = jnp.where(odd_slab, *ends)
        second_ref[index] = jnp.where(odd_slab, *ends[::-1])


BEHIND = 12
RINGS = 6


def final_kernel(
    freqs, member_ref, scalar_ref, depth_ref, ratios_ref, sums_ref, beside_ref, swapped_ref,
    other_ref, growth_ref, kept_ref, columns_ref, edges_ref,
    result_ref, level_ref, damping_ref, turning_ref, sems, *rings,
):
    member = member_ref[0]
    rows = depth_ref.shape[0]
    slab, slabs = lax.axis_index("slab"), lax.axis_size("slab")
    sect, sects = lax.axis_index("sect"), lax.axis_size("sect")
    above_ok = jnp.where(slab > 0, 1.0, 0.0)
    below_ok = jnp.where(slab < slabs - 1, 1.0, 0.0)
    left_ok = jnp.where(sect > 0, 1.0, 0.0)
    right_ok = jnp.where(sect < sects - 1, 1.0, 0.0)

    odd = lax.rem(slab, 2) == 1

    def framed(index):
        middle = jnp.concatenate([sums_ref[index], beside_ref[index]], axis=1)
        swapped, other = swapped_ref[index], other_ref[index]
        below = jnp.where(odd, other, swapped)
        above = jnp.where(odd, swapped, other)
        return jnp.concatenate([middle, below, above], axis=0)

    def around(values, axis):
        size = values.shape[axis]
        return pltpu.roll(values, 1, axis) + pltpu.roll(values, size - 1, axis)

    stress_x, stress_y = framed(0), framed(1)
    frame = stress_x.shape
    frame_row, frame_lane = iota(frame, 0), iota(frame, 1)
    row_ok = jnp.where(frame_row < rows, 1.0, jnp.where(frame_row < rows + SUB, below_ok, above_ok))
    lane_ok = jnp.where(
        frame_lane < LANES, 1.0, jnp.where(frame_lane < LANES + LANES // 2, right_ok, left_ok)
    )
    inside = row_ok * lane_ok / 4.5
    source = -((around(stress_x, 0) - 2.0 * stress_x) + (around(stress_y, 1) - 2.0 * stress_y))
    level = inside * source
    for _ in range(JAC):
        level = inside * (source + around(level, 0) + around(level, 1))
    level = level[:rows, :LANES]
    level_ref[...] = level
    damping = 1.0 / (1.0 + 4.0 * sums_ref[2] / (jnp.square(depth_ref[...] + level) + 1.0))
    tiles = rows // SUB
    damping_ref[...] = damping
    turning_ref[...] = columns_ref[...]
    tile_lane = iota((SUB, LANES), 1)

    def send(j, which, piece):
        part = pl.ds(piece * ND // 4, ND // 4)
        return pltpu.make_async_copy(
            rings[which].at[part], result_ref.at[j, part], sems.at[which, piece]
        )

    def frequency(j, which):
        @pl.when(j >= RINGS)
        def _():
            for piece in range(4):
                send(j - RINGS, which, piece).wait()

        base = (member * freqs + j) * CLASSES * KINDS
        high = scalar_ref[base + 3]

        def damped(direction, t, ratio, high_ratio):
            to_down, to_right = sides(direction // (ND // 4))
            part = slice(t * SUB, (t + 1) * SUB)
            target = 0 if to_right > 0 else LANES - 2
            at_side = (tile_lane >= target) & (tile_lane < target + 2)
            turn = (target - direction % GROUP * 2 * freqs) % LANES
            entered = turning_ref[direction // GROUP, part, :]
            if turn:
                entered = pltpu.roll(entered, turn, 1)
            value = kept_ref[j, direction, part, :] + jnp.where(at_side, entered, 0.0)
            if t == (0 if to_down > 0 else tiles - 1):
                edge = ((0 if to_down > 0 else 18) + row_slot(direction)) * freqs + j
                value += edges_ref[pl.ds(pl.multiple_of(edge * SUB, SUB), SUB), :]
            return value * (ratio + high_ratio * growth_ref[direction, part, :])

        pending = []
        for kind in range(CLASSES - 1):
            together = (0, 9, 18, 27) if kind == 0 else (kind, 18 - kind, 18 + kind, 36 - kind)
            scale = scalar_ref[base + kind * KINDS + 2]
            for t in range(tiles):
                part = slice(t * SUB, (t + 1) * SUB)
                ratio = scale * (ratios_ref[j, part, :] * damping_ref[part, :])
                high_ratio = high * ratio
                for direction in together:
                    pending.append((direction, part, damped(direction, t, ratio, high_ratio)))
                while len(pending) > BEHIND:
                    target, place, value = pending.pop(0)
                    rings[which][target, place, :] = value
        for target, place, value in pending:
            rings[which][target, place, :] = value
        for piece in range(4):
            send(j, which, piece).start()
        turned = [pltpu.roll(turning_ref[group], LANES - 2, 1) for group in range(GROUPS)]
        for group in range(GROUPS):
            turning_ref[group] = turned[group]

    def turn(index, carry):
        for which in range(RINGS):
            frequency(RINGS * index + which, which)
        return carry

    whole_turns = freqs // RINGS
    lax.fori_loop(0, whole_turns, turn, 0)
    for j in range(whole_turns * RINGS, freqs):
        frequency(jnp.int32(j), j % RINGS)
    for j in range(max(0, freqs - RINGS), freqs):
        for piece in range(4):
            send(j, j % RINGS, piece).wait()


def swap(values, axis, first):
    count = lax.axis_size(axis)
    pairs = [(i, i + 1) for i in range(first, count - 1, 2)]
    return lax.ppermute(values, axis, pairs + [(b, a) for a, b in pairs])


def others_sum(values, axis):
    count = lax.axis_size(axis)
    total = None
    for step in range(1, count):
        part = lax.ppermute(values, axis, [(i, (i + step) % count) for i in range(count)])
        total = part if total is None else total + part
    return jnp.zeros_like(values) if total is None else total


VMEM = pl.BlockSpec(memory_space=pltpu.VMEM)
SMEM = pl.BlockSpec(memory_space=pltpu.SMEM)
HBM = pl.BlockSpec(memory_space=pltpu.HBM)
ANY = pl.BlockSpec(memory_space=pl.ANY)


def in_vmem(*shape):
    return pltpu.VMEM(shape, jnp.float32)


def in_any(*shape):
    return jax.ShapeDtypeStruct(shape, jnp.float32)


def in_hbm(values):
    return pltpu.with_memory_space_constraint(values, pltpu.HBM)


def call(kernel, in_specs, out_shape, out_specs, flops, moved, scratch=(), aliases=None, limit=6):
    return pl.pallas_call(
        kernel,
        in_specs=in_specs,
        out_shape=out_shape,
        out_specs=out_specs,
        scratch_shapes=list(scratch),
        input_output_aliases=aliases or {},
        cost_estimate=pl.CostEstimate(flops=flops, bytes_accessed=moved, transcendentals=0),
        compiler_params=pltpu.CompilerParams(vmem_limit_bytes=limit << 20),
    )


def resident(spectrum, land_mask, ice_mask, wind_u, wind_v, depth):
    local_comp, rows, lanes = spectrum.shape
    freqs = local_comp // ND
    members = lax.axis_size("comp")
    member = lax.axis_index("comp").astype(jnp.int32).reshape(1)
    scalars, lane_table, row_table = numpy_tables(members, freqs)
    scalars, lane_table, row_table = map(jnp.asarray, (scalars, lane_table, row_table))
    cells = rows * lanes
    row_message = 2 * 18 * freqs + CORNERS
    block = (freqs, ND, rows, lanes)
    spectrum = spectrum.reshape(block)

    kept, growth, wet, swap_side, other_side, swap_row, other_row, edges = call(
        functools.partial(pack_kernel, freqs),
        [SMEM] + [HBM] * 7,
        (
            in_vmem(*block),
            in_any(ND, rows, lanes),
            in_any(rows, lanes),
            in_any(GROUPS // 2, rows, lanes),
            in_any(GROUPS // 2, rows, lanes),
            in_any(row_message, lanes),
            in_any(row_message, lanes),
            in_any(2 * 18 * freqs * SUB, lanes),
        ),
        (VMEM,) * 8,
        flops=local_comp * cells * 4,
        moved=local_comp * cells * 4,
        scratch=[
            pltpu.VMEM((DEPTH + 1, freqs, GROUP, rows, lanes), jnp.float32),
            pltpu.VMEM((GROUPS // 2, rows, lanes), jnp.float32),
            pltpu.VMEM((GROUPS // 2, rows, lanes), jnp.float32),
            pltpu.VMEM(lane_table.shape[1:], jnp.float32),
            pltpu.VMEM(row_table.shape[1:], jnp.float32),
            pltpu.VMEM((rows, lanes), jnp.int32),
            pltpu.VMEM((rows, lanes), jnp.int32),
            pltpu.VMEM((rows, lanes), jnp.float32),
            pltpu.VMEM((rows, lanes), jnp.float32),
            pltpu.SemaphoreType.DMA((6,)),
            pltpu.SemaphoreType.DMA((DEPTH + 1,)),
        ],
        limit=10,
    )(
        member,
        *map(in_hbm, (lane_table, row_table, land_mask, ice_mask, wind_u, wind_v, spectrum)),
    )

    def main_part(start, stop, masked, *before):
        return call(
            functools.partial(main_kernel, freqs, start, stop),
            [SMEM, SMEM, VMEM, VMEM, ANY] + ([ANY, VMEM, VMEM, VMEM] if before else []),
            (
                in_vmem(*block),
                in_any(freqs * rows, lanes),
                in_any(freqs * rows, lanes),
                in_any(rows, lanes),
            ),
            (VMEM,) * 4,
            flops=local_comp * cells * 16 * (stop - start) // freqs,
            moved=local_comp * cells * 8 * (stop - start) // freqs,
            scratch=[
                pltpu.VMEM((AHEAD, ND, rows, lanes), jnp.float32),
                pltpu.SemaphoreType.DMA((AHEAD,)),
            ]
            + [pltpu.VMEM((rows + 2 * SUB, lanes), jnp.float32)] * 8,
            aliases={4: 0, **({6 + index: 1 + index for index in range(3)} if before else {})},
            limit=8,
        )(member, scalars, wet, growth, masked, *before)

    early = max(1, freqs // 3)
    swap_side, other_side = swap(swap_side, "sect", 0), swap(other_side, "sect", 1)
    kept, *partial = main_part(0, early, kept)
    swap_row, other_row = call(
        functools.partial(corner_kernel, freqs),
        [VMEM, VMEM, VMEM, ANY, ANY, ANY],
        (in_any(row_message, lanes), in_any(row_message, lanes)),
        (ANY, ANY),
        flops=100,
        moved=1 << 15,
        scratch=[pltpu.VMEM((2, CORNERS, lanes), jnp.float32), pltpu.SemaphoreType.DMA((2,))],
        aliases={3: 0, 4: 1},
    )(wet, swap_side, other_side, swap_row, other_row, partial[-1])
    swapped_row = swap(swap_row, "slab", 0)
    other_row = swap(other_row, "slab", 1)
    kept, a_sums, b_sums, energy = main_part(early, freqs, kept, swap_row, *partial)

    columns, edges, energy = call(
        functools.partial(enter_kernel, freqs),
        [SMEM] + [VMEM] * 9,
        (
            in_any(GROUPS, rows, lanes),
            in_any(2 * 18 * freqs * SUB, lanes),
            in_any(rows, lanes),
        ),
        (VMEM,) * 3,
        flops=cells * 600,
        moved=cells * 200,
        aliases={8: 1, 9: 2},
    )(
        member, lane_table, row_table, wet, swap_side, other_side, swapped_row, other_row, edges,
        energy,
    )
    energy_there = others_sum(energy, "comp")
    a_sums, b_sums = call(
        functools.partial(entered_kernel, freqs),
        [SMEM] + [VMEM] * 10,
        (in_any(freqs * rows, lanes), in_any(freqs * rows, lanes)),
        (VMEM,) * 2,
        flops=cells * 600,
        moved=cells * 200,
        aliases={9: 0, 10: 1},
    )(
        member, lane_table, row_table, ice_mask, wind_u, wind_v, growth, columns, edges,
        a_sums, b_sums,
    )

    sums, ratios = call(
        functools.partial(stress_kernel, freqs),
        [SMEM, SMEM] + [VMEM] * 5,
        (in_any(3, rows, lanes), in_any(freqs, rows, lanes)),
        (VMEM, VMEM),
        flops=cells * freqs * 12,
        moved=cells * freqs * 8,
    )(member, scalars, wet, a_sums, b_sums, energy, energy_there)
    sums, stress = call(
        total_kernel,
        [VMEM, VMEM],
        (in_any(3, rows, lanes), in_any(2, rows, lanes)),
        (VMEM, VMEM),
        flops=cells * 3,
        moved=cells * 44,
    )(sums, others_sum(sums, "comp"))
    beside, first, second = call(
        strip_kernel,
        [VMEM, VMEM, VMEM],
        (in_any(2, rows, lanes), in_any(2, SUB, 2 * lanes), in_any(2, SUB, 2 * lanes)),
        (VMEM, VMEM, VMEM),
        flops=cells * 4,
        moved=cells * 36,
    )(stress, swap(stress, "sect", 0), swap(stress, "sect", 1))
    aside, beyond = swap(first, "slab", 0), swap(second, "slab", 1)

    result, level = call(
        functools.partial(final_kernel, freqs),
        [SMEM, SMEM] + [VMEM] * 10,
        (in_any(*block), in_any(rows, lanes)),
        (HBM, VMEM),
        flops=local_comp * cells * 6,
        moved=local_comp * cells * 8,
        scratch=[
            pltpu.VMEM((rows, lanes), jnp.float32),
            pltpu.VMEM((GROUPS, rows, lanes), jnp.float32),
            pltpu.SemaphoreType.DMA((RINGS, 4)),
        ]
        + [pltpu.VMEM((ND, rows, lanes), jnp.float32)] * RINGS,
        limit=12,
    )(
        member, scalars, depth, ratios, sums, beside, aside, beyond, growth, kept,
        columns, edges,
    )
    return result.reshape(local_comp, rows, lanes), level


def local(spectrum, *fields):
    local_comp, rows, lanes = spectrum.shape
    whole_rings = local_comp % ND == 0 and GROUP * 2 * (local_comp // ND) < LANES - 1
    if whole_rings and lanes == LANES and rows % SUB == 0:
        return resident(spectrum, *fields)
    return general(spectrum, *fields)


def solution(mesh):
    in_specs = (
        P("comp", "slab", "sect"),
        P("slab", "sect"),
        P("slab", "sect"),
        P("slab", "sect"),
        P("slab", "sect"),
        P("slab", "sect"),
    )
    out_specs = (P("comp", "slab", "sect"), P("slab", "sect"))
    return jax.shard_map(local, mesh=mesh, in_specs=in_specs, out_specs=out_specs, check_vma=False)
```

```python
import functools
import math

import jax
import jax.numpy as jnp
import numpy as np
from jax import lax
from jax.experimental import pallas as pl
from jax.experimental.pallas import tpu as pltpu
from jax.sharding import PartitionSpec as P

ND = 36
NF = 36
STEPS = 2
JAC = 4


def extended(cells, sides, width):
    for axis, dim in sides:
        count = lax.axis_size(axis)
        ends = count - 1
        head = lax.slice_in_dim(cells, 0, width, axis=dim)
        tail = lax.slice_in_dim(cells, cells.shape[dim] - width, cells.shape[dim], axis=dim)
        cells = jnp.concatenate(
            [
                lax.ppermute(tail, axis, [(i, (i + 1) % count) for i in range(ends)]),
                cells,
                lax.ppermute(head, axis, [((i + 1) % count, i) for i in range(ends)]),
            ],
            axis=dim,
        )
    return cells


def tables(index):
    freq_index = (index // ND).astype(jnp.float32)
    angle_index = (index % ND).astype(jnp.float32)
    heading = 2.0 * math.pi * angle_index / ND
    return (
        jnp.cos(heading),
        jnp.sin(heading),
        jnp.power(1.1, -freq_index),
        jnp.power(1.1, freq_index - (NF - 1)),
        0.5 + 0.5 * freq_index / (NF - 1),
    )


def column(values):
    return values[:, None, None]


def advect(spectra, wet_cells, speed_x, speed_y):
    padded = extended(spectra, (("slab", 1), ("sect", 2)), 1)
    upper_rows = padded[:, :-2, 1:-1]
    lower_rows = padded[:, 2:, 1:-1]
    left_cells = padded[:, 1:-1, :-2]
    right_cells = padded[:, 1:-1, 2:]
    change = (
        jnp.maximum(speed_x, 0.0) * (spectra - upper_rows)
        + jnp.minimum(speed_x, 0.0) * (lower_rows - spectra)
        + jnp.maximum(speed_y, 0.0) * (spectra - left_cells)
        + jnp.minimum(speed_y, 0.0) * (right_cells - spectra)
    )
    return (spectra - change) * wet_cells


def forcing(spectra, energy, wind_east, wind_north, ice_cover, cosine, sine, high_ratio):
    project = cosine * wind_east + sine * wind_north
    growth = 0.5 * high_ratio * jnp.square(jnp.maximum(project, 0.0)) * (1.0 - ice_cover)
    return spectra * (1.0 + growth) / (1.0 + 2.0 * high_ratio * jnp.square(energy))


def stress_weights(cosine, sine, shoaling):
    return jnp.stack(
        [shoaling * (cosine * cosine + 1.0) - 0.5, shoaling * (sine * sine + 1.0) - 0.5]
    )


def surge_solve(stress):
    padded = extended(stress, (("slab", 1), ("sect", 2)), 1)
    source_term = -(
        padded[0, 2:, 1:-1]
        + padded[0, :-2, 1:-1]
        - 2.0 * stress[0]
        + (padded[1, 1:-1, 2:] + padded[1, 1:-1, :-2] - 2.0 * stress[1])
    )
    surge_level = source_term / 4.5
    for _ in range(JAC):
        neighbours = extended(surge_level, (("slab", 0), ("sect", 1)), 1)
        surge_level = (
            source_term
            + neighbours[2:, 1:-1]
            + neighbours[:-2, 1:-1]
            + neighbours[1:-1, 2:]
            + neighbours[1:-1, :-2]
        ) / 4.5
    return surge_level


def general(spectrum, land_mask, ice_mask, wind_u, wind_v, depth):
    groups = lax.axis_size("comp")
    member = lax.axis_index("comp")
    local_comp, block_rows, block_cols = spectrum.shape
    point_rows = block_rows // groups
    total_comp = ND * NF
    wet_cells = (1 - land_mask).astype(jnp.float32)
    ice_cover = ice_mask.astype(jnp.float32)

    def own_rows(values):
        return lax.dynamic_slice_in_dim(values, member * point_rows, point_rows, values.ndim - 2)

    own_index = member * local_comp + jnp.arange(local_comp, dtype=jnp.int32)
    cosine, sine, low_ratio, high_ratio, shoaling = tables(own_index)
    spectra = spectrum * wet_cells
    for _ in range(STEPS):
        spectra = advect(
            spectra, wet_cells, column(0.7 * low_ratio * cosine), column(0.7 * low_ratio * sine)
        )
    points = lax.all_to_all(spectra, "comp", split_axis=1, concat_axis=0, tiled=True)
    cosine_full, sine_full, _, high_full, shoal_full = tables(
        jnp.arange(total_comp, dtype=jnp.int32)
    )
    energy = jnp.sum(points, axis=0) / total_comp
    sourced = forcing(
        points,
        energy,
        own_rows(wind_u),
        own_rows(wind_v),
        own_rows(ice_cover),
        column(cosine_full),
        column(sine_full),
        column(high_full),
    )
    stress = (
        jnp.einsum(
            "sk,krc->src",
            stress_weights(cosine_full, sine_full, shoal_full),
            sourced,
            precision=lax.Precision.HIGHEST,
        )
        / total_comp
    )
    stress_block = lax.all_gather(stress, "comp", axis=1, tiled=True)
    level_block = surge_solve(stress_block)
    final_energy = jnp.sum(sourced, axis=0) / total_comp
    damped = sourced / (
        1.0 + 4.0 * final_energy / (jnp.square(own_rows(depth) + own_rows(level_block)) + 1.0)
    )
    result = lax.all_to_all(damped, "comp", split_axis=0, concat_axis=1, tiled=True)
    return (result, level_block)


LANES = 128
SUB = 8
CLASSES = 10
KINDS = 5
GROUP = 3
GROUPS = ND // GROUP
CORNERS = 8


def class_of(direction):
    folded = direction % 18
    return folded if folded <= 9 else 18 - folded


def heads_down(direction):
    return direction < 9 or direction >= 27


def heads_right(direction):
    return direction < 18


def row_slot(direction):
    if direction < 9:
        return direction
    return direction - 18 if direction >= 27 else direction - 9


def numpy_tables(members, freqs):
    j = np.arange(members * freqs, dtype=np.float64)
    heading = 2.0 * np.pi * np.arange(ND) / ND
    cosine, sine = np.cos(heading), np.sin(heading)
    low = 1.1 ** (-j)
    high = 1.1 ** (j - (NF - 1))
    shoal = 0.5 + 0.5 * j / (NF - 1)
    step_x = 0.7 * low[:, None] * np.abs(cosine)
    step_y = 0.7 * low[:, None] * np.abs(sine)
    keep = 1.0 - step_x - step_y
    alpha, beta, scale = step_x / keep, step_y / keep, keep * keep
    classes = np.arange(CLASSES)
    square = np.broadcast_to(cosine * cosine, alpha.shape)
    scalars = np.stack(
        [
            alpha[:, classes],
            beta[:, classes],
            scale[:, classes],
            np.broadcast_to(high[:, None], (j.size, CLASSES)),
            np.broadcast_to(shoal[:, None], (j.size, CLASSES)),
        ],
        axis=-1,
    ).astype(np.float32)

    kinds = np.stack(
        [
            2.0 * beta,
            beta * beta,
            alpha * beta,
            scale,
            scale * square,
            np.broadcast_to(high[:, None], alpha.shape),
            np.broadcast_to(cosine, alpha.shape),
            np.broadcast_to(sine, alpha.shape),
        ]
    )
    lanes = np.zeros((members, GROUPS, 8, LANES), np.float32)
    packed = kinds.reshape(8, members, freqs, GROUPS, GROUP)
    packed = np.repeat(packed.transpose(1, 3, 0, 4, 2), 2, axis=-1)
    lanes[..., : GROUP * 2 * freqs] = packed.reshape(members, GROUPS, 8, -1)

    rows = np.stack(
        [2.0 * alpha, alpha * alpha, alpha * beta, scale, np.broadcast_to(high[:, None], alpha.shape)]
    )[:, :, classes]
    rows = rows.reshape(5, members, freqs, CLASSES).transpose(1, 3, 0, 2)
    rows = np.broadcast_to(rows[..., None], rows.shape + (LANES,)).astype(np.float32)
    return scalars.reshape(-1), lanes, rows


def odd_position(axis):
    return lax.rem(lax.axis_index(axis), 2) == 1


def iota(shape, axis):
    return lax.broadcasted_iota(jnp.int32, shape, axis)


def spread(values, column):
    return jnp.broadcast_to(values[:, column : column + 1], values.shape)


def shift_rows(values, step):
    rows = values.shape[0]
    edge = 0 if step > 0 else rows - 1
    moved = pltpu.roll(values, step % rows, 0)
    return jnp.where(iota(values.shape, 0) == edge, 0.0, moved)


def shift_lanes(values, step):
    lanes = values.shape[1]
    edge = 0 if step > 0 else lanes - 1
    moved = pltpu.roll(values, step % lanes, 1)
    return jnp.where(iota(values.shape, 1) == edge, 0.0, moved)


DEPTH = 2


def sides(quadrant):
    return 1 if quadrant in (0, 3) else -1, 1 if quadrant in (0, 1) else -1


def pack_kernel(
    freqs, member_ref, lanes_hbm, table_hbm, land_hbm, ice_hbm, east_hbm, north_hbm, spectrum_ref,
    growth_ref, wet_ref, swap_side_ref, other_side_ref, swap_row_ref, other_row_ref, edges_ref,
    kept_ref, right_ref, left_ref, lanes_ref, table_ref, land_ref, ice_ref, east_ref, north_ref, small_sems, sems,
):
    member = member_ref[0]
    small = [
        pltpu.make_async_copy(source, target, small_sems.at[index])
        for index, (source, target) in enumerate(
            (
                (land_hbm, land_ref),
                (ice_hbm, ice_ref),
                (east_hbm, east_ref),
                (north_hbm, north_ref),
                (lanes_hbm.at[member], lanes_ref),
                (table_hbm.at[member], table_ref),
            )
        )
    ]
    for copy in small:
        copy.start()

    rows = land_ref.shape[0]
    blocks_ref = kept_ref.reshape(freqs, ND, rows, LANES)

    def fetch(group):
        part = (slice(None), pl.ds(group * GROUP, GROUP))
        return pltpu.make_async_copy(spectrum_ref.at[part], blocks_ref.at[part], sems.at[group])

    fetch(0).start()
    edges_ref[...] = jnp.zeros_like(edges_ref)
    for copy in small:
        copy.wait()

    wet_cells = (1 - land_ref[...]).astype(jnp.float32)
    wet_ref[...] = wet_cells
    open_water = 0.5 * (1.0 - ice_ref[...].astype(jnp.float32))
    shape = wet_cells.shape
    tiles = rows // SUB
    for direction in range(ND):
        angle = 2.0 * math.pi * direction / ND
        project = math.cos(angle) * east_ref[...] + math.sin(angle) * north_ref[...]
        growth_ref[direction] = open_water * jnp.square(jnp.maximum(project, 0.0))

    for group in range(1, DEPTH):
        fetch(group).start()
    lane = iota(shape, 1)
    even = lane % 2 == 0
    tile_lane = iota((SUB, LANES), 1)
    for row_ref in (swap_row_ref, other_row_ref):
        row_ref[pl.ds(2 * 18 * freqs, CORNERS), :] = jnp.zeros((CORNERS, LANES), jnp.float32)
    odd_sect, odd_slab = odd_position("sect"), odd_position("slab")

    half = GROUPS // 2

    def gather_all(to_right):
        target_ref = right_ref if to_right else left_ref

        def gather(index, carry):
            group = index + (0 if to_right else half)
            fetch(group).wait()

            @pl.when(group + DEPTH < GROUPS)
            def _():
                fetch(group + DEPTH).start()

            packed = [jnp.zeros((SUB, LANES), jnp.float32) for _ in range(tiles)]
            for i in range(GROUP):
                for j in range(freqs):
                    place = i * 2 * freqs + 2 * j
                    here = (tile_lane >= place) & (tile_lane < place + 2)
                    turn = (place + 2 if to_right else place) % LANES
                    first = pl.multiple_of((j * ND + group * GROUP + i) * rows, SUB)
                    for tile in range(tiles):
                        cells = kept_ref[pl.ds(first + tile * SUB, SUB), :]
                        packed[tile] = jnp.where(here, pltpu.roll(cells, turn, 1), packed[tile])
            for tile in range(tiles):
                target_ref[index, tile * SUB : (tile + 1) * SUB, :] = packed[tile]
            return carry

        lax.fori_loop(0, half, gather, 0)

    def side_message(group):
        to_right, fore = group < half, 1 if heads_down(group * GROUP) else -1
        ahead, behind = (LANES - 1, LANES - 2) if to_right else (0, 1)
        wet_near, wet_far = spread(wet_cells, ahead), spread(wet_cells, behind)
        near_even = not to_right
        packed = right_ref[group] if to_right else left_ref[group - half]
        values = packed * jnp.where(even == near_even, wet_near, wet_far)
        near = pltpu.roll(values, 1 if near_even else LANES - 1, 1)
        table = lanes_ref[group]
        follow = wet_near * (table[1:2] * values + table[2:3] * shift_rows(near, fore))
        message = jnp.where(even == near_even, values, follow)
        return jnp.where(lane == LANES - 1, wet_near, message)

    def row_message(direction):
        to_down = heads_down(direction)
        near_row, far_row = (rows - 1, rows - 2) if to_down else (0, 1)
        wet_near = wet_cells[near_row : near_row + 1, :]
        wet_far = wet_cells[far_row : far_row + 1, :]
        table = table_ref.at[class_of(direction)]
        near = kept_ref[pl.ds(direction * rows + near_row, freqs, stride=ND * rows), :] * wet_near
        far = kept_ref[pl.ds(direction * rows + far_row, freqs, stride=ND * rows), :] * wet_far
        beside = shift_lanes(near, 1 if heads_right(direction) else -1)
        return near, wet_near * (table[1] * far + table[2] * beside)

    def row_messages(slots):
        for slot in slots:
            pairs = zip(row_message(by_slot[True, slot]), row_message(by_slot[False, slot]))
            for which, (down, up) in enumerate(pairs):
                first = (which * 18 + slot) * freqs
                swap_row_ref[first : first + freqs, :] = jnp.where(odd_slab, up, down)
                other_row_ref[first : first + freqs, :] = jnp.where(odd_slab, down, up)

    by_slot = {(heads_down(d), row_slot(d)): d for d in range(ND)}
    gather_all(True)
    rights = [side_message(index) for index in range(half)]
    for index in range(half):
        right_ref[index] = rights[index]
    row_messages(range(9))
    gather_all(False)
    for index in range(half):
        right, left = right_ref[index], side_message(index + half)
        swap_side_ref[index] = jnp.where(odd_sect, left, right)
        other_side_ref[index] = jnp.where(odd_sect, right, left)
    row_messages(range(9, 18))


def corner_kernel(
    freqs, wet_ref, swapped_ref, other_ref, swap_in, other_in, _after, swap_row_ref, other_row_ref,
    rows_ref, sems,
):
    rows = wet_ref.shape[0]
    odd_sect, odd_slab = odd_position("sect"), odd_position("slab")
    last = iota((1, LANES), 1) == LANES - 1
    rows_ref[...] = jnp.zeros_like(rows_ref)
    for i in range(6):
        from_left = i < 3
        column = 0 if from_left else LANES - 1
        ends = []
        for row, index in ((rows - 1, i), (0, i + 3 if from_left else i - 3)):
            swapped = swapped_ref[index, row : row + 1, :]
            other = other_ref[index, row : row + 1, :]
            came = jnp.where(odd_sect == from_left, swapped, other)
            own = jnp.broadcast_to(wet_ref[row : row + 1, column : column + 1], (1, LANES))
            ends.append(jnp.where(last, own, came))
        rows_ref[0, i : i + 1, :] = jnp.where(odd_slab, *ends[::-1])
        rows_ref[1, i : i + 1, :] = jnp.where(odd_slab, *ends)
    start = 2 * 18 * freqs
    copies = [
        pltpu.make_async_copy(
            rows_ref.at[which], ref.at[pl.ds(start, CORNERS), :], sems.at[which]
        )
        for which, ref in ((0, swap_row_ref), (1, other_row_ref))
    ]
    for copy in copies:
        copy.start()
    for copy in copies:
        copy.wait()


AHEAD = 3


def main_kernel(
    freqs, start, stop, member_ref, scalar_ref, wet_ref, growth_ref, spectrum_ref, *refs
):
    if start:
        _after, _kept_in, a_in, b_in, energy_in, *refs = refs
    kept_ref, a_ref, b_ref, energy_ref, ring_ref, sems, *first_refs = refs
    member = member_ref[0]
    nought = jnp.minimum(member, 0)
    rows = wet_ref.shape[0]
    tiles = rows // SUB

    def fetch(j):
        slot = lax.rem(j, AHEAD)
        return pltpu.make_async_copy(spectrum_ref.at[j], ring_ref.at[slot], sems.at[slot])

    fetch(jnp.int32(start)).start()

    lane = iota((SUB, LANES), 1)
    sub = iota((SUB, LANES), 0)
    not_first = jnp.where(lane == 0, 0.0, 1.0)
    not_last = jnp.where(lane == LANES - 1, 0.0, 1.0)
    top, bottom = sub == 0, sub == SUB - 1
    energy_ref[...] = energy_in[...] if start else jnp.zeros_like(energy_ref)
    for first_ref in first_refs:
        first_ref[...] = jnp.zeros_like(first_ref)

    def tile_at(tile):
        return pl.ds(tile * SUB, SUB)

    def row_shift(quadrant):
        return -1 if quadrant in (0, 3) else 1

    def parts_of(kind):
        if kind == 0:
            return ((0, 0, 0), (9, 1, 9), (18, 2, 0), (27, 3, 9))
        return ((kind, 0, kind), (18 - kind, 1, kind), (18 + kind, 2, kind), (36 - kind, 3, kind))

    def frequency(j, carry):
        fetch(j).wait()

        @pl.when(j == start)
        def _():
            for later in range(start + 1, min(start + AHEAD, stop)):
                fetch(jnp.int32(later)).start()

        slot = lax.rem(j, AHEAD)
        sums = [[None] * tiles for _ in range(3)]

        def add(which, t, value):
            have = sums[which][t]
            sums[which][t] = value if have is None else have + value
        base = (member * freqs + j) * CLASSES * KINDS
        at = [pl.ds(pl.multiple_of(j * rows, SUB) + t * SUB, SUB) for t in range(tiles)]

        def speeds(part):
            at_class = base + part[2] * KINDS
            beta = scalar_ref[at_class + 1]
            return scalar_ref[at_class], beta * (not_first if part[1] in (0, 1) else not_last)

        def beside(cells, quadrant):
            return pltpu.roll(cells, 1 if quadrant in (0, 1) else LANES - 1, 1)

        def first_step(kind):
            parts = parts_of(kind)
            speed = [speeds(part) for part in parts]
            wet = [wet_ref[tile_at(t), :] for t in range(tiles)]
            for (direction, quadrant, _), (alpha, across) in zip(parts, speed):
                shift = row_shift(quadrant)
                edge = top if shift < 0 else bottom
                target = first_refs[kind % 2 * 4 + quadrant]
                cells = [ring_ref[slot, direction, tile_at(t), :] * wet[t] for t in range(tiles)]
                turned = [pltpu.roll(cells[t], -shift % SUB, 0) for t in range(tiles)]
                for t in range(tiles):
                    before = turned[t + shift] if 0 <= t + shift < tiles else 0.0
                    ahead = jnp.where(edge, before, turned[t])
                    after = cells[t] + alpha * ahead + across * beside(cells[t], quadrant)
                    target[tile_at(t + 1), :] = wet[t] * after

        def second_step(kind):
            parts = parts_of(kind)
            scale, high = scalar_ref[base + kind * KINDS + 2], scalar_ref[base + 3]
            scaled_high = scale * high
            speed = [speeds(part) for part in parts]
            for t in range(tiles):
                moved, grown = [], []
                for (direction, quadrant, _), (alpha, across) in zip(parts, speed):
                    source = first_refs[kind % 2 * 4 + quadrant]
                    cells = source[tile_at(t + 1), :]
                    ahead = source[pl.ds((t + 1) * SUB + row_shift(quadrant) + nought, SUB), :]
                    after = cells + alpha * ahead + across * beside(cells, quadrant)
                    kept_ref[j, direction, tile_at(t), :] = after
                    moved.append(after)
                    grown.append(growth_ref[direction, tile_at(t), :] * after)
                if kind == 0:
                    plain_x, plain_y = scale * (moved[0] + moved[2]), scale * (moved[1] + moved[3])
                    grown_x = plain_x + scaled_high * (grown[0] + grown[2])
                    grown_y = plain_y + scaled_high * (grown[1] + grown[3])
                    square = math.cos(0.5 * math.pi) ** 2
                    add(0, t, plain_x + plain_y)
                    add(1, t, grown_x + grown_y)
                    add(2, t, grown_x + square * grown_y)
                else:
                    plain = scale * ((moved[0] + moved[1]) + (moved[2] + moved[3]))
                    whole = plain + scaled_high * ((grown[0] + grown[1]) + (grown[2] + grown[3]))
                    square = math.cos(2.0 * math.pi * kind / ND) ** 2
                    add(0, t, plain)
                    add(1, t, whole)
                    add(2, t, square * whole)

        first_step(0)
        for kind in range(CLASSES - 1):
            if kind + 1 < CLASSES - 1:
                first_step(kind + 1)
            second_step(kind)
        for t in range(tiles):
            energy_ref[tile_at(t), :] += sums[0][t]
            a_ref[at[t], :] = sums[1][t]
            b_ref[at[t], :] = sums[2][t]

        @pl.when(j + AHEAD < stop)
        def _():
            fetch(j + AHEAD).start()

        return carry

    lax.fori_loop(start, stop, frequency, 0)


def edge_rows(freqs, to_down, direction, at):
    first = ((0 if to_down else 18) + row_slot(direction)) * freqs * SUB
    return pl.ds(first + at, freqs, stride=SUB)


def enter_kernel(
    freqs, member_ref, lanes_ref, table_ref, wet_ref, swap_side_ref, other_side_ref, swap_row_ref,
    other_row_ref, _edges_in, energy_in, columns_ref, edges_ref, energy_ref,
):
    member = member_ref[0]
    wet_cells = wet_ref[...]
    shape = wet_cells.shape
    rows = shape[0]
    lane = iota(shape, 1)
    row = iota(shape, 0)
    even = lane % 2 == 0
    width = 2 * freqs
    used = lane < GROUP * width
    energy = energy_in[...]
    start = 2 * 18 * freqs
    odd_sect, odd_slab = odd_position("sect"), odd_position("slab")

    def from_rows(to_down, part):
        return jnp.where(odd_slab == to_down, swap_row_ref[part, :], other_row_ref[part, :])

    for to_right in (True, False):
        near_column, far_column = (0, 1) if to_right else (LANES - 1, LANES - 2)
        near_even = to_right
        wet_near, wet_far = spread(wet_cells, near_column), spread(wet_cells, far_column)
        total = jnp.zeros(shape, jnp.float32)
        for index in range(GROUPS // 2):
            group = index if to_right else index + GROUPS // 2
            to_down = heads_down(group * GROUP)
            fore = 1 if to_down else -1
            message = jnp.where(odd_sect == to_right, swap_side_ref[index], other_side_ref[index])
            table = lanes_ref[member, group]
            turn = LANES - 1 if near_even else 1
            entered = pltpu.roll(message, turn, 1)
            corner_index = index if to_down else (index - 3 if to_right else index + 3)
            corner = from_rows(to_down, slice(start + corner_index, start + corner_index + 1))
            edge = 0 if to_down else rows - 1
            paths = corner[:, LANES - 1 :] + message[edge : edge + 1, LANES - 1 :]
            corner = pltpu.roll(jnp.broadcast_to(corner, (SUB, LANES)), turn, 1)[0:1]
            corner = jnp.broadcast_to(paths, (1, LANES)) * corner
            diagonal = shift_rows(wet_near * entered, fore)
            diagonal = jnp.where(row == edge, jnp.broadcast_to(corner, shape), diagonal)
            near = wet_near * (table[0:1] * entered + message + table[2:3] * diagonal)
            far = wet_near * wet_far * (table[1:2] * message)
            change = jnp.where(used, jnp.where(even == near_even, near, far), 0.0)
            columns_ref[group] = change
            total += table[3:4] * change
        total += pltpu.roll(total, LANES - width, 1) + pltpu.roll(total, LANES - 2 * width, 1)
        target = 0 if to_right else LANES - 2
        inside = (lane >= target) & (lane < target + 2)
        for j in range(freqs):
            turned = pltpu.roll(total, (target - 2 * j) % LANES, 1)
            energy += jnp.where(inside, turned, 0.0)
    energy_ref[...] = energy

    for to_down in (True, False):
        near_row, far_row = (0, 1) if to_down else (rows - 1, rows - 2)
        wet_near = wet_cells[near_row : near_row + 1, :]
        wet_both = wet_near * wet_cells[far_row : far_row + 1, :]
        totals = [jnp.zeros((freqs, LANES), jnp.float32) for _ in range(2)]
        for direction in range(ND):
            if heads_down(direction) != to_down:
                continue
            slot = row_slot(direction) * freqs
            entered = from_rows(to_down, slice(slot, slot + freqs))
            follow = from_rows(to_down, slice(18 * freqs + slot, 18 * freqs + slot + freqs))
            table = table_ref.at[member, class_of(direction)]
            side = 1 if heads_right(direction) else -1
            diagonal = shift_lanes(wet_near * entered, side)
            near = wet_near * (table[0] * entered + follow + table[2] * diagonal)
            far = wet_both * (table[1] * entered)
            for place, (change, at) in enumerate(((near, near_row), (far, far_row))):
                edges_ref[edge_rows(freqs, to_down, direction, at % SUB), :] = change
                totals[place] += table[3] * change
        for total, at in zip(totals, (near_row, far_row)):
            energy_ref[at : at + 1, :] += jnp.sum(total, axis=0, keepdims=True)


def entered_kernel(
    freqs, member_ref, lanes_ref, table_ref, ice_ref, east_ref, north_ref, growth_ref, columns_ref,
    edges_ref, a_in, b_in, a_ref, b_ref,
):
    member = member_ref[0]
    shape = ice_ref.shape
    rows = shape[0]
    lane = iota(shape, 1)
    even = lane % 2 == 0
    width = 2 * freqs
    a_ref[...] = a_in[...]
    b_ref[...] = b_in[...]

    for to_right in (True, False):
        near_column, far_column = (0, 1) if to_right else (LANES - 1, LANES - 2)

        def packed_field(values):
            return jnp.where(
                even == to_right, spread(values, near_column), spread(values, far_column)
            )

        east, north = packed_field(east_ref[...]), packed_field(north_ref[...])
        open_water = 0.5 * (1.0 - packed_field(ice_ref[...].astype(jnp.float32)))
        sums = [jnp.zeros(shape, jnp.float32) for _ in range(2)]
        for index in range(GROUPS // 2):
            group = index if to_right else index + GROUPS // 2
            table = lanes_ref[member, group]
            project = table[6:7] * east + table[7:8] * north
            growth = open_water * jnp.square(jnp.maximum(project, 0.0))
            grown = columns_ref[group] * (1.0 + table[5:6] * growth)
            sums[0] += table[3:4] * grown
            sums[1] += table[4:5] * grown
        sums = [
            part + pltpu.roll(part, LANES - width, 1) + pltpu.roll(part, LANES - 2 * width, 1)
            for part in sums
        ]
        target = 0 if to_right else LANES - 2
        inside = (lane >= target) & (lane < target + 2)
        for j in range(freqs):
            turn = (target - 2 * j) % LANES
            block = slice(j * rows, (j + 1) * rows)
            place = [jnp.where(inside, pltpu.roll(part, turn, 1), 0.0) for part in sums]
            a_ref[block, :] += place[0]
            b_ref[block, :] += place[1]

    for to_down in (True, False):
        near_row, far_row = (0, 1) if to_down else (rows - 1, rows - 2)
        totals = [jnp.zeros((freqs, LANES), jnp.float32) for _ in range(4)]
        for direction in range(ND):
            if heads_down(direction) != to_down:
                continue
            table = table_ref.at[member, class_of(direction)]
            square = math.cos(2.0 * math.pi * direction / ND) ** 2
            for place, at in enumerate((near_row, far_row)):
                change = edges_ref[edge_rows(freqs, to_down, direction, at % SUB), :]
                growth = growth_ref[direction, at : at + 1, :]
                grown = (table[3] * change) * (1.0 + table[4] * growth)
                totals[2 * place] += grown
                totals[2 * place + 1] += square * grown
        for place, at in enumerate((near_row, far_row)):
            picked = pl.ds(at, freqs, stride=rows)
            a_ref[picked, :] += totals[2 * place]
            b_ref[picked, :] += totals[2 * place + 1]


def stress_kernel(
    freqs, member_ref, scalar_ref, wet_ref, a_ref, b_ref, own_ref, other_ref, sums_ref, ratio_ref
):
    member = member_ref[0]
    wet_cells = wet_ref[...]
    rows = wet_cells.shape[0]
    energy = wet_cells * (own_ref[...] + other_ref[...]) / (ND * NF)
    square = jnp.square(energy)

    sums = [jnp.zeros(wet_cells.shape, jnp.float32) for _ in range(3)]
    for j in range(freqs):
        base = (member * freqs + j) * CLASSES * KINDS
        high, shoal = scalar_ref[base + 3], scalar_ref[base + 4]
        block = slice(j * rows, (j + 1) * rows)
        ratio = wet_cells / (1.0 + (2.0 * high) * square)
        ratio_ref[j] = ratio
        whole = ratio * a_ref[block, :]
        along = ratio * b_ref[block, :]
        sums[0] += shoal * along + (shoal - 0.5) * whole
        sums[1] += (2.0 * shoal - 0.5) * whole - shoal * along
        sums[2] += whole
    for index in range(3):
        sums_ref[index] = sums[index] / (ND * NF)


def total_kernel(own_ref, other_ref, sums_ref, stress_ref):
    sums_ref[...] = own_ref[...] + other_ref[...]
    stress_ref[...] = sums_ref[0:2]


def strip_kernel(stress_ref, swapped_ref, other_ref, beside_ref, first_ref, second_ref):
    rows = stress_ref.shape[1]
    low_half = iota((rows, LANES), 1) < LANES // 2
    odd_sect = lax.rem(lax.axis_index("sect"), 2) == 1
    odd_slab = lax.rem(lax.axis_index("slab"), 2) == 1
    for index in range(2):
        swapped, other = swapped_ref[index], other_ref[index]
        beside = jnp.where(low_half != odd_sect, swapped, other)
        beside_ref[index] = beside
        ends = [
            jnp.concatenate([values[first : first + SUB] for values in (stress_ref[index], beside)], 1)
            for first in (0, rows - SUB)
        ]
        first_ref[index] = jnp.where(odd_slab, *ends)
        second_ref[index] = jnp.where(odd_slab, *ends[::-1])


BEHIND = 12
RINGS = 6


def final_kernel(
    freqs, member_ref, scalar_ref, depth_ref, ratios_ref, sums_ref, beside_ref, swapped_ref,
    other_ref, growth_ref, kept_ref, columns_ref, edges_ref,
    result_ref, level_ref, damping_ref, turning_ref, sems, *rings,
):
    member = member_ref[0]
    rows = depth_ref.shape[0]
    slab, slabs = lax.axis_index("slab"), lax.axis_size("slab")
    sect, sects = lax.axis_index("sect"), lax.axis_size("sect")
    above_ok = jnp.where(slab > 0, 1.0, 0.0)
    below_ok = jnp.where(slab < slabs - 1, 1.0, 0.0)
    left_ok = jnp.where(sect > 0, 1.0, 0.0)
    right_ok = jnp.where(sect < sects - 1, 1.0, 0.0)

    odd = lax.rem(slab, 2) == 1

    def framed(index):
        middle = jnp.concatenate([sums_ref[index], beside_ref[index]], axis=1)
        swapped, other = swapped_ref[index], other_ref[index]
        below = jnp.where(odd, other, swapped)
        above = jnp.where(odd, swapped, other)
        return jnp.concatenate([middle, below, above], axis=0)

    def around(values, axis):
        size = values.shape[axis]
        return pltpu.roll(values, 1, axis) + pltpu.roll(values, size - 1, axis)

    stress_x, stress_y = framed(0), framed(1)
    frame = stress_x.shape
    frame_row, frame_lane = iota(frame, 0), iota(frame, 1)
    row_ok = jnp.where(frame_row < rows, 1.0, jnp.where(frame_row < rows + SUB, below_ok, above_ok))
    lane_ok = jnp.where(
        frame_lane < LANES, 1.0, jnp.where(frame_lane < LANES + LANES // 2, right_ok, left_ok)
    )
    inside = row_ok * lane_ok / 4.5
    source = -((around(stress_x, 0) - 2.0 * stress_x) + (around(stress_y, 1) - 2.0 * stress_y))
    level = inside * source
    for _ in range(JAC):
        level = inside * (source + around(level, 0) + around(level, 1))
    level = level[:rows, :LANES]
    level_ref[...] = level
    damping = 1.0 / (1.0 + 4.0 * sums_ref[2] / (jnp.square(depth_ref[...] + level) + 1.0))
    tiles = rows // SUB
    damping_ref[...] = damping
    turning_ref[...] = columns_ref[...]
    tile_lane = iota((SUB, LANES), 1)

    def send(j, which, piece):
        part = pl.ds(piece * ND // 4, ND // 4)
        return pltpu.make_async_copy(
            rings[which].at[part], result_ref.at[j, part], sems.at[which, piece]
        )

    def frequency(j, which):
        @pl.when(j >= RINGS)
        def _():
            for piece in range(4):
                send(j - RINGS, which, piece).wait()

        base = (member * freqs + j) * CLASSES * KINDS
        high = scalar_ref[base + 3]

        def damped(direction, t, ratio, high_ratio):
            to_down, to_right = sides(direction // (ND // 4))
            part = slice(t * SUB, (t + 1) * SUB)
            target = 0 if to_right > 0 else LANES - 2
            at_side = (tile_lane >= target) & (tile_lane < target + 2)
            turn = (target - direction % GROUP * 2 * freqs) % LANES
            entered = turning_ref[direction // GROUP, part, :]
            if turn:
                entered = pltpu.roll(entered, turn, 1)
            value = kept_ref[j, direction, part, :] + jnp.where(at_side, entered, 0.0)
            if t == (0 if to_down > 0 else tiles - 1):
                edge = ((0 if to_down > 0 else 18) + row_slot(direction)) * freqs + j
                value += edges_ref[pl.ds(pl.multiple_of(edge * SUB, SUB), SUB), :]
            return value * (ratio + high_ratio * growth_ref[direction, part, :])

        pending = []
        for kind in range(CLASSES - 1):
            together = (0, 9, 18, 27) if kind == 0 else (kind, 18 - kind, 18 + kind, 36 - kind)
            scale = scalar_ref[base + kind * KINDS + 2]
            for t in range(tiles):
                part = slice(t * SUB, (t + 1) * SUB)
                ratio = scale * (ratios_ref[j, part, :] * damping_ref[part, :])
                high_ratio = high * ratio
                for direction in together:
                    pending.append((direction, part, damped(direction, t, ratio, high_ratio)))
                while len(pending) > BEHIND:
                    target, place, value = pending.pop(0)
                    rings[which][target, place, :] = value
        for target, place, value in pending:
            rings[which][target, place, :] = value
        for piece in range(4):
            send(j, which, piece).start()
        turned = [pltpu.roll(turning_ref[group], LANES - 2, 1) for group in range(GROUPS)]
        for group in range(GROUPS):
            turning_ref[group] = turned[group]

    def turn(index, carry):
        for which in range(RINGS):
            frequency(RINGS * index + which, which)
        return carry

    whole_turns = freqs // RINGS
    lax.fori_loop(0, whole_turns, turn, 0)
    for j in range(whole_turns * RINGS, freqs):
        frequency(jnp.int32(j), j % RINGS)
    for j in range(max(0, freqs - RINGS), freqs):
        for piece in range(4):
            send(j, j % RINGS, piece).wait()


def swap(values, axis, first):
    count = lax.axis_size(axis)
    pairs = [(i, i + 1) for i in range(first, count - 1, 2)]
    return lax.ppermute(values, axis, pairs + [(b, a) for a, b in pairs])


def others_sum(values, axis):
    count = lax.axis_size(axis)
    total = None
    for step in range(1, count):
        part = lax.ppermute(values, axis, [(i, (i + step) % count) for i in range(count)])
        total = part if total is None else total + part
    return jnp.zeros_like(values) if total is None else total


VMEM = pl.BlockSpec(memory_space=pltpu.VMEM)
SMEM = pl.BlockSpec(memory_space=pltpu.SMEM)
HBM = pl.BlockSpec(memory_space=pltpu.HBM)
ANY = pl.BlockSpec(memory_space=pl.ANY)


def in_vmem(*shape):
    return pltpu.VMEM(shape, jnp.float32)


def in_any(*shape):
    return jax.ShapeDtypeStruct(shape, jnp.float32)


def in_hbm(values):
    return pltpu.with_memory_space_constraint(values, pltpu.HBM)


def call(kernel, in_specs, out_shape, out_specs, flops, moved, scratch=(), aliases=None, limit=6):
    return pl.pallas_call(
        kernel,
        in_specs=in_specs,
        out_shape=out_shape,
        out_specs=out_specs,
        scratch_shapes=list(scratch),
        input_output_aliases=aliases or {},
        cost_estimate=pl.CostEstimate(flops=flops, bytes_accessed=moved, transcendentals=0),
        compiler_params=pltpu.CompilerParams(vmem_limit_bytes=limit << 20),
    )


def resident(spectrum, land_mask, ice_mask, wind_u, wind_v, depth):
    local_comp, rows, lanes = spectrum.shape
    freqs = local_comp // ND
    members = lax.axis_size("comp")
    member = lax.axis_index("comp").astype(jnp.int32).reshape(1)
    scalars, lane_table, row_table = numpy_tables(members, freqs)
    scalars, lane_table, row_table = map(jnp.asarray, (scalars, lane_table, row_table))
    cells = rows * lanes
    row_message = 2 * 18 * freqs + CORNERS
    block = (freqs, ND, rows, lanes)
    spectrum = spectrum.reshape(block)

    growth, wet, swap_side, other_side, swap_row, other_row, edges = call(
        functools.partial(pack_kernel, freqs),
        [SMEM] + [HBM] * 7,
        (
            in_any(ND, rows, lanes),
            in_any(rows, lanes),
            in_any(GROUPS // 2, rows, lanes),
            in_any(GROUPS // 2, rows, lanes),
            in_any(row_message, lanes),
            in_any(row_message, lanes),
            in_any(2 * 18 * freqs * SUB, lanes),
        ),
        (VMEM,) * 7,
        flops=local_comp * cells * 4,
        moved=local_comp * cells * 4,
        scratch=[
            pltpu.VMEM((local_comp * rows, lanes), jnp.float32),
            pltpu.VMEM((GROUPS // 2, rows, lanes), jnp.float32),
            pltpu.VMEM((GROUPS // 2, rows, lanes), jnp.float32),
            pltpu.VMEM(lane_table.shape[1:], jnp.float32),
            pltpu.VMEM(row_table.shape[1:], jnp.float32),
            pltpu.VMEM((rows, lanes), jnp.int32),
            pltpu.VMEM((rows, lanes), jnp.int32),
            pltpu.VMEM((rows, lanes), jnp.float32),
            pltpu.VMEM((rows, lanes), jnp.float32),
            pltpu.SemaphoreType.DMA((6,)),
            pltpu.SemaphoreType.DMA((GROUPS,)),
        ],
        limit=30,
    )(
        member,
        *map(in_hbm, (lane_table, row_table, land_mask, ice_mask, wind_u, wind_v, spectrum)),
    )

    def main_part(start, stop, *before):
        return call(
            functools.partial(main_kernel, freqs, start, stop),
            [SMEM, SMEM, VMEM, VMEM, HBM] + ([ANY, VMEM, VMEM, VMEM, VMEM] if before else []),
            (
                in_vmem(*block),
                in_any(freqs * rows, lanes),
                in_any(freqs * rows, lanes),
                in_any(rows, lanes),
            ),
            (VMEM,) * 4,
            flops=local_comp * cells * 16 * (stop - start) // freqs,
            moved=local_comp * cells * 8 * (stop - start) // freqs,
            scratch=[
                pltpu.VMEM((AHEAD, ND, rows, lanes), jnp.float32),
                pltpu.SemaphoreType.DMA((AHEAD,)),
            ]
            + [pltpu.VMEM((rows + 2 * SUB, lanes), jnp.float32)] * 8,
            aliases={6 + index: index for index in range(4)} if before else {},
            limit=8,
        )(member, scalars, wet, growth, in_hbm(spectrum), *before)

    early = max(1, freqs // 3)
    swap_side, other_side = swap(swap_side, "sect", 0), swap(other_side, "sect", 1)
    kept, *partial = main_part(0, early)
    swap_row, other_row = call(
        functools.partial(corner_kernel, freqs),
        [VMEM, VMEM, VMEM, ANY, ANY, ANY],
        (in_any(row_message, lanes), in_any(row_message, lanes)),
        (ANY, ANY),
        flops=100,
        moved=1 << 15,
        scratch=[pltpu.VMEM((2, CORNERS, lanes), jnp.float32), pltpu.SemaphoreType.DMA((2,))],
        aliases={3: 0, 4: 1},
    )(wet, swap_side, other_side, swap_row, other_row, partial[-1])
    swapped_row = swap(swap_row, "slab", 0)
    other_row = swap(other_row, "slab", 1)
    kept, a_sums, b_sums, energy = main_part(early, freqs, swap_row, kept, *partial)

    columns, edges, energy = call(
        functools.partial(enter_kernel, freqs),
        [SMEM] + [VMEM] * 9,
        (
            in_any(GROUPS, rows, lanes),
            in_any(2 * 18 * freqs * SUB, lanes),
            in_any(rows, lanes),
        ),
        (VMEM,) * 3,
        flops=cells * 600,
        moved=cells * 200,
        aliases={8: 1, 9: 2},
    )(
        member, lane_table, row_table, wet, swap_side, other_side, swapped_row, other_row, edges,
        energy,
    )
    energy_there = others_sum(energy, "comp")
    a_sums, b_sums = call(
        functools.partial(entered_kernel, freqs),
        [SMEM] + [VMEM] * 10,
        (in_any(freqs * rows, lanes), in_any(freqs * rows, lanes)),
        (VMEM,) * 2,
        flops=cells * 600,
        moved=cells * 200,
        aliases={9: 0, 10: 1},
    )(
        member, lane_table, row_table, ice_mask, wind_u, wind_v, growth, columns, edges,
        a_sums, b_sums,
    )

    sums, ratios = call(
        functools.partial(stress_kernel, freqs),
        [SMEM, SMEM] + [VMEM] * 5,
        (in_any(3, rows, lanes), in_any(freqs, rows, lanes)),
        (VMEM, VMEM),
        flops=cells * freqs * 12,
        moved=cells * freqs * 8,
    )(member, scalars, wet, a_sums, b_sums, energy, energy_there)
    sums, stress = call(
        total_kernel,
        [VMEM, VMEM],
        (in_any(3, rows, lanes), in_any(2, rows, lanes)),
        (VMEM, VMEM),
        flops=cells * 3,
        moved=cells * 44,
    )(sums, others_sum(sums, "comp"))
    beside, first, second = call(
        strip_kernel,
        [VMEM, VMEM, VMEM],
        (in_any(2, rows, lanes), in_any(2, SUB, 2 * lanes), in_any(2, SUB, 2 * lanes)),
        (VMEM, VMEM, VMEM),
        flops=cells * 4,
        moved=cells * 36,
    )(stress, swap(stress, "sect", 0), swap(stress, "sect", 1))
    aside, beyond = swap(first, "slab", 0), swap(second, "slab", 1)

    result, level = call(
        functools.partial(final_kernel, freqs),
        [SMEM, SMEM] + [VMEM] * 10,
        (in_any(*block), in_any(rows, lanes)),
        (HBM, VMEM),
        flops=local_comp * cells * 6,
        moved=local_comp * cells * 8,
        scratch=[
            pltpu.VMEM((rows, lanes), jnp.float32),
            pltpu.VMEM((GROUPS, rows, lanes), jnp.float32),
            pltpu.SemaphoreType.DMA((RINGS, 4)),
        ]
        + [pltpu.VMEM((ND, rows, lanes), jnp.float32)] * RINGS,
        limit=12,
    )(
        member, scalars, depth, ratios, sums, beside, aside, beyond, growth, kept,
        columns, edges,
    )
    return result.reshape(local_comp, rows, lanes), level


def local(spectrum, *fields):
    local_comp, rows, lanes = spectrum.shape
    whole_rings = local_comp % ND == 0 and GROUP * 2 * (local_comp // ND) < LANES - 1
    if whole_rings and lanes == LANES and rows % SUB == 0:
        return resident(spectrum, *fields)
    return general(spectrum, *fields)


def solution(mesh):
    in_specs = (
        P("comp", "slab", "sect"),
        P("slab", "sect"),
        P("slab", "sect"),
        P("slab", "sect"),
        P("slab", "sect"),
        P("slab", "sect"),
    )
    out_specs = (P("comp", "slab", "sect"), P("slab", "sect"))
    return jax.shard_map(local, mesh=mesh, in_specs=in_specs, out_specs=out_specs, check_vma=False)
```

```python
import functools
import math

import jax
import jax.numpy as jnp
import numpy as np
from jax import lax
from jax.experimental import pallas as pl
from jax.experimental.pallas import tpu as pltpu
from jax.sharding import PartitionSpec as P

ND = 36
NF = 36
STEPS = 2
JAC = 4


def extended(cells, sides, width):
    for axis, dim in sides:
        count = lax.axis_size(axis)
        ends = count - 1
        head = lax.slice_in_dim(cells, 0, width, axis=dim)
        tail = lax.slice_in_dim(cells, cells.shape[dim] - width, cells.shape[dim], axis=dim)
        cells = jnp.concatenate(
            [
                lax.ppermute(tail, axis, [(i, (i + 1) % count) for i in range(ends)]),
                cells,
                lax.ppermute(head, axis, [((i + 1) % count, i) for i in range(ends)]),
            ],
            axis=dim,
        )
    return cells


def tables(index):
    freq_index = (index // ND).astype(jnp.float32)
    angle_index = (index % ND).astype(jnp.float32)
    heading = 2.0 * math.pi * angle_index / ND
    return (
        jnp.cos(heading),
        jnp.sin(heading),
        jnp.power(1.1, -freq_index),
        jnp.power(1.1, freq_index - (NF - 1)),
        0.5 + 0.5 * freq_index / (NF - 1),
    )


def column(values):
    return values[:, None, None]


def advect(spectra, wet_cells, speed_x, speed_y):
    padded = extended(spectra, (("slab", 1), ("sect", 2)), 1)
    upper_rows = padded[:, :-2, 1:-1]
    lower_rows = padded[:, 2:, 1:-1]
    left_cells = padded[:, 1:-1, :-2]
    right_cells = padded[:, 1:-1, 2:]
    change = (
        jnp.maximum(speed_x, 0.0) * (spectra - upper_rows)
        + jnp.minimum(speed_x, 0.0) * (lower_rows - spectra)
        + jnp.maximum(speed_y, 0.0) * (spectra - left_cells)
        + jnp.minimum(speed_y, 0.0) * (right_cells - spectra)
    )
    return (spectra - change) * wet_cells


def forcing(spectra, energy, wind_east, wind_north, ice_cover, cosine, sine, high_ratio):
    project = cosine * wind_east + sine * wind_north
    growth = 0.5 * high_ratio * jnp.square(jnp.maximum(project, 0.0)) * (1.0 - ice_cover)
    return spectra * (1.0 + growth) / (1.0 + 2.0 * high_ratio * jnp.square(energy))


def stress_weights(cosine, sine, shoaling):
    return jnp.stack(
        [shoaling * (cosine * cosine + 1.0) - 0.5, shoaling * (sine * sine + 1.0) - 0.5]
    )


def surge_solve(stress):
    padded = extended(stress, (("slab", 1), ("sect", 2)), 1)
    source_term = -(
        padded[0, 2:, 1:-1]
        + padded[0, :-2, 1:-1]
        - 2.0 * stress[0]
        + (padded[1, 1:-1, 2:] + padded[1, 1:-1, :-2] - 2.0 * stress[1])
    )
    surge_level = source_term / 4.5
    for _ in range(JAC):
        neighbours = extended(surge_level, (("slab", 0), ("sect", 1)), 1)
        surge_level = (
            source_term
            + neighbours[2:, 1:-1]
            + neighbours[:-2, 1:-1]
            + neighbours[1:-1, 2:]
            + neighbours[1:-1, :-2]
        ) / 4.5
    return surge_level


def general(spectrum, land_mask, ice_mask, wind_u, wind_v, depth):
    groups = lax.axis_size("comp")
    member = lax.axis_index("comp")
    local_comp, block_rows, block_cols = spectrum.shape
    point_rows = block_rows // groups
    total_comp = ND * NF
    wet_cells = (1 - land_mask).astype(jnp.float32)
    ice_cover = ice_mask.astype(jnp.float32)

    def own_rows(values):
        return lax.dynamic_slice_in_dim(values, member * point_rows, point_rows, values.ndim - 2)

    own_index = member * local_comp + jnp.arange(local_comp, dtype=jnp.int32)
    cosine, sine, low_ratio, high_ratio, shoaling = tables(own_index)
    spectra = spectrum * wet_cells
    for _ in range(STEPS):
        spectra = advect(
            spectra, wet_cells, column(0.7 * low_ratio * cosine), column(0.7 * low_ratio * sine)
        )
    points = lax.all_to_all(spectra, "comp", split_axis=1, concat_axis=0, tiled=True)
    cosine_full, sine_full, _, high_full, shoal_full = tables(
        jnp.arange(total_comp, dtype=jnp.int32)
    )
    energy = jnp.sum(points, axis=0) / total_comp
    sourced = forcing(
        points,
        energy,
        own_rows(wind_u),
        own_rows(wind_v),
        own_rows(ice_cover),
        column(cosine_full),
        column(sine_full),
        column(high_full),
    )
    stress = (
        jnp.einsum(
            "sk,krc->src",
            stress_weights(cosine_full, sine_full, shoal_full),
            sourced,
            precision=lax.Precision.HIGHEST,
        )
        / total_comp
    )
    stress_block = lax.all_gather(stress, "comp", axis=1, tiled=True)
    level_block = surge_solve(stress_block)
    final_energy = jnp.sum(sourced, axis=0) / total_comp
    damped = sourced / (
        1.0 + 4.0 * final_energy / (jnp.square(own_rows(depth) + own_rows(level_block)) + 1.0)
    )
    result = lax.all_to_all(damped, "comp", split_axis=0, concat_axis=1, tiled=True)
    return (result, level_block)


LANES = 128
SUB = 8
CLASSES = 10
KINDS = 5
GROUP = 3
GROUPS = ND // GROUP
CORNERS = 8


def class_of(direction):
    folded = direction % 18
    return folded if folded <= 9 else 18 - folded


def heads_down(direction):
    return direction < 9 or direction >= 27


def heads_right(direction):
    return direction < 18


def row_slot(direction):
    if direction < 9:
        return direction
    return direction - 18 if direction >= 27 else direction - 9


def numpy_tables(members, freqs):
    j = np.arange(members * freqs, dtype=np.float64)
    heading = 2.0 * np.pi * np.arange(ND) / ND
    cosine, sine = np.cos(heading), np.sin(heading)
    low = 1.1 ** (-j)
    high = 1.1 ** (j - (NF - 1))
    shoal = 0.5 + 0.5 * j / (NF - 1)
    step_x = 0.7 * low[:, None] * np.abs(cosine)
    step_y = 0.7 * low[:, None] * np.abs(sine)
    keep = 1.0 - step_x - step_y
    alpha, beta, scale = step_x / keep, step_y / keep, keep * keep
    classes = np.arange(CLASSES)
    square = np.broadcast_to(cosine * cosine, alpha.shape)
    scalars = np.stack(
        [
            alpha[:, classes],
            beta[:, classes],
            scale[:, classes],
            np.broadcast_to(high[:, None], (j.size, CLASSES)),
            np.broadcast_to(shoal[:, None], (j.size, CLASSES)),
        ],
        axis=-1,
    ).astype(np.float32)

    kinds = np.stack(
        [
            2.0 * beta,
            beta * beta,
            alpha * beta,
            scale,
            scale * square,
            np.broadcast_to(high[:, None], alpha.shape),
            np.broadcast_to(cosine, alpha.shape),
            np.broadcast_to(sine, alpha.shape),
        ]
    )
    lanes = np.zeros((members, GROUPS, 8, LANES), np.float32)
    packed = kinds.reshape(8, members, freqs, GROUPS, GROUP)
    packed = np.repeat(packed.transpose(1, 3, 0, 4, 2), 2, axis=-1)
    lanes[..., : GROUP * 2 * freqs] = packed.reshape(members, GROUPS, 8, -1)

    rows = np.stack(
        [2.0 * alpha, alpha * alpha, alpha * beta, scale, np.broadcast_to(high[:, None], alpha.shape)]
    )[:, :, classes]
    rows = rows.reshape(5, members, freqs, CLASSES).transpose(1, 3, 0, 2)
    rows = np.broadcast_to(rows[..., None], rows.shape + (LANES,)).astype(np.float32)
    return scalars.reshape(-1), lanes, rows


def begin(copies):
    for copy in copies:
        copy.start()


def finish(copies):
    for copy in copies:
        copy.wait()


def odd_position(axis):
    return lax.rem(lax.axis_index(axis), 2) == 1


def iota(shape, axis):
    return lax.broadcasted_iota(jnp.int32, shape, axis)


def spread(values, column):
    return jnp.broadcast_to(values[:, column : column + 1], values.shape)


def shift_rows(values, step):
    rows = values.shape[0]
    edge = 0 if step > 0 else rows - 1
    moved = pltpu.roll(values, step % rows, 0)
    return jnp.where(iota(values.shape, 0) == edge, 0.0, moved)


def shift_lanes(values, step):
    lanes = values.shape[1]
    edge = 0 if step > 0 else lanes - 1
    moved = pltpu.roll(values, step % lanes, 1)
    return jnp.where(iota(values.shape, 1) == edge, 0.0, moved)


DEPTH = 4
SHARES = 3


def sides(quadrant):
    return 1 if quadrant in (0, 3) else -1, 1 if quadrant in (0, 1) else -1


def pack_kernel(
    freqs, member_ref, lanes_hbm, table_hbm, land_hbm, ice_hbm, east_hbm, north_hbm, spectrum_ref,
    growth_ref, wet_ref, swap_side_ref, other_side_ref, swap_row_ref, other_row_ref, edges_ref,
    kept_ref, right_ref, left_ref, lanes_ref, table_ref, land_ref, ice_ref, east_ref, north_ref, small_sems, sems,
):
    member = member_ref[0]
    small = [
        pltpu.make_async_copy(source, target, small_sems.at[index])
        for index, (source, target) in enumerate(
            (
                (land_hbm, land_ref),
                (ice_hbm, ice_ref),
                (east_hbm, east_ref),
                (north_hbm, north_ref),
                (lanes_hbm.at[member], lanes_ref),
                (table_hbm.at[member], table_ref),
            )
        )
    ]
    for copy in small:
        copy.start()

    rows = land_ref.shape[0]
    blocks_ref = kept_ref.reshape(freqs, ND, rows, LANES)

    def fetch(group):
        ends = [share * freqs // SHARES for share in range(SHARES + 1)]
        parts = [
            (pl.ds(first, last - first), pl.ds(group * GROUP, GROUP))
            for first, last in zip(ends, ends[1:])
            if last > first
        ]
        return [
            pltpu.make_async_copy(
                spectrum_ref.at[part], blocks_ref.at[part], sems.at[group, share]
            )
            for share, part in enumerate(parts)
        ]

    begin(fetch(0))
    edges_ref[...] = jnp.zeros_like(edges_ref)
    for copy in small:
        copy.wait()

    wet_cells = (1 - land_ref[...]).astype(jnp.float32)
    wet_ref[...] = wet_cells
    open_water = 0.5 * (1.0 - ice_ref[...].astype(jnp.float32))
    shape = wet_cells.shape
    tiles = rows // SUB
    for direction in range(ND):
        angle = 2.0 * math.pi * direction / ND
        project = math.cos(angle) * east_ref[...] + math.sin(angle) * north_ref[...]
        growth_ref[direction] = open_water * jnp.square(jnp.maximum(project, 0.0))

    for group in range(1, DEPTH):
        begin(fetch(group))
    lane = iota(shape, 1)
    even = lane % 2 == 0
    tile_lane = iota((SUB, LANES), 1)
    for row_ref in (swap_row_ref, other_row_ref):
        row_ref[pl.ds(2 * 18 * freqs, CORNERS), :] = jnp.zeros((CORNERS, LANES), jnp.float32)
    odd_sect, odd_slab = odd_position("sect"), odd_position("slab")

    half = GROUPS // 2

    def gather_all(to_right):
        target_ref = right_ref if to_right else left_ref

        def gather(index, carry):
            group = index + (0 if to_right else half)
            finish(fetch(group))

            @pl.when(group + DEPTH < GROUPS)
            def _():
                begin(fetch(group + DEPTH))

            packed = [jnp.zeros((SUB, LANES), jnp.float32) for _ in range(tiles)]
            for i in range(GROUP):
                for j in range(freqs):
                    place = i * 2 * freqs + 2 * j
                    here = (tile_lane >= place) & (tile_lane < place + 2)
                    turn = (place + 2 if to_right else place) % LANES
                    first = pl.multiple_of((j * ND + group * GROUP + i) * rows, SUB)
                    for tile in range(tiles):
                        cells = kept_ref[pl.ds(first + tile * SUB, SUB), :]
                        packed[tile] = jnp.where(here, pltpu.roll(cells, turn, 1), packed[tile])
            for tile in range(tiles):
                target_ref[index, tile * SUB : (tile + 1) * SUB, :] = packed[tile]
            return carry

        lax.fori_loop(0, half, gather, 0)

    def side_message(group):
        to_right, fore = group < half, 1 if heads_down(group * GROUP) else -1
        ahead, behind = (LANES - 1, LANES - 2) if to_right else (0, 1)
        wet_near, wet_far = spread(wet_cells, ahead), spread(wet_cells, behind)
        near_even = not to_right
        packed = right_ref[group] if to_right else left_ref[group - half]
        values = packed * jnp.where(even == near_even, wet_near, wet_far)
        near = pltpu.roll(values, 1 if near_even else LANES - 1, 1)
        table = lanes_ref[group]
        follow = wet_near * (table[1:2] * values + table[2:3] * shift_rows(near, fore))
        message = jnp.where(even == near_even, values, follow)
        return jnp.where(lane == LANES - 1, wet_near, message)

    def row_message(direction):
        to_down = heads_down(direction)
        near_row, far_row = (rows - 1, rows - 2) if to_down else (0, 1)
        wet_near = wet_cells[near_row : near_row + 1, :]
        wet_far = wet_cells[far_row : far_row + 1, :]
        table = table_ref.at[class_of(direction)]
        near = kept_ref[pl.ds(direction * rows + near_row, freqs, stride=ND * rows), :] * wet_near
        far = kept_ref[pl.ds(direction * rows + far_row, freqs, stride=ND * rows), :] * wet_far
        beside = shift_lanes(near, 1 if heads_right(direction) else -1)
        return near, wet_near * (table[1] * far + table[2] * beside)

    def row_messages(slots):
        for slot in slots:
            pairs = zip(row_message(by_slot[True, slot]), row_message(by_slot[False, slot]))
            for which, (down, up) in enumerate(pairs):
                first = (which * 18 + slot) * freqs
                swap_row_ref[first : first + freqs, :] = jnp.where(odd_slab, up, down)
                other_row_ref[first : first + freqs, :] = jnp.where(odd_slab, down, up)

    by_slot = {(heads_down(d), row_slot(d)): d for d in range(ND)}
    gather_all(True)
    rights = [side_message(index) for index in range(half)]
    for index in range(half):
        right_ref[index] = rights[index]
    row_messages(range(9))
    gather_all(False)
    for index in range(half):
        right, left = right_ref[index], side_message(index + half)
        swap_side_ref[index] = jnp.where(odd_sect, left, right)
        other_side_ref[index] = jnp.where(odd_sect, right, left)
    row_messages(range(9, 18))


def corner_kernel(
    freqs, wet_ref, swapped_ref, other_ref, swap_in, other_in, _after, swap_row_ref, other_row_ref,
    rows_ref, sems,
):
    rows = wet_ref.shape[0]
    odd_sect, odd_slab = odd_position("sect"), odd_position("slab")
    last = iota((1, LANES), 1) == LANES - 1
    rows_ref[...] = jnp.zeros_like(rows_ref)
    for i in range(6):
        from_left = i < 3
        column = 0 if from_left else LANES - 1
        ends = []
        for row, index in ((rows - 1, i), (0, i + 3 if from_left else i - 3)):
            swapped = swapped_ref[index, row : row + 1, :]
            other = other_ref[index, row : row + 1, :]
            came = jnp.where(odd_sect == from_left, swapped, other)
            own = jnp.broadcast_to(wet_ref[row : row + 1, column : column + 1], (1, LANES))
            ends.append(jnp.where(last, own, came))
        rows_ref[0, i : i + 1, :] = jnp.where(odd_slab, *ends[::-1])
        rows_ref[1, i : i + 1, :] = jnp.where(odd_slab, *ends)
    start = 2 * 18 * freqs
    copies = [
        pltpu.make_async_copy(
            rows_ref.at[which], ref.at[pl.ds(start, CORNERS), :], sems.at[which]
        )
        for which, ref in ((0, swap_row_ref), (1, other_row_ref))
    ]
    for copy in copies:
        copy.start()
    for copy in copies:
        copy.wait()


AHEAD = 6
PIECES = 4


def main_kernel(
    freqs, start, stop, member_ref, scalar_ref, wet_ref, growth_ref, spectrum_ref, *refs
):
    if start:
        _after, _kept_in, a_in, b_in, energy_in, *refs = refs
    kept_ref, a_ref, b_ref, energy_ref, ring_ref, sems, *first_refs = refs
    member = member_ref[0]
    nought = jnp.minimum(member, 0)
    rows = wet_ref.shape[0]
    tiles = rows // SUB

    def fetch(j):
        slot = lax.rem(j, AHEAD)
        parts = [pl.ds(piece * (ND // PIECES), ND // PIECES) for piece in range(PIECES)]
        return [
            pltpu.make_async_copy(
                spectrum_ref.at[j, part], ring_ref.at[slot, part], sems.at[slot, piece]
            )
            for piece, part in enumerate(parts)
        ]

    begin(fetch(jnp.int32(start)))

    lane = iota((SUB, LANES), 1)
    sub = iota((SUB, LANES), 0)
    not_first = jnp.where(lane == 0, 0.0, 1.0)
    not_last = jnp.where(lane == LANES - 1, 0.0, 1.0)
    top, bottom = sub == 0, sub == SUB - 1
    energy_ref[...] = energy_in[...] if start else jnp.zeros_like(energy_ref)
    for first_ref in first_refs:
        first_ref[...] = jnp.zeros_like(first_ref)

    def tile_at(tile):
        return pl.ds(tile * SUB, SUB)

    def row_shift(quadrant):
        return -1 if quadrant in (0, 3) else 1

    def parts_of(kind):
        if kind == 0:
            return ((0, 0, 0), (9, 1, 9), (18, 2, 0), (27, 3, 9))
        return ((kind, 0, kind), (18 - kind, 1, kind), (18 + kind, 2, kind), (36 - kind, 3, kind))

    def frequency(j, carry):
        finish(fetch(j))

        @pl.when(j == start)
        def _():
            for later in range(start + 1, min(start + AHEAD, stop)):
                begin(fetch(jnp.int32(later)))

        slot = lax.rem(j, AHEAD)
        sums = [[None] * tiles for _ in range(3)]

        def add(which, t, value):
            have = sums[which][t]
            sums[which][t] = value if have is None else have + value
        base = (member * freqs + j) * CLASSES * KINDS
        at = [pl.ds(pl.multiple_of(j * rows, SUB) + t * SUB, SUB) for t in range(tiles)]

        def speeds(part):
            at_class = base + part[2] * KINDS
            beta = scalar_ref[at_class + 1]
            return scalar_ref[at_class], beta * (not_first if part[1] in (0, 1) else not_last)

        def beside(cells, quadrant):
            return pltpu.roll(cells, 1 if quadrant in (0, 1) else LANES - 1, 1)

        def first_step(kind):
            parts = parts_of(kind)
            speed = [speeds(part) for part in parts]
            wet = [wet_ref[tile_at(t), :] for t in range(tiles)]
            for (direction, quadrant, _), (alpha, across) in zip(parts, speed):
                shift = row_shift(quadrant)
                edge = top if shift < 0 else bottom
                target = first_refs[kind % 2 * 4 + quadrant]
                cells = [ring_ref[slot, direction, tile_at(t), :] * wet[t] for t in range(tiles)]
                turned = [pltpu.roll(cells[t], -shift % SUB, 0) for t in range(tiles)]
                for t in range(tiles):
                    before = turned[t + shift] if 0 <= t + shift < tiles else 0.0
                    ahead = jnp.where(edge, before, turned[t])
                    after = cells[t] + alpha * ahead + across * beside(cells[t], quadrant)
                    target[tile_at(t + 1), :] = wet[t] * after

        def second_step(kind):
            parts = parts_of(kind)
            scale, high = scalar_ref[base + kind * KINDS + 2], scalar_ref[base + 3]
            scaled_high = scale * high
            speed = [speeds(part) for part in parts]
            for t in range(tiles):
                moved, grown = [], []
                for (direction, quadrant, _), (alpha, across) in zip(parts, speed):
                    source = first_refs[kind % 2 * 4 + quadrant]
                    cells = source[tile_at(t + 1), :]
                    ahead = source[pl.ds((t + 1) * SUB + row_shift(quadrant) + nought, SUB), :]
                    after = cells + alpha * ahead + across * beside(cells, quadrant)
                    kept_ref[j, direction, tile_at(t), :] = after
                    moved.append(after)
                    grown.append(growth_ref[direction, tile_at(t), :] * after)
                if kind == 0:
                    plain_x, plain_y = scale * (moved[0] + moved[2]), scale * (moved[1] + moved[3])
                    grown_x = plain_x + scaled_high * (grown[0] + grown[2])
                    grown_y = plain_y + scaled_high * (grown[1] + grown[3])
                    square = math.cos(0.5 * math.pi) ** 2
                    add(0, t, plain_x + plain_y)
                    add(1, t, grown_x + grown_y)
                    add(2, t, grown_x + square * grown_y)
                else:
                    plain = scale * ((moved[0] + moved[1]) + (moved[2] + moved[3]))
                    whole = plain + scaled_high * ((grown[0] + grown[1]) + (grown[2] + grown[3]))
                    square = math.cos(2.0 * math.pi * kind / ND) ** 2
                    add(0, t, plain)
                    add(1, t, whole)
                    add(2, t, square * whole)

        first_step(0)
        for kind in range(CLASSES - 1):
            if kind + 1 < CLASSES - 1:
                first_step(kind + 1)
            second_step(kind)
        for t in range(tiles):
            energy_ref[tile_at(t), :] += sums[0][t]
            a_ref[at[t], :] = sums[1][t]
            b_ref[at[t], :] = sums[2][t]

        @pl.when(j + AHEAD < stop)
        def _():
            begin(fetch(j + AHEAD))

        return carry

    lax.fori_loop(start, stop, frequency, 0)


def edge_rows(freqs, to_down, direction, at):
    first = ((0 if to_down else 18) + row_slot(direction)) * freqs * SUB
    return pl.ds(first + at, freqs, stride=SUB)


def enter_kernel(
    freqs, member_ref, lanes_ref, table_ref, wet_ref, swap_side_ref, other_side_ref, swap_row_ref,
    other_row_ref, _edges_in, energy_in, columns_ref, edges_ref, energy_ref,
):
    member = member_ref[0]
    wet_cells = wet_ref[...]
    shape = wet_cells.shape
    rows = shape[0]
    lane = iota(shape, 1)
    row = iota(shape, 0)
    even = lane % 2 == 0
    width = 2 * freqs
    used = lane < GROUP * width
    energy = energy_in[...]
    start = 2 * 18 * freqs
    odd_sect, odd_slab = odd_position("sect"), odd_position("slab")

    def from_rows(to_down, part):
        return jnp.where(odd_slab == to_down, swap_row_ref[part, :], other_row_ref[part, :])

    for to_right in (True, False):
        near_column, far_column = (0, 1) if to_right else (LANES - 1, LANES - 2)
        near_even = to_right
        wet_near, wet_far = spread(wet_cells, near_column), spread(wet_cells, far_column)
        total = jnp.zeros(shape, jnp.float32)
        for index in range(GROUPS // 2):
            group = index if to_right else index + GROUPS // 2
            to_down = heads_down(group * GROUP)
            fore = 1 if to_down else -1
            message = jnp.where(odd_sect == to_right, swap_side_ref[index], other_side_ref[index])
            table = lanes_ref[member, group]
            turn = LANES - 1 if near_even else 1
            entered = pltpu.roll(message, turn, 1)
            corner_index = index if to_down else (index - 3 if to_right else index + 3)
            corner = from_rows(to_down, slice(start + corner_index, start + corner_index + 1))
            edge = 0 if to_down else rows - 1
            paths = corner[:, LANES - 1 :] + message[edge : edge + 1, LANES - 1 :]
            corner = pltpu.roll(jnp.broadcast_to(corner, (SUB, LANES)), turn, 1)[0:1]
            corner = jnp.broadcast_to(paths, (1, LANES)) * corner
            diagonal = shift_rows(wet_near * entered, fore)
            diagonal = jnp.where(row == edge, jnp.broadcast_to(corner, shape), diagonal)
            near = wet_near * (table[0:1] * entered + message + table[2:3] * diagonal)
            far = wet_near * wet_far * (table[1:2] * message)
            change = jnp.where(used, jnp.where(even == near_even, near, far), 0.0)
            columns_ref[group] = change
            total += table[3:4] * change
        total += pltpu.roll(total, LANES - width, 1) + pltpu.roll(total, LANES - 2 * width, 1)
        target = 0 if to_right else LANES - 2
        inside = (lane >= target) & (lane < target + 2)
        for j in range(freqs):
            turned = pltpu.roll(total, (target - 2 * j) % LANES, 1)
            energy += jnp.where(inside, turned, 0.0)
    energy_ref[...] = energy

    for to_down in (True, False):
        near_row, far_row = (0, 1) if to_down else (rows - 1, rows - 2)
        wet_near = wet_cells[near_row : near_row + 1, :]
        wet_both = wet_near * wet_cells[far_row : far_row + 1, :]
        totals = [jnp.zeros((freqs, LANES), jnp.float32) for _ in range(2)]
        for direction in range(ND):
            if heads_down(direction) != to_down:
                continue
            slot = row_slot(direction) * freqs
            entered = from_rows(to_down, slice(slot, slot + freqs))
            follow = from_rows(to_down, slice(18 * freqs + slot, 18 * freqs + slot + freqs))
            table = table_ref.at[member, class_of(direction)]
            side = 1 if heads_right(direction) else -1
            diagonal = shift_lanes(wet_near * entered, side)
            near = wet_near * (table[0] * entered + follow + table[2] * diagonal)
            far = wet_both * (table[1] * entered)
            for place, (change, at) in enumerate(((near, near_row), (far, far_row))):
                edges_ref[edge_rows(freqs, to_down, direction, at % SUB), :] = change
                totals[place] += table[3] * change
        for total, at in zip(totals, (near_row, far_row)):
            energy_ref[at : at + 1, :] += jnp.sum(total, axis=0, keepdims=True)


def entered_kernel(
    freqs, member_ref, lanes_ref, table_ref, ice_ref, east_ref, north_ref, growth_ref, columns_ref,
    edges_ref, a_in, b_in, a_ref, b_ref,
):
    member = member_ref[0]
    shape = ice_ref.shape
    rows = shape[0]
    lane = iota(shape, 1)
    even = lane % 2 == 0
    width = 2 * freqs
    a_ref[...] = a_in[...]
    b_ref[...] = b_in[...]

    for to_right in (True, False):
        near_column, far_column = (0, 1) if to_right else (LANES - 1, LANES - 2)

        def packed_field(values):
            return jnp.where(
                even == to_right, spread(values, near_column), spread(values, far_column)
            )

        east, north = packed_field(east_ref[...]), packed_field(north_ref[...])
        open_water = 0.5 * (1.0 - packed_field(ice_ref[...].astype(jnp.float32)))
        sums = [jnp.zeros(shape, jnp.float32) for _ in range(2)]
        for index in range(GROUPS // 2):
            group = index if to_right else index + GROUPS // 2
            table = lanes_ref[member, group]
            project = table[6:7] * east + table[7:8] * north
            growth = open_water * jnp.square(jnp.maximum(project, 0.0))
            grown = columns_ref[group] * (1.0 + table[5:6] * growth)
            sums[0] += table[3:4] * grown
            sums[1] += table[4:5] * grown
        sums = [
            part + pltpu.roll(part, LANES - width, 1) + pltpu.roll(part, LANES - 2 * width, 1)
            for part in sums
        ]
        target = 0 if to_right else LANES - 2
        inside = (lane >= target) & (lane < target + 2)
        for j in range(freqs):
            turn = (target - 2 * j) % LANES
            block = slice(j * rows, (j + 1) * rows)
            place = [jnp.where(inside, pltpu.roll(part, turn, 1), 0.0) for part in sums]
            a_ref[block, :] += place[0]
            b_ref[block, :] += place[1]

    for to_down in (True, False):
        near_row, far_row = (0, 1) if to_down else (rows - 1, rows - 2)
        totals = [jnp.zeros((freqs, LANES), jnp.float32) for _ in range(4)]
        for direction in range(ND):
            if heads_down(direction) != to_down:
                continue
            table = table_ref.at[member, class_of(direction)]
            square = math.cos(2.0 * math.pi * direction / ND) ** 2
            for place, at in enumerate((near_row, far_row)):
                change = edges_ref[edge_rows(freqs, to_down, direction, at % SUB), :]
                growth = growth_ref[direction, at : at + 1, :]
                grown = (table[3] * change) * (1.0 + table[4] * growth)
                totals[2 * place] += grown
                totals[2 * place + 1] += square * grown
        for place, at in enumerate((near_row, far_row)):
            picked = pl.ds(at, freqs, stride=rows)
            a_ref[picked, :] += totals[2 * place]
            b_ref[picked, :] += totals[2 * place + 1]


def stress_kernel(
    freqs, member_ref, scalar_ref, wet_ref, a_ref, b_ref, own_ref, other_ref, sums_ref, ratio_ref
):
    member = member_ref[0]
    wet_cells = wet_ref[...]
    rows = wet_cells.shape[0]
    energy = wet_cells * (own_ref[...] + other_ref[...]) / (ND * NF)
    square = jnp.square(energy)

    sums = [jnp.zeros(wet_cells.shape, jnp.float32) for _ in range(3)]
    for j in range(freqs):
        base = (member * freqs + j) * CLASSES * KINDS
        high, shoal = scalar_ref[base + 3], scalar_ref[base + 4]
        block = slice(j * rows, (j + 1) * rows)
        ratio = wet_cells / (1.0 + (2.0 * high) * square)
        ratio_ref[j] = ratio
        whole = ratio * a_ref[block, :]
        along = ratio * b_ref[block, :]
        sums[0] += shoal * along + (shoal - 0.5) * whole
        sums[1] += (2.0 * shoal - 0.5) * whole - shoal * along
        sums[2] += whole
    for index in range(3):
        sums_ref[index] = sums[index] / (ND * NF)


def total_kernel(own_ref, other_ref, sums_ref, stress_ref):
    sums_ref[...] = own_ref[...] + other_ref[...]
    stress_ref[...] = sums_ref[0:2]


def strip_kernel(stress_ref, swapped_ref, other_ref, beside_ref, first_ref, second_ref):
    rows = stress_ref.shape[1]
    low_half = iota((rows, LANES), 1) < LANES // 2
    odd_sect = lax.rem(lax.axis_index("sect"), 2) == 1
    odd_slab = lax.rem(lax.axis_index("slab"), 2) == 1
    for index in range(2):
        swapped, other = swapped_ref[index], other_ref[index]
        beside = jnp.where(low_half != odd_sect, swapped, other)
        beside_ref[index] = beside
        ends = [
            jnp.concatenate([values[first : first + SUB] for values in (stress_ref[index], beside)], 1)
            for first in (0, rows - SUB)
        ]
        first_ref[index] = jnp.where(odd_slab, *ends)
        second_ref[index] = jnp.where(odd_slab, *ends[::-1])


BEHIND = 12
RINGS = 6


def final_kernel(
    freqs, member_ref, scalar_ref, depth_ref, ratios_ref, sums_ref, beside_ref, swapped_ref,
    other_ref, growth_ref, kept_ref, columns_ref, edges_ref,
    result_ref, level_ref, damping_ref, turning_ref, sems, *rings,
):
    member = member_ref[0]
    rows = depth_ref.shape[0]
    slab, slabs = lax.axis_index("slab"), lax.axis_size("slab")
    sect, sects = lax.axis_index("sect"), lax.axis_size("sect")
    above_ok = jnp.where(slab > 0, 1.0, 0.0)
    below_ok = jnp.where(slab < slabs - 1, 1.0, 0.0)
    left_ok = jnp.where(sect > 0, 1.0, 0.0)
    right_ok = jnp.where(sect < sects - 1, 1.0, 0.0)

    odd = lax.rem(slab, 2) == 1

    def framed(index):
        middle = jnp.concatenate([sums_ref[index], beside_ref[index]], axis=1)
        swapped, other = swapped_ref[index], other_ref[index]
        below = jnp.where(odd, other, swapped)
        above = jnp.where(odd, swapped, other)
        return jnp.concatenate([middle, below, above], axis=0)

    def around(values, axis):
        size = values.shape[axis]
        return pltpu.roll(values, 1, axis) + pltpu.roll(values, size - 1, axis)

    stress_x, stress_y = framed(0), framed(1)
    frame = stress_x.shape
    frame_row, frame_lane = iota(frame, 0), iota(frame, 1)
    row_ok = jnp.where(frame_row < rows, 1.0, jnp.where(frame_row < rows + SUB, below_ok, above_ok))
    lane_ok = jnp.where(
        frame_lane < LANES, 1.0, jnp.where(frame_lane < LANES + LANES // 2, right_ok, left_ok)
    )
    inside = row_ok * lane_ok / 4.5
    source = -((around(stress_x, 0) - 2.0 * stress_x) + (around(stress_y, 1) - 2.0 * stress_y))
    level = inside * source
    for _ in range(JAC):
        level = inside * (source + around(level, 0) + around(level, 1))
    level = level[:rows, :LANES]
    level_ref[...] = level
    damping = 1.0 / (1.0 + 4.0 * sums_ref[2] / (jnp.square(depth_ref[...] + level) + 1.0))
    tiles = rows // SUB
    damping_ref[...] = damping
    turning_ref[...] = columns_ref[...]
    tile_lane = iota((SUB, LANES), 1)

    def send(j, which, piece):
        part = pl.ds(piece * ND // 4, ND // 4)
        return pltpu.make_async_copy(
            rings[which].at[part], result_ref.at[j, part], sems.at[which, piece]
        )

    def frequency(j, which):
        @pl.when(j >= RINGS)
        def _():
            for piece in range(4):
                send(j - RINGS, which, piece).wait()

        base = (member * freqs + j) * CLASSES * KINDS
        high = scalar_ref[base + 3]

        def damped(direction, t, ratio, high_ratio):
            to_down, to_right = sides(direction // (ND // 4))
            part = slice(t * SUB, (t + 1) * SUB)
            target = 0 if to_right > 0 else LANES - 2
            at_side = (tile_lane >= target) & (tile_lane < target + 2)
            turn = (target - direction % GROUP * 2 * freqs) % LANES
            entered = turning_ref[direction // GROUP, part, :]
            if turn:
                entered = pltpu.roll(entered, turn, 1)
            value = kept_ref[j, direction, part, :] + jnp.where(at_side, entered, 0.0)
            if t == (0 if to_down > 0 else tiles - 1):
                edge = ((0 if to_down > 0 else 18) + row_slot(direction)) * freqs + j
                value += edges_ref[pl.ds(pl.multiple_of(edge * SUB, SUB), SUB), :]
            return value * (ratio + high_ratio * growth_ref[direction, part, :])

        pending = []
        for kind in range(CLASSES - 1):
            together = (0, 9, 18, 27) if kind == 0 else (kind, 18 - kind, 18 + kind, 36 - kind)
            scale = scalar_ref[base + kind * KINDS + 2]
            for t in range(tiles):
                part = slice(t * SUB, (t + 1) * SUB)
                ratio = scale * (ratios_ref[j, part, :] * damping_ref[part, :])
                high_ratio = high * ratio
                for direction in together:
                    pending.append((direction, part, damped(direction, t, ratio, high_ratio)))
                while len(pending) > BEHIND:
                    target, place, value = pending.pop(0)
                    rings[which][target, place, :] = value
        for target, place, value in pending:
            rings[which][target, place, :] = value
        for piece in range(4):
            send(j, which, piece).start()
        turned = [pltpu.roll(turning_ref[group], LANES - 2, 1) for group in range(GROUPS)]
        for group in range(GROUPS):
            turning_ref[group] = turned[group]

    def turn(index, carry):
        for which in range(RINGS):
            frequency(RINGS * index + which, which)
        return carry

    whole_turns = freqs // RINGS
    lax.fori_loop(0, whole_turns, turn, 0)
    for j in range(whole_turns * RINGS, freqs):
        frequency(jnp.int32(j), j % RINGS)
    for j in range(max(0, freqs - RINGS), freqs):
        for piece in range(4):
            send(j, j % RINGS, piece).wait()


def swap(values, axis, first):
    count = lax.axis_size(axis)
    pairs = [(i, i + 1) for i in range(first, count - 1, 2)]
    return lax.ppermute(values, axis, pairs + [(b, a) for a, b in pairs])


def others_sum(values, axis):
    count = lax.axis_size(axis)
    total = None
    for step in range(1, count):
        part = lax.ppermute(values, axis, [(i, (i + step) % count) for i in range(count)])
        total = part if total is None else total + part
    return jnp.zeros_like(values) if total is None else total


VMEM = pl.BlockSpec(memory_space=pltpu.VMEM)
SMEM = pl.BlockSpec(memory_space=pltpu.SMEM)
HBM = pl.BlockSpec(memory_space=pltpu.HBM)
ANY = pl.BlockSpec(memory_space=pl.ANY)


def in_vmem(*shape):
    return pltpu.VMEM(shape, jnp.float32)


def in_any(*shape):
    return jax.ShapeDtypeStruct(shape, jnp.float32)


def in_hbm(values):
    return pltpu.with_memory_space_constraint(values, pltpu.HBM)


def call(kernel, in_specs, out_shape, out_specs, flops, moved, scratch=(), aliases=None, limit=6):
    return pl.pallas_call(
        kernel,
        in_specs=in_specs,
        out_shape=out_shape,
        out_specs=out_specs,
        scratch_shapes=list(scratch),
        input_output_aliases=aliases or {},
        cost_estimate=pl.CostEstimate(flops=flops, bytes_accessed=moved, transcendentals=0),
        compiler_params=pltpu.CompilerParams(vmem_limit_bytes=limit << 20),
    )


def resident(spectrum, land_mask, ice_mask, wind_u, wind_v, depth):
    local_comp, rows, lanes = spectrum.shape
    freqs = local_comp // ND
    members = lax.axis_size("comp")
    member = lax.axis_index("comp").astype(jnp.int32).reshape(1)
    scalars, lane_table, row_table = numpy_tables(members, freqs)
    scalars, lane_table, row_table = map(jnp.asarray, (scalars, lane_table, row_table))
    cells = rows * lanes
    row_message = 2 * 18 * freqs + CORNERS
    block = (freqs, ND, rows, lanes)
    spectrum = spectrum.reshape(block)

    growth, wet, swap_side, other_side, swap_row, other_row, edges = call(
        functools.partial(pack_kernel, freqs),
        [SMEM] + [HBM] * 7,
        (
            in_any(ND, rows, lanes),
            in_any(rows, lanes),
            in_any(GROUPS // 2, rows, lanes),
            in_any(GROUPS // 2, rows, lanes),
            in_any(row_message, lanes),
            in_any(row_message, lanes),
            in_any(2 * 18 * freqs * SUB, lanes),
        ),
        (VMEM,) * 7,
        flops=local_comp * cells * 4,
        moved=local_comp * cells * 4,
        scratch=[
            pltpu.VMEM((local_comp * rows, lanes), jnp.float32),
            pltpu.VMEM((GROUPS // 2, rows, lanes), jnp.float32),
            pltpu.VMEM((GROUPS // 2, rows, lanes), jnp.float32),
            pltpu.VMEM(lane_table.shape[1:], jnp.float32),
            pltpu.VMEM(row_table.shape[1:], jnp.float32),
            pltpu.VMEM((rows, lanes), jnp.int32),
            pltpu.VMEM((rows, lanes), jnp.int32),
            pltpu.VMEM((rows, lanes), jnp.float32),
            pltpu.VMEM((rows, lanes), jnp.float32),
            pltpu.SemaphoreType.DMA((6,)),
            pltpu.SemaphoreType.DMA((GROUPS, SHARES)),
        ],
        limit=30,
    )(
        member,
        *map(in_hbm, (lane_table, row_table, land_mask, ice_mask, wind_u, wind_v, spectrum)),
    )

    def main_part(start, stop, *before):
        return call(
            functools.partial(main_kernel, freqs, start, stop),
            [SMEM, SMEM, VMEM, VMEM, HBM] + ([ANY, VMEM, VMEM, VMEM, VMEM] if before else []),
            (
                in_vmem(*block),
                in_any(freqs * rows, lanes),
                in_any(freqs * rows, lanes),
                in_any(rows, lanes),
            ),
            (VMEM,) * 4,
            flops=local_comp * cells * 16 * (stop - start) // freqs,
            moved=local_comp * cells * 8 * (stop - start) // freqs,
            scratch=[
                pltpu.VMEM((AHEAD, ND, rows, lanes), jnp.float32),
                pltpu.SemaphoreType.DMA((AHEAD, PIECES)),
            ]
            + [pltpu.VMEM((rows + 2 * SUB, lanes), jnp.float32)] * 8,
            aliases={6 + index: index for index in range(4)} if before else {},
            limit=12,
        )(member, scalars, wet, growth, in_hbm(spectrum), *before)

    early = max(1, freqs // 3)
    swap_side, other_side = swap(swap_side, "sect", 0), swap(other_side, "sect", 1)
    kept, *partial = main_part(0, early)
    swap_row, other_row = call(
        functools.partial(corner_kernel, freqs),
        [VMEM, VMEM, VMEM, ANY, ANY, ANY],
        (in_any(row_message, lanes), in_any(row_message, lanes)),
        (ANY, ANY),
        flops=100,
        moved=1 << 15,
        scratch=[pltpu.VMEM((2, CORNERS, lanes), jnp.float32), pltpu.SemaphoreType.DMA((2,))],
        aliases={3: 0, 4: 1},
    )(wet, swap_side, other_side, swap_row, other_row, partial[-1])
    swapped_row = swap(swap_row, "slab", 0)
    other_row = swap(other_row, "slab", 1)
    kept, a_sums, b_sums, energy = main_part(early, freqs, swap_row, kept, *partial)

    columns, edges, energy = call(
        functools.partial(enter_kernel, freqs),
        [SMEM] + [VMEM] * 9,
        (
            in_any(GROUPS, rows, lanes),
            in_any(2 * 18 * freqs * SUB, lanes),
            in_any(rows, lanes),
        ),
        (VMEM,) * 3,
        flops=cells * 600,
        moved=cells * 200,
        aliases={8: 1, 9: 2},
    )(
        member, lane_table, row_table, wet, swap_side, other_side, swapped_row, other_row, edges,
        energy,
    )
    energy_there = others_sum(energy, "comp")
    a_sums, b_sums = call(
        functools.partial(entered_kernel, freqs),
        [SMEM] + [VMEM] * 10,
        (in_any(freqs * rows, lanes), in_any(freqs * rows, lanes)),
        (VMEM,) * 2,
        flops=cells * 600,
        moved=cells * 200,
        aliases={9: 0, 10: 1},
    )(
        member, lane_table, row_table, ice_mask, wind_u, wind_v, growth, columns, edges,
        a_sums, b_sums,
    )

    sums, ratios = call(
        functools.partial(stress_kernel, freqs),
        [SMEM, SMEM] + [VMEM] * 5,
        (in_any(3, rows, lanes), in_any(freqs, rows, lanes)),
        (VMEM, VMEM),
        flops=cells * freqs * 12,
        moved=cells * freqs * 8,
    )(member, scalars, wet, a_sums, b_sums, energy, energy_there)
    sums, stress = call(
        total_kernel,
        [VMEM, VMEM],
        (in_any(3, rows, lanes), in_any(2, rows, lanes)),
        (VMEM, VMEM),
        flops=cells * 3,
        moved=cells * 44,
    )(sums, others_sum(sums, "comp"))
    beside, first, second = call(
        strip_kernel,
        [VMEM, VMEM, VMEM],
        (in_any(2, rows, lanes), in_any(2, SUB, 2 * lanes), in_any(2, SUB, 2 * lanes)),
        (VMEM, VMEM, VMEM),
        flops=cells * 4,
        moved=cells * 36,
    )(stress, swap(stress, "sect", 0), swap(stress, "sect", 1))
    aside, beyond = swap(first, "slab", 0), swap(second, "slab", 1)

    result, level = call(
        functools.partial(final_kernel, freqs),
        [SMEM, SMEM] + [VMEM] * 10,
        (in_any(*block), in_any(rows, lanes)),
        (HBM, VMEM),
        flops=local_comp * cells * 6,
        moved=local_comp * cells * 8,
        scratch=[
            pltpu.VMEM((rows, lanes), jnp.float32),
            pltpu.VMEM((GROUPS, rows, lanes), jnp.float32),
            pltpu.SemaphoreType.DMA((RINGS, 4)),
        ]
        + [pltpu.VMEM((ND, rows, lanes), jnp.float32)] * RINGS,
        limit=12,
    )(
        member, scalars, depth, ratios, sums, beside, aside, beyond, growth, kept,
        columns, edges,
    )
    return result.reshape(local_comp, rows, lanes), level


def local(spectrum, *fields):
    local_comp, rows, lanes = spectrum.shape
    whole_rings = local_comp % ND == 0 and GROUP * 2 * (local_comp // ND) < LANES - 1
    if whole_rings and lanes == LANES and rows % SUB == 0:
        return resident(spectrum, *fields)
    return general(spectrum, *fields)


def solution(mesh):
    in_specs = (
        P("comp", "slab", "sect"),
        P("slab", "sect"),
        P("slab", "sect"),
        P("slab", "sect"),
        P("slab", "sect"),
        P("slab", "sect"),
    )
    out_specs = (P("comp", "slab", "sect"), P("slab", "sect"))
    return jax.shard_map(local, mesh=mesh, in_specs=in_specs, out_specs=out_specs, check_vma=False)
```

```python
import functools
import math

import jax
import jax.numpy as jnp
import numpy as np
from jax import lax
from jax.experimental import pallas as pl
from jax.experimental.pallas import tpu as pltpu
from jax.sharding import PartitionSpec as P

ND = 36
NF = 36
STEPS = 2
JAC = 4


def extended(cells, sides, width):
    for axis, dim in sides:
        count = lax.axis_size(axis)
        ends = count - 1
        head = lax.slice_in_dim(cells, 0, width, axis=dim)
        tail = lax.slice_in_dim(cells, cells.shape[dim] - width, cells.shape[dim], axis=dim)
        cells = jnp.concatenate(
            [
                lax.ppermute(tail, axis, [(i, (i + 1) % count) for i in range(ends)]),
                cells,
                lax.ppermute(head, axis, [((i + 1) % count, i) for i in range(ends)]),
            ],
            axis=dim,
        )
    return cells


def tables(index):
    freq_index = (index // ND).astype(jnp.float32)
    angle_index = (index % ND).astype(jnp.float32)
    heading = 2.0 * math.pi * angle_index / ND
    return (
        jnp.cos(heading),
        jnp.sin(heading),
        jnp.power(1.1, -freq_index),
        jnp.power(1.1, freq_index - (NF - 1)),
        0.5 + 0.5 * freq_index / (NF - 1),
    )


def column(values):
    return values[:, None, None]


def advect(spectra, wet_cells, speed_x, speed_y):
    padded = extended(spectra, (("slab", 1), ("sect", 2)), 1)
    upper_rows = padded[:, :-2, 1:-1]
    lower_rows = padded[:, 2:, 1:-1]
    left_cells = padded[:, 1:-1, :-2]
    right_cells = padded[:, 1:-1, 2:]
    change = (
        jnp.maximum(speed_x, 0.0) * (spectra - upper_rows)
        + jnp.minimum(speed_x, 0.0) * (lower_rows - spectra)
        + jnp.maximum(speed_y, 0.0) * (spectra - left_cells)
        + jnp.minimum(speed_y, 0.0) * (right_cells - spectra)
    )
    return (spectra - change) * wet_cells


def forcing(spectra, energy, wind_east, wind_north, ice_cover, cosine, sine, high_ratio):
    project = cosine * wind_east + sine * wind_north
    growth = 0.5 * high_ratio * jnp.square(jnp.maximum(project, 0.0)) * (1.0 - ice_cover)
    return spectra * (1.0 + growth) / (1.0 + 2.0 * high_ratio * jnp.square(energy))


def stress_weights(cosine, sine, shoaling):
    return jnp.stack(
        [shoaling * (cosine * cosine + 1.0) - 0.5, shoaling * (sine * sine + 1.0) - 0.5]
    )


def surge_solve(stress):
    padded = extended(stress, (("slab", 1), ("sect", 2)), 1)
    source_term = -(
        padded[0, 2:, 1:-1]
        + padded[0, :-2, 1:-1]
        - 2.0 * stress[0]
        + (padded[1, 1:-1, 2:] + padded[1, 1:-1, :-2] - 2.0 * stress[1])
    )
    surge_level = source_term / 4.5
    for _ in range(JAC):
        neighbours = extended(surge_level, (("slab", 0), ("sect", 1)), 1)
        surge_level = (
            source_term
            + neighbours[2:, 1:-1]
            + neighbours[:-2, 1:-1]
            + neighbours[1:-1, 2:]
            + neighbours[1:-1, :-2]
        ) / 4.5
    return surge_level


def general(spectrum, land_mask, ice_mask, wind_u, wind_v, depth):
    groups = lax.axis_size("comp")
    member = lax.axis_index("comp")
    local_comp, block_rows, block_cols = spectrum.shape
    point_rows = block_rows // groups
    total_comp = ND * NF
    wet_cells = (1 - land_mask).astype(jnp.float32)
    ice_cover = ice_mask.astype(jnp.float32)

    def own_rows(values):
        return lax.dynamic_slice_in_dim(values, member * point_rows, point_rows, values.ndim - 2)

    own_index = member * local_comp + jnp.arange(local_comp, dtype=jnp.int32)
    cosine, sine, low_ratio, high_ratio, shoaling = tables(own_index)
    spectra = spectrum * wet_cells
    for _ in range(STEPS):
        spectra = advect(
            spectra, wet_cells, column(0.7 * low_ratio * cosine), column(0.7 * low_ratio * sine)
        )
    points = lax.all_to_all(spectra, "comp", split_axis=1, concat_axis=0, tiled=True)
    cosine_full, sine_full, _, high_full, shoal_full = tables(
        jnp.arange(total_comp, dtype=jnp.int32)
    )
    energy = jnp.sum(points, axis=0) / total_comp
    sourced = forcing(
        points,
        energy,
        own_rows(wind_u),
        own_rows(wind_v),
        own_rows(ice_cover),
        column(cosine_full),
        column(sine_full),
        column(high_full),
    )
    stress = (
        jnp.einsum(
            "sk,krc->src",
            stress_weights(cosine_full, sine_full, shoal_full),
            sourced,
            precision=lax.Precision.HIGHEST,
        )
        / total_comp
    )
    stress_block = lax.all_gather(stress, "comp", axis=1, tiled=True)
    level_block = surge_solve(stress_block)
    final_energy = jnp.sum(sourced, axis=0) / total_comp
    damped = sourced / (
        1.0 + 4.0 * final_energy / (jnp.square(own_rows(depth) + own_rows(level_block)) + 1.0)
    )
    result = lax.all_to_all(damped, "comp", split_axis=0, concat_axis=1, tiled=True)
    return (result, level_block)


LANES = 128
SUB = 8
CLASSES = 10
KINDS = 5
GROUP = 3
GROUPS = ND // GROUP
CORNERS = 8


def class_of(direction):
    folded = direction % 18
    return folded if folded <= 9 else 18 - folded


def heads_down(direction):
    return direction < 9 or direction >= 27


def heads_right(direction):
    return direction < 18


def row_slot(direction):
    if direction < 9:
        return direction
    return direction - 18 if direction >= 27 else direction - 9


def numpy_tables(members, freqs):
    j = np.arange(members * freqs, dtype=np.float64)
    heading = 2.0 * np.pi * np.arange(ND) / ND
    cosine, sine = np.cos(heading), np.sin(heading)
    low = 1.1 ** (-j)
    high = 1.1 ** (j - (NF - 1))
    shoal = 0.5 + 0.5 * j / (NF - 1)
    step_x = 0.7 * low[:, None] * np.abs(cosine)
    step_y = 0.7 * low[:, None] * np.abs(sine)
    keep = 1.0 - step_x - step_y
    alpha, beta, scale = step_x / keep, step_y / keep, keep * keep
    classes = np.arange(CLASSES)
    square = np.broadcast_to(cosine * cosine, alpha.shape)
    scalars = np.stack(
        [
            alpha[:, classes],
            beta[:, classes],
            scale[:, classes],
            np.broadcast_to(high[:, None], (j.size, CLASSES)),
            np.broadcast_to(shoal[:, None], (j.size, CLASSES)),
        ],
        axis=-1,
    ).astype(np.float32)

    kinds = np.stack(
        [
            2.0 * beta,
            beta * beta,
            alpha * beta,
            scale,
            scale * square,
            np.broadcast_to(high[:, None], alpha.shape),
            np.broadcast_to(cosine, alpha.shape),
            np.broadcast_to(sine, alpha.shape),
        ]
    )
    lanes = np.zeros((members, GROUPS, 8, LANES), np.float32)
    packed = kinds.reshape(8, members, freqs, GROUPS, GROUP)
    packed = np.repeat(packed.transpose(1, 3, 0, 4, 2), 2, axis=-1)
    lanes[..., : GROUP * 2 * freqs] = packed.reshape(members, GROUPS, 8, -1)

    rows = np.stack(
        [2.0 * alpha, alpha * alpha, alpha * beta, scale, np.broadcast_to(high[:, None], alpha.shape)]
    )[:, :, classes]
    rows = rows.reshape(5, members, freqs, CLASSES).transpose(1, 3, 0, 2)
    rows = np.broadcast_to(rows[..., None], rows.shape + (LANES,)).astype(np.float32)
    return scalars.reshape(-1), lanes, rows


def odd_position(axis):
    return lax.rem(lax.axis_index(axis), 2) == 1


def iota(shape, axis):
    return lax.broadcasted_iota(jnp.int32, shape, axis)


def spread(values, column):
    return jnp.broadcast_to(values[:, column : column + 1], values.shape)


def shift_rows(values, step):
    rows = values.shape[0]
    edge = 0 if step > 0 else rows - 1
    moved = pltpu.roll(values, step % rows, 0)
    return jnp.where(iota(values.shape, 0) == edge, 0.0, moved)


def shift_lanes(values, step):
    lanes = values.shape[1]
    edge = 0 if step > 0 else lanes - 1
    moved = pltpu.roll(values, step % lanes, 1)
    return jnp.where(iota(values.shape, 1) == edge, 0.0, moved)


DEPTH = 3


def sides(quadrant):
    return 1 if quadrant in (0, 3) else -1, 1 if quadrant in (0, 1) else -1


def pack_kernel(
    freqs, member_ref, lanes_hbm, table_hbm, land_hbm, ice_hbm, east_hbm, north_hbm, spectrum_ref,
    growth_ref, wet_ref, swap_side_ref, other_side_ref, swap_row_ref, other_row_ref, edges_ref,
    kept_ref, right_ref, left_ref, lanes_ref, table_ref, land_ref, ice_ref, east_ref, north_ref, small_sems, sems,
):
    member = member_ref[0]
    small = [
        pltpu.make_async_copy(source, target, small_sems.at[index])
        for index, (source, target) in enumerate(
            (
                (land_hbm, land_ref),
                (ice_hbm, ice_ref),
                (east_hbm, east_ref),
                (north_hbm, north_ref),
                (lanes_hbm.at[member], lanes_ref),
                (table_hbm.at[member], table_ref),
            )
        )
    ]
    for copy in small:
        copy.start()

    rows = land_ref.shape[0]
    blocks_ref = kept_ref.reshape(freqs, ND, rows, LANES)

    def fetch(group):
        part = (slice(None), pl.ds(group * GROUP, GROUP))
        return pltpu.make_async_copy(spectrum_ref.at[part], blocks_ref.at[part], sems.at[group])

    for group in range(DEPTH):
        fetch(group).start()
    edges_ref[...] = jnp.zeros_like(edges_ref)
    for copy in small:
        copy.wait()

    wet_cells = (1 - land_ref[...]).astype(jnp.float32)
    wet_ref[...] = wet_cells
    open_water = 0.5 * (1.0 - ice_ref[...].astype(jnp.float32))
    shape = wet_cells.shape
    tiles = rows // SUB
    for direction in range(ND):
        angle = 2.0 * math.pi * direction / ND
        project = math.cos(angle) * east_ref[...] + math.sin(angle) * north_ref[...]
        growth_ref[direction] = open_water * jnp.square(jnp.maximum(project, 0.0))

    lane = iota(shape, 1)
    even = lane % 2 == 0
    tile_lane = iota((SUB, LANES), 1)
    for row_ref in (swap_row_ref, other_row_ref):
        row_ref[pl.ds(2 * 18 * freqs, CORNERS), :] = jnp.zeros((CORNERS, LANES), jnp.float32)
    odd_sect, odd_slab = odd_position("sect"), odd_position("slab")

    half = GROUPS // 2

    def gather_all(to_right):
        target_ref = right_ref if to_right else left_ref

        def gather(index, carry):
            group = index + (0 if to_right else half)
            fetch(group).wait()

            @pl.when(group + DEPTH < GROUPS)
            def _():
                fetch(group + DEPTH).start()

            packed = [jnp.zeros((SUB, LANES), jnp.float32) for _ in range(tiles)]
            for i in range(GROUP):
                for j in range(freqs):
                    place = i * 2 * freqs + 2 * j
                    here = (tile_lane >= place) & (tile_lane < place + 2)
                    turn = (place + 2 if to_right else place) % LANES
                    first = pl.multiple_of((j * ND + group * GROUP + i) * rows, SUB)
                    for tile in range(tiles):
                        cells = kept_ref[pl.ds(first + tile * SUB, SUB), :]
                        packed[tile] = jnp.where(here, pltpu.roll(cells, turn, 1), packed[tile])
            for tile in range(tiles):
                target_ref[index, tile * SUB : (tile + 1) * SUB, :] = packed[tile]
            return carry

        lax.fori_loop(0, half, gather, 0)

    def side_message(group):
        to_right, fore = group < half, 1 if heads_down(group * GROUP) else -1
        ahead, behind = (LANES - 1, LANES - 2) if to_right else (0, 1)
        wet_near, wet_far = spread(wet_cells, ahead), spread(wet_cells, behind)
        near_even = not to_right
        packed = right_ref[group] if to_right else left_ref[group - half]
        values = packed * jnp.where(even == near_even, wet_near, wet_far)
        near = pltpu.roll(values, 1 if near_even else LANES - 1, 1)
        table = lanes_ref[group]
        follow = wet_near * (table[1:2] * values + table[2:3] * shift_rows(near, fore))
        message = jnp.where(even == near_even, values, follow)
        return jnp.where(lane == LANES - 1, wet_near, message)

    def row_message(direction):
        to_down = heads_down(direction)
        near_row, far_row = (rows - 1, rows - 2) if to_down else (0, 1)
        wet_near = wet_cells[near_row : near_row + 1, :]
        wet_far = wet_cells[far_row : far_row + 1, :]
        table = table_ref.at[class_of(direction)]
        near = kept_ref[pl.ds(direction * rows + near_row, freqs, stride=ND * rows), :] * wet_near
        far = kept_ref[pl.ds(direction * rows + far_row, freqs, stride=ND * rows), :] * wet_far
        beside = shift_lanes(near, 1 if heads_right(direction) else -1)
        return near, wet_near * (table[1] * far + table[2] * beside)

    def row_messages(slots):
        for slot in slots:
            pairs = zip(row_message(by_slot[True, slot]), row_message(by_slot[False, slot]))
            for which, (down, up) in enumerate(pairs):
                first = (which * 18 + slot) * freqs
                swap_row_ref[first : first + freqs, :] = jnp.where(odd_slab, up, down)
                other_row_ref[first : first + freqs, :] = jnp.where(odd_slab, down, up)

    by_slot = {(heads_down(d), row_slot(d)): d for d in range(ND)}
    gather_all(True)
    rights = [side_message(index) for index in range(half)]
    for index in range(half):
        right_ref[index] = rights[index]
    row_messages(range(9))
    gather_all(False)
    for index in range(half):
        right, left = right_ref[index], side_message(index + half)
        swap_side_ref[index] = jnp.where(odd_sect, left, right)
        other_side_ref[index] = jnp.where(odd_sect, right, left)
    row_messages(range(9, 18))


def corner_kernel(
    freqs, wet_ref, swapped_ref, other_ref, swap_in, other_in, _after, swap_row_ref, other_row_ref,
    rows_ref, sems,
):
    rows = wet_ref.shape[0]
    odd_sect, odd_slab = odd_position("sect"), odd_position("slab")
    last = iota((1, LANES), 1) == LANES - 1
    rows_ref[...] = jnp.zeros_like(rows_ref)
    for i in range(6):
        from_left = i < 3
        column = 0 if from_left else LANES - 1
        ends = []
        for row, index in ((rows - 1, i), (0, i + 3 if from_left else i - 3)):
            swapped = swapped_ref[index, row : row + 1, :]
            other = other_ref[index, row : row + 1, :]
            came = jnp.where(odd_sect == from_left, swapped, other)
            own = jnp.broadcast_to(wet_ref[row : row + 1, column : column + 1], (1, LANES))
            ends.append(jnp.where(last, own, came))
        rows_ref[0, i : i + 1, :] = jnp.where(odd_slab, *ends[::-1])
        rows_ref[1, i : i + 1, :] = jnp.where(odd_slab, *ends)
    start = 2 * 18 * freqs
    copies = [
        pltpu.make_async_copy(
            rows_ref.at[which], ref.at[pl.ds(start, CORNERS), :], sems.at[which]
        )
        for which, ref in ((0, swap_row_ref), (1, other_row_ref))
    ]
    for copy in copies:
        copy.start()
    for copy in copies:
        copy.wait()


AHEAD = 3


def main_kernel(
    freqs, start, stop, member_ref, scalar_ref, wet_ref, growth_ref, spectrum_ref, *refs
):
    if start:
        _after, _kept_in, a_in, b_in, energy_in, *refs = refs
    kept_ref, a_ref, b_ref, energy_ref, ring_ref, sems, *first_refs = refs
    member = member_ref[0]
    nought = jnp.minimum(member, 0)
    rows = wet_ref.shape[0]
    tiles = rows // SUB

    def fetch(j):
        slot = lax.rem(j, AHEAD)
        return pltpu.make_async_copy(spectrum_ref.at[j], ring_ref.at[slot], sems.at[slot])

    for j in range(start, min(start + AHEAD, stop)):
        fetch(jnp.int32(j)).start()

    lane = iota((SUB, LANES), 1)
    sub = iota((SUB, LANES), 0)
    not_first = jnp.where(lane == 0, 0.0, 1.0)
    not_last = jnp.where(lane == LANES - 1, 0.0, 1.0)
    top, bottom = sub == 0, sub == SUB - 1
    energy_ref[...] = energy_in[...] if start else jnp.zeros_like(energy_ref)
    for first_ref in first_refs:
        first_ref[...] = jnp.zeros_like(first_ref)

    def tile_at(tile):
        return pl.ds(tile * SUB, SUB)

    def row_shift(quadrant):
        return -1 if quadrant in (0, 3) else 1

    def parts_of(kind):
        if kind == 0:
            return ((0, 0, 0), (9, 1, 9), (18, 2, 0), (27, 3, 9))
        return ((kind, 0, kind), (18 - kind, 1, kind), (18 + kind, 2, kind), (36 - kind, 3, kind))

    def frequency(j, carry):
        fetch(j).wait()
        slot = lax.rem(j, AHEAD)
        sums = [[None] * tiles for _ in range(3)]

        def add(which, t, value):
            have = sums[which][t]
            sums[which][t] = value if have is None else have + value
        base = (member * freqs + j) * CLASSES * KINDS
        at = [pl.ds(pl.multiple_of(j * rows, SUB) + t * SUB, SUB) for t in range(tiles)]

        def speeds(part):
            at_class = base + part[2] * KINDS
            beta = scalar_ref[at_class + 1]
            return scalar_ref[at_class], beta * (not_first if part[1] in (0, 1) else not_last)

        def beside(cells, quadrant):
            return pltpu.roll(cells, 1 if quadrant in (0, 1) else LANES - 1, 1)

        def first_step(kind):
            parts = parts_of(kind)
            speed = [speeds(part) for part in parts]
            wet = [wet_ref[tile_at(t), :] for t in range(tiles)]
            for (direction, quadrant, _), (alpha, across) in zip(parts, speed):
                shift = row_shift(quadrant)
                edge = top if shift < 0 else bottom
                target = first_refs[kind % 2 * 4 + quadrant]
                cells = [ring_ref[slot, direction, tile_at(t), :] * wet[t] for t in range(tiles)]
                turned = [pltpu.roll(cells[t], -shift % SUB, 0) for t in range(tiles)]
                for t in range(tiles):
                    before = turned[t + shift] if 0 <= t + shift < tiles else 0.0
                    ahead = jnp.where(edge, before, turned[t])
                    after = cells[t] + alpha * ahead + across * beside(cells[t], quadrant)
                    target[tile_at(t + 1), :] = wet[t] * after

        def second_step(kind):
            parts = parts_of(kind)
            scale, high = scalar_ref[base + kind * KINDS + 2], scalar_ref[base + 3]
            scaled_high = scale * high
            speed = [speeds(part) for part in parts]
            for t in range(tiles):
                moved, grown = [], []
                for (direction, quadrant, _), (alpha, across) in zip(parts, speed):
                    source = first_refs[kind % 2 * 4 + quadrant]
                    cells = source[tile_at(t + 1), :]
                    ahead = source[pl.ds((t + 1) * SUB + row_shift(quadrant) + nought, SUB), :]
                    after = cells + alpha * ahead + across * beside(cells, quadrant)
                    kept_ref[j, direction, tile_at(t), :] = after
                    moved.append(after)
                    grown.append(growth_ref[direction, tile_at(t), :] * after)
                if kind == 0:
                    plain_x, plain_y = scale * (moved[0] + moved[2]), scale * (moved[1] + moved[3])
                    grown_x = plain_x + scaled_high * (grown[0] + grown[2])
                    grown_y = plain_y + scaled_high * (grown[1] + grown[3])
                    square = math.cos(0.5 * math.pi) ** 2
                    add(0, t, plain_x + plain_y)
                    add(1, t, grown_x + grown_y)
                    add(2, t, grown_x + square * grown_y)
                else:
                    plain = scale * ((moved[0] + moved[1]) + (moved[2] + moved[3]))
                    whole = plain + scaled_high * ((grown[0] + grown[1]) + (grown[2] + grown[3]))
                    square = math.cos(2.0 * math.pi * kind / ND) ** 2
                    add(0, t, plain)
                    add(1, t, whole)
                    add(2, t, square * whole)

        first_step(0)
        for kind in range(CLASSES - 1):
            if kind + 1 < CLASSES - 1:
                first_step(kind + 1)
            second_step(kind)
        for t in range(tiles):
            energy_ref[tile_at(t), :] += sums[0][t]
            a_ref[at[t], :] = sums[1][t]
            b_ref[at[t], :] = sums[2][t]

        @pl.when(j + AHEAD < stop)
        def _():
            fetch(j + AHEAD).start()

        return carry

    lax.fori_loop(start, stop, frequency, 0)


def edge_rows(freqs, to_down, direction, at):
    first = ((0 if to_down else 18) + row_slot(direction)) * freqs * SUB
    return pl.ds(first + at, freqs, stride=SUB)


def enter_kernel(
    freqs, member_ref, lanes_ref, table_ref, wet_ref, swap_side_ref, other_side_ref, swap_row_ref,
    other_row_ref, _edges_in, energy_in, columns_ref, edges_ref, energy_ref,
):
    member = member_ref[0]
    wet_cells = wet_ref[...]
    shape = wet_cells.shape
    rows = shape[0]
    lane = iota(shape, 1)
    row = iota(shape, 0)
    even = lane % 2 == 0
    width = 2 * freqs
    used = lane < GROUP * width
    energy = energy_in[...]
    start = 2 * 18 * freqs
    odd_sect, odd_slab = odd_position("sect"), odd_position("slab")

    def from_rows(to_down, part):
        return jnp.where(odd_slab == to_down, swap_row_ref[part, :], other_row_ref[part, :])

    for to_right in (True, False):
        near_column, far_column = (0, 1) if to_right else (LANES - 1, LANES - 2)
        near_even = to_right
        wet_near, wet_far = spread(wet_cells, near_column), spread(wet_cells, far_column)
        total = jnp.zeros(shape, jnp.float32)
        for index in range(GROUPS // 2):
            group = index if to_right else index + GROUPS // 2
            to_down = heads_down(group * GROUP)
            fore = 1 if to_down else -1
            message = jnp.where(odd_sect == to_right, swap_side_ref[index], other_side_ref[index])
            table = lanes_ref[member, group]
            turn = LANES - 1 if near_even else 1
            entered = pltpu.roll(message, turn, 1)
            corner_index = index if to_down else (index - 3 if to_right else index + 3)
            corner = from_rows(to_down, slice(start + corner_index, start + corner_index + 1))
            edge = 0 if to_down else rows - 1
            paths = corner[:, LANES - 1 :] + message[edge : edge + 1, LANES - 1 :]
            corner = pltpu.roll(jnp.broadcast_to(corner, (SUB, LANES)), turn, 1)[0:1]
            corner = jnp.broadcast_to(paths, (1, LANES)) * corner
            diagonal = shift_rows(wet_near * entered, fore)
            diagonal = jnp.where(row == edge, jnp.broadcast_to(corner, shape), diagonal)
            near = wet_near * (table[0:1] * entered + message + table[2:3] * diagonal)
            far = wet_near * wet_far * (table[1:2] * message)
            change = jnp.where(used, jnp.where(even == near_even, near, far), 0.0)
            columns_ref[group] = change
            total += table[3:4] * change
        total += pltpu.roll(total, LANES - width, 1) + pltpu.roll(total, LANES - 2 * width, 1)
        target = 0 if to_right else LANES - 2
        inside = (lane >= target) & (lane < target + 2)
        for j in range(freqs):
            turned = pltpu.roll(total, (target - 2 * j) % LANES, 1)
            energy += jnp.where(inside, turned, 0.0)
    energy_ref[...] = energy

    for to_down in (True, False):
        near_row, far_row = (0, 1) if to_down else (rows - 1, rows - 2)
        wet_near = wet_cells[near_row : near_row + 1, :]
        wet_both = wet_near * wet_cells[far_row : far_row + 1, :]
        totals = [jnp.zeros((freqs, LANES), jnp.float32) for _ in range(2)]
        for direction in range(ND):
            if heads_down(direction) != to_down:
                continue
            slot = row_slot(direction) * freqs
            entered = from_rows(to_down, slice(slot, slot + freqs))
            follow = from_rows(to_down, slice(18 * freqs + slot, 18 * freqs + slot + freqs))
            table = table_ref.at[member, class_of(direction)]
            side = 1 if heads_right(direction) else -1
            diagonal = shift_lanes(wet_near * entered, side)
            near = wet_near * (table[0] * entered + follow + table[2] * diagonal)
            far = wet_both * (table[1] * entered)
            for place, (change, at) in enumerate(((near, near_row), (far, far_row))):
                edges_ref[edge_rows(freqs, to_down, direction, at % SUB), :] = change
                totals[place] += table[3] * change
        for total, at in zip(totals, (near_row, far_row)):
            energy_ref[at : at + 1, :] += jnp.sum(total, axis=0, keepdims=True)


def entered_kernel(
    freqs, member_ref, lanes_ref, table_ref, ice_ref, east_ref, north_ref, growth_ref, columns_ref,
    edges_ref, a_in, b_in, a_ref, b_ref,
):
    member = member_ref[0]
    shape = ice_ref.shape
    rows = shape[0]
    lane = iota(shape, 1)
    even = lane % 2 == 0
    width = 2 * freqs
    a_ref[...] = a_in[...]
    b_ref[...] = b_in[...]

    for to_right in (True, False):
        near_column, far_column = (0, 1) if to_right else (LANES - 1, LANES - 2)

        def packed_field(values):
            return jnp.where(
                even == to_right, spread(values, near_column), spread(values, far_column)
            )

        east, north = packed_field(east_ref[...]), packed_field(north_ref[...])
        open_water = 0.5 * (1.0 - packed_field(ice_ref[...].astype(jnp.float32)))
        sums = [jnp.zeros(shape, jnp.float32) for _ in range(2)]
        for index in range(GROUPS // 2):
            group = index if to_right else index + GROUPS // 2
            table = lanes_ref[member, group]
            project = table[6:7] * east + table[7:8] * north
            growth = open_water * jnp.square(jnp.maximum(project, 0.0))
            grown = columns_ref[group] * (1.0 + table[5:6] * growth)
            sums[0] += table[3:4] * grown
            sums[1] += table[4:5] * grown
        sums = [
            part + pltpu.roll(part, LANES - width, 1) + pltpu.roll(part, LANES - 2 * width, 1)
            for part in sums
        ]
        target = 0 if to_right else LANES - 2
        inside = (lane >= target) & (lane < target + 2)
        for j in range(freqs):
            turn = (target - 2 * j) % LANES
            block = slice(j * rows, (j + 1) * rows)
            place = [jnp.where(inside, pltpu.roll(part, turn, 1), 0.0) for part in sums]
            a_ref[block, :] += place[0]
            b_ref[block, :] += place[1]

    for to_down in (True, False):
        near_row, far_row = (0, 1) if to_down else (rows - 1, rows - 2)
        totals = [jnp.zeros((freqs, LANES), jnp.float32) for _ in range(4)]
        for direction in range(ND):
            if heads_down(direction) != to_down:
                continue
            table = table_ref.at[member, class_of(direction)]
            square = math.cos(2.0 * math.pi * direction / ND) ** 2
            for place, at in enumerate((near_row, far_row)):
                change = edges_ref[edge_rows(freqs, to_down, direction, at % SUB), :]
                growth = growth_ref[direction, at : at + 1, :]
                grown = (table[3] * change) * (1.0 + table[4] * growth)
                totals[2 * place] += grown
                totals[2 * place + 1] += square * grown
        for place, at in enumerate((near_row, far_row)):
            picked = pl.ds(at, freqs, stride=rows)
            a_ref[picked, :] += totals[2 * place]
            b_ref[picked, :] += totals[2 * place + 1]


def stress_kernel(
    freqs, member_ref, scalar_ref, wet_ref, a_ref, b_ref, own_ref, other_ref, sums_ref, ratio_ref
):
    member = member_ref[0]
    wet_cells = wet_ref[...]
    rows = wet_cells.shape[0]
    energy = wet_cells * (own_ref[...] + other_ref[...]) / (ND * NF)
    square = jnp.square(energy)

    sums = [jnp.zeros(wet_cells.shape, jnp.float32) for _ in range(3)]
    for j in range(freqs):
        base = (member * freqs + j) * CLASSES * KINDS
        high, shoal = scalar_ref[base + 3], scalar_ref[base + 4]
        block = slice(j * rows, (j + 1) * rows)
        ratio = wet_cells / (1.0 + (2.0 * high) * square)
        ratio_ref[j] = ratio
        whole = ratio * a_ref[block, :]
        along = ratio * b_ref[block, :]
        sums[0] += shoal * along + (shoal - 0.5) * whole
        sums[1] += (2.0 * shoal - 0.5) * whole - shoal * along
        sums[2] += whole
    for index in range(3):
        sums_ref[index] = sums[index] / (ND * NF)


def total_kernel(own_ref, other_ref, sums_ref, stress_ref):
    sums_ref[...] = own_ref[...] + other_ref[...]
    stress_ref[...] = sums_ref[0:2]


def strip_kernel(stress_ref, swapped_ref, other_ref, beside_ref, first_ref, second_ref):
    rows = stress_ref.shape[1]
    low_half = iota((rows, LANES), 1) < LANES // 2
    odd_sect = lax.rem(lax.axis_index("sect"), 2) == 1
    odd_slab = lax.rem(lax.axis_index("slab"), 2) == 1
    for index in range(2):
        swapped, other = swapped_ref[index], other_ref[index]
        beside = jnp.where(low_half != odd_sect, swapped, other)
        beside_ref[index] = beside
        ends = [
            jnp.concatenate([values[first : first + SUB] for values in (stress_ref[index], beside)], 1)
            for first in (0, rows - SUB)
        ]
        first_ref[index] = jnp.where(odd_slab, *ends)
        second_ref[index] = jnp.where(odd_slab, *ends[::-1])


BEHIND = 12
RINGS = 6


def final_kernel(
    freqs, member_ref, scalar_ref, depth_ref, ratios_ref, sums_ref, beside_ref, swapped_ref,
    other_ref, growth_ref, kept_ref, columns_ref, edges_ref,
    result_ref, level_ref, damping_ref, turning_ref, sems, *rings,
):
    member = member_ref[0]
    rows = depth_ref.shape[0]
    slab, slabs = lax.axis_index("slab"), lax.axis_size("slab")
    sect, sects = lax.axis_index("sect"), lax.axis_size("sect")
    above_ok = jnp.where(slab > 0, 1.0, 0.0)
    below_ok = jnp.where(slab < slabs - 1, 1.0, 0.0)
    left_ok = jnp.where(sect > 0, 1.0, 0.0)
    right_ok = jnp.where(sect < sects - 1, 1.0, 0.0)

    odd = lax.rem(slab, 2) == 1

    def framed(index):
        middle = jnp.concatenate([sums_ref[index], beside_ref[index]], axis=1)
        swapped, other = swapped_ref[index], other_ref[index]
        below = jnp.where(odd, other, swapped)
        above = jnp.where(odd, swapped, other)
        return jnp.concatenate([middle, below, above], axis=0)

    def around(values, axis):
        size = values.shape[axis]
        return pltpu.roll(values, 1, axis) + pltpu.roll(values, size - 1, axis)

    stress_x, stress_y = framed(0), framed(1)
    frame = stress_x.shape
    frame_row, frame_lane = iota(frame, 0), iota(frame, 1)
    row_ok = jnp.where(frame_row < rows, 1.0, jnp.where(frame_row < rows + SUB, below_ok, above_ok))
    lane_ok = jnp.where(
        frame_lane < LANES, 1.0, jnp.where(frame_lane < LANES + LANES // 2, right_ok, left_ok)
    )
    inside = row_ok * lane_ok / 4.5
    source = -((around(stress_x, 0) - 2.0 * stress_x) + (around(stress_y, 1) - 2.0 * stress_y))
    level = inside * source
    for _ in range(JAC):
        level = inside * (source + around(level, 0) + around(level, 1))
    level = level[:rows, :LANES]
    level_ref[...] = level
    damping = 1.0 / (1.0 + 4.0 * sums_ref[2] / (jnp.square(depth_ref[...] + level) + 1.0))
    tiles = rows // SUB
    damping_ref[...] = damping
    turning_ref[...] = columns_ref[...]
    tile_lane = iota((SUB, LANES), 1)

    def send(j, which, piece):
        part = pl.ds(piece * ND // 4, ND // 4)
        return pltpu.make_async_copy(
            rings[which].at[part], result_ref.at[j, part], sems.at[which, piece]
        )

    def frequency(j, which):
        @pl.when(j >= RINGS)
        def _():
            for piece in range(4):
                send(j - RINGS, which, piece).wait()

        base = (member * freqs + j) * CLASSES * KINDS
        high = scalar_ref[base + 3]

        def damped(direction, t, ratio, high_ratio):
            to_down, to_right = sides(direction // (ND // 4))
            part = slice(t * SUB, (t + 1) * SUB)
            target = 0 if to_right > 0 else LANES - 2
            at_side = (tile_lane >= target) & (tile_lane < target + 2)
            turn = (target - direction % GROUP * 2 * freqs) % LANES
            entered = turning_ref[direction // GROUP, part, :]
            if turn:
                entered = pltpu.roll(entered, turn, 1)
            value = kept_ref[j, direction, part, :] + jnp.where(at_side, entered, 0.0)
            if t == (0 if to_down > 0 else tiles - 1):
                edge = ((0 if to_down > 0 else 18) + row_slot(direction)) * freqs + j
                value += edges_ref[pl.ds(pl.multiple_of(edge * SUB, SUB), SUB), :]
            return value * (ratio + high_ratio * growth_ref[direction, part, :])

        pending = []
        for kind in range(CLASSES - 1):
            together = (0, 9, 18, 27) if kind == 0 else (kind, 18 - kind, 18 + kind, 36 - kind)
            scale = scalar_ref[base + kind * KINDS + 2]
            for t in range(tiles):
                part = slice(t * SUB, (t + 1) * SUB)
                ratio = scale * (ratios_ref[j, part, :] * damping_ref[part, :])
                high_ratio = high * ratio
                for direction in together:
                    pending.append((direction, part, damped(direction, t, ratio, high_ratio)))
                while len(pending) > BEHIND:
                    target, place, value = pending.pop(0)
                    rings[which][target, place, :] = value
        for target, place, value in pending:
            rings[which][target, place, :] = value
        for piece in range(4):
            send(j, which, piece).start()
        turned = [pltpu.roll(turning_ref[group], LANES - 2, 1) for group in range(GROUPS)]
        for group in range(GROUPS):
            turning_ref[group] = turned[group]

    def turn(index, carry):
        for which in range(RINGS):
            frequency(RINGS * index + which, which)
        return carry

    whole_turns = freqs // RINGS
    lax.fori_loop(0, whole_turns, turn, 0)
    for j in range(whole_turns * RINGS, freqs):
        frequency(jnp.int32(j), j % RINGS)
    for j in range(max(0, freqs - RINGS), freqs):
        for piece in range(4):
            send(j, j % RINGS, piece).wait()


def swap(values, axis, first):
    count = lax.axis_size(axis)
    pairs = [(i, i + 1) for i in range(first, count - 1, 2)]
    return lax.ppermute(values, axis, pairs + [(b, a) for a, b in pairs])


def others_sum(values, axis):
    count = lax.axis_size(axis)
    total = None
    for step in range(1, count):
        part = lax.ppermute(values, axis, [(i, (i + step) % count) for i in range(count)])
        total = part if total is None else total + part
    return jnp.zeros_like(values) if total is None else total


VMEM = pl.BlockSpec(memory_space=pltpu.VMEM)
SMEM = pl.BlockSpec(memory_space=pltpu.SMEM)
HBM = pl.BlockSpec(memory_space=pltpu.HBM)
ANY = pl.BlockSpec(memory_space=pl.ANY)


def in_vmem(*shape):
    return pltpu.VMEM(shape, jnp.float32)


def in_any(*shape):
    return jax.ShapeDtypeStruct(shape, jnp.float32)


def in_hbm(values):
    return pltpu.with_memory_space_constraint(values, pltpu.HBM)


def call(kernel, in_specs, out_shape, out_specs, flops, moved, scratch=(), aliases=None, limit=6):
    return pl.pallas_call(
        kernel,
        in_specs=in_specs,
        out_shape=out_shape,
        out_specs=out_specs,
        scratch_shapes=list(scratch),
        input_output_aliases=aliases or {},
        cost_estimate=pl.CostEstimate(flops=flops, bytes_accessed=moved, transcendentals=0),
        compiler_params=pltpu.CompilerParams(vmem_limit_bytes=limit << 20),
    )


def resident(spectrum, land_mask, ice_mask, wind_u, wind_v, depth):
    local_comp, rows, lanes = spectrum.shape
    freqs = local_comp // ND
    members = lax.axis_size("comp")
    member = lax.axis_index("comp").astype(jnp.int32).reshape(1)
    scalars, lane_table, row_table = numpy_tables(members, freqs)
    scalars, lane_table, row_table = map(jnp.asarray, (scalars, lane_table, row_table))
    cells = rows * lanes
    row_message = 2 * 18 * freqs + CORNERS
    block = (freqs, ND, rows, lanes)
    spectrum = spectrum.reshape(block)

    growth, wet, swap_side, other_side, swap_row, other_row, edges = call(
        functools.partial(pack_kernel, freqs),
        [SMEM] + [HBM] * 7,
        (
            in_any(ND, rows, lanes),
            in_any(rows, lanes),
            in_any(GROUPS // 2, rows, lanes),
            in_any(GROUPS // 2, rows, lanes),
            in_any(row_message, lanes),
            in_any(row_message, lanes),
            in_any(2 * 18 * freqs * SUB, lanes),
        ),
        (VMEM,) * 7,
        flops=local_comp * cells * 4,
        moved=local_comp * cells * 4,
        scratch=[
            pltpu.VMEM((local_comp * rows, lanes), jnp.float32),
            pltpu.VMEM((GROUPS // 2, rows, lanes), jnp.float32),
            pltpu.VMEM((GROUPS // 2, rows, lanes), jnp.float32),
            pltpu.VMEM(lane_table.shape[1:], jnp.float32),
            pltpu.VMEM(row_table.shape[1:], jnp.float32),
            pltpu.VMEM((rows, lanes), jnp.int32),
            pltpu.VMEM((rows, lanes), jnp.int32),
            pltpu.VMEM((rows, lanes), jnp.float32),
            pltpu.VMEM((rows, lanes), jnp.float32),
            pltpu.SemaphoreType.DMA((6,)),
            pltpu.SemaphoreType.DMA((GROUPS,)),
        ],
        limit=30,
    )(
        member,
        *map(in_hbm, (lane_table, row_table, land_mask, ice_mask, wind_u, wind_v, spectrum)),
    )

    def main_part(start, stop, *before):
        return call(
            functools.partial(main_kernel, freqs, start, stop),
            [SMEM, SMEM, VMEM, VMEM, HBM] + ([ANY, VMEM, VMEM, VMEM, VMEM] if before else []),
            (
                in_vmem(*block),
                in_any(freqs * rows, lanes),
                in_any(freqs * rows, lanes),
                in_any(rows, lanes),
            ),
            (VMEM,) * 4,
            flops=local_comp * cells * 16 * (stop - start) // freqs,
            moved=local_comp * cells * 8 * (stop - start) // freqs,
            scratch=[
                pltpu.VMEM((AHEAD, ND, rows, lanes), jnp.float32),
                pltpu.SemaphoreType.DMA((AHEAD,)),
            ]
            + [pltpu.VMEM((rows + 2 * SUB, lanes), jnp.float32)] * 8,
            aliases={6 + index: index for index in range(4)} if before else {},
            limit=8,
        )(member, scalars, wet, growth, in_hbm(spectrum), *before)

    early = max(1, freqs // 3)
    swap_side, other_side = swap(swap_side, "sect", 0), swap(other_side, "sect", 1)
    kept, *partial = main_part(0, early)
    swap_row, other_row = call(
        functools.partial(corner_kernel, freqs),
        [VMEM, VMEM, VMEM, ANY, ANY, ANY],
        (in_any(row_message, lanes), in_any(row_message, lanes)),
        (ANY, ANY),
        flops=100,
        moved=1 << 15,
        scratch=[pltpu.VMEM((2, CORNERS, lanes), jnp.float32), pltpu.SemaphoreType.DMA((2,))],
        aliases={3: 0, 4: 1},
    )(wet, swap_side, other_side, swap_row, other_row, partial[-1])
    swapped_row = swap(swap_row, "slab", 0)
    other_row = swap(other_row, "slab", 1)
    kept, a_sums, b_sums, energy = main_part(early, freqs, swap_row, kept, *partial)

    columns, edges, energy = call(
        functools.partial(enter_kernel, freqs),
        [SMEM] + [VMEM] * 9,
        (
            in_any(GROUPS, rows, lanes),
            in_any(2 * 18 * freqs * SUB, lanes),
            in_any(rows, lanes),
        ),
        (VMEM,) * 3,
        flops=cells * 600,
        moved=cells * 200,
        aliases={8: 1, 9: 2},
    )(
        member, lane_table, row_table, wet, swap_side, other_side, swapped_row, other_row, edges,
        energy,
    )
    energy_there = others_sum(energy, "comp")
    a_sums, b_sums = call(
        functools.partial(entered_kernel, freqs),
        [SMEM] + [VMEM] * 10,
        (in_any(freqs * rows, lanes), in_any(freqs * rows, lanes)),
        (VMEM,) * 2,
        flops=cells * 600,
        moved=cells * 200,
        aliases={9: 0, 10: 1},
    )(
        member, lane_table, row_table, ice_mask, wind_u, wind_v, growth, columns, edges,
        a_sums, b_sums,
    )

    sums, ratios = call(
        functools.partial(stress_kernel, freqs),
        [SMEM, SMEM] + [VMEM] * 5,
        (in_any(3, rows, lanes), in_any(freqs, rows, lanes)),
        (VMEM, VMEM),
        flops=cells * freqs * 12,
        moved=cells * freqs * 8,
    )(member, scalars, wet, a_sums, b_sums, energy, energy_there)
    sums, stress = call(
        total_kernel,
        [VMEM, VMEM],
        (in_any(3, rows, lanes), in_any(2, rows, lanes)),
        (VMEM, VMEM),
        flops=cells * 3,
        moved=cells * 44,
    )(sums, others_sum(sums, "comp"))
    beside, first, second = call(
        strip_kernel,
        [VMEM, VMEM, VMEM],
        (in_any(2, rows, lanes), in_any(2, SUB, 2 * lanes), in_any(2, SUB, 2 * lanes)),
        (VMEM, VMEM, VMEM),
        flops=cells * 4,
        moved=cells * 36,
    )(stress, swap(stress, "sect", 0), swap(stress, "sect", 1))
    aside, beyond = swap(first, "slab", 0), swap(second, "slab", 1)

    result, level = call(
        functools.partial(final_kernel, freqs),
        [SMEM, SMEM] + [VMEM] * 10,
        (in_any(*block), in_any(rows, lanes)),
        (HBM, VMEM),
        flops=local_comp * cells * 6,
        moved=local_comp * cells * 8,
        scratch=[
            pltpu.VMEM((rows, lanes), jnp.float32),
            pltpu.VMEM((GROUPS, rows, lanes), jnp.float32),
            pltpu.SemaphoreType.DMA((RINGS, 4)),
        ]
        + [pltpu.VMEM((ND, rows, lanes), jnp.float32)] * RINGS,
        limit=12,
    )(
        member, scalars, depth, ratios, sums, beside, aside, beyond, growth, kept,
        columns, edges,
    )
    return result.reshape(local_comp, rows, lanes), level


def local(spectrum, *fields):
    local_comp, rows, lanes = spectrum.shape
    whole_rings = local_comp % ND == 0 and GROUP * 2 * (local_comp // ND) < LANES - 1
    if whole_rings and lanes == LANES and rows % SUB == 0:
        return resident(spectrum, *fields)
    return general(spectrum, *fields)


def solution(mesh):
    in_specs = (
        P("comp", "slab", "sect"),
        P("slab", "sect"),
        P("slab", "sect"),
        P("slab", "sect"),
        P("slab", "sect"),
        P("slab", "sect"),
    )
    out_specs = (P("comp", "slab", "sect"), P("slab", "sect"))
    return jax.shard_map(local, mesh=mesh, in_specs=in_specs, out_specs=out_specs, check_vma=False)
```
